32 devices in a mesh: fsdp: 8 (over z, y), tp: 4 (over x, core).
Axes of the slice: x: 2, y: 2, z: 4, core: 2. Of those that a mesh axis runs over, the one named last changes fastest.
Arguments:
- tokens: bfloat16 [2, 3072, 1600], P(None, ('fsdp', 'tp')), may hold values from -6 to 6
- qkv_weight: bfloat16 [2, 1600, 4800], P(None, 'fsdp'), may hold values from -0.15625 to 0.15625
- query_bias: bfloat16 [2, 1600], P(None, 'fsdp'), may hold values from -3 to 3
- value_bias: bfloat16 [2, 1600], P(None, 'fsdp'), may hold values from -3 to 3
- out_weight: bfloat16 [2, 1600, 1600], P(None, 'fsdp'), may hold values from -0.625 to 0.625
- out_bias: bfloat16 [2, 1600], P(None, 'fsdp'), may hold values from -3 to 3
- fc_weight: bfloat16 [2, 1600, 6400], P(None, 'fsdp', 'tp'), may hold values from -0.15625 to 0.15625
- fc_bias: bfloat16 [2, 4, 1600], P(None, 'tp', 'fsdp'), may hold values from -3 to 3
- proj_weight: bfloat16 [2, 6400, 1600], P(None, 'tp', 'fsdp'), may hold values from -0.109375 to 0.109375
- proj_bias: bfloat16 [2, 1600], P(None, 'fsdp'), may hold values from -3 to 3
- first_gain: bfloat16 [2, 1600], P(None, 'fsdp'), may hold values from 0.5 to 1.5
- first_bias: bfloat16 [2, 1600], P(None, 'fsdp'), may hold values from -3 to 3
- second_gain: bfloat16 [2, 1600], P(None, 'fsdp'), may hold values from 0.5 to 1.5
- second_bias: bfloat16 [2, 1600], P(None, 'fsdp'), may hold values from -3 to 3
- out_grad: bfloat16 [2, 3072, 1600], P(None, ('fsdp', 'tp')), may hold values from -6 to 6
Outputs:
- out_tokens: bfloat16 [2, 3072, 1600], P(None, ('fsdp', 'tp'))
- tokens_grad: float32 [2, 3072, 1600], P(None, ('fsdp', 'tp'))
- qkv_weight_grad: float32 [2, 1600, 4800], P(None, 'fsdp')
- query_bias_grad: float32 [2, 1600], P(None, 'fsdp')
- value_bias_grad: float32 [2, 1600], P(None, 'fsdp')
- out_weight_grad: float32 [2, 1600, 1600], P(None, 'fsdp')
- out_bias_grad: float32 [2, 1600], P(None, 'fsdp')
- fc_weight_grad: float32 [2, 1600, 6400], P(None, 'fsdp', 'tp')
- fc_bias_grad: float32 [2, 4, 1600], P(None, 'tp', 'fsdp')
- proj_weight_grad: float32 [2, 6400, 1600], P(None, 'tp', 'fsdp')
- proj_bias_grad: float32 [2, 1600], P(None, 'fsdp')
- first_gain_grad: float32 [2, 1600], P(None, 'fsdp')
- first_bias_grad: float32 [2, 1600], P(None, 'fsdp')
- second_gain_grad: float32 [2, 1600], P(None, 'fsdp')
- second_bias_grad: float32 [2, 1600], P(None, 'fsdp')
The draws below stay inside these ranges and needn't reach their ends.
All inputs are finite; a program needn't handle non-finite values.
Results may differ from the reference program's by a relative error of at most 0.018.
Values may be sent and summed in bfloat16 or wider, within the bound.
A program may use at most 384 MiB of HBM per device.

```python
import jax
import jax.numpy as jnp
from jax import lax

D = 1600
HEADS = 25
HEAD = 64
FF = 6400
GROUP = 8
PROMPT_DEV = 128
CONT_LEN = 256
MICRO = 2
LAYERS = 2
PROMPT = 1024
TOK_DEV = 384
ROWS = 3072
N_FSDP = 8
N_TP = 4


def block_levels(key, shape, split, smallest, largest):
    loudness, own = 1.0, jax.random.fold_in(key, 6)
    for position, shards_of in split:
        draws = jnp.exp(jax.random.uniform(jax.random.fold_in(own, position), (shards_of,), jnp.float32, smallest / len(split), largest / len(split)))
        loudness = loudness * jnp.repeat(draws, shape[position] // shards_of).reshape([-1 if axis == position else 1 for axis in range(len(shape))])
    return loudness


def gaussian(own_key, extent, width, limit, split=(), held_as=jnp.bfloat16):
    values = jax.random.normal(own_key, extent, jnp.float32) * width
    if len(split) > 0:
        values = block_levels(own_key, extent, split, -0.22, 0.18) * values
    return jnp.clip(values, min=-limit, max=limit).astype(held_as)


def setup_inputs(seed: int = 0) -> dict:
    seeds = jax.random.split(jax.random.key(seed), 16)
    tokens = gaussian(seeds[0], (MICRO, ROWS, D), 1.0, 6.0, ((1, 32),))
    qkv_weight = gaussian(seeds[1], (LAYERS, D, 3 * D), D ** -0.5, 0.15625, ((1, 8),))
    query_bias = gaussian(seeds[2], (LAYERS, D), 0.5, 3.0, ((1, 8),))
    value_bias = gaussian(seeds[3], (LAYERS, D), 0.5, 3.0, ((1, 8),))
    out_weight = gaussian(seeds[4], (LAYERS, D, D), (D // 16) ** -0.5, 0.625, ((1, 8),))
    out_bias = gaussian(seeds[5], (LAYERS, D), 0.5, 3.0, ((1, 8),))
    fc_weight = gaussian(seeds[6], (LAYERS, D, FF), D ** -0.5, 0.15625, ((1, 8), (2, 4)))
    fc_bias = gaussian(seeds[7], (LAYERS, N_TP, FF // N_TP), 0.5, 3.0, ((1, 4), (2, 8)))
    proj_weight = gaussian(seeds[8], (LAYERS, FF, D), (FF // 2) ** -0.5, 0.109375, ((1, 4), (2, 8)))
    proj_bias = gaussian(seeds[9], (LAYERS, D), 0.5, 3.0, ((1, 8),))
    first_gain = jnp.clip(1.0 + 0.1 * jax.random.normal(seeds[10], (LAYERS, D), jnp.float32), 0.5, 1.5).astype(jnp.bfloat16)
    first_bias = gaussian(seeds[11], (LAYERS, D), 0.5, 3.0, ((1, 8),))
    second_gain = jnp.clip(1.0 + 0.1 * jax.random.normal(seeds[12], (LAYERS, D), jnp.float32), 0.5, 1.5).astype(jnp.bfloat16)
    second_bias = gaussian(seeds[13], (LAYERS, D), 0.5, 3.0, ((1, 8),))
    out_grad = gaussian(seeds[14], (MICRO, ROWS, D), 1.0, 6.0, ((1, 32),))
    return {"tokens": tokens, "qkv_weight": qkv_weight, "query_bias": query_bias, "value_bias": value_bias, "out_weight": out_weight, "out_bias": out_bias, "fc_weight": fc_weight, "fc_bias": fc_bias, "proj_weight": proj_weight, "proj_bias": proj_bias, "first_gain": first_gain, "first_bias": first_bias, "second_gain": second_gain, "second_bias": second_bias, "out_grad": out_grad}


@jax.custom_vjp
def low(v):
    return lax.optimization_barrier(v.astype(jnp.bfloat16)).astype(jnp.float32)

@jax.custom_vjp
def low_back(v):
    return v

def low_keep(v):
    return (low(v), None)

def low_pass(kept, grad):
    return (grad,)

def back_keep(v):
    return (v, None)

def back_low(kept, grad):
    return (low(grad),)
low.defvjp(low_keep, low_pass)
low_back.defvjp(back_keep, back_low)
norm_eps = 1e-05

def layer_norm(x, gain, bias):
    centred = x - lax.optimization_barrier(jnp.mean(x, -1, keepdims=True))
    spread = lax.optimization_barrier(jnp.mean(centred * centred, -1, keepdims=True))
    return centred * lax.rsqrt(spread + norm_eps) * gain + bias

def product(left, right):
    return jnp.dot(left, right, precision=lax.Precision.HIGHEST)

def key_mask(rows, member):
    query_at = rows[:, None]
    key_at = lax.broadcasted_iota(jnp.int32, (1, PROMPT + CONT_LEN), 1)
    in_prompt = query_at < PROMPT_DEV
    prompt_pos = member * PROMPT_DEV + query_at
    cont_pos = query_at - PROMPT_DEV
    prompt_ok = in_prompt & (key_at <= prompt_pos)
    cont_ok = jnp.logical_not(in_prompt) & ((key_at < PROMPT) | (key_at - PROMPT <= cont_pos))
    return prompt_ok | cont_ok

def attend_block(inputs):
    query, keys, values, member = inputs
    heads_q = query.reshape(TOK_DEV, HEADS, HEAD)
    heads_k = keys.reshape(PROMPT + CONT_LEN, HEADS, HEAD)
    heads_v = values.reshape(PROMPT + CONT_LEN, HEADS, HEAD)
    scores = low_back(HEAD ** (-0.5) * jnp.einsum('qhd,khd->hqk', heads_q, heads_k, precision=lax.Precision.HIGHEST))
    allowed = key_mask(lax.iota(jnp.int32, TOK_DEV), member)
    masked = jnp.where(allowed[None], scores, -1e+30)
    probs = jax.nn.softmax(masked, axis=-1)
    mixed = jnp.einsum('hqk,khd->qhd', low(probs), heads_v, precision=lax.Precision.HIGHEST)
    return mixed.reshape(TOK_DEV, D)

def with_prompt(part):
    groups = N_FSDP // GROUP
    prompt = part[:, :, :PROMPT_DEV].reshape(MICRO, groups, PROMPT, D)
    shared = jnp.repeat(prompt, GROUP, axis=1)
    return jnp.concatenate([shared, part[:, :, PROMPT_DEV:]], axis=2)

def block(x, members, params):
    qkv_w, query_b, value_b, out_w, out_b, fc_w, fc_b, proj_w, proj_b, gain_one, bias_one, gain_two, bias_two = params
    normed = low(layer_norm(x, gain_one, bias_one))
    projected = product(normed, qkv_w) + jnp.concatenate([query_b, jnp.zeros_like(query_b), value_b])
    query = low_back(low(projected[..., :D]))
    key = low_back(low(projected[..., D:2 * D]))
    value = low_back(low(projected[..., 2 * D:]))
    keys = with_prompt(key)
    values = with_prompt(value)
    count = MICRO * N_FSDP
    mixed = lax.map(jax.checkpoint(attend_block), (query.reshape(count, TOK_DEV, D), keys.reshape(count, PROMPT + CONT_LEN, D), values.reshape(count, PROMPT + CONT_LEN, D), members))
    mixed = low_back(low(mixed.reshape(x.shape)))
    x_mid = x + low_back(product(mixed, out_w) + out_b)
    second = low(layer_norm(x_mid, gain_two, bias_two))
    hidden_pre = low_back(product(second, fc_w) + fc_b)
    hidden = low(jax.nn.gelu(hidden_pre, approximate=True))
    return x_mid + low_back(product(hidden, proj_w) + proj_b)

def reference(tokens, qkv_weight, query_bias, value_bias, out_weight, out_bias, fc_weight, fc_bias, proj_weight, proj_bias, first_gain, first_bias, second_gain, second_bias, out_grad):
    weights = [qkv_weight, query_bias, value_bias, out_weight, out_bias, fc_weight, fc_bias.reshape(LAYERS, FF), proj_weight, proj_bias, first_gain, first_bias, second_gain, second_bias]
    weights = [w.astype(jnp.float32) for w in weights]
    members = (lax.iota(jnp.int32, MICRO * N_FSDP) % GROUP).astype(jnp.int32)

    def forward(x, *params):
        state = x.reshape(MICRO, N_FSDP, TOK_DEV, D)
        for layer in range(LAYERS):
            state = block(state, members, [w[layer] for w in params])
        return state.reshape(MICRO, ROWS, D)
    result, pullback = jax.vjp(forward, tokens.astype(jnp.float32), *weights)
    grads = pullback(out_grad.astype(jnp.float32))
    return (result.astype(jnp.bfloat16), grads[0], grads[1], grads[2], grads[3], grads[4], grads[5], grads[6], grads[7].reshape(LAYERS, N_TP, FF // N_TP), grads[8], grads[9], grads[10], grads[11], grads[12], grads[13])
```

```python
import functools

import jax
import jax.numpy as jnp
from jax import lax
from jax.experimental import pallas as pl
from jax.experimental.pallas import tpu as pltpu
from jax.sharding import PartitionSpec as P

D = 1600
HEADS = 25
HEAD = 64
GROUP = 8
PROMPT_DEV = 128
CONT_LEN = 256
TOK_DEV = 384
MICRO = 2
LAYERS = 2
PROMPT = 1024
KEYS = PROMPT + CONT_LEN
CHUNK = 128

f32 = jnp.float32
bf16 = jnp.bfloat16
norm_eps = 1e-05
NN = (((1,), (0,)), ((), ()))
NT = (((1,), (1,)), ((), ()))
TN = (((0,), (0,)), ((), ()))


def mm(left, right, dims=NN):
    return lax.dot_general(left, right, dims, preferred_element_type=f32)


def swapped(value, axis, mask):
    pairs = [(source, source ^ mask) for source in range(lax.axis_size(axis))]
    return lax.ppermute(value, axis, pairs)


def layer_norm(x, gain, bias):
    centred = x - jnp.mean(x, -1, keepdims=True)
    spread = jnp.mean(centred * centred, -1, keepdims=True)
    return centred * lax.rsqrt(spread + norm_eps) * gain + bias


def gelu_tanh(value):
    return jax.nn.gelu(value, approximate=True)


def by_offset(stacked, index):
    return jnp.take(stacked, index ^ jnp.arange(stacked.shape[0]), axis=0)


def tp_gather(value):
    n = lax.axis_size("tp")
    held = value[None]
    mask = n // 2
    order = [0]
    while mask:
        held = jnp.concatenate([held, swapped(held, "tp", mask)], axis=0)
        order = order + [o ^ mask for o in order]
        mask //= 2
    place = [order.index(k) for k in range(n)]
    held = jnp.stack([held[p] for p in place])
    return by_offset(held, lax.axis_index("tp"))


def tp_scatter(parts):
    held = by_offset(parts, lax.axis_index("tp"))
    mask = 1
    while mask < lax.axis_size("tp"):
        arrived = swapped(held[1::2].astype(bf16), "tp", mask)
        held = held[0::2].astype(f32) + arrived.astype(f32)
        mask *= 2
    return held[0]


def group_gather(value, member):
    along = [value] + [swapped(value, "fsdp", k) for k in (2, 4, 6)]
    across = [swapped(piece, "fsdp", 1) for piece in along]
    stacked = jnp.stack([piece for pair in zip(along, across) for piece in pair])
    return by_offset(stacked, member)


def group_scatter(parts, member):
    held = by_offset(parts, member)
    arrived = swapped(held[1::2], "fsdp", 1)
    summed = held[0::2].astype(f32) + arrived.astype(f32)
    total = summed[0]
    for k in (1, 2, 3):
        total = total + swapped(summed[k].astype(bf16), "fsdp", 2 * k).astype(f32)
    return total


def key_limit(member):
    row = lax.broadcasted_iota(jnp.int32, (1, TOK_DEV), 1)
    return jnp.where(row < PROMPT_DEV, member * PROMPT_DEV + row, PROMPT - PROMPT_DEV + row)


def half_of(value, half):
    lane = lax.broadcasted_iota(jnp.int32, value.shape, 1)
    return jnp.where((lane >= HEAD * half) & (lane < HEAD * (half + 1)), value, jnp.zeros_like(value))


def fold(value, op):
    return op(value.reshape(value.shape[0] // 8, 8, value.shape[1]), axis=0)


N_PROMPT_CHUNKS = PROMPT // CHUNK
N_CONT_CHUNKS = CONT_LEN // CHUNK


def over_keys(body, prompt_ref, own_ref, carry):
    def prompt_step(c, carry):
        at = pl.ds(pl.multiple_of(c * CHUNK, CHUNK), CHUNK)
        return body(c, lambda refs: refs[0][0, at, :], carry)

    def own_step(c, carry):
        at = pl.ds(pl.multiple_of(PROMPT_DEV + c * CHUNK, CHUNK), CHUNK)
        return body(N_PROMPT_CHUNKS + c, lambda refs: refs[1][0, at, :], carry)

    carry = lax.fori_loop(0, N_PROMPT_CHUNKS, prompt_step, carry)
    return lax.fori_loop(0, N_CONT_CHUNKS, own_step, carry)


def attn_fwd_kernel(q_ref, kp_ref, vp_ref, k_ref, v_ref, out_ref, lse_ref, s_ref, p_ref, o_ref):
    member = lax.rem(lax.axis_index("fsdp"), GROUP)
    limit = key_limit(member)
    sub = lax.broadcasted_iota(jnp.int32, (CHUNK, TOK_DEV), 0)
    pair = pl.program_id(1)

    def head(half):
        qh = half_of(q_ref[0], half)

        def first(c, load, top):
            s = mm(load((kp_ref, k_ref)), qh, NT)
            s = jnp.where(sub + c * CHUNK <= limit, s, -1e30)
            s_ref[pl.ds(pl.multiple_of(c * CHUNK, CHUNK), CHUNK), :] = s
            return jnp.maximum(top, fold(s, jnp.max))

        top = over_keys(first, kp_ref, k_ref, jnp.full((8, TOK_DEV), -1e30, f32))
        top = jnp.max(top, axis=0, keepdims=True)

        def second(c, total):
            at = pl.ds(pl.multiple_of(c * CHUNK, CHUNK), CHUNK)
            p = jnp.exp(s_ref[at, :] - top)
            p_ref[at, :] = p.astype(bf16)
            return total + fold(p, jnp.sum)

        total = lax.fori_loop(0, KEYS // CHUNK, second, jnp.zeros((8, TOK_DEV), f32))
        total = jnp.sum(total, axis=0, keepdims=True)
        out = mm(vp_ref[0], p_ref[:PROMPT, :], TN) + mm(v_ref[0, PROMPT_DEV:, :], p_ref[PROMPT:, :], TN)
        rows = slice(HEAD * half, HEAD * (half + 1))
        o_ref[rows, :] = out[rows, :] / total
        lse_ref[0, 0, half : half + 1, :] = top + jnp.log(total)

    head(0)

    @pl.when(pair < HEAD_PAIRS - 1)
    def _():
        head(1)

    @pl.when(pair == HEAD_PAIRS - 1)
    def _():
        o_ref[HEAD:, :] = jnp.zeros((HEAD, TOK_DEV), f32)

    out_ref[0] = o_ref[...].T.astype(bf16)


HEAD_PAIRS = 4
WIDE = HEAD_PAIRS * 2 * HEAD


def pair_spec(rows):
    return pl.BlockSpec((1, rows, 2 * HEAD), lambda m, h: (m, 0, h))


LSE_SPEC = pl.BlockSpec((1, 1, 8, TOK_DEV), lambda m, h: (m, h, 0, 0))


def attn_fwd(query, keys_p, values_p, key, value):
    return pl.pallas_call(
        attn_fwd_kernel,
        grid=(MICRO, HEAD_PAIRS),
        out_shape=(
            jax.ShapeDtypeStruct((MICRO, TOK_DEV, WIDE), bf16),
            jax.ShapeDtypeStruct((MICRO, HEAD_PAIRS, 8, TOK_DEV), f32),
        ),
        in_specs=[pair_spec(TOK_DEV), pair_spec(PROMPT), pair_spec(PROMPT), pair_spec(TOK_DEV), pair_spec(TOK_DEV)],
        out_specs=(pair_spec(TOK_DEV), LSE_SPEC),
        scratch_shapes=[
            pltpu.VMEM((KEYS, TOK_DEV), f32),
            pltpu.VMEM((KEYS, TOK_DEV), bf16),
            pltpu.VMEM((2 * HEAD, TOK_DEV), f32),
        ],
        compiler_params=pltpu.CompilerParams(vmem_limit_bytes=32 * 2**20),
        cost_estimate=pl.CostEstimate(
            flops=2 * 7 * MICRO * TOK_DEV * KEYS * 256 * 2, bytes_accessed=16 * 2**20, transcendentals=0
        ),
    )(query, keys_p, values_p, key, value)


def attn_bwd_kernel(
    q_ref, kp_ref, vp_ref, k_ref, v_ref, g_ref, lse_ref,
    dq_ref, dkp_ref, dvp_ref, dkc_ref, dvc_ref, p_ref, dp_ref, ds_ref, o_ref,
):
    member = lax.rem(lax.axis_index("fsdp"), GROUP)
    limit = key_limit(member)
    sub = lax.broadcasted_iota(jnp.int32, (CHUNK, TOK_DEV), 0)
    pair = pl.program_id(1)

    def put(ref, at, value, half):
        if half:
            value = value + ref[0, at, :].astype(f32)
        ref[0, at, :] = value.astype(ref.dtype)

    def head(half):
        qh = half_of(q_ref[0], half)
        gh = half_of(g_ref[0], half)
        lse = lse_ref[0, 0, half : half + 1, :]

        def first(c, load, inner):
            at = pl.ds(pl.multiple_of(c * CHUNK, CHUNK), CHUNK)
            s = mm(load((kp_ref, k_ref)), qh, NT)
            p = jnp.exp(jnp.where(sub + c * CHUNK <= limit, s, -1e30) - lse)
            dp = mm(load((vp_ref, v_ref)), gh, NT)
            p_ref[at, :] = p
            dp_ref[at, :] = dp
            return inner + fold(p * dp, jnp.sum)

        inner = over_keys(first, kp_ref, k_ref, jnp.zeros((8, TOK_DEV), f32))
        inner = jnp.sum(inner, axis=0, keepdims=True)

        def second(c, base, dk_ref, dv_ref):
            at = pl.ds(pl.multiple_of(base + c * CHUNK, CHUNK), CHUNK)
            to = pl.ds(pl.multiple_of(c * CHUNK, CHUNK), CHUNK)
            p = p_ref[at, :]
            ds = (p * (dp_ref[at, :] - inner)).astype(bf16)
            ds_ref[at, :] = ds
            put(dv_ref, to, mm(p.astype(bf16), gh), half)
            put(dk_ref, to, mm(ds, qh), half)

        @pl.loop(0, N_PROMPT_CHUNKS)
        def _(c):
            second(c, 0, dkp_ref, dvp_ref)

        @pl.loop(0, N_CONT_CHUNKS)
        def _(c):
            second(c, PROMPT, dkc_ref, dvc_ref)

        dq = mm(kp_ref[0], ds_ref[:PROMPT, :], TN) + mm(k_ref[0, PROMPT_DEV:, :], ds_ref[PROMPT:, :], TN)
        rows = slice(HEAD * half, HEAD * (half + 1))
        o_ref[rows, :] = dq[rows, :] * HEAD ** (-0.5)

    head(0)

    @pl.when(pair < HEAD_PAIRS - 1)
    def _():
        head(1)

    @pl.when(pair == HEAD_PAIRS - 1)
    def _():
        o_ref[HEAD:, :] = jnp.zeros((HEAD, TOK_DEV), f32)

    dq_ref[0] = o_ref[...].T.astype(bf16)


def attn_bwd(query, keys_p, values_p, key, value, grad, lse):
    own = [pair_spec(TOK_DEV)] * 2
    return pl.pallas_call(
        attn_bwd_kernel,
        grid=(MICRO, HEAD_PAIRS),
        out_shape=(
            jax.ShapeDtypeStruct((MICRO, TOK_DEV, WIDE), bf16),
            jax.ShapeDtypeStruct((MICRO, PROMPT, WIDE), bf16),
            jax.ShapeDtypeStruct((MICRO, PROMPT, WIDE), bf16),
            jax.ShapeDtypeStruct((MICRO, CONT_LEN, WIDE), bf16),
            jax.ShapeDtypeStruct((MICRO, CONT_LEN, WIDE), bf16),
        ),
        in_specs=[pair_spec(TOK_DEV), pair_spec(PROMPT), pair_spec(PROMPT)] + own + [pair_spec(TOK_DEV), LSE_SPEC],
        out_specs=(pair_spec(TOK_DEV), pair_spec(PROMPT), pair_spec(PROMPT), pair_spec(CONT_LEN), pair_spec(CONT_LEN)),
        scratch_shapes=[
            pltpu.VMEM((KEYS, TOK_DEV), f32),
            pltpu.VMEM((KEYS, TOK_DEV), f32),
            pltpu.VMEM((KEYS, TOK_DEV), bf16),
            pltpu.VMEM((2 * HEAD, TOK_DEV), f32),
        ],
        compiler_params=pltpu.CompilerParams(vmem_limit_bytes=32 * 2**20),
        cost_estimate=pl.CostEstimate(
            flops=5 * 7 * MICRO * TOK_DEV * KEYS * 256 * 2, bytes_accessed=32 * 2**20, transcendentals=0
        ),
    )(query, keys_p, values_p, key, value, grad, lse)


def by_block(rows, n_tp):
    cols = rows.shape[-1]
    return rows.reshape(n_tp, MICRO, -1, cols).swapaxes(0, 1).reshape(MICRO, -1, cols)


def by_device(blocks, n_tp):
    cols = blocks.shape[-1]
    return blocks.reshape(MICRO, n_tp, -1, cols).swapaxes(0, 1).reshape(-1, cols)


def widen(value):
    return jnp.pad(value, [(0, 0)] * (value.ndim - 1) + [(0, WIDE - value.shape[-1])])


def forward_layer(x, weights, vecs, fc_bias, member, cols, n_tp):
    w_qkv, w_out, w_fc, w_proj = weights
    rows = x.shape[0]
    width = w_out.shape[0]
    normed = layer_norm(x, vecs[0], vecs[1]).astype(bf16)
    normed_all = tp_gather(normed).reshape(-1, D)
    projected = mm(normed_all, w_qkv)
    query_bias, value_bias = (lax.dynamic_slice_in_dim(vecs[i], cols, width) for i in (2, 3))
    query = (projected[:, :width] + query_bias).astype(bf16) * HEAD ** (-0.5)
    key = projected[:, width : 2 * width].astype(bf16)
    value = (projected[:, 2 * width :] + value_bias).astype(bf16)
    query, key, value = (by_block(part, n_tp) for part in (query, key, value))
    shared = group_gather(jnp.stack([key[:, :PROMPT_DEV], value[:, :PROMPT_DEV]]), member)
    shared = shared.transpose(1, 2, 0, 3, 4).reshape(2, MICRO, PROMPT, width)
    query, key, value, keys_p, values_p = (
        widen(part) for part in (query, key, value, shared[0], shared[1])
    )
    mixed, lse = attn_fwd(query, keys_p, values_p, key, value)
    mixed = by_device(mixed[:, :, :width], n_tp)
    part = mm(mixed, w_out).astype(bf16)
    x_mid = x + (tp_scatter(part.reshape(n_tp, rows, D)) + vecs[4])
    second = layer_norm(x_mid, vecs[5], vecs[6]).astype(bf16)
    second_all = tp_gather(second).reshape(-1, D)
    hidden_pre = mm(second_all, w_fc) + fc_bias
    hidden = gelu_tanh(hidden_pre).astype(bf16)
    part = mm(hidden, w_proj, NT).astype(bf16)
    x_next = x_mid + tp_scatter(part.reshape(n_tp, rows, D)) + vecs[7]
    saved = (x, normed_all, query, keys_p, values_p, key, value, lse, mixed, x_mid, second_all, hidden_pre, hidden)
    return x_next, saved


def fsdp_sum(part):
    return lax.psum_scatter(part.astype(bf16), "fsdp", scatter_dimension=0, tiled=True).astype(f32)


def heads_joined(parts, n_tp):
    step = HEADS // n_tp * HEAD
    return jnp.concatenate([parts[t][..., :step] for t in range(n_tp - 1)] + [parts[n_tp - 1]], axis=-1)


def backward_layer(grad_x, weights, vecs, saved, member, cols, n_tp):
    w_qkv, w_out, w_fc, w_proj = weights
    x, normed_all, query, keys_p, values_p, key, value, lse, mixed, x_mid, second_all, hidden_pre, hidden = saved
    rows = x.shape[0]
    width = w_out.shape[0]
    grad_branch = grad_x.astype(bf16)
    grad_proj_bias = jnp.sum(grad_branch.astype(f32), 0)
    branch_all = tp_gather(grad_branch).reshape(-1, D)
    proj_sum = fsdp_sum(mm(branch_all, hidden, TN))
    grad_hidden = mm(branch_all, w_proj)
    _, gelu_back = jax.vjp(gelu_tanh, hidden_pre)
    grad_pre = gelu_back(grad_hidden)[0].astype(bf16)
    fc_sum = fsdp_sum(mm(second_all, grad_pre, TN))
    grad_fc_bias = jnp.sum(grad_pre.astype(f32), 0)
    part = mm(grad_pre, w_fc, NT).astype(bf16)
    grad_second = tp_scatter(part.reshape(n_tp, rows, D))
    _, norm_back = jax.vjp(layer_norm, x_mid, vecs[5], vecs[6])
    grad_from_norm, grad_gain_two, grad_bias_two = norm_back(grad_second)
    grad_mid = grad_x + grad_from_norm
    grad_attn = grad_mid.astype(bf16)
    grad_out_bias = jnp.sum(grad_attn.astype(f32), 0)
    attn_all = tp_gather(grad_attn).reshape(-1, D)
    mixed_all = heads_joined(lax.all_gather(mixed, "tp"), n_tp)
    out_sum = fsdp_sum(mm(mixed_all, lax.dynamic_slice_in_dim(attn_all, cols, width, 1), TN))
    grad_mixed = widen(by_block(mm(attn_all, w_out, NT).astype(bf16), n_tp))
    dq, dkp, dvp, dkc, dvc = attn_bwd(query, keys_p, values_p, key, value, grad_mixed, lse)
    shared = jnp.stack([dkp[:, :, :width], dvp[:, :, :width]]).reshape(2, MICRO, GROUP, PROMPT_DEV, width)
    own = group_scatter(shared.transpose(2, 0, 1, 3, 4), member).astype(bf16)
    dk = jnp.concatenate([own[0], dkc[:, :, :width]], axis=1)
    dv = jnp.concatenate([own[1], dvc[:, :, :width]], axis=1)
    grad_qkv = by_device(jnp.concatenate([dq[:, :, :width], dk, dv], axis=2), n_tp)
    qkv_sum = fsdp_sum(mm(normed_all, grad_qkv, TN))
    column_sums = jnp.sum(grad_qkv.astype(f32), 0)
    part = mm(grad_qkv, w_qkv, NT).astype(bf16)
    grad_normed = tp_scatter(part.reshape(n_tp, rows, D))
    _, first_back = jax.vjp(layer_norm, x, vecs[0], vecs[1])
    grad_from_first, grad_gain_one, grad_bias_one = first_back(grad_normed)
    grad_in = grad_mid + grad_from_first

    def placed(part):
        return lax.dynamic_update_slice_in_dim(jnp.zeros((D,), f32), part, cols, 0)

    vector_grads = jnp.stack(
        [
            grad_gain_one,
            grad_bias_one,
            placed(column_sums[:width]),
            placed(column_sums[2 * width :]),
            grad_out_bias,
            grad_gain_two,
            grad_bias_two,
            grad_proj_bias,
        ]
    )
    vector_sum = lax.psum(lax.psum_scatter(vector_grads, "fsdp", scatter_dimension=1, tiled=True), "tp")
    fc_bias_sum = lax.psum_scatter(grad_fc_bias, "fsdp", scatter_dimension=0, tiled=True)
    qkv_all = lax.all_gather(qkv_sum.astype(bf16).reshape(-1, 3, width), "tp")
    out_all = lax.all_gather(out_sum.astype(bf16), "tp")
    qkv_grad = heads_joined(qkv_all, n_tp).reshape(-1, 3 * D).astype(f32)
    out_grad = heads_joined(out_all, n_tp).astype(f32)
    return grad_in, (qkv_grad, out_grad, fc_sum, proj_sum.T, fc_bias_sum, vector_sum)


def local(
    tokens,
    qkv_weight,
    query_bias,
    value_bias,
    out_weight,
    out_bias,
    fc_weight,
    fc_bias,
    proj_weight,
    proj_bias,
    first_gain,
    first_bias,
    second_gain,
    second_bias,
    out_grad,
):
    n_tp = lax.axis_size("tp")
    tp = lax.axis_index("tp")
    row_count = tokens.shape[1]
    member = lax.axis_index("fsdp") % GROUP
    step = HEADS // n_tp * HEAD
    width = D - step * (n_tp - 1)
    cols = tp * step
    keep = (lax.iota(jnp.int32, width) < step) | (tp == n_tp - 1)

    def gathered(part):
        return lax.all_gather(part, "fsdp", axis=0, tiled=True)

    vectors = jnp.stack(
        [first_gain, first_bias, query_bias, value_bias, out_bias, second_gain, second_bias, proj_bias, fc_bias[:, 0]]
    )
    vectors = lax.all_gather(vectors, "fsdp", axis=2, tiled=True).astype(f32)

    weights = []
    for layer in range(LAYERS):
        qkv_cols = jnp.concatenate(
            [lax.dynamic_slice_in_dim(qkv_weight[layer], cols + i * D, width, 1) for i in range(3)], axis=1
        )
        w_qkv = gathered(qkv_cols)
        out_cols = gathered(lax.dynamic_slice_in_dim(out_weight[layer], cols, width, 1))
        out_parts = jnp.stack([out_cols[t * step : t * step + width] for t in range(n_tp)])
        w_out = heads_joined(lax.all_to_all(out_parts, "tp", 0, 0), n_tp)
        w_out = jnp.where(keep[:, None], w_out, jnp.zeros_like(w_out))
        w_fc = gathered(fc_weight[layer])
        w_proj = gathered(proj_weight[layer].T)
        weights.append((w_qkv, w_out, w_fc, w_proj))

    state = tokens.astype(f32).reshape(MICRO * row_count, D)
    saves = []
    for layer in range(LAYERS):
        state, saved = forward_layer(
            state, weights[layer], vectors[:8, layer], vectors[8, layer], member, cols, n_tp
        )
        saves.append(saved)
    out_tokens = state.astype(bf16).reshape(tokens.shape)
    grad = out_grad.astype(f32).reshape(MICRO * row_count, D)
    sums = [None] * LAYERS
    for layer in reversed(range(LAYERS)):
        grad, sums[layer] = backward_layer(
            grad, weights[layer], vectors[:8, layer], saves[layer], member, cols, n_tp
        )
    qkv_g, out_g, fc_g, proj_g, fc_bias_g, vec_g = (
        jnp.stack([sums[layer][i] for layer in range(LAYERS)]) for i in range(6)
    )
    return (
        out_tokens,
        grad.reshape(tokens.shape),
        qkv_g,
        vec_g[:, 2],
        vec_g[:, 3],
        out_g,
        vec_g[:, 4],
        fc_g,
        fc_bias_g[:, None],
        proj_g,
        vec_g[:, 7],
        vec_g[:, 0],
        vec_g[:, 1],
        vec_g[:, 5],
        vec_g[:, 6],
    )


def solution(mesh):
    rows = P(None, ("fsdp", "tp"), None)
    weight = P(None, "fsdp", None)
    vector = P(None, "fsdp")
    fc_in = P(None, "fsdp", "tp")
    hidden = P(None, "tp", "fsdp")
    in_specs = (
        rows, weight, vector, vector, weight, vector, fc_in, hidden, hidden,
        vector, vector, vector, vector, vector, rows,
    )
    out_specs = (
        rows, rows, weight, vector, vector, weight, vector, fc_in, hidden, hidden,
        vector, vector, vector, vector, vector,
    )
    return jax.shard_map(local, mesh=mesh, in_specs=in_specs, out_specs=out_specs, check_vma=False)
```

```python
import functools

import jax
import jax.numpy as jnp
from jax import lax
from jax.experimental import pallas as pl
from jax.experimental.pallas import tpu as pltpu
from jax.sharding import PartitionSpec as P

D = 1600
HEADS = 25
HEAD = 64
GROUP = 8
PROMPT_DEV = 128
CONT_LEN = 256
TOK_DEV = 384
MICRO = 2
LAYERS = 2
PROMPT = 1024
KEYS = PROMPT + CONT_LEN
CHUNK = 128

f32 = jnp.float32
bf16 = jnp.bfloat16
norm_eps = 1e-05
NN = (((1,), (0,)), ((), ()))
NT = (((1,), (1,)), ((), ()))
TN = (((0,), (0,)), ((), ()))


def mm(left, right, dims=NN):
    return lax.dot_general(left, right, dims, preferred_element_type=f32)


def swapped(value, axis, mask):
    pairs = [(source, source ^ mask) for source in range(lax.axis_size(axis))]
    return lax.ppermute(value, axis, pairs)


def layer_norm(x, gain, bias):
    centred = x - jnp.mean(x, -1, keepdims=True)
    spread = jnp.mean(centred * centred, -1, keepdims=True)
    return centred * lax.rsqrt(spread + norm_eps) * gain + bias


def gelu_tanh(value):
    return jax.nn.gelu(value, approximate=True)


def by_offset(stacked, index):
    return jnp.take(stacked, index ^ jnp.arange(stacked.shape[0]), axis=0)


def tp_gather(value):
    n = lax.axis_size("tp")
    held = value[None]
    mask = n // 2
    order = [0]
    while mask:
        held = jnp.concatenate([held, swapped(held, "tp", mask)], axis=0)
        order = order + [o ^ mask for o in order]
        mask //= 2
    place = [order.index(k) for k in range(n)]
    held = jnp.stack([held[p] for p in place])
    return by_offset(held, lax.axis_index("tp"))


def tp_scatter(parts):
    held = by_offset(parts, lax.axis_index("tp"))
    mask = 1
    while mask < lax.axis_size("tp"):
        arrived = swapped(held[1::2].astype(bf16), "tp", mask)
        held = held[0::2].astype(f32) + arrived.astype(f32)
        mask *= 2
    return held[0]


def group_gather(value, member):
    along = [value] + [swapped(value, "fsdp", k) for k in (2, 4, 6)]
    across = [swapped(piece, "fsdp", 1) for piece in along]
    stacked = jnp.stack([piece for pair in zip(along, across) for piece in pair])
    return by_offset(stacked, member)


def group_scatter(parts, member):
    held = by_offset(parts, member)
    arrived = swapped(held[1::2], "fsdp", 1)
    summed = held[0::2].astype(f32) + arrived.astype(f32)
    total = summed[0]
    for k in (1, 2, 3):
        total = total + swapped(summed[k].astype(bf16), "fsdp", 2 * k).astype(f32)
    return total


def key_limit(member):
    row = lax.broadcasted_iota(jnp.int32, (1, TOK_DEV), 1)
    return jnp.where(row < PROMPT_DEV, member * PROMPT_DEV + row, PROMPT - PROMPT_DEV + row)


def half_of(value, half):
    lane = lax.broadcasted_iota(jnp.int32, value.shape, 1)
    return jnp.where((lane >= HEAD * half) & (lane < HEAD * (half + 1)), value, jnp.zeros_like(value))


def fold(value, op):
    return op(value.reshape(value.shape[0] // 8, 8, value.shape[1]), axis=0)


N_PROMPT_CHUNKS = PROMPT // CHUNK
N_CONT_CHUNKS = CONT_LEN // CHUNK


def over_keys(body, prompt_ref, own_ref, carry):
    def prompt_step(c, carry):
        at = pl.ds(pl.multiple_of(c * CHUNK, CHUNK), CHUNK)
        return body(c, lambda refs: refs[0][0, at, :], carry)

    def own_step(c, carry):
        at = pl.ds(pl.multiple_of(PROMPT_DEV + c * CHUNK, CHUNK), CHUNK)
        return body(N_PROMPT_CHUNKS + c, lambda refs: refs[1][0, at, :], carry)

    carry = lax.fori_loop(0, N_PROMPT_CHUNKS, prompt_step, carry)
    return lax.fori_loop(0, N_CONT_CHUNKS, own_step, carry)


def attn_fwd_kernel(q_ref, kp_ref, vp_ref, k_ref, v_ref, out_ref, lse_ref, s_ref, p_ref, o_ref):
    member = lax.rem(lax.axis_index("fsdp"), GROUP)
    limit = key_limit(member)
    sub = lax.broadcasted_iota(jnp.int32, (CHUNK, TOK_DEV), 0)
    pair = pl.program_id(1)

    def head(half):
        qh = half_of(q_ref[0], half)

        def first(c, load, top):
            s = mm(load((kp_ref, k_ref)), qh, NT)
            s = jnp.where(sub + c * CHUNK <= limit, s, -1e30)
            s_ref[pl.ds(pl.multiple_of(c * CHUNK, CHUNK), CHUNK), :] = s
            return jnp.maximum(top, fold(s, jnp.max))

        top = over_keys(first, kp_ref, k_ref, jnp.full((8, TOK_DEV), -1e30, f32))
        top = jnp.max(top, axis=0, keepdims=True)

        def second(c, total):
            at = pl.ds(pl.multiple_of(c * CHUNK, CHUNK), CHUNK)
            p = jnp.exp(s_ref[at, :] - top)
            p_ref[at, :] = p.astype(bf16)
            return total + fold(p, jnp.sum)

        total = lax.fori_loop(0, KEYS // CHUNK, second, jnp.zeros((8, TOK_DEV), f32))
        total = jnp.sum(total, axis=0, keepdims=True)
        out = mm(vp_ref[0], p_ref[:PROMPT, :], TN) + mm(v_ref[0, PROMPT_DEV:, :], p_ref[PROMPT:, :], TN)
        rows = slice(HEAD * half, HEAD * (half + 1))
        o_ref[rows, :] = out[rows, :] / total
        lse_ref[0, 0, half : half + 1, :] = top + jnp.log(total)

    head(0)

    @pl.when(pair < HEAD_PAIRS - 1)
    def _():
        head(1)

    @pl.when(pair == HEAD_PAIRS - 1)
    def _():
        o_ref[HEAD:, :] = jnp.zeros((HEAD, TOK_DEV), f32)

    out_ref[0] = o_ref[...].T.astype(bf16)


HEAD_PAIRS = 4
WIDE = HEAD_PAIRS * 2 * HEAD


def pair_spec(rows):
    return pl.BlockSpec((1, rows, 2 * HEAD), lambda m, h: (m, 0, h))


LSE_SPEC = pl.BlockSpec((1, 1, 8, TOK_DEV), lambda m, h: (m, h, 0, 0))


def attn_fwd(query, keys_p, values_p, key, value):
    return pl.pallas_call(
        attn_fwd_kernel,
        grid=(MICRO, HEAD_PAIRS),
        out_shape=(
            jax.ShapeDtypeStruct((MICRO, TOK_DEV, WIDE), bf16),
            jax.ShapeDtypeStruct((MICRO, HEAD_PAIRS, 8, TOK_DEV), f32),
        ),
        in_specs=[pair_spec(TOK_DEV), pair_spec(PROMPT), pair_spec(PROMPT), pair_spec(TOK_DEV), pair_spec(TOK_DEV)],
        out_specs=(pair_spec(TOK_DEV), LSE_SPEC),
        scratch_shapes=[
            pltpu.VMEM((KEYS, TOK_DEV), f32),
            pltpu.VMEM((KEYS, TOK_DEV), bf16),
            pltpu.VMEM((2 * HEAD, TOK_DEV), f32),
        ],
        compiler_params=pltpu.CompilerParams(vmem_limit_bytes=32 * 2**20),
        cost_estimate=pl.CostEstimate(
            flops=2 * 7 * MICRO * TOK_DEV * KEYS * 256 * 2, bytes_accessed=16 * 2**20, transcendentals=0
        ),
    )(query, keys_p, values_p, key, value)


def attn_bwd_kernel(
    q_ref, kp_ref, vp_ref, k_ref, v_ref, g_ref, lse_ref,
    dq_ref, dkp_ref, dvp_ref, dkc_ref, dvc_ref, p_ref, dp_ref, ds_ref, o_ref,
):
    member = lax.rem(lax.axis_index("fsdp"), GROUP)
    limit = key_limit(member)
    sub = lax.broadcasted_iota(jnp.int32, (CHUNK, TOK_DEV), 0)
    pair = pl.program_id(1)

    def put(ref, at, value, half):
        if half:
            value = value + ref[0, at, :].astype(f32)
        ref[0, at, :] = value.astype(ref.dtype)

    def head(half):
        qh = half_of(q_ref[0], half)
        gh = half_of(g_ref[0], half)
        lse = lse_ref[0, 0, half : half + 1, :]

        def first(c, load, inner):
            at = pl.ds(pl.multiple_of(c * CHUNK, CHUNK), CHUNK)
            s = mm(load((kp_ref, k_ref)), qh, NT)
            p = jnp.exp(jnp.where(sub + c * CHUNK <= limit, s, -1e30) - lse)
            dp = mm(load((vp_ref, v_ref)), gh, NT)
            p_ref[at, :] = p
            dp_ref[at, :] = dp
            return inner + fold(p * dp, jnp.sum)

        inner = over_keys(first, kp_ref, k_ref, jnp.zeros((8, TOK_DEV), f32))
        inner = jnp.sum(inner, axis=0, keepdims=True)

        def second(c, base, dk_ref, dv_ref):
            at = pl.ds(pl.multiple_of(base + c * CHUNK, CHUNK), CHUNK)
            to = pl.ds(pl.multiple_of(c * CHUNK, CHUNK), CHUNK)
            p = p_ref[at, :]
            ds = (p * (dp_ref[at, :] - inner)).astype(bf16)
            ds_ref[at, :] = ds
            put(dv_ref, to, mm(p.astype(bf16), gh), half)
            put(dk_ref, to, mm(ds, qh), half)

        @pl.loop(0, N_PROMPT_CHUNKS)
        def _(c):
            second(c, 0, dkp_ref, dvp_ref)

        @pl.loop(0, N_CONT_CHUNKS)
        def _(c):
            second(c, PROMPT, dkc_ref, dvc_ref)

        dq = mm(kp_ref[0], ds_ref[:PROMPT, :], TN) + mm(k_ref[0, PROMPT_DEV:, :], ds_ref[PROMPT:, :], TN)
        rows = slice(HEAD * half, HEAD * (half + 1))
        o_ref[rows, :] = dq[rows, :] * HEAD ** (-0.5)

    head(0)

    @pl.when(pair < HEAD_PAIRS - 1)
    def _():
        head(1)

    @pl.when(pair == HEAD_PAIRS - 1)
    def _():
        o_ref[HEAD:, :] = jnp.zeros((HEAD, TOK_DEV), f32)

    dq_ref[0] = o_ref[...].T.astype(bf16)


def attn_bwd(query, keys_p, values_p, key, value, grad, lse):
    own = [pair_spec(TOK_DEV)] * 2
    return pl.pallas_call(
        attn_bwd_kernel,
        grid=(MICRO, HEAD_PAIRS),
        out_shape=(
            jax.ShapeDtypeStruct((MICRO, TOK_DEV, WIDE), bf16),
            jax.ShapeDtypeStruct((MICRO, PROMPT, WIDE), bf16),
            jax.ShapeDtypeStruct((MICRO, PROMPT, WIDE), bf16),
            jax.ShapeDtypeStruct((MICRO, CONT_LEN, WIDE), bf16),
            jax.ShapeDtypeStruct((MICRO, CONT_LEN, WIDE), bf16),
        ),
        in_specs=[pair_spec(TOK_DEV), pair_spec(PROMPT), pair_spec(PROMPT)] + own + [pair_spec(TOK_DEV), LSE_SPEC],
        out_specs=(pair_spec(TOK_DEV), pair_spec(PROMPT), pair_spec(PROMPT), pair_spec(CONT_LEN), pair_spec(CONT_LEN)),
        scratch_shapes=[
            pltpu.VMEM((KEYS, TOK_DEV), f32),
            pltpu.VMEM((KEYS, TOK_DEV), f32),
            pltpu.VMEM((KEYS, TOK_DEV), bf16),
            pltpu.VMEM((2 * HEAD, TOK_DEV), f32),
        ],
        compiler_params=pltpu.CompilerParams(vmem_limit_bytes=32 * 2**20),
        cost_estimate=pl.CostEstimate(
            flops=5 * 7 * MICRO * TOK_DEV * KEYS * 256 * 2, bytes_accessed=32 * 2**20, transcendentals=0
        ),
    )(query, keys_p, values_p, key, value, grad, lse)


def by_block(rows, n_tp):
    cols = rows.shape[-1]
    return rows.reshape(n_tp, MICRO, -1, cols).swapaxes(0, 1).reshape(MICRO, -1, cols)


def by_device(blocks, n_tp):
    cols = blocks.shape[-1]
    return blocks.reshape(MICRO, n_tp, -1, cols).swapaxes(0, 1).reshape(-1, cols)


def widen(value):
    return jnp.pad(value, [(0, 0)] * (value.ndim - 1) + [(0, WIDE - value.shape[-1])])


MESH = pl.DeviceIdType.MESH
ANY = pl.BlockSpec(memory_space=pl.ANY)
IN_VMEM = pl.BlockSpec(memory_space=pltpu.VMEM)
TILE = 512
ROW_CHUNK = 32


class Peers:
    def __init__(self):
        self.f = lax.axis_index("fsdp")
        self.t = lax.axis_index("tp")
        x, c = self.t // 2, self.t % 2
        self.x = x
        self.core = 2 * x + 1 - c
        self.over = 2 * (1 - x) + c
        self.diag = 2 * (1 - x) + 1 - c

    def greet(self):
        barrier = pltpu.get_barrier_semaphore()
        for t in (self.core, self.over):
            pl.semaphore_signal(barrier, inc=1, device_id=(self.f, t), device_id_type=MESH)
        pl.semaphore_wait(barrier, 2)

    def copy(self, source, target, sems, index, t):
        return pltpu.make_async_remote_copy(
            src_ref=source,
            dst_ref=target,
            send_sem=sems[0].at[index],
            recv_sem=sems[1].at[index],
            device_id=(self.f, t),
            device_id_type=MESH,
        )


class Gather:
    def __init__(self, peers, buf, sems):
        self.p, self.buf, self.sems = peers, buf, sems

    def piece(self, slot, index, t):
        return self.p.copy(self.buf.at[slot], self.buf.at[slot], self.sems, index, t)

    def start(self):
        p = self.p
        self.piece(p.t, 1, p.over).start()
        self.piece(p.t, 0, p.core).start()

    def wait_chip(self):
        self.piece(self.p.core, 0, self.p.core).wait_recv()

    def relay(self):
        p = self.p
        self.piece(p.over, 1, p.over).wait_recv()
        self.piece(p.over, 2, p.core).start()

    def wait_diag(self):
        self.piece(self.p.diag, 2, self.p.core).wait_recv()

    def finish(self):
        p = self.p
        self.piece(p.t, 1, p.over).wait_send()
        self.piece(p.t, 0, p.core).wait_send()
        self.piece(p.over, 2, p.core).wait_send()


class Scatter:
    def __init__(self, peers, part, from_core, over_out, from_over, sems):
        self.p, self.part, self.sems = peers, part, sems
        self.from_core, self.over_out, self.from_over = from_core, over_out, from_over

    def far_to_core(self):
        return self.p.copy(self.part.at[self.p.diag], self.from_core.at[0], self.sems, 3, self.p.core)

    def near_to_core(self):
        return self.p.copy(self.part.at[self.p.core], self.from_core.at[1], self.sems, 4, self.p.core)

    def to_over(self):
        return self.p.copy(self.over_out, self.from_over, self.sems, 5, self.p.over)

    def send_over(self):
        self.far_to_core().wait_recv()

        @pl.loop(0, self.over_out.shape[0] // ROW_CHUNK)
        def _(i):
            at = pl.ds(pl.multiple_of(i * ROW_CHUNK, ROW_CHUNK), ROW_CHUNK)
            total = self.part[self.p.over, at, :].astype(f32) + self.from_core[0, at, :].astype(f32)
            self.over_out[at, :] = total.astype(bf16)

        self.to_over().start()

    def wait(self):
        self.near_to_core().wait_recv()
        self.to_over().wait_recv()

    def rows(self, at):
        return (
            self.part[self.p.t, at, :].astype(f32)
            + self.from_core[1, at, :].astype(f32)
            + self.from_over[at, :].astype(f32)
        )

    def finish(self):
        for copy in (self.far_to_core(), self.near_to_core(), self.to_over()):
            copy.wait_send()


def row_chunks(rows, body):
    @pl.loop(0, rows // ROW_CHUNK)
    def _(i):
        body(pl.ds(pl.multiple_of(i * ROW_CHUNK, ROW_CHUNK), ROW_CHUNK))


def tiles(extent, body):
    whole = extent // TILE

    @pl.loop(0, whole)
    def _(i):
        body(pl.ds(pl.multiple_of(i * TILE, TILE), TILE))

    if extent % TILE:
        body(pl.ds(whole * TILE, extent % TILE))


def pair_rows(ref, x):
    both = ref[pl.ds(2 * x, 2)]
    return both.reshape(2 * both.shape[1], both.shape[2])


def put_pair(ref, x, at, value):
    ref[pl.ds(2 * x, 2), :, at] = value.reshape(2, value.shape[0] // 2, value.shape[1]).astype(ref.dtype)


def norm_stats(x):
    centred = x - jnp.mean(x, -1, keepdims=True)
    scale = lax.rsqrt(jnp.mean(centred * centred, -1, keepdims=True) + norm_eps)
    return centred * scale, scale


def ff_fwd_kernel(
    x_ref, vec_ref, fcb_ref, wfc_hbm, wproj_hbm,
    out_ref, all_hbm, pre_hbm, hid_hbm,
    wfc, wproj, buf, pre, hid, part, from_core, over_out, from_over, send, recv, local,
):
    p = Peers()
    rows = x_ref.shape[0]
    sems = (send, recv)
    gather = Gather(p, buf, sems)
    scatter = Scatter(p, part, from_core, over_out, from_over, sems)
    load_fc = pltpu.make_async_copy(wfc_hbm, wfc, local.at[0])
    load_proj = pltpu.make_async_copy(wproj_hbm, wproj, local.at[1])
    load_fc.start()
    load_proj.start()

    def norm(at):
        hat, _ = norm_stats(x_ref[at, :])
        buf[p.t, at, :] = (hat * vec_ref[5:6, :] + vec_ref[6:7, :]).astype(bf16)

    row_chunks(rows, norm)
    p.greet()
    gather.start()
    gather.wait_chip()
    load_fc.wait()

    def up(x):
        def tile(at):
            value = mm(pair_rows(buf, x), wfc[:, at]) + fcb_ref[:, at]
            put_pair(pre, x, at, value)
            put_pair(hid, x, at, gelu_tanh(value))

        tiles(wfc.shape[1], tile)

    def down(x):
        def tile(at):
            put_pair(part, x, at, mm(pair_rows(hid, x), wproj[at, :], NT))

        tiles(wproj.shape[0], tile)

    up(p.x)
    gather.relay()
    gather.wait_diag()
    keep_all = pltpu.make_async_copy(buf, all_hbm, local.at[2])
    keep_all.start()
    up(1 - p.x)
    keep_pre = pltpu.make_async_copy(pre, pre_hbm, local.at[3])
    keep_hid = pltpu.make_async_copy(hid, hid_hbm, local.at[4])
    keep_pre.start()
    keep_hid.start()
    load_proj.wait()
    down(1 - p.x)
    scatter.far_to_core().start()
    scatter.send_over()
    down(p.x)
    scatter.near_to_core().start()
    scatter.wait()

    def final(at):
        out_ref[at, :] = x_ref[at, :] + scatter.rows(at) + vec_ref[7:8, :]

    row_chunks(rows, final)
    gather.finish()
    scatter.finish()
    for copy in (keep_all, keep_pre, keep_hid):
        copy.wait()


def scatter_scratch(n_tp, rows):
    return [
        pltpu.VMEM((n_tp, rows, D), bf16),
        pltpu.VMEM((2, rows, D), bf16),
        pltpu.VMEM((rows, D), bf16),
        pltpu.VMEM((rows, D), bf16),
        pltpu.SemaphoreType.DMA((6,)),
        pltpu.SemaphoreType.DMA((6,)),
    ]


def params(collective_id):
    return pltpu.CompilerParams(collective_id=collective_id, has_side_effects=True, vmem_limit_bytes=60 * 2**20)


def ff_fwd(x, vecs, fc_bias, w_fc, w_proj, n_tp):
    rows, width = x.shape[0], w_fc.shape[1]
    block = (n_tp, rows)
    return pl.pallas_call(
        ff_fwd_kernel,
        out_shape=(
            jax.ShapeDtypeStruct((rows, D), f32),
            jax.ShapeDtypeStruct(block + (D,), bf16),
            jax.ShapeDtypeStruct(block + (width,), f32),
            jax.ShapeDtypeStruct(block + (width,), bf16),
        ),
        in_specs=[IN_VMEM, IN_VMEM, IN_VMEM, ANY, ANY],
        out_specs=(IN_VMEM, ANY, ANY, ANY),
        scratch_shapes=[
            pltpu.VMEM((D, width), bf16),
            pltpu.VMEM((D, width), bf16),
            pltpu.VMEM(block + (D,), bf16),
            pltpu.VMEM(block + (width,), f32),
            pltpu.VMEM(block + (width,), bf16),
        ]
        + scatter_scratch(n_tp, rows)
        + [pltpu.SemaphoreType.DMA((5,))],
        compiler_params=params(1),
        cost_estimate=pl.CostEstimate(
            flops=4 * n_tp * rows * D * width, bytes_accessed=40 * 2**20, transcendentals=n_tp * rows * width
        ),
    )(x, vecs, fc_bias, w_fc, w_proj)


def gelu_slope(u):
    a = 0.7978845608028654
    square = u * u
    t = jnp.tanh(a * (u + 0.044715 * u * square))
    return 0.5 * (1.0 + t) + 0.5 * u * (1.0 - t * t) * (a * (1.0 + 3 * 0.044715 * square))


def norm_back(x, dy, gain):
    hat, scale = norm_stats(x)
    d_hat = dy * gain
    inner = d_hat - jnp.mean(d_hat, -1, keepdims=True) - hat * jnp.mean(d_hat * hat, -1, keepdims=True)
    return scale * inner, dy * hat


def add_rows(ref, row, value):
    ref[row : row + 1, :] += jnp.sum(value, axis=0, keepdims=True)


def ff_bwd_kernel(
    g_ref, x_ref, vec_ref, all_hbm, pre_hbm, hid_hbm, wfc_hbm, wproj_hbm,
    out_ref, sums_ref, fcb_ref, dfc_hbm, dproj_hbm,
    wfc, wproj, buf, other, pre, dpre, stage, part, from_core, over_out, from_over, send, recv, local,
):
    p = Peers()
    rows = x_ref.shape[0]
    n_tp, width = buf.shape[0], wfc.shape[1]
    sems = (send, recv)
    gather = Gather(p, buf, sems)
    scatter = Scatter(p, part, from_core, over_out, from_over, sems)
    load_proj = pltpu.make_async_copy(wproj_hbm, wproj, local.at[0])
    load_pre = pltpu.make_async_copy(pre_hbm, pre, local.at[1])
    load_fc = pltpu.make_async_copy(wfc_hbm, wfc, local.at[2])
    load_other = pltpu.make_async_copy(hid_hbm, other, local.at[3])
    for copy in (load_proj, load_pre, load_fc, load_other):
        copy.start()
    sums_ref[...] = jnp.zeros_like(sums_ref)
    fcb_ref[...] = jnp.zeros_like(fcb_ref)

    def lower(at):
        low = g_ref[at, :].astype(bf16)
        buf[p.t, at, :] = low
        add_rows(sums_ref, 7, low.astype(f32))

    row_chunks(rows, lower)
    p.greet()
    gather.start()
    gather.wait_chip()
    load_proj.wait()
    load_pre.wait()

    def through(x):
        def tile(at):
            d_hidden = mm(pair_rows(buf, x), wproj[:, at])
            u = pre[pl.ds(2 * x, 2), :, at].reshape(2 * rows, -1)
            low = (gelu_slope(u) * d_hidden).astype(bf16)
            put_pair(dpre, x, at, low)
            fcb_ref[:, at] += jnp.sum(low.astype(f32), axis=0, keepdims=True)

        tiles(width, tile)

    def down(x):
        def tile(at):
            put_pair(part, x, at, mm(pair_rows(dpre, x), wfc[at, :], NT))

        tiles(D, tile)

    through(p.x)
    gather.relay()
    gather.wait_diag()
    through(1 - p.x)
    load_fc.wait()
    down(1 - p.x)
    scatter.far_to_core().start()
    scatter.send_over()
    down(p.x)
    scatter.near_to_core().start()

    def outer(left, right, target, sem):
        whole = D // TILE
        rest = D - whole * TILE
        flat = right[...].reshape(n_tp * rows, width)

        def tile(i, size):
            at = pl.ds(pl.multiple_of(i * TILE, TILE), size)
            value = mm(left[:, :, at].reshape(n_tp * rows, size), flat, TN)
            stage[at, :] = value.astype(bf16)

        @pl.loop(0, whole)
        def _(i):
            tile(i, TILE)

        if rest:
            tile(whole, rest)
        return pltpu.make_async_copy(stage, target, sem)

    load_other.wait()
    store = outer(buf, other, dproj_hbm, local.at[4])
    store.start()
    gather.finish()
    load_all = pltpu.make_async_copy(all_hbm, buf, local.at[5])
    load_all.start()
    scatter.wait()

    def final(at):
        dy = scatter.rows(at)
        dx, d_gain = norm_back(x_ref[at, :], dy, vec_ref[5:6, :])
        add_rows(sums_ref, 5, d_gain)
        add_rows(sums_ref, 6, dy)
        out_ref[at, :] = g_ref[at, :] + dx

    row_chunks(rows, final)
    load_all.wait()
    store.wait()
    store = outer(buf, dpre, dfc_hbm, local.at[6])
    store.start()
    scatter.finish()
    store.wait()


def ff_bwd(grad, x, vecs, all_rows, pre, hidden, w_fc, w_proj, n_tp):
    rows, width = x.shape[0], w_fc.shape[1]
    block = (n_tp, rows)
    return pl.pallas_call(
        ff_bwd_kernel,
        out_shape=(
            jax.ShapeDtypeStruct((rows, D), f32),
            jax.ShapeDtypeStruct((8, D), f32),
            jax.ShapeDtypeStruct((1, width), f32),
            jax.ShapeDtypeStruct((D, width), bf16),
            jax.ShapeDtypeStruct((D, width), bf16),
        ),
        in_specs=[IN_VMEM, IN_VMEM, IN_VMEM, ANY, ANY, ANY, ANY, ANY],
        out_specs=(IN_VMEM, IN_VMEM, IN_VMEM, ANY, ANY),
        scratch_shapes=[
            pltpu.VMEM((D, width), bf16),
            pltpu.VMEM((D, width), bf16),
            pltpu.VMEM(block + (D,), bf16),
            pltpu.VMEM(block + (width,), bf16),
            pltpu.VMEM(block + (width,), f32),
            pltpu.VMEM(block + (width,), bf16),
            pltpu.VMEM((D, width), bf16),
        ]
        + scatter_scratch(n_tp, rows)
        + [pltpu.SemaphoreType.DMA((7,))],
        compiler_params=params(2),
        cost_estimate=pl.CostEstimate(
            flops=8 * n_tp * rows * D * width, bytes_accessed=50 * 2**20, transcendentals=n_tp * rows * width
        ),
    )(grad, x, vecs, all_rows, pre, hidden, w_fc, w_proj)


def forward_layer(x, weights, vecs, fc_bias, member, cols, n_tp):
    w_qkv, w_out, w_fc, w_proj = weights
    rows = x.shape[0]
    width = w_out.shape[0]
    normed = layer_norm(x, vecs[0], vecs[1]).astype(bf16)
    normed_all = tp_gather(normed).reshape(-1, D)
    projected = mm(normed_all, w_qkv)
    query_bias, value_bias = (lax.dynamic_slice_in_dim(vecs[i], cols, width) for i in (2, 3))
    query = (projected[:, :width] + query_bias).astype(bf16) * HEAD ** (-0.5)
    key = projected[:, width : 2 * width].astype(bf16)
    value = (projected[:, 2 * width :] + value_bias).astype(bf16)
    query, key, value = (by_block(part, n_tp) for part in (query, key, value))
    shared = group_gather(jnp.stack([key[:, :PROMPT_DEV], value[:, :PROMPT_DEV]]), member)
    shared = shared.transpose(1, 2, 0, 3, 4).reshape(2, MICRO, PROMPT, width)
    query, key, value, keys_p, values_p = (
        widen(part) for part in (query, key, value, shared[0], shared[1])
    )
    mixed, lse = attn_fwd(query, keys_p, values_p, key, value)
    mixed = by_device(mixed[:, :, :width], n_tp)
    part = mm(mixed, w_out).astype(bf16)
    x_mid = x + (tp_scatter(part.reshape(n_tp, rows, D)) + vecs[4])
    x_next, second_all, hidden_pre, hidden = ff_fwd(x_mid, vecs, fc_bias[None], w_fc, w_proj, n_tp)
    saved = (x, normed_all, query, keys_p, values_p, key, value, lse, mixed, x_mid, second_all, hidden_pre, hidden)
    return x_next, saved


def fsdp_sum(part):
    return lax.psum_scatter(part.astype(bf16), "fsdp", scatter_dimension=0, tiled=True).astype(f32)


def heads_joined(parts, n_tp):
    step = HEADS // n_tp * HEAD
    return jnp.concatenate([parts[t][..., :step] for t in range(n_tp - 1)] + [parts[n_tp - 1]], axis=-1)


def backward_layer(grad_x, weights, vecs, saved, member, cols, n_tp):
    w_qkv, w_out, w_fc, w_proj = weights
    x, normed_all, query, keys_p, values_p, key, value, lse, mixed, x_mid, second_all, hidden_pre, hidden = saved
    rows = x.shape[0]
    width = w_out.shape[0]
    grad_mid, ff_sums, grad_fc_bias, grad_fc, grad_proj = ff_bwd(
        grad_x, x_mid, vecs, second_all, hidden_pre, hidden, w_fc, w_proj, n_tp
    )
    proj_sum, fc_sum = fsdp_sum(grad_proj), fsdp_sum(grad_fc)
    grad_attn = grad_mid.astype(bf16)
    grad_out_bias = jnp.sum(grad_attn.astype(f32), 0)
    attn_all = tp_gather(grad_attn).reshape(-1, D)
    mixed_all = heads_joined(lax.all_gather(mixed, "tp"), n_tp)
    out_sum = fsdp_sum(mm(mixed_all, lax.dynamic_slice_in_dim(attn_all, cols, width, 1), TN))
    grad_mixed = widen(by_block(mm(attn_all, w_out, NT).astype(bf16), n_tp))
    dq, dkp, dvp, dkc, dvc = attn_bwd(query, keys_p, values_p, key, value, grad_mixed, lse)
    shared = jnp.stack([dkp[:, :, :width], dvp[:, :, :width]]).reshape(2, MICRO, GROUP, PROMPT_DEV, width)
    own = group_scatter(shared.transpose(2, 0, 1, 3, 4), member).astype(bf16)
    dk = jnp.concatenate([own[0], dkc[:, :, :width]], axis=1)
    dv = jnp.concatenate([own[1], dvc[:, :, :width]], axis=1)
    grad_qkv = by_device(jnp.concatenate([dq[:, :, :width], dk, dv], axis=2), n_tp)
    qkv_sum = fsdp_sum(mm(normed_all, grad_qkv, TN))
    column_sums = jnp.sum(grad_qkv.astype(f32), 0)
    part = mm(grad_qkv, w_qkv, NT).astype(bf16)
    grad_normed = tp_scatter(part.reshape(n_tp, rows, D))
    _, first_back = jax.vjp(layer_norm, x, vecs[0], vecs[1])
    grad_from_first, grad_gain_one, grad_bias_one = first_back(grad_normed)
    grad_in = grad_mid + grad_from_first

    def placed(part):
        return lax.dynamic_update_slice_in_dim(jnp.zeros((D,), f32), part, cols, 0)

    vector_grads = jnp.stack(
        [
            grad_gain_one,
            grad_bias_one,
            placed(column_sums[:width]),
            placed(column_sums[2 * width :]),
            grad_out_bias,
            ff_sums[5],
            ff_sums[6],
            ff_sums[7],
        ]
    )
    vector_sum = lax.psum(lax.psum_scatter(vector_grads, "fsdp", scatter_dimension=1, tiled=True), "tp")
    fc_bias_sum = lax.psum_scatter(grad_fc_bias[0], "fsdp", scatter_dimension=0, tiled=True)
    qkv_all = lax.all_gather(qkv_sum.astype(bf16).reshape(-1, 3, width), "tp")
    out_all = lax.all_gather(out_sum.astype(bf16), "tp")
    qkv_grad = heads_joined(qkv_all, n_tp).reshape(-1, 3 * D).astype(f32)
    out_grad = heads_joined(out_all, n_tp).astype(f32)
    return grad_in, (qkv_grad, out_grad, fc_sum, proj_sum.T, fc_bias_sum, vector_sum)


def local(
    tokens,
    qkv_weight,
    query_bias,
    value_bias,
    out_weight,
    out_bias,
    fc_weight,
    fc_bias,
    proj_weight,
    proj_bias,
    first_gain,
    first_bias,
    second_gain,
    second_bias,
    out_grad,
):
    n_tp = lax.axis_size("tp")
    tp = lax.axis_index("tp")
    row_count = tokens.shape[1]
    member = lax.axis_index("fsdp") % GROUP
    step = HEADS // n_tp * HEAD
    width = D - step * (n_tp - 1)
    cols = tp * step
    keep = (lax.iota(jnp.int32, width) < step) | (tp == n_tp - 1)

    def gathered(part):
        return lax.all_gather(part, "fsdp", axis=0, tiled=True)

    vectors = jnp.stack(
        [first_gain, first_bias, query_bias, value_bias, out_bias, second_gain, second_bias, proj_bias, fc_bias[:, 0]]
    )
    vectors = lax.all_gather(vectors, "fsdp", axis=2, tiled=True).astype(f32)

    weights = []
    for layer in range(LAYERS):
        qkv_cols = jnp.concatenate(
            [lax.dynamic_slice_in_dim(qkv_weight[layer], cols + i * D, width, 1) for i in range(3)], axis=1
        )
        w_qkv = gathered(qkv_cols)
        out_cols = gathered(lax.dynamic_slice_in_dim(out_weight[layer], cols, width, 1))
        out_parts = jnp.stack([out_cols[t * step : t * step + width] for t in range(n_tp)])
        w_out = heads_joined(lax.all_to_all(out_parts, "tp", 0, 0), n_tp)
        w_out = jnp.where(keep[:, None], w_out, jnp.zeros_like(w_out))
        w_fc = gathered(fc_weight[layer])
        w_proj = gathered(proj_weight[layer].T)
        weights.append((w_qkv, w_out, w_fc, w_proj))

    state = tokens.astype(f32).reshape(MICRO * row_count, D)
    saves = []
    for layer in range(LAYERS):
        state, saved = forward_layer(
            state, weights[layer], vectors[:8, layer], vectors[8, layer], member, cols, n_tp
        )
        saves.append(saved)
    out_tokens = state.astype(bf16).reshape(tokens.shape)
    grad = out_grad.astype(f32).reshape(MICRO * row_count, D)
    sums = [None] * LAYERS
    for layer in reversed(range(LAYERS)):
        grad, sums[layer] = backward_layer(
            grad, weights[layer], vectors[:8, layer], saves[layer], member, cols, n_tp
        )
    qkv_g, out_g, fc_g, proj_g, fc_bias_g, vec_g = (
        jnp.stack([sums[layer][i] for layer in range(LAYERS)]) for i in range(6)
    )
    return (
        out_tokens,
        grad.reshape(tokens.shape),
        qkv_g,
        vec_g[:, 2],
        vec_g[:, 3],
        out_g,
        vec_g[:, 4],
        fc_g,
        fc_bias_g[:, None],
        proj_g,
        vec_g[:, 7],
        vec_g[:, 0],
        vec_g[:, 1],
        vec_g[:, 5],
        vec_g[:, 6],
    )


def solution(mesh):
    rows = P(None, ("fsdp", "tp"), None)
    weight = P(None, "fsdp", None)
    vector = P(None, "fsdp")
    fc_in = P(None, "fsdp", "tp")
    hidden = P(None, "tp", "fsdp")
    in_specs = (
        rows, weight, vector, vector, weight, vector, fc_in, hidden, hidden,
        vector, vector, vector, vector, vector, rows,
    )
    out_specs = (
        rows, rows, weight, vector, vector, weight, vector, fc_in, hidden, hidden,
        vector, vector, vector, vector, vector,
    )
    return jax.shard_map(local, mesh=mesh, in_specs=in_specs, out_specs=out_specs, check_vma=False)
```

```python
import functools

import jax
import jax.numpy as jnp
from jax import lax
from jax.experimental import pallas as pl
from jax.experimental.pallas import tpu as pltpu
from jax.sharding import PartitionSpec as P

D = 1600
HEADS = 25
HEAD = 64
GROUP = 8
PROMPT_DEV = 128
CONT_LEN = 256
TOK_DEV = 384
MICRO = 2
LAYERS = 2
PROMPT = 1024
KEYS = PROMPT + CONT_LEN
CHUNK = 128

f32 = jnp.float32
bf16 = jnp.bfloat16
norm_eps = 1e-05
NN = (((1,), (0,)), ((), ()))
NT = (((1,), (1,)), ((), ()))
TN = (((0,), (0,)), ((), ()))


def mm(left, right, dims=NN):
    return lax.dot_general(left, right, dims, preferred_element_type=f32)


def gelu_tanh(value):
    return jax.nn.gelu(value, approximate=True)


MESH = pl.DeviceIdType.MESH
ANY = pl.BlockSpec(memory_space=pl.ANY)
IN_VMEM = pl.BlockSpec(memory_space=pltpu.VMEM)
TILE = 512
ROW_CHUNK = 32


class Peers:
    def __init__(self):
        self.f = lax.axis_index("fsdp")
        self.t = lax.axis_index("tp")
        x, c = self.t // 2, self.t % 2
        self.x = x
        self.core = 2 * x + 1 - c
        self.over = 2 * (1 - x) + c
        self.diag = 2 * (1 - x) + 1 - c

    def greet(self):
        barrier = pltpu.get_barrier_semaphore()
        for t in (self.core, self.over):
            pl.semaphore_signal(barrier, inc=1, device_id=(self.f, t), device_id_type=MESH)
        pl.semaphore_wait(barrier, 2)

    def copy(self, source, target, sems, index, t):
        return pltpu.make_async_remote_copy(
            src_ref=source,
            dst_ref=target,
            send_sem=sems[0].at[index],
            recv_sem=sems[1].at[index],
            device_id=(self.f, t),
            device_id_type=MESH,
        )


class Gather:
    def __init__(self, peers, buf, sems):
        self.p, self.buf, self.sems = peers, buf, sems

    def piece(self, slot, index, t):
        return self.p.copy(self.buf.at[slot], self.buf.at[slot], self.sems, index, t)

    def start(self):
        p = self.p
        self.piece(p.t, 1, p.over).start()
        self.piece(p.t, 0, p.core).start()

    def wait_chip(self):
        self.piece(self.p.core, 0, self.p.core).wait_recv()

    def relay(self):
        p = self.p
        self.piece(p.over, 1, p.over).wait_recv()
        self.piece(p.over, 2, p.core).start()

    def wait_diag(self):
        self.piece(self.p.diag, 2, self.p.core).wait_recv()

    def finish(self):
        p = self.p
        self.piece(p.t, 1, p.over).wait_send()
        self.piece(p.t, 0, p.core).wait_send()
        self.piece(p.over, 2, p.core).wait_send()


class Scatter:
    def __init__(self, peers, part, from_core, over_out, from_over, sems):
        self.p, self.part, self.sems = peers, part, sems
        self.from_core, self.over_out, self.from_over = from_core, over_out, from_over

    def far_to_core(self):
        return self.p.copy(self.part.at[self.p.diag], self.from_core.at[0], self.sems, 3, self.p.core)

    def near_to_core(self):
        return self.p.copy(self.part.at[self.p.core], self.from_core.at[1], self.sems, 4, self.p.core)

    def to_over(self):
        return self.p.copy(self.over_out, self.from_over, self.sems, 5, self.p.over)

    def send_over(self):
        self.far_to_core().wait_recv()

        @pl.loop(0, self.over_out.shape[0] // ROW_CHUNK)
        def _(i):
            at = pl.ds(pl.multiple_of(i * ROW_CHUNK, ROW_CHUNK), ROW_CHUNK)
            total = self.part[self.p.over, at, :].astype(f32) + self.from_core[0, at, :].astype(f32)
            self.over_out[at, :] = total.astype(bf16)

        self.to_over().start()

    def wait(self):
        self.near_to_core().wait_recv()
        self.to_over().wait_recv()

    def rows(self, at):
        return (
            self.part[self.p.t, at, :].astype(f32)
            + self.from_core[1, at, :].astype(f32)
            + self.from_over[at, :].astype(f32)
        )

    def finish(self):
        for copy in (self.far_to_core(), self.near_to_core(), self.to_over()):
            copy.wait_send()


class Group:
    def __init__(self):
        f = lax.axis_index("fsdp")
        self.t = lax.axis_index("tp")
        self.member = f % GROUP
        self.base = f - self.member
        self.z, self.y = self.member // 2, self.member % 2

    def at(self, z, y):
        return z * 2 + y

    def ahead(self, k):
        return (self.z + k) % 4

    def behind(self, k):
        return (self.z + 4 - k) % 4

    def greet(self, peers):
        barrier = pltpu.get_barrier_semaphore()
        others = [self.at(self.z, 1 - self.y)] + [self.at(self.ahead(k), self.y) for k in (1, 2, 3)]
        for member in others:
            pl.semaphore_signal(
                barrier, inc=1, device_id=(self.base + member, self.t), device_id_type=MESH
            )
        for t in (peers.core, peers.over):
            pl.semaphore_signal(barrier, inc=1, device_id=(peers.f, t), device_id_type=MESH)
        pl.semaphore_wait(barrier, 6)

    def copy(self, source, target, sems, index, member):
        return pltpu.make_async_remote_copy(
            src_ref=source,
            dst_ref=target,
            send_sem=sems[0].at[index],
            recv_sem=sems[1].at[index],
            device_id=(self.base + member, self.t),
            device_id_type=MESH,
        )


class Background:
    def __init__(self, group, kinds, sources, targets, sems):
        self.g, self.sems = group, sems
        self.items = list(zip(kinds, sources, targets))

    def copies(self):
        g = self.g
        made = []
        for n, (kind, source, target) in enumerate(self.items):
            if kind == "y":
                made.append(g.copy(source.at[:, 1 - g.y], target, self.sems, 3 * n, g.at(g.z, 1 - g.y)))
            else:
                for k in (1, 2, 3):
                    to = g.ahead(k)
                    made.append(
                        g.copy(source.at[to], target.at[k - 1], self.sems, 3 * n + k - 1, g.at(to, g.y))
                    )
        return made

    def start(self):
        for copy in self.copies():
            copy.start()

    def finish(self):
        for copy in self.copies():
            copy.wait()


def sent_shapes(payload):
    return tuple(
        jax.ShapeDtypeStruct((4 if kind == "y" else 3,) + a.shape[-2:], a.dtype) for kind, a in payload
    )


def sent_scratch(payload):
    return [pltpu.SemaphoreType.DMA((3 * len(payload) + 1,))] * 2


def row_chunks(rows, body):
    @pl.loop(0, rows // ROW_CHUNK)
    def _(i):
        body(pl.ds(pl.multiple_of(i * ROW_CHUNK, ROW_CHUNK), ROW_CHUNK))


def tiles(extent, body):
    whole = extent // TILE

    @pl.loop(0, whole)
    def _(i):
        body(pl.ds(pl.multiple_of(i * TILE, TILE), TILE))

    if extent % TILE:
        body(pl.ds(whole * TILE, extent % TILE))


def pair_rows(ref, x):
    both = ref[pl.ds(2 * x, 2)]
    return both.reshape(2 * both.shape[1], both.shape[2])


def put_pair(ref, x, at, value):
    ref[pl.ds(2 * x, 2), :, at] = value.reshape(2, value.shape[0] // 2, value.shape[1]).astype(ref.dtype)


def norm_stats(x):
    centred = x - jnp.mean(x, -1, keepdims=True)
    scale = lax.rsqrt(jnp.mean(centred * centred, -1, keepdims=True) + norm_eps)
    return centred * scale, scale


def lanes_up(width):
    return -(-width // 128) * 128


def proj_part(w_b, width):
    return w_b.at[:, lanes_up(width) :]


def ff_fwd_kernel(
    x_ref, vec_ref, fcb_ref, wb_hbm,
    out_ref, all_hbm, pre_hbm, hid_hbm,
    wfc, wproj, buf, pre, hid, part, from_core, over_out, from_over, send, recv, local,
):
    p = Peers()
    rows = x_ref.shape[0]
    sems = (send, recv)
    gather = Gather(p, buf, sems)
    scatter = Scatter(p, part, from_core, over_out, from_over, sems)
    width = fcb_ref.shape[1]
    load_fc = pltpu.make_async_copy(wb_hbm.at[:, : wfc.shape[1]], wfc, local.at[0])
    load_proj = pltpu.make_async_copy(proj_part(wb_hbm, width), wproj, local.at[1])
    load_fc.start()
    load_proj.start()

    def norm(at):
        hat, _ = norm_stats(x_ref[at, :])
        buf[p.t, at, :] = (hat * vec_ref[5:6, :] + vec_ref[6:7, :]).astype(bf16)

    row_chunks(rows, norm)
    p.greet()
    gather.start()
    gather.wait_chip()
    load_fc.wait()

    def up(x):
        def tile(at):
            value = mm(pair_rows(buf, x), wfc[:, at]) + fcb_ref[:, at]
            put_pair(pre, x, at, value)
            put_pair(hid, x, at, gelu_tanh(value))

        tiles(width, tile)

    def down(x):
        def tile(at):
            put_pair(part, x, at, mm(pair_rows(hid, x), wproj[at, :width], NT))

        tiles(D, tile)

    up(p.x)
    gather.relay()
    gather.wait_diag()
    keep_all = pltpu.make_async_copy(buf, all_hbm, local.at[2])
    keep_all.start()
    up(1 - p.x)
    keep_pre = pltpu.make_async_copy(pre, pre_hbm, local.at[3])
    keep_hid = pltpu.make_async_copy(hid, hid_hbm, local.at[4])
    keep_pre.start()
    keep_hid.start()
    load_proj.wait()
    down(1 - p.x)
    scatter.far_to_core().start()
    scatter.send_over()
    down(p.x)
    scatter.near_to_core().start()
    scatter.wait()

    def final(at):
        out_ref[at, :] = x_ref[at, :] + scatter.rows(at) + vec_ref[7:8, :]

    row_chunks(rows, final)
    gather.finish()
    scatter.finish()
    for copy in (keep_all, keep_pre, keep_hid):
        copy.wait()


def scatter_scratch(n_tp, rows):
    return [
        pltpu.VMEM((n_tp, rows, D), bf16),
        pltpu.VMEM((2, rows, D), bf16),
        pltpu.VMEM((rows, D), bf16),
        pltpu.VMEM((rows, D), bf16),
        pltpu.SemaphoreType.DMA((6,)),
        pltpu.SemaphoreType.DMA((6,)),
    ]


def params(collective_id):
    return pltpu.CompilerParams(collective_id=collective_id, has_side_effects=True, vmem_limit_bytes=60 * 2**20)


def ff_fwd(x, vecs, fc_bias, w_b, n_tp):
    rows, width = x.shape[0], fc_bias.shape[1]
    block = (n_tp, rows)
    return pl.pallas_call(
        ff_fwd_kernel,
        out_shape=(
            jax.ShapeDtypeStruct((rows, D), f32),
            jax.ShapeDtypeStruct(block + (D,), bf16),
            jax.ShapeDtypeStruct(block + (width,), f32),
            jax.ShapeDtypeStruct(block + (width,), bf16),
        ),
        in_specs=[IN_VMEM, IN_VMEM, IN_VMEM, ANY],
        out_specs=(IN_VMEM, ANY, ANY, ANY),
        scratch_shapes=[
            pltpu.VMEM((D, lanes_up(width)), bf16),
            pltpu.VMEM((D, lanes_up(width)), bf16),
            pltpu.VMEM(block + (D,), bf16),
            pltpu.VMEM(block + (width,), f32),
            pltpu.VMEM(block + (width,), bf16),
        ]
        + scatter_scratch(n_tp, rows)
        + [pltpu.SemaphoreType.DMA((5,))],
        compiler_params=params(1),
        cost_estimate=pl.CostEstimate(
            flops=4 * n_tp * rows * D * width, bytes_accessed=40 * 2**20, transcendentals=n_tp * rows * width
        ),
    )(x, vecs, fc_bias, w_b)


def gelu_slope(u):
    a = 0.7978845608028654
    square = u * u
    t = jnp.tanh(a * (u + 0.044715 * u * square))
    return 0.5 * (1.0 + t) + 0.5 * u * (1.0 - t * t) * (a * (1.0 + 3 * 0.044715 * square))


def norm_back(x, dy, gain):
    hat, scale = norm_stats(x)
    d_hat = dy * gain
    inner = d_hat - jnp.mean(d_hat, -1, keepdims=True) - hat * jnp.mean(d_hat * hat, -1, keepdims=True)
    return scale * inner, dy * hat


def add_rows(ref, row, value):
    ref[row : row + 1, :] += jnp.sum(value, axis=0, keepdims=True)


def ff_bwd_kernel(kinds, *refs):
    n = len(kinds)
    g_ref, x_ref, vec_ref, all_hbm, pre_hbm, hid_hbm, wb_hbm = refs[:7]
    sources, refs = refs[7 : 7 + n], refs[7 + n :]
    out_ref, sums_ref, fcb_ref, dfc_hbm, dproj_hbm = refs[:5]
    targets, refs = refs[5 : 5 + n], refs[5 + n :]
    wfc, wproj, buf, other, pre, dpre, stage, part, from_core, over_out, from_over, send, recv, local = refs[:14]
    p, g = Peers(), Group()
    background = Background(g, kinds, sources, targets, refs[14:])
    rows = x_ref.shape[0]
    n_tp, width = buf.shape[0], fcb_ref.shape[1]
    sems = (send, recv)
    gather = Gather(p, buf, sems)
    scatter = Scatter(p, part, from_core, over_out, from_over, sems)
    load_proj = pltpu.make_async_copy(proj_part(wb_hbm, width), wproj, local.at[0])
    load_pre = pltpu.make_async_copy(pre_hbm, pre, local.at[1])
    load_fc = pltpu.make_async_copy(wb_hbm.at[:, : wfc.shape[1]], wfc, local.at[2])
    load_other = pltpu.make_async_copy(hid_hbm, other, local.at[3])
    for copy in (load_proj, load_pre, load_fc, load_other):
        copy.start()
    sums_ref[...] = jnp.zeros_like(sums_ref)
    fcb_ref[...] = jnp.zeros_like(fcb_ref)

    def lower(at):
        low = g_ref[at, :].astype(bf16)
        buf[p.t, at, :] = low
        add_rows(sums_ref, 7, low.astype(f32))

    row_chunks(rows, lower)
    if n:
        g.greet(p)
    else:
        p.greet()
    gather.start()
    background.start()
    gather.wait_chip()
    load_proj.wait()
    load_pre.wait()

    def through(x):
        def tile(at):
            d_hidden = mm(pair_rows(buf, x), wproj[:, at])
            u = pre[pl.ds(2 * x, 2), :, at].reshape(2 * rows, -1)
            low = (gelu_slope(u) * d_hidden).astype(bf16)
            put_pair(dpre, x, at, low)
            fcb_ref[:, at] += jnp.sum(low.astype(f32), axis=0, keepdims=True)

        tiles(width, tile)

    def down(x):
        def tile(at):
            put_pair(part, x, at, mm(pair_rows(dpre, x), wfc[at, :width], NT))

        tiles(D, tile)

    through(p.x)
    gather.relay()
    gather.wait_diag()
    through(1 - p.x)
    load_fc.wait()
    down(1 - p.x)
    scatter.far_to_core().start()
    scatter.send_over()
    down(p.x)
    scatter.near_to_core().start()

    def outer(left, right, target, sem):
        whole = D // TILE
        rest = D - whole * TILE
        flat = right[...].reshape(n_tp * rows, width)

        def tile(i, size):
            at = pl.ds(pl.multiple_of(i * TILE, TILE), size)
            value = mm(left[:, :, at].reshape(n_tp * rows, size), flat, TN)
            stage[at, :] = value.astype(bf16)

        @pl.loop(0, whole)
        def _(i):
            tile(i, TILE)

        if rest:
            tile(whole, rest)
        return pltpu.make_async_copy(stage, target, sem)

    load_other.wait()
    store = outer(buf, other, dproj_hbm, local.at[4])
    store.start()
    gather.finish()
    load_all = pltpu.make_async_copy(all_hbm, buf, local.at[5])
    load_all.start()
    scatter.wait()

    def final(at):
        dy = scatter.rows(at)
        dx, d_gain = norm_back(x_ref[at, :], dy, vec_ref[5:6, :])
        add_rows(sums_ref, 5, d_gain)
        add_rows(sums_ref, 6, dy)
        out_ref[at, :] = g_ref[at, :] + dx

    row_chunks(rows, final)
    load_all.wait()
    store.wait()
    store = outer(buf, dpre, dfc_hbm, local.at[6])
    store.start()
    scatter.finish()
    store.wait()
    background.finish()


def ff_bwd(grad, x, vecs, all_rows, pre, hidden, w_b, n_tp, payload, collective_id):
    rows, width = x.shape[0], pre.shape[2]
    block = (n_tp, rows)
    return pl.pallas_call(
        functools.partial(ff_bwd_kernel, tuple(kind for kind, _ in payload)),
        out_shape=(
            jax.ShapeDtypeStruct((rows, D), f32),
            jax.ShapeDtypeStruct((8, D), f32),
            jax.ShapeDtypeStruct((1, width), f32),
            jax.ShapeDtypeStruct((D, width), bf16),
            jax.ShapeDtypeStruct((D, width), bf16),
        )
        + sent_shapes(payload),
        in_specs=[IN_VMEM] * 3 + [ANY] * (4 + len(payload)),
        out_specs=(IN_VMEM, IN_VMEM, IN_VMEM) + (ANY,) * (2 + len(payload)),
        scratch_shapes=[
            pltpu.VMEM((D, lanes_up(width)), bf16),
            pltpu.VMEM((D, lanes_up(width)), bf16),
            pltpu.VMEM(block + (D,), bf16),
            pltpu.VMEM(block + (width,), bf16),
            pltpu.VMEM(block + (width,), f32),
            pltpu.VMEM(block + (width,), bf16),
            pltpu.VMEM((D, width), bf16),
        ]
        + scatter_scratch(n_tp, rows)
        + [pltpu.SemaphoreType.DMA((7,))]
        + sent_scratch(payload),
        compiler_params=params(collective_id),
        cost_estimate=pl.CostEstimate(
            flops=8 * n_tp * rows * D * width, bytes_accessed=50 * 2**20, transcendentals=n_tp * rows * width
        ),
    )(grad, x, vecs, all_rows, pre, hidden, w_b, *(a for _, a in payload))


class Share:
    def __init__(self, group, kv, sems):
        self.g, self.kv, self.sems = group, kv, sems
        self.partner = group.at(group.z, 1 - group.y)

    def piece(self, member, micro, index, to):
        ref = self.kv.at[member, micro]
        return self.g.copy(ref, ref, self.sems, micro * 7 + index, to)

    def own(self, micro):
        g = self.g
        return [self.piece(g.member, micro, 0, self.partner)] + [
            self.piece(g.member, micro, k, g.at(g.ahead(k), g.y)) for k in (1, 2, 3)
        ]

    def relayed(self, micro):
        g = self.g
        return [self.piece(g.at(g.behind(k), g.y), micro, 3 + k, self.partner) for k in (1, 2, 3)]

    def start(self, micro):
        for copy in self.own(micro):
            copy.start()

    def relay(self, micro):
        g = self.g
        for k, copy in zip((1, 2, 3), self.relayed(micro)):
            self.piece(g.at(g.behind(k), g.y), micro, k, self.partner).wait_recv()
            copy.start()

    def wait(self, micro):
        g = self.g
        self.piece(self.partner, micro, 0, self.partner).wait_recv()
        for k in (1, 2, 3):
            self.piece(g.at(g.behind(k), 1 - g.y), micro, 3 + k, self.partner).wait_recv()

    def finish(self, micro):
        for copy in self.own(micro) + self.relayed(micro):
            copy.wait_send()


class GroupSum:
    def __init__(self, group, parts, from_y, to_z, from_z, sems):
        self.g, self.parts, self.sems = group, parts, sems
        self.from_y, self.to_z, self.from_z = from_y, to_z, from_z

    def across(self, micro):
        g = self.g
        return g.copy(
            self.parts.at[micro, :, 1 - g.y], self.from_y.at[micro], self.sems, micro * 4, g.at(g.z, 1 - g.y)
        )

    def along(self, micro, k):
        g = self.g
        to = g.ahead(k)
        return g.copy(
            self.to_z.at[micro, to], self.from_z.at[micro, k - 1], self.sems, micro * 4 + k, g.at(to, g.y)
        )

    def start(self, micro):
        self.across(micro).start()

    def turn(self, micro):
        self.across(micro).wait_recv()

        @pl.loop(0, 4)
        def _(z):
            for kv in range(2):
                total = self.parts[micro, z, self.g.y, kv].astype(f32) + self.from_y[micro, z, kv].astype(f32)
                self.to_z[micro, z, kv] = total.astype(bf16)

        for k in (1, 2, 3):
            self.along(micro, k).start()

    def wait(self, micro):
        for k in (1, 2, 3):
            self.along(micro, k).wait_recv()

    def total(self, micro, kv):
        g = self.g
        value = self.parts[micro, g.z, g.y, kv].astype(f32) + self.from_y[micro, g.z, kv].astype(f32)
        for k in range(3):
            value = value + self.from_z[micro, k, kv].astype(f32)
        return value.astype(bf16)

    def finish(self, micro):
        self.across(micro).wait_send()
        for k in (1, 2, 3):
            self.along(micro, k).wait_send()


WIDE = 512
HEAD_PAIRS = WIDE // (2 * HEAD)
PROMPT_CHUNKS = PROMPT // CHUNK
CONT_CHUNKS = CONT_LEN // CHUNK


def chunk_at(c, base=0):
    return pl.ds(pl.multiple_of(base + c * CHUNK, CHUNK), CHUNK)


def key_limit(member):
    row = lax.broadcasted_iota(jnp.int32, (1, TOK_DEV), 1)
    return jnp.where(row < PROMPT_DEV, member * PROMPT_DEV + row, PROMPT - PROMPT_DEV + row)


def half_of(value, half):
    lane = lax.broadcasted_iota(jnp.int32, value.shape, 1)
    return jnp.where((lane >= HEAD * half) & (lane < HEAD * (half + 1)), value, jnp.zeros_like(value))


def fold(value, op):
    return op(value.reshape(value.shape[0] // 8, 8, value.shape[1]), axis=0)


def over_keys(body, prompt, own, carry):
    carry = lax.fori_loop(0, PROMPT_CHUNKS, lambda c, carry: body(c, lambda i: prompt(c, i), carry), carry)
    return lax.fori_loop(
        0, CONT_CHUNKS, lambda c, carry: body(PROMPT_CHUNKS + c, lambda i: own(c, i), carry), carry
    )


def head_pairs(head, finish):
    @pl.loop(0, HEAD_PAIRS)
    def _(pair):
        lanes = pl.ds(pl.multiple_of(pair * 2 * HEAD, 2 * HEAD), 2 * HEAD)
        head(pair, lanes, 0)

        @pl.when(pair < HEAD_PAIRS - 1)
        def _():
            head(pair, lanes, 1)

        finish(pair, lanes)


def to_slots(target, micro, first, value, lanes):
    per = target.shape[1] // MICRO
    row = first
    while row < first + value.shape[0]:
        slot, within = row // per, row % per
        count = min(per - within, first + value.shape[0] - row)
        target[slot, micro * per + within : micro * per + within + count, lanes] = value[
            row - first : row - first + count
        ]
        row += count


def pair_to_blocks(target, x, value):
    per = value.shape[0] // (2 * MICRO)
    for core in range(2):
        for micro in range(MICRO):
            at = pl.ds(pl.multiple_of((2 * x + core) * per, per), per)
            first = (core * MICRO + micro) * per
            target[micro, at, :] = value[first : first + per]


def attn_fwd_kernel(
    x_ref, vec_ref, bias_ref, wqkv_hbm, wout_hbm,
    out_ref, lse_ref, all_hbm, own_hbm, kv_hbm, mix_hbm,
    wqkv, wout, buf, own, kv, mix, s_ref, p_ref, o_ref,
    part, from_core, over_out, from_over, send, recv, gsend, grecv, local,
):
    p, g = Peers(), Group()
    rows = x_ref.shape[0]
    sems = (send, recv)
    gather = Gather(p, buf, sems)
    scatter = Scatter(p, part, from_core, over_out, from_over, sems)
    share = Share(g, kv, (gsend, grecv))
    load_qkv = pltpu.make_async_copy(wqkv_hbm.at[:, : 3 * WIDE], wqkv, local.at[0])
    load_out = pltpu.make_async_copy(wout_hbm, wout, local.at[1])
    load_qkv.start()
    load_out.start()

    def norm(at):
        hat, _ = norm_stats(x_ref[at, :])
        buf[p.t, at, :] = (hat * vec_ref[0:1, :] + vec_ref[1:2, :]).astype(bf16)

    row_chunks(rows, norm)
    g.greet(p)
    gather.start()
    gather.wait_chip()
    load_qkv.wait()

    def project(x):
        for i in range(3):
            value = mm(pair_rows(buf, x), wqkv[:, i * WIDE : (i + 1) * WIDE]) + bias_ref[i : i + 1, :]
            low = value.astype(bf16)
            if i == 0:
                low = low * HEAD ** (-0.5)
            pair_to_blocks(own.at[i], x, low)

    project(p.x)
    gather.relay()
    gather.wait_diag()
    project(1 - p.x)
    for micro in range(MICRO):
        for i in range(2):
            kv[g.member, micro, i] = own[1 + i, micro, :PROMPT_DEV, :]
        share.start(micro)
    keep_all = pltpu.make_async_copy(buf, all_hbm, local.at[2])
    keep_own = pltpu.make_async_copy(own, own_hbm, local.at[3])
    keep_all.start()
    keep_own.start()
    limit = key_limit(g.member)
    sub = lax.broadcasted_iota(jnp.int32, (CHUNK, TOK_DEV), 0)

    for micro in range(MICRO):
        if micro == 0:
            share.relay(0)
        share.wait(micro)
        if micro == 0:
            share.relay(1)

        def head(pair, lanes, half, micro=micro):
            qh = half_of(own[0, micro, :, lanes], half)

            def first(c, load, top):
                s = jnp.where(sub + c * CHUNK <= limit, mm(load(0), qh, NT), -1e30)
                s_ref[chunk_at(c), :] = s
                return jnp.maximum(top, fold(s, jnp.max))

            top = over_keys(
                first,
                lambda c, i: kv[c, micro, i, :, lanes],
                lambda c, i: own[1 + i, micro, chunk_at(c, PROMPT_DEV), lanes],
                jnp.full((8, TOK_DEV), -1e30, f32),
            )
            top = jnp.max(top, axis=0, keepdims=True)

            def second(c, total):
                e = jnp.exp(s_ref[chunk_at(c), :] - top)
                p_ref[chunk_at(c), :] = e.astype(bf16)
                return total + fold(e, jnp.sum)

            total = lax.fori_loop(0, KEYS // CHUNK, second, jnp.zeros((8, TOK_DEV), f32))
            total = jnp.sum(total, axis=0, keepdims=True)
            values = kv[:, micro, 1, :, lanes].reshape(PROMPT, 2 * HEAD)
            out = mm(values, p_ref[:PROMPT, :], TN) + mm(own[2, micro, PROMPT_DEV:, lanes], p_ref[PROMPT:, :], TN)
            at = slice(HEAD * half, HEAD * (half + 1))
            o_ref[at, :] = out[at, :] / total
            lse_ref[micro, pair, half : half + 1, :] = top + jnp.log(total)

        def finish(pair, lanes, micro=micro):
            @pl.when(pair == HEAD_PAIRS - 1)
            def _():
                o_ref[HEAD:, :] = jnp.zeros((HEAD, TOK_DEV), f32)

            to_slots(mix, micro, 0, o_ref[...].T.astype(bf16), lanes)

        head_pairs(head, finish)

    keep_kv = pltpu.make_async_copy(kv, kv_hbm, local.at[4])
    keep_mix = pltpu.make_async_copy(mix, mix_hbm, local.at[5])
    keep_kv.start()
    keep_mix.start()
    load_out.wait()

    def down(x):
        def tile(at):
            put_pair(part, x, at, mm(pair_rows(mix, x), wout[:, at]))

        tiles(D, tile)

    down(1 - p.x)
    scatter.far_to_core().start()
    scatter.send_over()
    down(p.x)
    scatter.near_to_core().start()
    scatter.wait()

    def final(at):
        out_ref[at, :] = x_ref[at, :] + (scatter.rows(at) + vec_ref[4:5, :])

    row_chunks(rows, final)
    gather.finish()
    scatter.finish()
    for micro in range(MICRO):
        share.finish(micro)
    for copy in (keep_all, keep_own, keep_kv, keep_mix):
        copy.wait()


def attn_shapes(n_tp, rows):
    return (
        ((n_tp, rows, D), bf16),
        ((3, MICRO, TOK_DEV, WIDE), bf16),
        ((GROUP, MICRO, 2, PROMPT_DEV, WIDE), bf16),
        ((n_tp, rows, WIDE), bf16),
    )


def attn_fwd(x, vecs, biases, w_qkv, w_out, n_tp, collective_id):
    rows = x.shape[0]
    saved = attn_shapes(n_tp, rows)
    return pl.pallas_call(
        attn_fwd_kernel,
        out_shape=(
            jax.ShapeDtypeStruct((rows, D), f32),
            jax.ShapeDtypeStruct((MICRO, HEAD_PAIRS, 8, TOK_DEV), f32),
        )
        + tuple(jax.ShapeDtypeStruct(*s) for s in saved),
        in_specs=[IN_VMEM, IN_VMEM, IN_VMEM, ANY, ANY],
        out_specs=(IN_VMEM, IN_VMEM, ANY, ANY, ANY, ANY),
        scratch_shapes=[pltpu.VMEM((D, 3 * WIDE), bf16), pltpu.VMEM((WIDE, D), bf16)]
        + [pltpu.VMEM(*s) for s in saved]
        + [
            pltpu.VMEM((KEYS, TOK_DEV), f32),
            pltpu.VMEM((KEYS, TOK_DEV), bf16),
            pltpu.VMEM((2 * HEAD, TOK_DEV), f32),
        ]
        + scatter_scratch(n_tp, rows)
        + [
            pltpu.SemaphoreType.DMA((7 * MICRO,)),
            pltpu.SemaphoreType.DMA((7 * MICRO,)),
            pltpu.SemaphoreType.DMA((6,)),
        ],
        compiler_params=params(collective_id),
        cost_estimate=pl.CostEstimate(flops=10**11, bytes_accessed=30 * 2**20, transcendentals=0),
    )(x, vecs, biases, w_qkv, w_out)


def attn_bwd_kernel(kinds, *refs):
    n = len(kinds)
    g_ref, x_ref, vec_ref, lse_ref, all_hbm, own_hbm, kv_hbm, mix_hbm, wqkv_hbm, wout_hbm = refs[:10]
    sources, refs = refs[10 : 10 + n], refs[10 + n :]
    out_ref, sums_ref, cols_ref, dqkv_hbm, dout_hbm = refs[:5]
    targets, refs = refs[5 : 5 + n], refs[5 + n :]
    wqkv, wout, buf, other, own, kv, gm, dkv, from_y, to_z, from_z, dkc, dqkv, stage, stage_out = refs[:15]
    p_ref, dp_ref, ds_ref, o_ref = refs[15:19]
    part, from_core, over_out, from_over, send, recv, gsend, grecv, local = refs[19:28]
    p, g = Peers(), Group()
    background = Background(g, kinds, sources, targets, refs[28:])
    rows = x_ref.shape[0]
    n_tp = buf.shape[0]
    out_width = stage_out.shape[1]
    out_step = (D - out_width) // (n_tp - 1)
    sems = (send, recv)
    gather = Gather(p, buf, sems)
    scatter = Scatter(p, part, from_core, over_out, from_over, sems)
    reduce = GroupSum(g, dkv, from_y, to_z, from_z, (gsend, grecv))
    load_out = pltpu.make_async_copy(wout_hbm, wout, local.at[0])
    load_own = pltpu.make_async_copy(own_hbm, own, local.at[1])
    load_kv = pltpu.make_async_copy(kv_hbm, kv, local.at[2])
    load_qkv = pltpu.make_async_copy(wqkv_hbm.at[:, : 3 * WIDE], wqkv, local.at[3])
    load_mix = pltpu.make_async_copy(mix_hbm, other, local.at[4])
    for copy in (load_out, load_own, load_kv, load_qkv, load_mix):
        copy.start()
    sums_ref[...] = jnp.zeros_like(sums_ref)

    def lower(at):
        low = g_ref[at, :].astype(bf16)
        buf[p.t, at, :] = low
        add_rows(sums_ref, 4, low.astype(f32))

    row_chunks(rows, lower)
    g.greet(p)
    gather.start()
    background.start()
    gather.wait_chip()
    load_out.wait()

    def mixed_back(x):
        pair_to_blocks(gm, x, mm(pair_rows(buf, x), wout[...], NT).astype(bf16))

    mixed_back(p.x)
    gather.relay()
    gather.wait_diag()
    mixed_back(1 - p.x)
    load_own.wait()
    load_kv.wait()
    limit = key_limit(g.member)
    sub = lax.broadcasted_iota(jnp.int32, (CHUNK, TOK_DEV), 0)

    for micro in range(MICRO):

        def head(pair, lanes, half, micro=micro):
            if micro == 1 and half == 0:

                @pl.when(pair == HEAD_PAIRS - 1)
                def _():
                    reduce.turn(0)

            qh = half_of(own[0, micro, :, lanes], half)
            gh = half_of(gm[micro, :, lanes], half)
            lse = lse_ref[micro, pair, half : half + 1, :]

            def first(c, load, inner):
                s = jnp.where(sub + c * CHUNK <= limit, mm(load(0), qh, NT), -1e30)
                e = jnp.exp(s - lse)
                dp = mm(load(1), gh, NT)
                p_ref[chunk_at(c), :] = e
                dp_ref[chunk_at(c), :] = dp
                return inner + fold(e * dp, jnp.sum)

            inner = over_keys(
                first,
                lambda c, i: kv[c, micro, i, :, lanes],
                lambda c, i: own[1 + i, micro, chunk_at(c, PROMPT_DEV), lanes],
                jnp.zeros((8, TOK_DEV), f32),
            )
            inner = jnp.sum(inner, axis=0, keepdims=True)

            def second(c, put):
                e = p_ref[chunk_at(c), :]
                ds = (e * (dp_ref[chunk_at(c), :] - inner)).astype(bf16)
                ds_ref[chunk_at(c), :] = ds
                put(0, mm(ds, qh))
                put(1, mm(e.astype(bf16), gh))

            @pl.loop(0, PROMPT_CHUNKS)
            def _(c):
                def put(i, value):
                    at = (micro, c // 2, c % 2, i, slice(None), lanes)
                    if half:
                        value = value + dkv[at].astype(f32)
                    dkv[at] = value.astype(bf16)

                second(c, put)

            @pl.loop(0, CONT_CHUNKS)
            def _(c):
                def put(i, value):
                    at = (i, chunk_at(c), lanes)
                    if half:
                        value = value + dkc[at].astype(f32)
                    dkc[at] = value.astype(bf16)

                second(PROMPT_CHUNKS + c, put)

            keys = kv[:, micro, 0, :, lanes].reshape(PROMPT, 2 * HEAD)
            dq = mm(keys, ds_ref[:PROMPT, :], TN) + mm(own[1, micro, PROMPT_DEV:, lanes], ds_ref[PROMPT:, :], TN)
            at = slice(HEAD * half, HEAD * (half + 1))
            o_ref[at, :] = dq[at, :] * HEAD ** (-0.5)

        def finish(pair, lanes, micro=micro):
            @pl.when(pair == HEAD_PAIRS - 1)
            def _():
                o_ref[HEAD:, :] = jnp.zeros((HEAD, TOK_DEV), f32)

            to_slots(dqkv, micro, 0, o_ref[...].T.astype(bf16), lanes)

        head_pairs(head, finish)
        reduce.start(micro)
        for i in range(2):
            to_slots(dqkv, micro, PROMPT_DEV, dkc[i], slice((1 + i) * WIDE, (2 + i) * WIDE))

    load_mix.wait()
    columns = pl.ds(pl.multiple_of(p.t * out_step, 128), out_width)

    def outer(source, target, right, body):
        flat = right.reshape(n_tp * rows, right.shape[-1])

        def tile(at):
            left = source[:, :, at].reshape(n_tp * rows, -1)
            target[at, :] = mm(left, flat, TN).astype(bf16)

        body(D, tile)

    outer(other, stage_out, buf[:, :, columns], tiles)
    keep_out = pltpu.make_async_copy(stage_out, dout_hbm, local.at[5])
    keep_out.start()
    load_all = pltpu.make_async_copy(all_hbm, other, local.at[6])
    load_all.start()
    reduce.turn(1)
    for micro in range(MICRO):
        reduce.wait(micro)
        for i in range(2):
            to_slots(dqkv, micro, 0, reduce.total(micro, i), slice((1 + i) * WIDE, (2 + i) * WIDE))
    load_qkv.wait()

    def down(x):
        def tile(at):
            put_pair(part, x, at, mm(pair_rows(dqkv, x), wqkv[at, :], NT))

        tiles(D, tile)

    down(1 - p.x)
    scatter.far_to_core().start()
    scatter.send_over()
    down(p.x)
    scatter.near_to_core().start()
    load_all.wait()
    outer(other, stage, dqkv[...], tiles)
    keep_qkv = pltpu.make_async_copy(stage, dqkv_hbm, local.at[7])
    keep_qkv.start()
    cols_ref[...] = jnp.zeros_like(cols_ref)

    @pl.loop(0, n_tp * rows // ROW_CHUNK)
    def _(i):
        per = rows // ROW_CHUNK
        at = pl.ds(pl.multiple_of((i % per) * ROW_CHUNK, ROW_CHUNK), ROW_CHUNK)
        add_rows(cols_ref, 0, dqkv[i // per, at, :].astype(f32))

    scatter.wait()

    def final(at):
        dy = scatter.rows(at)
        dx, d_gain = norm_back(x_ref[at, :], dy, vec_ref[0:1, :])
        add_rows(sums_ref, 0, d_gain)
        add_rows(sums_ref, 1, dy)
        out_ref[at, :] = g_ref[at, :] + dx

    row_chunks(rows, final)
    gather.finish()
    scatter.finish()
    for micro in range(MICRO):
        reduce.finish(micro)
    keep_out.wait()
    keep_qkv.wait()
    background.finish()


def attn_bwd(grad, x, vecs, lse, all_rows, own, kv, mixed_all, w_a, w_out, out_width, n_tp, payload, collective_id):
    rows = x.shape[0]
    pieces = (MICRO, 4, 2, 2, PROMPT_DEV, WIDE)
    return pl.pallas_call(
        functools.partial(attn_bwd_kernel, tuple(kind for kind, _ in payload)),
        out_shape=(
            jax.ShapeDtypeStruct((rows, D), f32),
            jax.ShapeDtypeStruct((8, D), f32),
            jax.ShapeDtypeStruct((1, 3 * WIDE), f32),
            jax.ShapeDtypeStruct((D, 3 * WIDE), bf16),
            jax.ShapeDtypeStruct((D, out_width), bf16),
        )
        + sent_shapes(payload),
        in_specs=[IN_VMEM] * 4 + [ANY] * (6 + len(payload)),
        out_specs=(IN_VMEM, IN_VMEM, IN_VMEM) + (ANY,) * (2 + len(payload)),
        scratch_shapes=[
            pltpu.VMEM((D, 3 * WIDE), bf16),
            pltpu.VMEM((WIDE, D), bf16),
            pltpu.VMEM((n_tp, rows, D), bf16),
            pltpu.VMEM((n_tp, rows, D), bf16),
            pltpu.VMEM((3, MICRO, TOK_DEV, WIDE), bf16),
            pltpu.VMEM((GROUP, MICRO, 2, PROMPT_DEV, WIDE), bf16),
            pltpu.VMEM((MICRO, TOK_DEV, WIDE), bf16),
            pltpu.VMEM(pieces, bf16),
            pltpu.VMEM((MICRO, 4, 2, PROMPT_DEV, WIDE), bf16),
            pltpu.VMEM((MICRO, 4, 2, PROMPT_DEV, WIDE), bf16),
            pltpu.VMEM((MICRO, 3, 2, PROMPT_DEV, WIDE), bf16),
            pltpu.VMEM((2, CONT_LEN, WIDE), bf16),
            pltpu.VMEM((n_tp, rows, 3 * WIDE), bf16),
            pltpu.VMEM((D, 3 * WIDE), bf16),
            pltpu.VMEM((D, out_width), bf16),
            pltpu.VMEM((KEYS, TOK_DEV), f32),
            pltpu.VMEM((KEYS, TOK_DEV), f32),
            pltpu.VMEM((KEYS, TOK_DEV), bf16),
            pltpu.VMEM((2 * HEAD, TOK_DEV), f32),
        ]
        + scatter_scratch(n_tp, rows)
        + [
            pltpu.SemaphoreType.DMA((4 * MICRO,)),
            pltpu.SemaphoreType.DMA((4 * MICRO,)),
            pltpu.SemaphoreType.DMA((8,)),
        ]
        + sent_scratch(payload),
        compiler_params=params(collective_id),
        cost_estimate=pl.CostEstimate(flops=2 * 10**11, bytes_accessed=50 * 2**20, transcendentals=0),
    )(grad, x, vecs, lse, all_rows, own, kv, mixed_all, w_a, w_out, *(a for _, a in payload))


def send_kernel(kinds, *refs):
    n = len(kinds)
    g = Group()
    background = Background(g, kinds, refs[:n], refs[n : 2 * n], refs[2 * n :])
    barrier = pltpu.get_barrier_semaphore()
    others = []
    if "y" in kinds:
        others += [g.at(g.z, 1 - g.y)]
    if "z" in kinds:
        others += [g.at(g.ahead(k), g.y) for k in (1, 2, 3)]
    for member in others:
        pl.semaphore_signal(barrier, inc=1, device_id=(g.base + member, g.t), device_id_type=MESH)
    pl.semaphore_wait(barrier, len(others))
    background.start()
    background.finish()


def send_only(payload, collective_id):
    return pl.pallas_call(
        functools.partial(send_kernel, tuple(kind for kind, _ in payload)),
        out_shape=sent_shapes(payload),
        in_specs=[ANY] * len(payload),
        out_specs=(ANY,) * len(payload),
        scratch_shapes=sent_scratch(payload),
        compiler_params=params(collective_id),
    )(*(a for _, a in payload))


def forward_layer(x, layer, weights, vecs, fc_bias, cols, n_tp):
    w_a, w_out, w_b = weights
    width = D - HEADS // n_tp * HEAD * (n_tp - 1)
    query_bias, value_bias = (lax.dynamic_slice_in_dim(vecs[i], cols, width) for i in (2, 3))
    biases = widen(jnp.stack([query_bias, jnp.zeros_like(query_bias), value_bias]))
    x_mid, lse, all_rows, own, kv, mixed = attn_fwd(x, vecs, biases, w_a, w_out, n_tp, 5 + layer)
    x_next, second_all, hidden_pre, hidden = ff_fwd(x_mid, vecs, fc_bias[None], w_b, n_tp)
    mixed_all = heads_joined(lax.all_gather(mixed[:, :, :width], "tp"), n_tp)
    return x_next, (x, lse, all_rows, own, kv, mixed_all, x_mid, second_all, hidden_pre, hidden)


def fsdp_sum(part):
    return lax.psum_scatter(part, "fsdp", scatter_dimension=0, tiled=True).astype(f32)


def heads_joined(parts, n_tp):
    step = HEADS // n_tp * HEAD
    return jnp.concatenate([parts[t][..., :step] for t in range(n_tp - 1)] + [parts[n_tp - 1]], axis=-1)


def widen(value, axis=-1):
    pads = [(0, 0)] * value.ndim
    pads[axis] = (0, WIDE - value.shape[axis])
    return jnp.pad(value, pads)


def to_y(part):
    return ("y", part.reshape(4, 2, -1, part.shape[1]))


def to_z(part, arrived):
    own = lax.dynamic_index_in_dim(part.reshape(4, 2, -1, part.shape[1]), lax.axis_index("fsdp") % 2, 1, False)
    return ("z", (own.astype(f32) + arrived.astype(f32)).astype(bf16))


def owned(summed, arrived):
    own = lax.dynamic_index_in_dim(summed[1], lax.axis_index("fsdp") // 2, 0, False)
    return own.astype(f32) + jnp.sum(arrived.astype(f32), 0)


def vector_sums(ff_sums, attn_sums, col_sums, fc_bias_sums, cols, width):
    def placed(part):
        return lax.dynamic_update_slice_in_dim(jnp.zeros((D,), f32), part, cols, 0)

    vector_grads = jnp.stack(
        [
            attn_sums[0],
            attn_sums[1],
            placed(col_sums[0, :width]),
            placed(col_sums[0, 2 * WIDE : 2 * WIDE + width]),
            attn_sums[4],
            ff_sums[5],
            ff_sums[6],
            ff_sums[7],
        ]
    )
    vector_sum = lax.psum(lax.psum_scatter(vector_grads, "fsdp", scatter_dimension=1, tiled=True), "tp")
    return vector_sum, lax.psum_scatter(fc_bias_sums[0], "fsdp", scatter_dimension=0, tiled=True)


def backward(grad, weights, vecs, saves, cols, n_tp):
    width = D - HEADS // n_tp * HEAD * (n_tp - 1)
    staged = lax.axis_size("fsdp") == GROUP
    sums = [None] * LAYERS
    parts = [None] * LAYERS
    waiting_y, waiting_z, done = [], [], {}

    def load(limit_z, limit_y):
        chosen_z = [waiting_z.pop(0) for _ in range(min(limit_z, len(waiting_z)))]
        chosen_y = [waiting_y.pop(0) for _ in range(min(limit_y, len(waiting_y)))]
        return chosen_z, chosen_y, [item for _, item in chosen_z] + [to_y(part) for _, part in chosen_y]

    def unload(chosen_z, chosen_y, arrived):
        for (name, item), got in zip(chosen_z, arrived):
            done[name] = owned(item, got)
        for (name, part), got in zip(chosen_y, arrived[len(chosen_z) :]):
            waiting_z.append((name, to_z(part, got)))

    def produced(layer, names, values):
        for name, value in zip(names, values):
            if staged:
                waiting_y.append(((layer, name), value))
            else:
                done[layer, name] = fsdp_sum(value)

    plan = {(1, 0): (0, 0), (1, 1): (0, 2), (0, 0): (1, 2), (0, 1): (3, 2)}
    for layer in reversed(range(LAYERS)):
        w_a, w_out, w_b = weights[layer]
        x, lse, all_rows, own, kv, mixed_all, x_mid, second_all, hidden_pre, hidden = saves[layer]
        chosen_z, chosen_y, payload = load(*plan[layer, 0])
        grad, ff_sums, fc_bias_sums, grad_fc, grad_proj, *arrived = ff_bwd(
            grad, x_mid, vecs[layer], second_all, hidden_pre, hidden, w_b, n_tp, payload, 10 + layer
        )
        unload(chosen_z, chosen_y, arrived)
        produced(layer, ("proj", "fc"), (grad_proj, grad_fc))
        chosen_z, chosen_y, payload = load(*plan[layer, 1])
        grad, attn_sums, col_sums, grad_qkv, grad_out, *arrived = attn_bwd(
            grad, x, vecs[layer], lse, all_rows, own, kv, mixed_all, w_a, w_out, width, n_tp, payload, 20 + layer
        )
        unload(chosen_z, chosen_y, arrived)
        produced(layer, ("qkv", "out"), (grad_qkv, grad_out))
        parts[layer] = (ff_sums, attn_sums, col_sums, fc_bias_sums)
    number = 30
    while waiting_y or waiting_z:
        chosen_z, chosen_y, payload = load(9, 9)
        unload(chosen_z, chosen_y, send_only(payload, number))
        number += 1
    for layer in range(LAYERS):
        vector_sum, fc_bias_sum = vector_sums(*parts[layer], cols, width)
        qkv_all = lax.all_gather(done[layer, "qkv"].astype(bf16).reshape(-1, 3, WIDE)[:, :, :width], "tp")
        out_all = lax.all_gather(done[layer, "out"].astype(bf16), "tp")
        qkv_grad = heads_joined(qkv_all, n_tp).reshape(-1, 3 * D).astype(f32)
        out_grad = heads_joined(out_all, n_tp).astype(f32)
        sums[layer] = (qkv_grad, out_grad, done[layer, "fc"], done[layer, "proj"].T, fc_bias_sum, vector_sum)
    return grad, sums


def local(
    tokens,
    qkv_weight,
    query_bias,
    value_bias,
    out_weight,
    out_bias,
    fc_weight,
    fc_bias,
    proj_weight,
    proj_bias,
    first_gain,
    first_bias,
    second_gain,
    second_bias,
    out_grad,
):
    n_tp = lax.axis_size("tp")
    tp = lax.axis_index("tp")
    row_count = tokens.shape[1]
    step = HEADS // n_tp * HEAD
    width = D - step * (n_tp - 1)
    cols = tp * step
    keep = (lax.iota(jnp.int32, width) < step) | (tp == n_tp - 1)

    def gathered(part):
        return lax.all_gather(part, "fsdp", axis=0, tiled=True)

    vectors = jnp.stack(
        [first_gain, first_bias, query_bias, value_bias, out_bias, second_gain, second_bias, proj_bias, fc_bias[:, 0]]
    ).reshape(9 * LAYERS, -1)

    weights = []
    for layer in range(LAYERS):
        sides = [widen(lax.dynamic_slice_in_dim(qkv_weight[layer], cols + i * D, width, 1)) for i in range(3)]
        sides.append(widen(lax.dynamic_slice_in_dim(out_weight[layer], cols, width, 1)))
        if layer == 0:
            sides.append(jnp.pad(vectors.T, ((0, 0), (0, 128 - 9 * LAYERS))))
        w_a = gathered(jnp.concatenate(sides, axis=1))
        if layer == 0:
            vectors = w_a[:, 4 * WIDE : 4 * WIDE + 9 * LAYERS].T.astype(f32).reshape(9, LAYERS, D)
        out_cols = w_a[:, 3 * WIDE : 3 * WIDE + width]
        out_parts = jnp.stack([out_cols[t * step : t * step + width] for t in range(n_tp)])
        w_out = heads_joined(lax.all_to_all(out_parts, "tp", 0, 0), n_tp)
        w_out = widen(jnp.where(keep[:, None], w_out, jnp.zeros_like(w_out)), 0)
        fc, proj = fc_weight[layer], proj_weight[layer].T
        more = ((0, 0), (0, lanes_up(fc.shape[1]) - fc.shape[1]))
        w_b = gathered(jnp.concatenate([jnp.pad(fc, more), jnp.pad(proj, more)], axis=1))
        weights.append((w_a, w_out, w_b))

    state = tokens.astype(f32).reshape(MICRO * row_count, D)
    saves = []
    for layer in range(LAYERS):
        state, saved = forward_layer(
            state, layer, weights[layer], vectors[:8, layer], vectors[8, layer], cols, n_tp
        )
        saves.append(saved)
    out_tokens = state.astype(bf16).reshape(tokens.shape)
    grad = out_grad.astype(f32).reshape(MICRO * row_count, D)
    grad, sums = backward(
        grad, weights, [vectors[:8, layer] for layer in range(LAYERS)], saves, cols, n_tp
    )
    qkv_g, out_g, fc_g, proj_g, fc_bias_g, vec_g = (
        jnp.stack([sums[layer][i] for layer in range(LAYERS)]) for i in range(6)
    )
    return (
        out_tokens,
        grad.reshape(tokens.shape),
        qkv_g,
        vec_g[:, 2],
        vec_g[:, 3],
        out_g,
        vec_g[:, 4],
        fc_g,
        fc_bias_g[:, None],
        proj_g,
        vec_g[:, 7],
        vec_g[:, 0],
        vec_g[:, 1],
        vec_g[:, 5],
        vec_g[:, 6],
    )


def solution(mesh):
    rows = P(None, ("fsdp", "tp"), None)
    weight = P(None, "fsdp", None)
    vector = P(None, "fsdp")
    fc_in = P(None, "fsdp", "tp")
    hidden = P(None, "tp", "fsdp")
    in_specs = (
        rows, weight, vector, vector, weight, vector, fc_in, hidden, hidden,
        vector, vector, vector, vector, vector, rows,
    )
    out_specs = (
        rows, rows, weight, vector, vector, weight, vector, fc_in, hidden, hidden,
        vector, vector, vector, vector, vector,
    )
    return jax.shard_map(local, mesh=mesh, in_specs=in_specs, out_specs=out_specs, check_vma=False)
```

```python
import functools

import jax
import jax.numpy as jnp
from jax import lax
from jax.experimental import pallas as pl
from jax.experimental.pallas import tpu as pltpu
from jax.sharding import PartitionSpec as P

D = 1600
HEADS = 25
HEAD = 64
GROUP = 8
PROMPT_DEV = 128
CONT_LEN = 256
TOK_DEV = 384
MICRO = 2
LAYERS = 2
PROMPT = 1024
KEYS = PROMPT + CONT_LEN
CHUNK = 128

f32 = jnp.float32
bf16 = jnp.bfloat16
norm_eps = 1e-05
NN = (((1,), (0,)), ((), ()))
NT = (((1,), (1,)), ((), ()))
TN = (((0,), (0,)), ((), ()))


def mm(left, right, dims=NN):
    return lax.dot_general(left, right, dims, preferred_element_type=f32)


def gelu_tanh(value):
    return jax.nn.gelu(value, approximate=True)


MESH = pl.DeviceIdType.MESH
ANY = pl.BlockSpec(memory_space=pl.ANY)
IN_VMEM = pl.BlockSpec(memory_space=pltpu.VMEM)
TILE = 512
ROW_CHUNK = 32


class Peers:
    def __init__(self):
        self.f = lax.axis_index("fsdp")
        self.t = lax.axis_index("tp")
        x, c = self.t // 2, self.t % 2
        self.x = x
        self.core = 2 * x + 1 - c
        self.over = 2 * (1 - x) + c
        self.diag = 2 * (1 - x) + 1 - c

    def greet(self):
        barrier = pltpu.get_barrier_semaphore()
        for t in (self.core, self.over):
            pl.semaphore_signal(barrier, inc=1, device_id=(self.f, t), device_id_type=MESH)
        pl.semaphore_wait(barrier, 2)

    def copy(self, source, target, sems, index, t):
        return pltpu.make_async_remote_copy(
            src_ref=source,
            dst_ref=target,
            send_sem=sems[0].at[index],
            recv_sem=sems[1].at[index],
            device_id=(self.f, t),
            device_id_type=MESH,
        )


class Gather:
    def __init__(self, peers, buf, sems):
        self.p, self.buf, self.sems = peers, buf, sems

    def piece(self, slot, index, t):
        return self.p.copy(self.buf.at[slot], self.buf.at[slot], self.sems, index, t)

    def start(self):
        p = self.p
        self.piece(p.t, 1, p.over).start()
        self.piece(p.t, 0, p.core).start()

    def wait_chip(self):
        self.piece(self.p.core, 0, self.p.core).wait_recv()

    def relay(self):
        p = self.p
        self.piece(p.over, 1, p.over).wait_recv()
        self.piece(p.over, 2, p.core).start()

    def wait_diag(self):
        self.piece(self.p.diag, 2, self.p.core).wait_recv()

    def finish(self):
        p = self.p
        self.piece(p.t, 1, p.over).wait_send()
        self.piece(p.t, 0, p.core).wait_send()
        self.piece(p.over, 2, p.core).wait_send()


class Scatter:
    def __init__(self, peers, part, from_core, over_out, from_over, sems):
        self.p, self.part, self.sems = peers, part, sems
        self.from_core, self.over_out, self.from_over = from_core, over_out, from_over

    def far_to_core(self):
        return self.p.copy(self.part.at[self.p.diag], self.from_core.at[0], self.sems, 3, self.p.core)

    def near_to_core(self):
        return self.p.copy(self.part.at[self.p.core], self.from_core.at[1], self.sems, 4, self.p.core)

    def to_over(self):
        return self.p.copy(self.over_out, self.from_over, self.sems, 5, self.p.over)

    def send_over(self):
        self.far_to_core().wait_recv()

        @pl.loop(0, self.over_out.shape[0] // ROW_CHUNK)
        def _(i):
            at = pl.ds(pl.multiple_of(i * ROW_CHUNK, ROW_CHUNK), ROW_CHUNK)
            total = self.part[self.p.over, at, :].astype(f32) + self.from_core[0, at, :].astype(f32)
            self.over_out[at, :] = total.astype(bf16)

        self.to_over().start()

    def wait(self):
        self.near_to_core().wait_recv()
        self.to_over().wait_recv()

    def rows(self, at):
        return (
            self.part[self.p.t, at, :].astype(f32)
            + self.from_core[1, at, :].astype(f32)
            + self.from_over[at, :].astype(f32)
        )

    def finish(self):
        for copy in (self.far_to_core(), self.near_to_core(), self.to_over()):
            copy.wait_send()


class Group:
    def __init__(self):
        f = lax.axis_index("fsdp")
        self.t = lax.axis_index("tp")
        self.member = f % GROUP
        self.base = f - self.member
        self.z, self.y = self.member // 2, self.member % 2

    def at(self, z, y):
        return z * 2 + y

    def ahead(self, k):
        return (self.z + k) % 4

    def behind(self, k):
        return (self.z + 4 - k) % 4

    def greet(self, peers, with_diag=False):
        barrier = pltpu.get_barrier_semaphore()
        others = [self.at(self.z, 1 - self.y)] + [self.at(self.ahead(k), self.y) for k in (1, 2, 3)]
        for member in others:
            pl.semaphore_signal(
                barrier, inc=1, device_id=(self.base + member, self.t), device_id_type=MESH
            )
        near = [peers.core, peers.over] + [peers.diag] * with_diag
        for t in near:
            pl.semaphore_signal(barrier, inc=1, device_id=(peers.f, t), device_id_type=MESH)
        pl.semaphore_wait(barrier, 4 + len(near))

    def copy(self, source, target, sems, index, member):
        return pltpu.make_async_remote_copy(
            src_ref=source,
            dst_ref=target,
            send_sem=sems[0].at[index],
            recv_sem=sems[1].at[index],
            device_id=(self.base + member, self.t),
            device_id_type=MESH,
        )


class Background:
    def __init__(self, group, peers, kinds, sources, targets, sems):
        self.g, self.p, self.sems = group, peers, sems
        self.items = list(zip(kinds, sources, targets))

    def block_copies(self, n, source, target):
        p, sems = self.p, self.sems
        return (
            p.copy(source, target.at[p.t], sems, 4 * n, p.core),
            p.copy(source, target.at[p.t], sems, 4 * n + 1, p.over),
            p.copy(target.at[p.over], target.at[p.over], sems, 4 * n + 2, p.core),
            pltpu.make_async_copy(source, target.at[p.t], sems[0].at[4 * n + 3]),
        )

    def copies(self):
        g = self.g
        made = []
        for n, (kind, source, target) in enumerate(self.items):
            if kind == "y":
                made.append(g.copy(source.at[:, 1 - g.y], target, self.sems, 4 * n, g.at(g.z, 1 - g.y)))
            elif kind == "z":
                for k in (1, 2, 3):
                    to = g.ahead(k)
                    made.append(
                        g.copy(source.at[to], target.at[k - 1], self.sems, 4 * n + k - 1, g.at(to, g.y))
                    )
        return made

    def start(self):
        for copy in self.copies():
            copy.start()
        for n, (kind, source, target) in enumerate(self.items):
            if kind == "t":
                to_core, to_over, _, local = self.block_copies(n, source, target)
                to_over.start()
                to_core.start()
                local.start()

    def finish(self):
        p = self.p
        for n, (kind, source, target) in enumerate(self.items):
            if kind == "t":
                p.copy(source, target.at[p.over], self.sems, 4 * n + 1, p.over).wait_recv()
                self.block_copies(n, source, target)[2].start()
        for copy in self.copies():
            copy.wait()
        for n, (kind, source, target) in enumerate(self.items):
            if kind == "t":
                p.copy(source, target.at[p.core], self.sems, 4 * n, p.core).wait_recv()
                p.copy(source, target.at[p.diag], self.sems, 4 * n + 2, p.core).wait_recv()
                to_core, to_over, relay, local = self.block_copies(n, source, target)
                for copy in (to_core, to_over, relay):
                    copy.wait_send()
                local.wait()


def sent_shapes(payload):
    return tuple(
        jax.ShapeDtypeStruct((3 if kind == "z" else 4,) + a.shape[-2:], a.dtype) for kind, a in payload
    )


def sent_scratch(payload):
    return [pltpu.SemaphoreType.DMA((4 * len(payload) + 1,))] * 2


def row_chunks(rows, body):
    @pl.loop(0, rows // ROW_CHUNK)
    def _(i):
        body(pl.ds(pl.multiple_of(i * ROW_CHUNK, ROW_CHUNK), ROW_CHUNK))


def tiles(extent, body):
    whole = extent // TILE

    @pl.loop(0, whole)
    def _(i):
        body(pl.ds(pl.multiple_of(i * TILE, TILE), TILE))

    if extent % TILE:
        body(pl.ds(whole * TILE, extent % TILE))


def pair_rows(ref, x):
    both = ref[pl.ds(2 * x, 2)]
    return both.reshape(2 * both.shape[1], both.shape[2])


def put_pair(ref, x, at, value):
    ref[pl.ds(2 * x, 2), :, at] = value.reshape(2, value.shape[0] // 2, value.shape[1]).astype(ref.dtype)


def norm_stats(x):
    centred = x - jnp.mean(x, -1, keepdims=True)
    scale = lax.rsqrt(jnp.mean(centred * centred, -1, keepdims=True) + norm_eps)
    return centred * scale, scale


def lanes_up(width):
    return -(-width // 128) * 128


def proj_part(w_b, width):
    return w_b.at[:, lanes_up(width) :]


def ff_fwd_kernel(
    x_ref, vec_ref, fcb_ref, wb_hbm,
    out_ref, all_hbm, pre_hbm, hid_hbm,
    wfc, wproj, buf, pre, hid, part, from_core, over_out, from_over, send, recv, local,
):
    p = Peers()
    rows = x_ref.shape[0]
    sems = (send, recv)
    gather = Gather(p, buf, sems)
    scatter = Scatter(p, part, from_core, over_out, from_over, sems)
    width = fcb_ref.shape[1]
    load_fc = pltpu.make_async_copy(wb_hbm.at[:, : wfc.shape[1]], wfc, local.at[0])
    load_proj = pltpu.make_async_copy(proj_part(wb_hbm, width), wproj, local.at[1])
    load_fc.start()
    load_proj.start()

    def norm(at):
        hat, _ = norm_stats(x_ref[at, :])
        buf[p.t, at, :] = (hat * vec_ref[5:6, :] + vec_ref[6:7, :]).astype(bf16)

    row_chunks(rows, norm)
    p.greet()
    gather.start()
    gather.wait_chip()
    load_fc.wait()

    def up(x):
        def tile(at):
            value = mm(pair_rows(buf, x), wfc[:, at]) + fcb_ref[:, at]
            put_pair(pre, x, at, value)
            put_pair(hid, x, at, gelu_tanh(value))

        tiles(width, tile)

    def down(x):
        def tile(at):
            put_pair(part, x, at, mm(pair_rows(hid, x), wproj[at, :width], NT))

        tiles(D, tile)

    up(p.x)
    gather.relay()
    gather.wait_diag()
    keep_all = pltpu.make_async_copy(buf, all_hbm, local.at[2])
    keep_all.start()
    up(1 - p.x)
    keep_pre = pltpu.make_async_copy(pre, pre_hbm, local.at[3])
    keep_hid = pltpu.make_async_copy(hid, hid_hbm, local.at[4])
    keep_pre.start()
    keep_hid.start()
    load_proj.wait()
    down(1 - p.x)
    scatter.far_to_core().start()
    scatter.send_over()
    down(p.x)
    scatter.near_to_core().start()
    scatter.wait()

    def final(at):
        out_ref[at, :] = x_ref[at, :] + scatter.rows(at) + vec_ref[7:8, :]

    row_chunks(rows, final)
    gather.finish()
    scatter.finish()
    for copy in (keep_all, keep_pre, keep_hid):
        copy.wait()


def scatter_scratch(n_tp, rows):
    return [
        pltpu.VMEM((n_tp, rows, D), bf16),
        pltpu.VMEM((2, rows, D), bf16),
        pltpu.VMEM((rows, D), bf16),
        pltpu.VMEM((rows, D), bf16),
        pltpu.SemaphoreType.DMA((6,)),
        pltpu.SemaphoreType.DMA((6,)),
    ]


def params(collective_id):
    return pltpu.CompilerParams(collective_id=collective_id, has_side_effects=True, vmem_limit_bytes=60 * 2**20)


def ff_fwd(x, vecs, fc_bias, w_b, n_tp):
    rows, width = x.shape[0], fc_bias.shape[1]
    block = (n_tp, rows)
    return pl.pallas_call(
        ff_fwd_kernel,
        out_shape=(
            jax.ShapeDtypeStruct((rows, D), f32),
            jax.ShapeDtypeStruct(block + (D,), bf16),
            jax.ShapeDtypeStruct(block + (width,), f32),
            jax.ShapeDtypeStruct(block + (width,), bf16),
        ),
        in_specs=[IN_VMEM, IN_VMEM, IN_VMEM, ANY],
        out_specs=(IN_VMEM, ANY, ANY, ANY),
        scratch_shapes=[
            pltpu.VMEM((D, lanes_up(width)), bf16),
            pltpu.VMEM((D, lanes_up(width)), bf16),
            pltpu.VMEM(block + (D,), bf16),
            pltpu.VMEM(block + (width,), f32),
            pltpu.VMEM(block + (width,), bf16),
        ]
        + scatter_scratch(n_tp, rows)
        + [pltpu.SemaphoreType.DMA((5,))],
        compiler_params=params(1),
        cost_estimate=pl.CostEstimate(
            flops=4 * n_tp * rows * D * width, bytes_accessed=40 * 2**20, transcendentals=n_tp * rows * width
        ),
    )(x, vecs, fc_bias, w_b)


def gelu_slope(u):
    a = 0.7978845608028654
    square = u * u
    t = jnp.tanh(a * (u + 0.044715 * u * square))
    return 0.5 * (1.0 + t) + 0.5 * u * (1.0 - t * t) * (a * (1.0 + 3 * 0.044715 * square))


def norm_back(x, dy, gain):
    hat, scale = norm_stats(x)
    d_hat = dy * gain
    inner = d_hat - jnp.mean(d_hat, -1, keepdims=True) - hat * jnp.mean(d_hat * hat, -1, keepdims=True)
    return scale * inner, dy * hat


def add_rows(ref, row, value):
    ref[row : row + 1, :] += jnp.sum(value, axis=0, keepdims=True)


def ff_bwd_kernel(kinds, *refs):
    n = len(kinds)
    g_ref, x_ref, vec_ref, all_hbm, pre_hbm, hid_hbm, wb_hbm = refs[:7]
    sources, refs = refs[7 : 7 + n], refs[7 + n :]
    out_ref, sums_ref, fcb_ref, dfc_hbm, dproj_hbm = refs[:5]
    targets, refs = refs[5 : 5 + n], refs[5 + n :]
    wfc, wproj, buf, other, pre, dpre, stage, part, from_core, over_out, from_over, send, recv, local = refs[:14]
    p, g = Peers(), Group()
    background = Background(g, p, kinds, sources, targets, refs[14:])
    rows = x_ref.shape[0]
    n_tp, width = buf.shape[0], fcb_ref.shape[1]
    sems = (send, recv)
    gather = Gather(p, buf, sems)
    scatter = Scatter(p, part, from_core, over_out, from_over, sems)
    load_proj = pltpu.make_async_copy(proj_part(wb_hbm, width), wproj, local.at[0])
    load_pre = pltpu.make_async_copy(pre_hbm, pre, local.at[1])
    load_fc = pltpu.make_async_copy(wb_hbm.at[:, : wfc.shape[1]], wfc, local.at[2])
    load_other = pltpu.make_async_copy(hid_hbm, other, local.at[3])
    for copy in (load_proj, load_pre, load_fc, load_other):
        copy.start()
    sums_ref[...] = jnp.zeros_like(sums_ref)
    fcb_ref[...] = jnp.zeros_like(fcb_ref)

    def lower(at):
        low = g_ref[at, :].astype(bf16)
        buf[p.t, at, :] = low
        add_rows(sums_ref, 7, low.astype(f32))

    row_chunks(rows, lower)
    if n:
        g.greet(p)
    else:
        p.greet()
    gather.start()
    background.start()
    gather.wait_chip()
    load_proj.wait()
    load_pre.wait()

    def through(x):
        def tile(at):
            d_hidden = mm(pair_rows(buf, x), wproj[:, at])
            u = pre[pl.ds(2 * x, 2), :, at].reshape(2 * rows, -1)
            low = (gelu_slope(u) * d_hidden).astype(bf16)
            put_pair(dpre, x, at, low)
            fcb_ref[:, at] += jnp.sum(low.astype(f32), axis=0, keepdims=True)

        tiles(width, tile)

    def down(x):
        def tile(at):
            put_pair(part, x, at, mm(pair_rows(dpre, x), wfc[at, :width], NT))

        tiles(D, tile)

    through(p.x)
    gather.relay()
    gather.wait_diag()
    through(1 - p.x)
    load_fc.wait()
    down(1 - p.x)
    scatter.far_to_core().start()
    scatter.send_over()
    down(p.x)
    scatter.near_to_core().start()

    def outer(left, right, target, sem):
        whole = D // TILE
        rest = D - whole * TILE
        flat = right[...].reshape(n_tp * rows, width)

        def tile(i, size):
            at = pl.ds(pl.multiple_of(i * TILE, TILE), size)
            value = mm(left[:, :, at].reshape(n_tp * rows, size), flat, TN)
            stage[at, :] = value.astype(bf16)

        @pl.loop(0, whole)
        def _(i):
            tile(i, TILE)

        if rest:
            tile(whole, rest)
        return pltpu.make_async_copy(stage, target, sem)

    load_other.wait()
    store = outer(buf, other, dproj_hbm, local.at[4])
    store.start()
    gather.finish()
    load_all = pltpu.make_async_copy(all_hbm, buf, local.at[5])
    load_all.start()
    scatter.wait()

    def final(at):
        dy = scatter.rows(at)
        dx, d_gain = norm_back(x_ref[at, :], dy, vec_ref[5:6, :])
        add_rows(sums_ref, 5, d_gain)
        add_rows(sums_ref, 6, dy)
        out_ref[at, :] = g_ref[at, :] + dx

    row_chunks(rows, final)
    load_all.wait()
    store.wait()
    store = outer(buf, dpre, dfc_hbm, local.at[6])
    store.start()
    scatter.finish()
    store.wait()
    background.finish()


def ff_bwd(grad, x, vecs, all_rows, pre, hidden, w_b, n_tp, payload, collective_id):
    rows, width = x.shape[0], pre.shape[2]
    block = (n_tp, rows)
    return pl.pallas_call(
        functools.partial(ff_bwd_kernel, tuple(kind for kind, _ in payload)),
        out_shape=(
            jax.ShapeDtypeStruct((rows, D), f32),
            jax.ShapeDtypeStruct((8, D), f32),
            jax.ShapeDtypeStruct((1, width), f32),
            jax.ShapeDtypeStruct((D, width), bf16),
            jax.ShapeDtypeStruct((D, width), bf16),
        )
        + sent_shapes(payload),
        in_specs=[IN_VMEM] * 3 + [ANY] * (4 + len(payload)),
        out_specs=(IN_VMEM, IN_VMEM, IN_VMEM) + (ANY,) * (2 + len(payload)),
        scratch_shapes=[
            pltpu.VMEM((D, lanes_up(width)), bf16),
            pltpu.VMEM((D, lanes_up(width)), bf16),
            pltpu.VMEM(block + (D,), bf16),
            pltpu.VMEM(block + (width,), bf16),
            pltpu.VMEM(block + (width,), f32),
            pltpu.VMEM(block + (width,), bf16),
            pltpu.VMEM((D, width), bf16),
        ]
        + scatter_scratch(n_tp, rows)
        + [pltpu.SemaphoreType.DMA((7,))]
        + sent_scratch(payload),
        compiler_params=params(collective_id),
        cost_estimate=pl.CostEstimate(
            flops=8 * n_tp * rows * D * width, bytes_accessed=50 * 2**20, transcendentals=n_tp * rows * width
        ),
    )(grad, x, vecs, all_rows, pre, hidden, w_b, *(a for _, a in payload))


class Share:
    def __init__(self, group, kv, sems):
        self.g, self.kv, self.sems = group, kv, sems
        self.partner = group.at(group.z, 1 - group.y)

    def piece(self, member, micro, index, to):
        ref = self.kv.at[member, micro]
        return self.g.copy(ref, ref, self.sems, micro * 7 + index, to)

    def own(self, micro):
        g = self.g
        return [self.piece(g.member, micro, 0, self.partner)] + [
            self.piece(g.member, micro, k, g.at(g.ahead(k), g.y)) for k in (1, 2, 3)
        ]

    def relayed(self, micro):
        g = self.g
        return [self.piece(g.at(g.behind(k), g.y), micro, 3 + k, self.partner) for k in (1, 2, 3)]

    def start(self, micro):
        for copy in self.own(micro):
            copy.start()

    def relay(self, micro):
        g = self.g
        for k, copy in zip((1, 2, 3), self.relayed(micro)):
            self.piece(g.at(g.behind(k), g.y), micro, k, self.partner).wait_recv()
            copy.start()

    def wait(self, micro):
        g = self.g
        self.piece(self.partner, micro, 0, self.partner).wait_recv()
        for k in (1, 2, 3):
            self.piece(g.at(g.behind(k), 1 - g.y), micro, 3 + k, self.partner).wait_recv()

    def finish(self, micro):
        for copy in self.own(micro) + self.relayed(micro):
            copy.wait_send()


class GroupSum:
    def __init__(self, group, parts, from_y, to_z, from_z, sems):
        self.g, self.parts, self.sems = group, parts, sems
        self.from_y, self.to_z, self.from_z = from_y, to_z, from_z

    def across(self, micro):
        g = self.g
        return g.copy(
            self.parts.at[micro, :, 1 - g.y], self.from_y.at[micro], self.sems, micro * 4, g.at(g.z, 1 - g.y)
        )

    def along(self, micro, k):
        g = self.g
        to = g.ahead(k)
        return g.copy(
            self.to_z.at[micro, to], self.from_z.at[micro, k - 1], self.sems, micro * 4 + k, g.at(to, g.y)
        )

    def start(self, micro):
        self.across(micro).start()

    def turn(self, micro):
        self.across(micro).wait_recv()

        @pl.loop(0, 4)
        def _(z):
            for kv in range(2):
                total = self.parts[micro, z, self.g.y, kv].astype(f32) + self.from_y[micro, z, kv].astype(f32)
                self.to_z[micro, z, kv] = total.astype(bf16)

        for k in (1, 2, 3):
            self.along(micro, k).start()

    def wait(self, micro):
        for k in (1, 2, 3):
            self.along(micro, k).wait_recv()

    def total(self, micro, kv):
        g = self.g
        value = self.parts[micro, g.z, g.y, kv].astype(f32) + self.from_y[micro, g.z, kv].astype(f32)
        for k in range(3):
            value = value + self.from_z[micro, k, kv].astype(f32)
        return value.astype(bf16)

    def finish(self, micro):
        self.across(micro).wait_send()
        for k in (1, 2, 3):
            self.along(micro, k).wait_send()


WIDE = 512
HEAD_PAIRS = WIDE // (2 * HEAD)
PROMPT_CHUNKS = PROMPT // CHUNK
CONT_CHUNKS = CONT_LEN // CHUNK


def chunk_at(c, base=0):
    return pl.ds(pl.multiple_of(base + c * CHUNK, CHUNK), CHUNK)


def key_limit(member):
    row = lax.broadcasted_iota(jnp.int32, (1, TOK_DEV), 1)
    return jnp.where(row < PROMPT_DEV, member * PROMPT_DEV + row, PROMPT - PROMPT_DEV + row)


def half_of(value, half):
    lane = lax.broadcasted_iota(jnp.int32, value.shape, 1)
    return jnp.where((lane >= HEAD * half) & (lane < HEAD * (half + 1)), value, jnp.zeros_like(value))


def fold(value, op):
    return op(value.reshape(value.shape[0] // 8, 8, value.shape[1]), axis=0)


def over_keys(body, prompt, own, carry):
    carry = lax.fori_loop(0, PROMPT_CHUNKS, lambda c, carry: body(c, lambda i: prompt(c, i), carry), carry)
    return lax.fori_loop(
        0, CONT_CHUNKS, lambda c, carry: body(PROMPT_CHUNKS + c, lambda i: own(c, i), carry), carry
    )


def head_pairs(head, finish):
    @pl.loop(0, HEAD_PAIRS)
    def _(pair):
        lanes = pl.ds(pl.multiple_of(pair * 2 * HEAD, 2 * HEAD), 2 * HEAD)
        head(pair, lanes, 0)

        @pl.when(pair < HEAD_PAIRS - 1)
        def _():
            head(pair, lanes, 1)

        finish(pair, lanes)


def to_slots(target, micro, first, value, lanes):
    per = target.shape[1] // MICRO
    row = first
    while row < first + value.shape[0]:
        slot, within = row // per, row % per
        count = min(per - within, first + value.shape[0] - row)
        target[slot, micro * per + within : micro * per + within + count, lanes] = value[
            row - first : row - first + count
        ]
        row += count


def pair_to_blocks(target, x, value):
    per = value.shape[0] // (2 * MICRO)
    for core in range(2):
        for micro in range(MICRO):
            at = pl.ds(pl.multiple_of((2 * x + core) * per, per), per)
            first = (core * MICRO + micro) * per
            target[micro, at, :] = value[first : first + per]


def attn_fwd_kernel(
    x_ref, vec_ref, bias_ref, wqkv_hbm,
    out_ref, lse_ref, all_hbm, own_hbm, kv_hbm, mix_hbm, wout_hbm,
    wqkv, wout, wparts, buf, own, kv, mix, s_ref, p_ref, o_ref,
    part, from_core, over_out, from_over, send, recv, gsend, grecv, wsend, wrecv, local,
):
    p, g = Peers(), Group()
    rows = x_ref.shape[0]
    n_tp = buf.shape[0]
    step = HEADS // n_tp * HEAD
    width = wparts.shape[1]
    sems = (send, recv)
    gather = Gather(p, buf, sems)
    scatter = Scatter(p, part, from_core, over_out, from_over, sems)
    share = Share(g, kv, (gsend, grecv))
    load_qkv = pltpu.make_async_copy(wqkv_hbm.at[:, : 3 * WIDE], wqkv, local.at[0])
    load_qkv.start()

    def rows_for(t):
        return wqkv_hbm.at[pl.ds(pl.multiple_of(t * step, 128), width), 3 * WIDE : 4 * WIDE]

    keep_part = pltpu.make_async_copy(rows_for(p.t), wparts.at[p.t], local.at[1])
    keep_part.start()
    give_parts = [
        p.copy(rows_for(t), wparts.at[p.t], (wsend, wrecv), i, t) for i, t in enumerate((p.core, p.over, p.diag))
    ]

    def norm(at):
        hat, _ = norm_stats(x_ref[at, :])
        buf[p.t, at, :] = (hat * vec_ref[0:1, :] + vec_ref[1:2, :]).astype(bf16)

    row_chunks(rows, norm)
    g.greet(p, True)
    gather.start()
    for copy in give_parts:
        copy.start()
    gather.wait_chip()
    load_qkv.wait()

    def project(x):
        for i in range(3):
            value = mm(pair_rows(buf, x), wqkv[:, i * WIDE : (i + 1) * WIDE]) + bias_ref[i : i + 1, :]
            low = value.astype(bf16)
            if i == 0:
                low = low * HEAD ** (-0.5)
            pair_to_blocks(own.at[i], x, low)

    project(p.x)
    gather.relay()
    gather.wait_diag()
    project(1 - p.x)
    for micro in range(MICRO):
        for i in range(2):
            kv[g.member, micro, i] = own[1 + i, micro, :PROMPT_DEV, :]
        share.start(micro)
    keep_all = pltpu.make_async_copy(buf, all_hbm, local.at[2])
    keep_own = pltpu.make_async_copy(own, own_hbm, local.at[3])
    keep_all.start()
    keep_own.start()
    limit = key_limit(g.member)
    sub = lax.broadcasted_iota(jnp.int32, (CHUNK, TOK_DEV), 0)

    for micro in range(MICRO):
        if micro == 0:
            share.relay(0)
        share.wait(micro)
        if micro == 0:
            share.relay(1)

        def head(pair, lanes, half, micro=micro):
            qh = half_of(own[0, micro, :, lanes], half)

            def first(c, load, top):
                s = jnp.where(sub + c * CHUNK <= limit, mm(load(0), qh, NT), -1e30)
                s_ref[chunk_at(c), :] = s
                return jnp.maximum(top, fold(s, jnp.max))

            top = over_keys(
                first,
                lambda c, i: kv[c, micro, i, :, lanes],
                lambda c, i: own[1 + i, micro, chunk_at(c, PROMPT_DEV), lanes],
                jnp.full((8, TOK_DEV), -1e30, f32),
            )
            top = jnp.max(top, axis=0, keepdims=True)

            def second(c, total):
                e = jnp.exp(s_ref[chunk_at(c), :] - top)
                p_ref[chunk_at(c), :] = e.astype(bf16)
                return total + fold(e, jnp.sum)

            total = lax.fori_loop(0, KEYS // CHUNK, second, jnp.zeros((8, TOK_DEV), f32))
            total = jnp.sum(total, axis=0, keepdims=True)
            values = kv[:, micro, 1, :, lanes].reshape(PROMPT, 2 * HEAD)
            out = mm(values, p_ref[:PROMPT, :], TN) + mm(own[2, micro, PROMPT_DEV:, lanes], p_ref[PROMPT:, :], TN)
            at = slice(HEAD * half, HEAD * (half + 1))
            o_ref[at, :] = out[at, :] / total
            lse_ref[micro, pair, half : half + 1, :] = top + jnp.log(total)

        def finish(pair, lanes, micro=micro):
            @pl.when(pair == HEAD_PAIRS - 1)
            def _():
                o_ref[HEAD:, :] = jnp.zeros((HEAD, TOK_DEV), f32)

            to_slots(mix, micro, 0, o_ref[...].T.astype(bf16), lanes)

        head_pairs(head, finish)

    keep_kv = pltpu.make_async_copy(kv, kv_hbm, local.at[4])
    keep_mix = pltpu.make_async_copy(mix, mix_hbm, local.at[5])
    keep_kv.start()
    keep_mix.start()
    keep_part.wait()
    for i, t in enumerate((p.core, p.over, p.diag)):
        p.copy(rows_for(t), wparts.at[t], (wsend, wrecv), i, t).wait_recv()
    for t in range(n_tp):
        count = min(WIDE, D - t * step)
        wout[:width, t * step : t * step + count] = wparts[t, :, :count]
    wout[width:, :] = jnp.zeros((WIDE - width, D), bf16)

    @pl.when(p.t < n_tp - 1)
    def _():
        wout[step:width, :] = jnp.zeros((width - step, D), bf16)

    keep_out = pltpu.make_async_copy(wout, wout_hbm, local.at[6])
    keep_out.start()

    def down(x):
        def tile(at):
            put_pair(part, x, at, mm(pair_rows(mix, x), wout[:, at]))

        tiles(D, tile)

    down(1 - p.x)
    scatter.far_to_core().start()
    scatter.send_over()
    down(p.x)
    scatter.near_to_core().start()
    scatter.wait()

    def final(at):
        out_ref[at, :] = x_ref[at, :] + (scatter.rows(at) + vec_ref[4:5, :])

    row_chunks(rows, final)
    gather.finish()
    scatter.finish()
    for micro in range(MICRO):
        share.finish(micro)
    for copy in give_parts:
        copy.wait_send()
    for copy in (keep_all, keep_own, keep_kv, keep_mix, keep_out):
        copy.wait()


def attn_shapes(n_tp, rows):
    return (
        ((n_tp, rows, D), bf16),
        ((3, MICRO, TOK_DEV, WIDE), bf16),
        ((GROUP, MICRO, 2, PROMPT_DEV, WIDE), bf16),
        ((n_tp, rows, WIDE), bf16),
    )


def attn_fwd(x, vecs, biases, w_a, n_tp, collective_id):
    rows = x.shape[0]
    width = D - HEADS // n_tp * HEAD * (n_tp - 1)
    saved = attn_shapes(n_tp, rows)
    return pl.pallas_call(
        attn_fwd_kernel,
        out_shape=(
            jax.ShapeDtypeStruct((rows, D), f32),
            jax.ShapeDtypeStruct((MICRO, HEAD_PAIRS, 8, TOK_DEV), f32),
        )
        + tuple(jax.ShapeDtypeStruct(*s) for s in saved + (((WIDE, D), bf16),)),
        in_specs=[IN_VMEM, IN_VMEM, IN_VMEM, ANY],
        out_specs=(IN_VMEM, IN_VMEM, ANY, ANY, ANY, ANY, ANY),
        scratch_shapes=[pltpu.VMEM((D, 3 * WIDE), bf16), pltpu.VMEM((WIDE, D), bf16), pltpu.VMEM((n_tp, width, WIDE), bf16)]
        + [pltpu.VMEM(*s) for s in saved]
        + [
            pltpu.VMEM((KEYS, TOK_DEV), f32),
            pltpu.VMEM((KEYS, TOK_DEV), bf16),
            pltpu.VMEM((2 * HEAD, TOK_DEV), f32),
        ]
        + scatter_scratch(n_tp, rows)
        + [
            pltpu.SemaphoreType.DMA((7 * MICRO,)),
            pltpu.SemaphoreType.DMA((7 * MICRO,)),
            pltpu.SemaphoreType.DMA((3,)),
            pltpu.SemaphoreType.DMA((3,)),
            pltpu.SemaphoreType.DMA((7,)),
        ],
        compiler_params=params(collective_id),
        cost_estimate=pl.CostEstimate(flops=10**11, bytes_accessed=30 * 2**20, transcendentals=0),
    )(x, vecs, biases, w_a)


def attn_bwd_kernel(kinds, *refs):
    n = len(kinds)
    g_ref, x_ref, vec_ref, lse_ref, all_hbm, own_hbm, kv_hbm, mix_hbm, wqkv_hbm, wout_hbm = refs[:10]
    sources, refs = refs[10 : 10 + n], refs[10 + n :]
    out_ref, sums_ref, cols_ref, dqkv_hbm, dout_hbm = refs[:5]
    targets, refs = refs[5 : 5 + n], refs[5 + n :]
    wqkv, wout, buf, other, own, kv, gm, dkv, from_y, to_z, from_z, dkc, dqkv, stage, stage_out = refs[:15]
    p_ref, dp_ref, ds_ref, o_ref = refs[15:19]
    part, from_core, over_out, from_over, send, recv, gsend, grecv, local = refs[19:28]
    p, g = Peers(), Group()
    background = Background(g, p, kinds, sources, targets, refs[28:])
    rows = x_ref.shape[0]
    n_tp = buf.shape[0]
    out_width = stage_out.shape[1]
    out_step = (D - out_width) // (n_tp - 1)
    sems = (send, recv)
    gather = Gather(p, buf, sems)
    scatter = Scatter(p, part, from_core, over_out, from_over, sems)
    reduce = GroupSum(g, dkv, from_y, to_z, from_z, (gsend, grecv))
    load_out = pltpu.make_async_copy(wout_hbm, wout, local.at[0])
    load_own = pltpu.make_async_copy(own_hbm, own, local.at[1])
    load_kv = pltpu.make_async_copy(kv_hbm, kv, local.at[2])
    load_qkv = pltpu.make_async_copy(wqkv_hbm.at[:, : 3 * WIDE], wqkv, local.at[3])
    load_mix = pltpu.make_async_copy(mix_hbm, other, local.at[4])
    for copy in (load_out, load_own, load_kv, load_qkv, load_mix):
        copy.start()
    sums_ref[...] = jnp.zeros_like(sums_ref)

    def lower(at):
        low = g_ref[at, :].astype(bf16)
        buf[p.t, at, :] = low
        add_rows(sums_ref, 4, low.astype(f32))

    row_chunks(rows, lower)
    g.greet(p)
    gather.start()
    background.start()
    gather.wait_chip()
    load_out.wait()

    def mixed_back(x):
        pair_to_blocks(gm, x, mm(pair_rows(buf, x), wout[...], NT).astype(bf16))

    mixed_back(p.x)
    gather.relay()
    gather.wait_diag()
    mixed_back(1 - p.x)
    load_own.wait()
    load_kv.wait()
    limit = key_limit(g.member)
    sub = lax.broadcasted_iota(jnp.int32, (CHUNK, TOK_DEV), 0)

    for micro in range(MICRO):

        def head(pair, lanes, half, micro=micro):
            if micro == 1 and half == 0:

                @pl.when(pair == HEAD_PAIRS - 1)
                def _():
                    reduce.turn(0)

            qh = half_of(own[0, micro, :, lanes], half)
            gh = half_of(gm[micro, :, lanes], half)
            lse = lse_ref[micro, pair, half : half + 1, :]

            def first(c, load, inner):
                s = jnp.where(sub + c * CHUNK <= limit, mm(load(0), qh, NT), -1e30)
                e = jnp.exp(s - lse)
                dp = mm(load(1), gh, NT)
                p_ref[chunk_at(c), :] = e
                dp_ref[chunk_at(c), :] = dp
                return inner + fold(e * dp, jnp.sum)

            inner = over_keys(
                first,
                lambda c, i: kv[c, micro, i, :, lanes],
                lambda c, i: own[1 + i, micro, chunk_at(c, PROMPT_DEV), lanes],
                jnp.zeros((8, TOK_DEV), f32),
            )
            inner = jnp.sum(inner, axis=0, keepdims=True)

            def second(c, put):
                e = p_ref[chunk_at(c), :]
                ds = (e * (dp_ref[chunk_at(c), :] - inner)).astype(bf16)
                ds_ref[chunk_at(c), :] = ds
                put(0, mm(ds, qh))
                put(1, mm(e.astype(bf16), gh))

            @pl.loop(0, PROMPT_CHUNKS)
            def _(c):
                def put(i, value):
                    at = (micro, c // 2, c % 2, i, slice(None), lanes)
                    if half:
                        value = value + dkv[at].astype(f32)
                    dkv[at] = value.astype(bf16)

                second(c, put)

            @pl.loop(0, CONT_CHUNKS)
            def _(c):
                def put(i, value):
                    at = (i, chunk_at(c), lanes)
                    if half:
                        value = value + dkc[at].astype(f32)
                    dkc[at] = value.astype(bf16)

                second(PROMPT_CHUNKS + c, put)

            keys = kv[:, micro, 0, :, lanes].reshape(PROMPT, 2 * HEAD)
            dq = mm(keys, ds_ref[:PROMPT, :], TN) + mm(own[1, micro, PROMPT_DEV:, lanes], ds_ref[PROMPT:, :], TN)
            at = slice(HEAD * half, HEAD * (half + 1))
            o_ref[at, :] = dq[at, :] * HEAD ** (-0.5)

        def finish(pair, lanes, micro=micro):
            @pl.when(pair == HEAD_PAIRS - 1)
            def _():
                o_ref[HEAD:, :] = jnp.zeros((HEAD, TOK_DEV), f32)

            to_slots(dqkv, micro, 0, o_ref[...].T.astype(bf16), lanes)

        head_pairs(head, finish)
        reduce.start(micro)
        for i in range(2):
            to_slots(dqkv, micro, PROMPT_DEV, dkc[i], slice((1 + i) * WIDE, (2 + i) * WIDE))

    load_mix.wait()
    columns = pl.ds(pl.multiple_of(p.t * out_step, 128), out_width)

    def outer(source, target, right, body):
        flat = right.reshape(n_tp * rows, right.shape[-1])

        def tile(at):
            left = source[:, :, at].reshape(n_tp * rows, -1)
            target[at, :] = mm(left, flat, TN).astype(bf16)

        body(D, tile)

    outer(other, stage_out, buf[:, :, columns], tiles)
    keep_out = pltpu.make_async_copy(stage_out, dout_hbm, local.at[5])
    keep_out.start()
    load_all = pltpu.make_async_copy(all_hbm, other, local.at[6])
    load_all.start()
    reduce.turn(1)
    for micro in range(MICRO):
        reduce.wait(micro)
        for i in range(2):
            to_slots(dqkv, micro, 0, reduce.total(micro, i), slice((1 + i) * WIDE, (2 + i) * WIDE))
    load_qkv.wait()

    def down(x):
        def tile(at):
            put_pair(part, x, at, mm(pair_rows(dqkv, x), wqkv[at, :], NT))

        tiles(D, tile)

    down(1 - p.x)
    scatter.far_to_core().start()
    scatter.send_over()
    down(p.x)
    scatter.near_to_core().start()
    load_all.wait()
    outer(other, stage, dqkv[...], tiles)
    keep_qkv = pltpu.make_async_copy(stage, dqkv_hbm, local.at[7])
    keep_qkv.start()
    cols_ref[...] = jnp.zeros_like(cols_ref)

    @pl.loop(0, n_tp * rows // ROW_CHUNK)
    def _(i):
        per = rows // ROW_CHUNK
        at = pl.ds(pl.multiple_of((i % per) * ROW_CHUNK, ROW_CHUNK), ROW_CHUNK)
        add_rows(cols_ref, 0, dqkv[i // per, at, :].astype(f32))

    scatter.wait()

    def final(at):
        dy = scatter.rows(at)
        dx, d_gain = norm_back(x_ref[at, :], dy, vec_ref[0:1, :])
        add_rows(sums_ref, 0, d_gain)
        add_rows(sums_ref, 1, dy)
        out_ref[at, :] = g_ref[at, :] + dx

    row_chunks(rows, final)
    gather.finish()
    scatter.finish()
    for micro in range(MICRO):
        reduce.finish(micro)
    keep_out.wait()
    keep_qkv.wait()
    background.finish()


def attn_bwd(grad, x, vecs, lse, all_rows, own, kv, mixed_all, w_a, w_out, out_width, n_tp, payload, collective_id):
    rows = x.shape[0]
    pieces = (MICRO, 4, 2, 2, PROMPT_DEV, WIDE)
    return pl.pallas_call(
        functools.partial(attn_bwd_kernel, tuple(kind for kind, _ in payload)),
        out_shape=(
            jax.ShapeDtypeStruct((rows, D), f32),
            jax.ShapeDtypeStruct((8, D), f32),
            jax.ShapeDtypeStruct((1, 3 * WIDE), f32),
            jax.ShapeDtypeStruct((D, 3 * WIDE), bf16),
            jax.ShapeDtypeStruct((D, out_width), bf16),
        )
        + sent_shapes(payload),
        in_specs=[IN_VMEM] * 4 + [ANY] * (6 + len(payload)),
        out_specs=(IN_VMEM, IN_VMEM, IN_VMEM) + (ANY,) * (2 + len(payload)),
        scratch_shapes=[
            pltpu.VMEM((D, 3 * WIDE), bf16),
            pltpu.VMEM((WIDE, D), bf16),
            pltpu.VMEM((n_tp, rows, D), bf16),
            pltpu.VMEM((n_tp, rows, D), bf16),
            pltpu.VMEM((3, MICRO, TOK_DEV, WIDE), bf16),
            pltpu.VMEM((GROUP, MICRO, 2, PROMPT_DEV, WIDE), bf16),
            pltpu.VMEM((MICRO, TOK_DEV, WIDE), bf16),
            pltpu.VMEM(pieces, bf16),
            pltpu.VMEM((MICRO, 4, 2, PROMPT_DEV, WIDE), bf16),
            pltpu.VMEM((MICRO, 4, 2, PROMPT_DEV, WIDE), bf16),
            pltpu.VMEM((MICRO, 3, 2, PROMPT_DEV, WIDE), bf16),
            pltpu.VMEM((2, CONT_LEN, WIDE), bf16),
            pltpu.VMEM((n_tp, rows, 3 * WIDE), bf16),
            pltpu.VMEM((D, 3 * WIDE), bf16),
            pltpu.VMEM((D, out_width), bf16),
            pltpu.VMEM((KEYS, TOK_DEV), f32),
            pltpu.VMEM((KEYS, TOK_DEV), f32),
            pltpu.VMEM((KEYS, TOK_DEV), bf16),
            pltpu.VMEM((2 * HEAD, TOK_DEV), f32),
        ]
        + scatter_scratch(n_tp, rows)
        + [
            pltpu.SemaphoreType.DMA((4 * MICRO,)),
            pltpu.SemaphoreType.DMA((4 * MICRO,)),
            pltpu.SemaphoreType.DMA((8,)),
        ]
        + sent_scratch(payload),
        compiler_params=params(collective_id),
        cost_estimate=pl.CostEstimate(flops=2 * 10**11, bytes_accessed=50 * 2**20, transcendentals=0),
    )(grad, x, vecs, lse, all_rows, own, kv, mixed_all, w_a, w_out, *(a for _, a in payload))


def send_kernel(kinds, *refs):
    n = len(kinds)
    p, g = Peers(), Group()
    background = Background(g, p, kinds, refs[:n], refs[n : 2 * n], refs[2 * n :])
    barrier = pltpu.get_barrier_semaphore()
    others = []
    if "y" in kinds:
        others += [g.at(g.z, 1 - g.y)]
    if "z" in kinds:
        others += [g.at(g.ahead(k), g.y) for k in (1, 2, 3)]
    for member in others:
        pl.semaphore_signal(barrier, inc=1, device_id=(g.base + member, g.t), device_id_type=MESH)
    near = [p.core, p.over] if "t" in kinds else []
    for t in near:
        pl.semaphore_signal(barrier, inc=1, device_id=(p.f, t), device_id_type=MESH)
    pl.semaphore_wait(barrier, len(others) + len(near))
    background.start()
    background.finish()


def send_only(payload, collective_id):
    return pl.pallas_call(
        functools.partial(send_kernel, tuple(kind for kind, _ in payload)),
        out_shape=sent_shapes(payload),
        in_specs=[ANY] * len(payload),
        out_specs=(ANY,) * len(payload),
        scratch_shapes=sent_scratch(payload),
        compiler_params=params(collective_id),
    )(*(a for _, a in payload))


def forward_layer(x, layer, weights, vecs, fc_bias, cols, n_tp):
    w_a, w_b = weights
    width = D - HEADS // n_tp * HEAD * (n_tp - 1)
    query_bias, value_bias = (lax.dynamic_slice_in_dim(vecs[i], cols, width) for i in (2, 3))
    biases = widen(jnp.stack([query_bias, jnp.zeros_like(query_bias), value_bias]))
    x_mid, lse, all_rows, own, kv, mixed, w_out = attn_fwd(x, vecs, biases, w_a, n_tp, 5 + layer)
    x_next, second_all, hidden_pre, hidden = ff_fwd(x_mid, vecs, fc_bias[None], w_b, n_tp)
    mixed_all = heads_joined(lax.all_gather(mixed[:, :, :width], "tp"), n_tp)
    return x_next, (x, w_out, lse, all_rows, own, kv, mixed_all, x_mid, second_all, hidden_pre, hidden)


def fsdp_sum(part):
    return lax.psum_scatter(part, "fsdp", scatter_dimension=0, tiled=True).astype(f32)


def heads_joined(parts, n_tp):
    step = HEADS // n_tp * HEAD
    return jnp.concatenate([parts[t][..., :step] for t in range(n_tp - 1)] + [parts[n_tp - 1]], axis=-1)


def widen(value, axis=-1):
    pads = [(0, 0)] * value.ndim
    pads[axis] = (0, WIDE - value.shape[axis])
    return jnp.pad(value, pads)


def to_y(part):
    return ("y", part.reshape(4, 2, -1, part.shape[1]))


def to_z(part, arrived):
    own = lax.dynamic_index_in_dim(part.reshape(4, 2, -1, part.shape[1]), lax.axis_index("fsdp") % 2, 1, False)
    return ("z", (own.astype(f32) + arrived.astype(f32)).astype(bf16))


def owned(summed, arrived):
    own = lax.dynamic_index_in_dim(summed[1], lax.axis_index("fsdp") // 2, 0, False)
    return own.astype(f32) + jnp.sum(arrived.astype(f32), 0)


def with_vectors(grad_out, ff_sums, attn_sums, col_sums, fc_bias_sums, cols):
    width = grad_out.shape[1]

    def placed(part):
        return lax.dynamic_update_slice_in_dim(jnp.zeros((1, D), f32), part, cols, 1)

    vector_grads = jnp.concatenate(
        [
            attn_sums[:2],
            placed(col_sums[:, :width]),
            placed(col_sums[:, 2 * WIDE : 2 * WIDE + width]),
            attn_sums[4:5],
            ff_sums[5:],
            fc_bias_sums,
        ]
    )
    return widen(jnp.concatenate([grad_out, vector_grads.astype(bf16).T], axis=1))


def backward(grad, weights, vecs, saves, cols, n_tp):
    width = D - HEADS // n_tp * HEAD * (n_tp - 1)
    staged = lax.axis_size("fsdp") == GROUP
    sums = [None] * LAYERS
    joined = [None] * LAYERS
    waiting_y, waiting_z, waiting_t, done = [], [], [], {}

    def load(limit_z, limit_y):
        chosen_z = [waiting_z.pop(0) for _ in range(min(limit_z, len(waiting_z)))]
        chosen_y = [waiting_y.pop(0) for _ in range(min(limit_y, len(waiting_y)))]
        return chosen_z, chosen_y, [item for _, item in chosen_z] + [to_y(part) for _, part in chosen_y]

    def unload(chosen_z, chosen_y, arrived):
        for (name, item), got in zip(chosen_z, arrived):
            done[name] = owned(item, got)
        for (name, part), got in zip(chosen_y, arrived[len(chosen_z) :]):
            waiting_z.append((name, to_z(part, got)))

    def produced(layer, names, values):
        for name, value in zip(names, values):
            if staged:
                waiting_y.append(((layer, name), value))
            else:
                done[layer, name] = fsdp_sum(value)

    plan = {(1, 0): (0, 0), (1, 1): (0, 2), (0, 0): (1, 2), (0, 1): (3, 2)}
    for layer in reversed(range(LAYERS)):
        w_a, w_b = weights[layer]
        x, w_out, lse, all_rows, own, kv, mixed_all, x_mid, second_all, hidden_pre, hidden = saves[layer]
        chosen_z, chosen_y, payload = load(*plan[layer, 0])
        grad, ff_sums, fc_bias_sums, grad_fc, grad_proj, *arrived = ff_bwd(
            grad, x_mid, vecs[layer], second_all, hidden_pre, hidden, w_b, n_tp, payload, 10 + layer
        )
        unload(chosen_z, chosen_y, arrived)
        produced(layer, ("proj", "fc"), (grad_proj, grad_fc))
        chosen_z, chosen_y, payload = load(*plan[layer, 1])
        grad, attn_sums, col_sums, grad_qkv, grad_out, *arrived = attn_bwd(
            grad, x, vecs[layer], lse, all_rows, own, kv, mixed_all, w_a, w_out, width, n_tp, payload, 20 + layer
        )
        unload(chosen_z, chosen_y, arrived)
        grad_out = with_vectors(grad_out, ff_sums, attn_sums, col_sums, fc_bias_sums, cols)
        produced(layer, ("qkv", "out"), (grad_qkv, grad_out))
    number = 30
    asked = set()
    while len(asked) < LAYERS or waiting_t:
        chosen_z, chosen_y, payload = load(9, 9)
        chosen_t, waiting_t = waiting_t, []
        arrived = []
        if payload or chosen_t:
            arrived = list(send_only(payload + [("t", part) for _, part in chosen_t], number))
            number += 1
        unload(chosen_z, chosen_y, arrived)
        for (layer, _), got in zip(chosen_t, arrived[len(payload) :]):
            joined[layer] = got
        for layer in range(LAYERS):
            if layer not in asked and (layer, "qkv") in done and (layer, "out") in done:
                asked.add(layer)
                both = jnp.concatenate([done[layer, "qkv"], done[layer, "out"]], axis=1).astype(bf16)
                waiting_t.append((layer, both))
    for layer in range(LAYERS):
        got = joined[layer]
        qkv_grad = jnp.concatenate(
            [heads_joined(got[:, :, i * WIDE : i * WIDE + width], n_tp) for i in range(3)], axis=1
        ).astype(f32)
        out_grad = heads_joined(got[:, :, 3 * WIDE : 3 * WIDE + width], n_tp).astype(f32)
        vector_sum = jnp.sum(got[:, :, 3 * WIDE + width : 3 * WIDE + width + 8].astype(f32), 0).T
        fc_bias_sum = done[layer, "out"][:, width + 8]
        sums[layer] = (qkv_grad, out_grad, done[layer, "fc"], done[layer, "proj"].T, fc_bias_sum, vector_sum)
    return grad, sums


def local(
    tokens,
    qkv_weight,
    query_bias,
    value_bias,
    out_weight,
    out_bias,
    fc_weight,
    fc_bias,
    proj_weight,
    proj_bias,
    first_gain,
    first_bias,
    second_gain,
    second_bias,
    out_grad,
):
    n_tp = lax.axis_size("tp")
    tp = lax.axis_index("tp")
    row_count = tokens.shape[1]
    step = HEADS // n_tp * HEAD
    width = D - step * (n_tp - 1)
    cols = tp * step

    last = []

    def gathered(part):
        if last:
            part, _ = lax.optimization_barrier((part, last.pop()))
        whole = lax.all_gather(part, "fsdp", axis=0, tiled=True)
        last.append(whole[:8, :128])
        return whole

    vectors = jnp.stack(
        [first_gain, first_bias, query_bias, value_bias, out_bias, second_gain, second_bias, proj_bias, fc_bias[:, 0]]
    ).reshape(9 * LAYERS, -1)

    weights = []
    for layer in range(LAYERS):
        sides = [widen(lax.dynamic_slice_in_dim(qkv_weight[layer], cols + i * D, width, 1)) for i in range(3)]
        sides.append(widen(lax.dynamic_slice_in_dim(out_weight[layer], cols, width, 1)))
        if layer == 0:
            sides.append(jnp.pad(vectors.T, ((0, 0), (0, 128 - 9 * LAYERS))))
        w_a = gathered(jnp.concatenate(sides, axis=1))
        if layer == 0:
            vectors = w_a[:, 4 * WIDE : 4 * WIDE + 9 * LAYERS].T.astype(f32).reshape(9, LAYERS, D)
        fc, proj = fc_weight[layer], proj_weight[layer].T
        more = ((0, 0), (0, lanes_up(fc.shape[1]) - fc.shape[1]))
        w_b = gathered(jnp.concatenate([jnp.pad(fc, more), jnp.pad(proj, more)], axis=1))
        weights.append((w_a, w_b))

    state = tokens.astype(f32).reshape(MICRO * row_count, D)
    saves = []
    for layer in range(LAYERS):
        state, saved = forward_layer(
            state, layer, weights[layer], vectors[:8, layer], vectors[8, layer], cols, n_tp
        )
        saves.append(saved)
    out_tokens = state.astype(bf16).reshape(tokens.shape)
    grad = out_grad.astype(f32).reshape(MICRO * row_count, D)
    grad, sums = backward(
        grad, weights, [vectors[:8, layer] for layer in range(LAYERS)], saves, cols, n_tp
    )
    qkv_g, out_g, fc_g, proj_g, fc_bias_g, vec_g = (
        jnp.stack([sums[layer][i] for layer in range(LAYERS)]) for i in range(6)
    )
    return (
        out_tokens,
        grad.reshape(tokens.shape),
        qkv_g,
        vec_g[:, 2],
        vec_g[:, 3],
        out_g,
        vec_g[:, 4],
        fc_g,
        fc_bias_g[:, None],
        proj_g,
        vec_g[:, 7],
        vec_g[:, 0],
        vec_g[:, 1],
        vec_g[:, 5],
        vec_g[:, 6],
    )


def solution(mesh):
    rows = P(None, ("fsdp", "tp"), None)
    weight = P(None, "fsdp", None)
    vector = P(None, "fsdp")
    fc_in = P(None, "fsdp", "tp")
    hidden = P(None, "tp", "fsdp")
    in_specs = (
        rows, weight, vector, vector, weight, vector, fc_in, hidden, hidden,
        vector, vector, vector, vector, vector, rows,
    )
    out_specs = (
        rows, rows, weight, vector, vector, weight, vector, fc_in, hidden, hidden,
        vector, vector, vector, vector, vector,
    )
    return jax.shard_map(local, mesh=mesh, in_specs=in_specs, out_specs=out_specs, check_vma=False)
```

```python
import functools

import jax
import jax.numpy as jnp
from jax import lax
from jax.experimental import pallas as pl
from jax.experimental.pallas import tpu as pltpu
from jax.sharding import PartitionSpec as P

D = 1600
HEADS = 25
HEAD = 64
GROUP = 8
PROMPT_DEV = 128
CONT_LEN = 256
TOK_DEV = 384
MICRO = 2
LAYERS = 2
PROMPT = 1024
KEYS = PROMPT + CONT_LEN
CHUNK = 128

f32 = jnp.float32
bf16 = jnp.bfloat16
norm_eps = 1e-05
NN = (((1,), (0,)), ((), ()))
NT = (((1,), (1,)), ((), ()))
TN = (((0,), (0,)), ((), ()))


def mm(left, right, dims=NN):
    return lax.dot_general(left, right, dims, preferred_element_type=f32)


def gelu_tanh(value):
    return jax.nn.gelu(value, approximate=True)


MESH = pl.DeviceIdType.MESH
ANY = pl.BlockSpec(memory_space=pl.ANY)
IN_VMEM = pl.BlockSpec(memory_space=pltpu.VMEM)
TILE = 512
ROW_CHUNK = 32


class Peers:
    def __init__(self):
        self.f = lax.axis_index("fsdp")
        self.t = lax.axis_index("tp")
        x, c = self.t // 2, self.t % 2
        self.x = x
        self.core = 2 * x + 1 - c
        self.over = 2 * (1 - x) + c
        self.diag = 2 * (1 - x) + 1 - c

    def greet(self):
        barrier = pltpu.get_barrier_semaphore()
        for t in (self.core, self.over):
            pl.semaphore_signal(barrier, inc=1, device_id=(self.f, t), device_id_type=MESH)
        pl.semaphore_wait(barrier, 2)

    def copy(self, source, target, sems, index, t):
        return pltpu.make_async_remote_copy(
            src_ref=source,
            dst_ref=target,
            send_sem=sems[0].at[index],
            recv_sem=sems[1].at[index],
            device_id=(self.f, t),
            device_id_type=MESH,
        )


class Gather:
    def __init__(self, peers, buf, sems):
        self.p, self.buf, self.sems = peers, buf, sems

    def piece(self, slot, index, t):
        return self.p.copy(self.buf.at[slot], self.buf.at[slot], self.sems, index, t)

    def start(self):
        p = self.p
        self.piece(p.t, 1, p.over).start()
        self.piece(p.t, 0, p.core).start()

    def wait_chip(self):
        self.piece(self.p.core, 0, self.p.core).wait_recv()

    def relay(self):
        p = self.p
        self.piece(p.over, 1, p.over).wait_recv()
        self.piece(p.over, 2, p.core).start()

    def wait_diag(self):
        self.piece(self.p.diag, 2, self.p.core).wait_recv()

    def finish(self):
        p = self.p
        self.piece(p.t, 1, p.over).wait_send()
        self.piece(p.t, 0, p.core).wait_send()
        self.piece(p.over, 2, p.core).wait_send()


class Scatter:
    def __init__(self, peers, part, from_core, over_out, from_over, sems):
        self.p, self.part, self.sems = peers, part, sems
        self.from_core, self.over_out, self.from_over = from_core, over_out, from_over

    def far_to_core(self):
        return self.p.copy(self.part.at[self.p.diag], self.from_core.at[0], self.sems, 3, self.p.core)

    def near_to_core(self):
        return self.p.copy(self.part.at[self.p.core], self.from_core.at[1], self.sems, 4, self.p.core)

    def to_over(self):
        return self.p.copy(self.over_out, self.from_over, self.sems, 5, self.p.over)

    def send_over(self):
        self.far_to_core().wait_recv()

        @pl.loop(0, self.over_out.shape[0] // ROW_CHUNK)
        def _(i):
            at = pl.ds(pl.multiple_of(i * ROW_CHUNK, ROW_CHUNK), ROW_CHUNK)
            total = self.part[self.p.over, at, :].astype(f32) + self.from_core[0, at, :].astype(f32)
            self.over_out[at, :] = total.astype(bf16)

        self.to_over().start()

    def wait(self):
        self.near_to_core().wait_recv()
        self.to_over().wait_recv()

    def rows(self, at):
        return (
            self.part[self.p.t, at, :].astype(f32)
            + self.from_core[1, at, :].astype(f32)
            + self.from_over[at, :].astype(f32)
        )

    def finish(self):
        for copy in (self.far_to_core(), self.near_to_core(), self.to_over()):
            copy.wait_send()


class Group:
    def __init__(self):
        f = lax.axis_index("fsdp")
        self.t = lax.axis_index("tp")
        self.member = f % GROUP
        self.base = f - self.member
        self.z, self.y = self.member // 2, self.member % 2

    def at(self, z, y):
        return z * 2 + y

    def ahead(self, k):
        return (self.z + k) % 4

    def behind(self, k):
        return (self.z + 4 - k) % 4

    def greet(self, peers, with_diag=False):
        barrier = pltpu.get_barrier_semaphore()
        others = [self.at(self.z, 1 - self.y)] + [self.at(self.ahead(k), self.y) for k in (1, 2, 3)]
        for member in others:
            pl.semaphore_signal(
                barrier, inc=1, device_id=(self.base + member, self.t), device_id_type=MESH
            )
        near = [peers.core, peers.over] + [peers.diag] * with_diag
        for t in near:
            pl.semaphore_signal(barrier, inc=1, device_id=(peers.f, t), device_id_type=MESH)
        pl.semaphore_wait(barrier, 4 + len(near))

    def copy(self, source, target, sems, index, member):
        return pltpu.make_async_remote_copy(
            src_ref=source,
            dst_ref=target,
            send_sem=sems[0].at[index],
            recv_sem=sems[1].at[index],
            device_id=(self.base + member, self.t),
            device_id_type=MESH,
        )


class Background:
    def __init__(self, group, peers, kinds, sources, targets, sems):
        self.g, self.p, self.sems = group, peers, sems
        self.items = list(zip(kinds, sources, targets))

    def block_copies(self, n, source, target):
        p, sems = self.p, self.sems
        return (
            p.copy(source, target.at[p.t], sems, 4 * n, p.core),
            p.copy(source, target.at[p.t], sems, 4 * n + 1, p.over),
            p.copy(target.at[p.over], target.at[p.over], sems, 4 * n + 2, p.core),
            pltpu.make_async_copy(source, target.at[p.t], sems[0].at[4 * n + 3]),
        )

    def copies(self):
        g = self.g
        made = []
        for n, (kind, source, target) in enumerate(self.items):
            if kind == "y":
                made.append(g.copy(source.at[:, 1 - g.y], target, self.sems, 4 * n, g.at(g.z, 1 - g.y)))
            elif kind == "z":
                for k in (1, 2, 3):
                    to = g.ahead(k)
                    made.append(
                        g.copy(source.at[to], target.at[k - 1], self.sems, 4 * n + k - 1, g.at(to, g.y))
                    )
        return made

    def start(self):
        for copy in self.copies():
            copy.start()
        for n, (kind, source, target) in enumerate(self.items):
            if kind == "t":
                to_core, to_over, _, local = self.block_copies(n, source, target)
                to_over.start()
                to_core.start()
                local.start()

    def finish(self):
        p = self.p
        for n, (kind, source, target) in enumerate(self.items):
            if kind == "t":
                p.copy(source, target.at[p.over], self.sems, 4 * n + 1, p.over).wait_recv()
                self.block_copies(n, source, target)[2].start()
        for copy in self.copies():
            copy.wait()
        for n, (kind, source, target) in enumerate(self.items):
            if kind == "t":
                p.copy(source, target.at[p.core], self.sems, 4 * n, p.core).wait_recv()
                p.copy(source, target.at[p.diag], self.sems, 4 * n + 2, p.core).wait_recv()
                to_core, to_over, relay, local = self.block_copies(n, source, target)
                for copy in (to_core, to_over, relay):
                    copy.wait_send()
                local.wait()


class Spread:
    def __init__(self, group, source, target, sems, chunks):
        self.g, self.source, self.target, self.sems = group, source, target, sems
        count = source.shape[1] // 128
        ends = [128 * (count * (c + 1) // chunks) for c in range(chunks)]
        self.columns = [slice(a, b) for a, b in zip([0] + ends, ends)]
        self.partner = group.at(group.z, 1 - group.y)

    def piece(self, member, c, index, to, own=False):
        target = self.target.at[member, :, self.columns[c]]
        source = self.source.at[:, self.columns[c]] if own else target
        return self.g.copy(source, target, self.sems, 7 * c + index, to)

    def own(self, c):
        g = self.g
        return [self.piece(g.member, c, k, g.at(g.ahead(k), g.y), True) for k in (1, 2, 3)] + [
            self.piece(g.member, c, 0, self.partner, True)
        ]

    def relayed(self, c):
        g = self.g
        return [self.piece(g.at(g.behind(k), g.y), c, 3 + k, self.partner) for k in (1, 2, 3)]

    def keep(self):
        return pltpu.make_async_copy(
            self.source, self.target.at[self.g.member], self.sems[0].at[7 * len(self.columns)]
        )

    def start(self, first=0, last=None):
        if first == 0:
            self.keep().start()
        for c in range(len(self.columns))[first:last]:
            for copy in self.own(c):
                copy.start()

    def relay(self, c):
        g = self.g
        for k, copy in zip((1, 2, 3), self.relayed(c)):
            self.piece(g.at(g.behind(k), g.y), c, k, self.partner).wait_recv()
            copy.start()

    def finish(self):
        g = self.g
        for c in range(len(self.columns)):
            self.piece(self.partner, c, 0, self.partner).wait_recv()
            for k in (1, 2, 3):
                self.piece(g.at(g.behind(k), 1 - g.y), c, 3 + k, self.partner).wait_recv()
            for copy in self.own(c) + self.relayed(c):
                copy.wait_send()
        self.keep().wait()


def spread_parts(shard, chunks):
    if shard is None:
        return (), (), []
    whole = jax.ShapeDtypeStruct((GROUP,) + shard.shape, shard.dtype)
    return (shard,), (whole,), [pltpu.SemaphoreType.DMA((7 * chunks + 1,))] * 2


def spread_kernel(chunks, source, target, send, recv):
    g = Group()
    barrier = pltpu.get_barrier_semaphore()
    others = [g.at(g.z, 1 - g.y)] + [g.at(g.ahead(k), g.y) for k in (1, 2, 3)]
    for member in others:
        pl.semaphore_signal(barrier, inc=1, device_id=(g.base + member, g.t), device_id_type=MESH)
    pl.semaphore_wait(barrier, len(others))
    spread = Spread(g, source, target, (send, recv), chunks)
    spread.start()
    for c in range(chunks):
        spread.relay(c)
    spread.finish()


def spread_only(shard, chunks, collective_id):
    operands, results, scratch = spread_parts(shard, chunks)
    return pl.pallas_call(
        functools.partial(spread_kernel, chunks),
        out_shape=results[0],
        in_specs=[ANY],
        out_specs=ANY,
        scratch_shapes=scratch,
        compiler_params=params(collective_id),
    )(shard)


def sent_shapes(payload):
    return tuple(
        jax.ShapeDtypeStruct((3 if kind == "z" else 4,) + a.shape[-2:], a.dtype) for kind, a in payload
    )


def sent_scratch(payload):
    return [pltpu.SemaphoreType.DMA((4 * len(payload) + 1,))] * 2


def row_chunks(rows, body):
    @pl.loop(0, rows // ROW_CHUNK)
    def _(i):
        body(pl.ds(pl.multiple_of(i * ROW_CHUNK, ROW_CHUNK), ROW_CHUNK))


def tiles(extent, body):
    whole = extent // TILE

    @pl.loop(0, whole)
    def _(i):
        body(pl.ds(pl.multiple_of(i * TILE, TILE), TILE))

    if extent % TILE:
        body(pl.ds(whole * TILE, extent % TILE))


def pair_rows(ref, x):
    both = ref[pl.ds(2 * x, 2)]
    return both.reshape(2 * both.shape[1], both.shape[2])


def put_pair(ref, x, at, value):
    ref[pl.ds(2 * x, 2), :, at] = value.reshape(2, value.shape[0] // 2, value.shape[1]).astype(ref.dtype)


def norm_stats(x):
    centred = x - jnp.mean(x, -1, keepdims=True)
    scale = lax.rsqrt(jnp.mean(centred * centred, -1, keepdims=True) + norm_eps)
    return centred * scale, scale


def lanes_up(width):
    return -(-width // 128) * 128


def proj_part(w_b, width):
    return w_b.at[:, lanes_up(width) :]


FF_CHUNKS = 3
ATTN_CHUNKS = 5


def ff_fwd_kernel(n, *refs):
    x_ref, vec_ref, fcb_ref, wb_hbm = refs[:4]
    shard, refs = refs[4 : 4 + n], refs[4 + n :]
    out_ref, all_hbm, pre_hbm, hid_hbm = refs[:4]
    whole, refs = refs[4 : 4 + n], refs[4 + n :]
    wfc, wproj, buf, pre, hid, part, from_core, over_out, from_over, send, recv, local = refs[:12]
    p, g = Peers(), Group()
    spread = Spread(g, shard[0], whole[0], refs[12:], FF_CHUNKS) if n else None
    rows = x_ref.shape[0]
    sems = (send, recv)
    gather = Gather(p, buf, sems)
    scatter = Scatter(p, part, from_core, over_out, from_over, sems)
    width = fcb_ref.shape[1]
    load_fc = pltpu.make_async_copy(wb_hbm.at[:, : wfc.shape[1]], wfc, local.at[0])
    load_proj = pltpu.make_async_copy(proj_part(wb_hbm, width), wproj, local.at[1])
    load_fc.start()
    load_proj.start()

    def norm(at):
        hat, _ = norm_stats(x_ref[at, :])
        buf[p.t, at, :] = (hat * vec_ref[5:6, :] + vec_ref[6:7, :]).astype(bf16)

    row_chunks(rows, norm)
    if n:
        g.greet(p)
    else:
        p.greet()
    gather.start()
    if n:
        spread.start()
    gather.wait_chip()
    load_fc.wait()

    def up(x):
        def tile(at):
            value = mm(pair_rows(buf, x), wfc[:, at]) + fcb_ref[:, at]
            put_pair(pre, x, at, value)
            put_pair(hid, x, at, gelu_tanh(value))

        tiles(width, tile)

    def down(x):
        def tile(at):
            put_pair(part, x, at, mm(pair_rows(hid, x), wproj[at, :width], NT))

        tiles(D, tile)

    up(p.x)
    if n:
        spread.relay(0)
    gather.relay()
    gather.wait_diag()
    keep_all = pltpu.make_async_copy(buf, all_hbm, local.at[2])
    keep_all.start()
    up(1 - p.x)
    keep_pre = pltpu.make_async_copy(pre, pre_hbm, local.at[3])
    keep_hid = pltpu.make_async_copy(hid, hid_hbm, local.at[4])
    keep_pre.start()
    keep_hid.start()
    load_proj.wait()
    down(1 - p.x)
    scatter.far_to_core().start()
    scatter.send_over()
    if n:
        spread.relay(1)
    down(p.x)
    scatter.near_to_core().start()
    if n:
        spread.relay(2)
    scatter.wait()

    def final(at):
        out_ref[at, :] = x_ref[at, :] + scatter.rows(at) + vec_ref[7:8, :]

    row_chunks(rows, final)
    gather.finish()
    scatter.finish()
    for copy in (keep_all, keep_pre, keep_hid):
        copy.wait()
    if n:
        spread.finish()


def scatter_scratch(n_tp, rows):
    return [
        pltpu.VMEM((n_tp, rows, D), bf16),
        pltpu.VMEM((2, rows, D), bf16),
        pltpu.VMEM((rows, D), bf16),
        pltpu.VMEM((rows, D), bf16),
        pltpu.SemaphoreType.DMA((6,)),
        pltpu.SemaphoreType.DMA((6,)),
    ]


def params(collective_id):
    return pltpu.CompilerParams(collective_id=collective_id, has_side_effects=True, vmem_limit_bytes=60 * 2**20)


def ff_fwd(x, vecs, fc_bias, w_b, n_tp, shard, collective_id):
    rows, width = x.shape[0], fc_bias.shape[1]
    block = (n_tp, rows)
    operands, results, sems = spread_parts(shard, FF_CHUNKS)
    return pl.pallas_call(
        functools.partial(ff_fwd_kernel, len(operands)),
        out_shape=(
            jax.ShapeDtypeStruct((rows, D), f32),
            jax.ShapeDtypeStruct(block + (D,), bf16),
            jax.ShapeDtypeStruct(block + (width,), f32),
            jax.ShapeDtypeStruct(block + (width,), bf16),
        )
        + results,
        in_specs=[IN_VMEM, IN_VMEM, IN_VMEM, ANY] + [ANY] * len(operands),
        out_specs=(IN_VMEM, ANY, ANY, ANY) + (ANY,) * len(operands),
        scratch_shapes=[
            pltpu.VMEM((D, lanes_up(width)), bf16),
            pltpu.VMEM((D, lanes_up(width)), bf16),
            pltpu.VMEM(block + (D,), bf16),
            pltpu.VMEM(block + (width,), f32),
            pltpu.VMEM(block + (width,), bf16),
        ]
        + scatter_scratch(n_tp, rows)
        + [pltpu.SemaphoreType.DMA((5,))]
        + sems,
        compiler_params=params(collective_id),
        cost_estimate=pl.CostEstimate(
            flops=4 * n_tp * rows * D * width, bytes_accessed=40 * 2**20, transcendentals=n_tp * rows * width
        ),
    )(x, vecs, fc_bias, w_b, *operands)


def gelu_slope(u):
    a = 0.7978845608028654
    square = u * u
    t = jnp.tanh(a * (u + 0.044715 * u * square))
    return 0.5 * (1.0 + t) + 0.5 * u * (1.0 - t * t) * (a * (1.0 + 3 * 0.044715 * square))


def norm_back(x, dy, gain):
    hat, scale = norm_stats(x)
    d_hat = dy * gain
    inner = d_hat - jnp.mean(d_hat, -1, keepdims=True) - hat * jnp.mean(d_hat * hat, -1, keepdims=True)
    return scale * inner, dy * hat


def add_rows(ref, row, value):
    ref[row : row + 1, :] += jnp.sum(value, axis=0, keepdims=True)


def ff_bwd_kernel(kinds, *refs):
    n = len(kinds)
    g_ref, x_ref, vec_ref, all_hbm, pre_hbm, hid_hbm, wb_hbm = refs[:7]
    sources, refs = refs[7 : 7 + n], refs[7 + n :]
    out_ref, sums_ref, fcb_ref, dfc_hbm, dproj_hbm = refs[:5]
    targets, refs = refs[5 : 5 + n], refs[5 + n :]
    wfc, wproj, buf, other, pre, dpre, stage, part, from_core, over_out, from_over, send, recv, local = refs[:14]
    p, g = Peers(), Group()
    background = Background(g, p, kinds, sources, targets, refs[14:])
    rows = x_ref.shape[0]
    n_tp, width = buf.shape[0], fcb_ref.shape[1]
    sems = (send, recv)
    gather = Gather(p, buf, sems)
    scatter = Scatter(p, part, from_core, over_out, from_over, sems)
    load_proj = pltpu.make_async_copy(proj_part(wb_hbm, width), wproj, local.at[0])
    load_pre = pltpu.make_async_copy(pre_hbm, pre, local.at[1])
    load_fc = pltpu.make_async_copy(wb_hbm.at[:, : wfc.shape[1]], wfc, local.at[2])
    load_other = pltpu.make_async_copy(hid_hbm, other, local.at[3])
    for copy in (load_proj, load_pre, load_fc, load_other):
        copy.start()
    sums_ref[...] = jnp.zeros_like(sums_ref)
    fcb_ref[...] = jnp.zeros_like(fcb_ref)

    def lower(at):
        low = g_ref[at, :].astype(bf16)
        buf[p.t, at, :] = low
        add_rows(sums_ref, 7, low.astype(f32))

    row_chunks(rows, lower)
    if n:
        g.greet(p)
    else:
        p.greet()
    gather.start()
    background.start()
    gather.wait_chip()
    load_proj.wait()
    load_pre.wait()

    def through(x):
        def tile(at):
            d_hidden = mm(pair_rows(buf, x), wproj[:, at])
            u = pre[pl.ds(2 * x, 2), :, at].reshape(2 * rows, -1)
            low = (gelu_slope(u) * d_hidden).astype(bf16)
            put_pair(dpre, x, at, low)
            fcb_ref[:, at] += jnp.sum(low.astype(f32), axis=0, keepdims=True)

        tiles(width, tile)

    def down(x):
        def tile(at):
            put_pair(part, x, at, mm(pair_rows(dpre, x), wfc[at, :width], NT))

        tiles(D, tile)

    through(p.x)
    gather.relay()
    gather.wait_diag()
    through(1 - p.x)
    load_fc.wait()
    down(1 - p.x)
    scatter.far_to_core().start()
    scatter.send_over()
    down(p.x)
    scatter.near_to_core().start()

    def outer(left, right, target, sem):
        whole = D // TILE
        rest = D - whole * TILE
        flat = right[...].reshape(n_tp * rows, width)

        def tile(i, size):
            at = pl.ds(pl.multiple_of(i * TILE, TILE), size)
            value = mm(left[:, :, at].reshape(n_tp * rows, size), flat, TN)
            stage[at, :] = value.astype(bf16)

        @pl.loop(0, whole)
        def _(i):
            tile(i, TILE)

        if rest:
            tile(whole, rest)
        return pltpu.make_async_copy(stage, target, sem)

    load_other.wait()
    store = outer(buf, other, dproj_hbm, local.at[4])
    store.start()
    gather.finish()
    load_all = pltpu.make_async_copy(all_hbm, buf, local.at[5])
    load_all.start()
    scatter.wait()

    def final(at):
        dy = scatter.rows(at)
        dx, d_gain = norm_back(x_ref[at, :], dy, vec_ref[5:6, :])
        add_rows(sums_ref, 5, d_gain)
        add_rows(sums_ref, 6, dy)
        out_ref[at, :] = g_ref[at, :] + dx

    row_chunks(rows, final)
    load_all.wait()
    store.wait()
    store = outer(buf, dpre, dfc_hbm, local.at[6])
    store.start()
    scatter.finish()
    store.wait()
    background.finish()


def ff_bwd(grad, x, vecs, all_rows, pre, hidden, w_b, n_tp, payload, collective_id):
    rows, width = x.shape[0], pre.shape[2]
    block = (n_tp, rows)
    return pl.pallas_call(
        functools.partial(ff_bwd_kernel, tuple(kind for kind, _ in payload)),
        out_shape=(
            jax.ShapeDtypeStruct((rows, D), f32),
            jax.ShapeDtypeStruct((8, D), f32),
            jax.ShapeDtypeStruct((1, width), f32),
            jax.ShapeDtypeStruct((D, width), bf16),
            jax.ShapeDtypeStruct((D, width), bf16),
        )
        + sent_shapes(payload),
        in_specs=[IN_VMEM] * 3 + [ANY] * (4 + len(payload)),
        out_specs=(IN_VMEM, IN_VMEM, IN_VMEM) + (ANY,) * (2 + len(payload)),
        scratch_shapes=[
            pltpu.VMEM((D, lanes_up(width)), bf16),
            pltpu.VMEM((D, lanes_up(width)), bf16),
            pltpu.VMEM(block + (D,), bf16),
            pltpu.VMEM(block + (width,), bf16),
            pltpu.VMEM(block + (width,), f32),
            pltpu.VMEM(block + (width,), bf16),
            pltpu.VMEM((D, width), bf16),
        ]
        + scatter_scratch(n_tp, rows)
        + [pltpu.SemaphoreType.DMA((7,))]
        + sent_scratch(payload),
        compiler_params=params(collective_id),
        cost_estimate=pl.CostEstimate(
            flops=8 * n_tp * rows * D * width, bytes_accessed=50 * 2**20, transcendentals=n_tp * rows * width
        ),
    )(grad, x, vecs, all_rows, pre, hidden, w_b, *(a for _, a in payload))


class Share:
    def __init__(self, group, kv, sems):
        self.g, self.kv, self.sems = group, kv, sems
        self.partner = group.at(group.z, 1 - group.y)

    def piece(self, member, micro, index, to):
        ref = self.kv.at[member, micro]
        return self.g.copy(ref, ref, self.sems, micro * 7 + index, to)

    def own(self, micro):
        g = self.g
        return [self.piece(g.member, micro, 0, self.partner)] + [
            self.piece(g.member, micro, k, g.at(g.ahead(k), g.y)) for k in (1, 2, 3)
        ]

    def relayed(self, micro):
        g = self.g
        return [self.piece(g.at(g.behind(k), g.y), micro, 3 + k, self.partner) for k in (1, 2, 3)]

    def start(self, micro):
        for copy in self.own(micro):
            copy.start()

    def relay(self, micro):
        g = self.g
        for k, copy in zip((1, 2, 3), self.relayed(micro)):
            self.piece(g.at(g.behind(k), g.y), micro, k, self.partner).wait_recv()
            copy.start()

    def wait(self, micro):
        g = self.g
        self.piece(self.partner, micro, 0, self.partner).wait_recv()
        for k in (1, 2, 3):
            self.piece(g.at(g.behind(k), 1 - g.y), micro, 3 + k, self.partner).wait_recv()

    def finish(self, micro):
        for copy in self.own(micro) + self.relayed(micro):
            copy.wait_send()


class GroupSum:
    def __init__(self, group, parts, from_y, to_z, from_z, sems):
        self.g, self.parts, self.sems = group, parts, sems
        self.from_y, self.to_z, self.from_z = from_y, to_z, from_z

    def across(self, micro):
        g = self.g
        return g.copy(
            self.parts.at[micro, :, 1 - g.y], self.from_y.at[micro], self.sems, micro * 4, g.at(g.z, 1 - g.y)
        )

    def along(self, micro, k):
        g = self.g
        to = g.ahead(k)
        return g.copy(
            self.to_z.at[micro, to], self.from_z.at[micro, k - 1], self.sems, micro * 4 + k, g.at(to, g.y)
        )

    def start(self, micro):
        self.across(micro).start()

    def turn(self, micro):
        self.across(micro).wait_recv()

        @pl.loop(0, 4)
        def _(z):
            for kv in range(2):
                total = self.parts[micro, z, self.g.y, kv].astype(f32) + self.from_y[micro, z, kv].astype(f32)
                self.to_z[micro, z, kv] = total.astype(bf16)

        for k in (1, 2, 3):
            self.along(micro, k).start()

    def wait(self, micro):
        for k in (1, 2, 3):
            self.along(micro, k).wait_recv()

    def total(self, micro, kv):
        g = self.g
        value = self.parts[micro, g.z, g.y, kv].astype(f32) + self.from_y[micro, g.z, kv].astype(f32)
        for k in range(3):
            value = value + self.from_z[micro, k, kv].astype(f32)
        return value.astype(bf16)

    def finish(self, micro):
        self.across(micro).wait_send()
        for k in (1, 2, 3):
            self.along(micro, k).wait_send()


WIDE = 512
HEAD_PAIRS = WIDE // (2 * HEAD)
PROMPT_CHUNKS = PROMPT // CHUNK
CONT_CHUNKS = CONT_LEN // CHUNK


def chunk_at(c, base=0):
    return pl.ds(pl.multiple_of(base + c * CHUNK, CHUNK), CHUNK)


def key_limit(member):
    row = lax.broadcasted_iota(jnp.int32, (1, TOK_DEV), 1)
    return jnp.where(row < PROMPT_DEV, member * PROMPT_DEV + row, PROMPT - PROMPT_DEV + row)


def half_of(value, half):
    lane = lax.broadcasted_iota(jnp.int32, value.shape, 1)
    return jnp.where((lane >= HEAD * half) & (lane < HEAD * (half + 1)), value, jnp.zeros_like(value))


def fold(value, op):
    return op(value.reshape(value.shape[0] // 8, 8, value.shape[1]), axis=0)


def over_keys(body, prompt, own, carry):
    carry = lax.fori_loop(0, PROMPT_CHUNKS, lambda c, carry: body(c, lambda i: prompt(c, i), carry), carry)
    return lax.fori_loop(
        0, CONT_CHUNKS, lambda c, carry: body(PROMPT_CHUNKS + c, lambda i: own(c, i), carry), carry
    )


def head_pairs(head, finish):
    @pl.loop(0, HEAD_PAIRS)
    def _(pair):
        lanes = pl.ds(pl.multiple_of(pair * 2 * HEAD, 2 * HEAD), 2 * HEAD)
        head(pair, lanes, 0)

        @pl.when(pair < HEAD_PAIRS - 1)
        def _():
            head(pair, lanes, 1)

        finish(pair, lanes)


def to_slots(target, micro, first, value, lanes):
    per = target.shape[1] // MICRO
    row = first
    while row < first + value.shape[0]:
        slot, within = row // per, row % per
        count = min(per - within, first + value.shape[0] - row)
        target[slot, micro * per + within : micro * per + within + count, lanes] = value[
            row - first : row - first + count
        ]
        row += count


def pair_to_blocks(target, x, value):
    per = value.shape[0] // (2 * MICRO)
    for core in range(2):
        for micro in range(MICRO):
            at = pl.ds(pl.multiple_of((2 * x + core) * per, per), per)
            first = (core * MICRO + micro) * per
            target[micro, at, :] = value[first : first + per]


def attn_fwd_kernel(n, *refs):
    x_ref, vec_ref, bias_ref, wqkv_hbm = refs[:4]
    shard, refs = refs[4 : 4 + n], refs[4 + n :]
    out_ref, lse_ref, all_hbm, own_hbm, kv_hbm, mix_hbm, wout_hbm = refs[:7]
    whole, refs = refs[7 : 7 + n], refs[7 + n :]
    wqkv, wout, wparts, buf, own, kv, mix, s_ref, p_ref, o_ref = refs[:10]
    part, from_core, over_out, from_over, send, recv, gsend, grecv, wsend, wrecv, local = refs[10:21]
    p, g = Peers(), Group()
    spread = Spread(g, shard[0], whole[0], refs[21:], ATTN_CHUNKS) if n else None
    rows = x_ref.shape[0]
    n_tp = buf.shape[0]
    step = HEADS // n_tp * HEAD
    width = wparts.shape[1]
    sems = (send, recv)
    gather = Gather(p, buf, sems)
    scatter = Scatter(p, part, from_core, over_out, from_over, sems)
    share = Share(g, kv, (gsend, grecv))
    load_qkv = pltpu.make_async_copy(wqkv_hbm.at[:, : 3 * WIDE], wqkv, local.at[0])
    load_qkv.start()

    def rows_for(t):
        return wqkv_hbm.at[pl.ds(pl.multiple_of(t * step, 128), width), 3 * WIDE : 4 * WIDE]

    keep_part = pltpu.make_async_copy(rows_for(p.t), wparts.at[p.t], local.at[1])
    keep_part.start()
    give_parts = [
        p.copy(rows_for(t), wparts.at[p.t], (wsend, wrecv), i, t) for i, t in enumerate((p.core, p.over, p.diag))
    ]

    def norm(at):
        hat, _ = norm_stats(x_ref[at, :])
        buf[p.t, at, :] = (hat * vec_ref[0:1, :] + vec_ref[1:2, :]).astype(bf16)

    row_chunks(rows, norm)
    g.greet(p, True)
    gather.start()
    for copy in give_parts:
        copy.start()
    if n:
        spread.start(0, 1)
    gather.wait_chip()
    load_qkv.wait()

    def project(x):
        for i in range(3):
            value = mm(pair_rows(buf, x), wqkv[:, i * WIDE : (i + 1) * WIDE]) + bias_ref[i : i + 1, :]
            low = value.astype(bf16)
            if i == 0:
                low = low * HEAD ** (-0.5)
            pair_to_blocks(own.at[i], x, low)

    project(p.x)
    gather.relay()
    gather.wait_diag()
    project(1 - p.x)
    for micro in range(MICRO):
        for i in range(2):
            kv[g.member, micro, i] = own[1 + i, micro, :PROMPT_DEV, :]
        share.start(micro)
    if n:
        spread.start(1)
        spread.relay(0)
    keep_all = pltpu.make_async_copy(buf, all_hbm, local.at[2])
    keep_own = pltpu.make_async_copy(own, own_hbm, local.at[3])
    keep_all.start()
    keep_own.start()
    limit = key_limit(g.member)
    sub = lax.broadcasted_iota(jnp.int32, (CHUNK, TOK_DEV), 0)

    for micro in range(MICRO):
        if micro == 0:
            share.relay(0)
        share.wait(micro)

        def head(pair, lanes, half, micro=micro):
            if half == 0:

                @pl.when(pair == 1)
                def _():
                    if micro == 0:
                        share.relay(1)
                    elif n:
                        spread.relay(2)

                @pl.when(pair == HEAD_PAIRS - 1)
                def _():
                    if n:
                        spread.relay(1 + 2 * micro)

            qh = half_of(own[0, micro, :, lanes], half)

            def first(c, load, top):
                s = jnp.where(sub + c * CHUNK <= limit, mm(load(0), qh, NT), -1e30)
                s_ref[chunk_at(c), :] = s
                return jnp.maximum(top, fold(s, jnp.max))

            top = over_keys(
                first,
                lambda c, i: kv[c, micro, i, :, lanes],
                lambda c, i: own[1 + i, micro, chunk_at(c, PROMPT_DEV), lanes],
                jnp.full((8, TOK_DEV), -1e30, f32),
            )
            top = jnp.max(top, axis=0, keepdims=True)

            def second(c, total):
                e = jnp.exp(s_ref[chunk_at(c), :] - top)
                p_ref[chunk_at(c), :] = e.astype(bf16)
                return total + fold(e, jnp.sum)

            total = lax.fori_loop(0, KEYS // CHUNK, second, jnp.zeros((8, TOK_DEV), f32))
            total = jnp.sum(total, axis=0, keepdims=True)
            values = kv[:, micro, 1, :, lanes].reshape(PROMPT, 2 * HEAD)
            out = mm(values, p_ref[:PROMPT, :], TN) + mm(own[2, micro, PROMPT_DEV:, lanes], p_ref[PROMPT:, :], TN)
            at = slice(HEAD * half, HEAD * (half + 1))
            o_ref[at, :] = out[at, :] / total
            lse_ref[micro, pair, half : half + 1, :] = top + jnp.log(total)

        def finish(pair, lanes, micro=micro):
            @pl.when(pair == HEAD_PAIRS - 1)
            def _():
                o_ref[HEAD:, :] = jnp.zeros((HEAD, TOK_DEV), f32)

            to_slots(mix, micro, 0, o_ref[...].T.astype(bf16), lanes)

        head_pairs(head, finish)

    keep_kv = pltpu.make_async_copy(kv, kv_hbm, local.at[4])
    keep_mix = pltpu.make_async_copy(mix, mix_hbm, local.at[5])
    keep_kv.start()
    keep_mix.start()
    keep_part.wait()
    for i, t in enumerate((p.core, p.over, p.diag)):
        p.copy(rows_for(t), wparts.at[t], (wsend, wrecv), i, t).wait_recv()
    for t in range(n_tp):
        count = min(WIDE, D - t * step)
        wout[:width, t * step : t * step + count] = wparts[t, :, :count]
    wout[width:, :] = jnp.zeros((WIDE - width, D), bf16)

    @pl.when(p.t < n_tp - 1)
    def _():
        wout[step:width, :] = jnp.zeros((width - step, D), bf16)

    keep_out = pltpu.make_async_copy(wout, wout_hbm, local.at[6])
    keep_out.start()

    def down(x):
        def tile(at):
            put_pair(part, x, at, mm(pair_rows(mix, x), wout[:, at]))

        tiles(D, tile)

    down(1 - p.x)
    scatter.far_to_core().start()
    scatter.send_over()
    down(p.x)
    scatter.near_to_core().start()
    if n:
        spread.relay(4)
    scatter.wait()

    def final(at):
        out_ref[at, :] = x_ref[at, :] + (scatter.rows(at) + vec_ref[4:5, :])

    row_chunks(rows, final)
    gather.finish()
    scatter.finish()
    for micro in range(MICRO):
        share.finish(micro)
    for copy in give_parts:
        copy.wait_send()
    for copy in (keep_all, keep_own, keep_kv, keep_mix, keep_out):
        copy.wait()
    if n:
        spread.finish()


def attn_shapes(n_tp, rows):
    return (
        ((n_tp, rows, D), bf16),
        ((3, MICRO, TOK_DEV, WIDE), bf16),
        ((GROUP, MICRO, 2, PROMPT_DEV, WIDE), bf16),
        ((n_tp, rows, WIDE), bf16),
    )


def attn_fwd(x, vecs, biases, w_a, n_tp, shard, collective_id):
    rows = x.shape[0]
    width = D - HEADS // n_tp * HEAD * (n_tp - 1)
    saved = attn_shapes(n_tp, rows)
    operands, results, sems = spread_parts(shard, ATTN_CHUNKS)
    return pl.pallas_call(
        functools.partial(attn_fwd_kernel, len(operands)),
        out_shape=(
            jax.ShapeDtypeStruct((rows, D), f32),
            jax.ShapeDtypeStruct((MICRO, HEAD_PAIRS, 8, TOK_DEV), f32),
        )
        + tuple(jax.ShapeDtypeStruct(*s) for s in saved + (((WIDE, D), bf16),))
        + results,
        in_specs=[IN_VMEM, IN_VMEM, IN_VMEM, ANY] + [ANY] * len(operands),
        out_specs=(IN_VMEM, IN_VMEM) + (ANY,) * (5 + len(operands)),
        scratch_shapes=[pltpu.VMEM((D, 3 * WIDE), bf16), pltpu.VMEM((WIDE, D), bf16), pltpu.VMEM((n_tp, width, WIDE), bf16)]
        + [pltpu.VMEM(*s) for s in saved]
        + [
            pltpu.VMEM((KEYS, TOK_DEV), f32),
            pltpu.VMEM((KEYS, TOK_DEV), bf16),
            pltpu.VMEM((2 * HEAD, TOK_DEV), f32),
        ]
        + scatter_scratch(n_tp, rows)
        + [
            pltpu.SemaphoreType.DMA((7 * MICRO,)),
            pltpu.SemaphoreType.DMA((7 * MICRO,)),
            pltpu.SemaphoreType.DMA((3,)),
            pltpu.SemaphoreType.DMA((3,)),
            pltpu.SemaphoreType.DMA((7,)),
        ]
        + sems,
        compiler_params=params(collective_id),
        cost_estimate=pl.CostEstimate(flops=10**11, bytes_accessed=30 * 2**20, transcendentals=0),
    )(x, vecs, biases, w_a, *operands)


def attn_bwd_kernel(kinds, *refs):
    n = len(kinds)
    g_ref, x_ref, vec_ref, lse_ref, all_hbm, own_hbm, kv_hbm, mix_hbm, wqkv_hbm, wout_hbm = refs[:10]
    sources, refs = refs[10 : 10 + n], refs[10 + n :]
    out_ref, sums_ref, cols_ref, dqkv_hbm, dout_hbm = refs[:5]
    targets, refs = refs[5 : 5 + n], refs[5 + n :]
    wqkv, wout, buf, other, own, kv, gm, dkv, from_y, to_z, from_z, dkc, dqkv, stage, stage_out = refs[:15]
    p_ref, dp_ref, ds_ref, o_ref = refs[15:19]
    part, from_core, over_out, from_over, send, recv, gsend, grecv, local = refs[19:28]
    p, g = Peers(), Group()
    background = Background(g, p, kinds, sources, targets, refs[28:])
    rows = x_ref.shape[0]
    n_tp = buf.shape[0]
    out_width = stage_out.shape[1]
    out_step = (D - out_width) // (n_tp - 1)
    sems = (send, recv)
    gather = Gather(p, buf, sems)
    scatter = Scatter(p, part, from_core, over_out, from_over, sems)
    reduce = GroupSum(g, dkv, from_y, to_z, from_z, (gsend, grecv))
    load_out = pltpu.make_async_copy(wout_hbm, wout, local.at[0])
    load_own = pltpu.make_async_copy(own_hbm, own, local.at[1])
    load_kv = pltpu.make_async_copy(kv_hbm, kv, local.at[2])
    load_qkv = pltpu.make_async_copy(wqkv_hbm.at[:, : 3 * WIDE], wqkv, local.at[3])
    load_mix = pltpu.make_async_copy(mix_hbm, other, local.at[4])
    for copy in (load_out, load_own, load_kv, load_qkv, load_mix):
        copy.start()
    sums_ref[...] = jnp.zeros_like(sums_ref)

    def lower(at):
        low = g_ref[at, :].astype(bf16)
        buf[p.t, at, :] = low
        add_rows(sums_ref, 4, low.astype(f32))

    row_chunks(rows, lower)
    g.greet(p)
    gather.start()
    background.start()
    gather.wait_chip()
    load_out.wait()

    def mixed_back(x):
        pair_to_blocks(gm, x, mm(pair_rows(buf, x), wout[...], NT).astype(bf16))

    mixed_back(p.x)
    gather.relay()
    gather.wait_diag()
    mixed_back(1 - p.x)
    load_own.wait()
    load_kv.wait()
    limit = key_limit(g.member)
    sub = lax.broadcasted_iota(jnp.int32, (CHUNK, TOK_DEV), 0)

    for micro in range(MICRO):

        def head(pair, lanes, half, micro=micro):
            if micro == 1 and half == 0:

                @pl.when(pair == HEAD_PAIRS - 1)
                def _():
                    reduce.turn(0)

            qh = half_of(own[0, micro, :, lanes], half)
            gh = half_of(gm[micro, :, lanes], half)
            lse = lse_ref[micro, pair, half : half + 1, :]

            def first(c, load, inner):
                s = jnp.where(sub + c * CHUNK <= limit, mm(load(0), qh, NT), -1e30)
                e = jnp.exp(s - lse)
                dp = mm(load(1), gh, NT)
                p_ref[chunk_at(c), :] = e
                dp_ref[chunk_at(c), :] = dp
                return inner + fold(e * dp, jnp.sum)

            inner = over_keys(
                first,
                lambda c, i: kv[c, micro, i, :, lanes],
                lambda c, i: own[1 + i, micro, chunk_at(c, PROMPT_DEV), lanes],
                jnp.zeros((8, TOK_DEV), f32),
            )
            inner = jnp.sum(inner, axis=0, keepdims=True)

            def second(c, put):
                e = p_ref[chunk_at(c), :]
                ds = (e * (dp_ref[chunk_at(c), :] - inner)).astype(bf16)
                ds_ref[chunk_at(c), :] = ds
                put(0, mm(ds, qh))
                put(1, mm(e.astype(bf16), gh))

            @pl.loop(0, PROMPT_CHUNKS)
            def _(c):
                def put(i, value):
                    at = (micro, c // 2, c % 2, i, slice(None), lanes)
                    if half:
                        value = value + dkv[at].astype(f32)
                    dkv[at] = value.astype(bf16)

                second(c, put)

            @pl.loop(0, CONT_CHUNKS)
            def _(c):
                def put(i, value):
                    at = (i, chunk_at(c), lanes)
                    if half:
                        value = value + dkc[at].astype(f32)
                    dkc[at] = value.astype(bf16)

                second(PROMPT_CHUNKS + c, put)

            keys = kv[:, micro, 0, :, lanes].reshape(PROMPT, 2 * HEAD)
            dq = mm(keys, ds_ref[:PROMPT, :], TN) + mm(own[1, micro, PROMPT_DEV:, lanes], ds_ref[PROMPT:, :], TN)
            at = slice(HEAD * half, HEAD * (half + 1))
            o_ref[at, :] = dq[at, :] * HEAD ** (-0.5)

        def finish(pair, lanes, micro=micro):
            @pl.when(pair == HEAD_PAIRS - 1)
            def _():
                o_ref[HEAD:, :] = jnp.zeros((HEAD, TOK_DEV), f32)

            to_slots(dqkv, micro, 0, o_ref[...].T.astype(bf16), lanes)

        head_pairs(head, finish)
        reduce.start(micro)
        for i in range(2):
            to_slots(dqkv, micro, PROMPT_DEV, dkc[i], slice((1 + i) * WIDE, (2 + i) * WIDE))

    load_mix.wait()
    columns = pl.ds(pl.multiple_of(p.t * out_step, 128), out_width)

    def outer(source, target, right, body):
        flat = right.reshape(n_tp * rows, right.shape[-1])

        def tile(at):
            left = source[:, :, at].reshape(n_tp * rows, -1)
            target[at, :] = mm(left, flat, TN).astype(bf16)

        body(D, tile)

    outer(other, stage_out, buf[:, :, columns], tiles)
    keep_out = pltpu.make_async_copy(stage_out, dout_hbm, local.at[5])
    keep_out.start()
    load_all = pltpu.make_async_copy(all_hbm, other, local.at[6])
    load_all.start()
    reduce.turn(1)
    for micro in range(MICRO):
        reduce.wait(micro)
        for i in range(2):
            to_slots(dqkv, micro, 0, reduce.total(micro, i), slice((1 + i) * WIDE, (2 + i) * WIDE))
    load_qkv.wait()

    def down(x):
        def tile(at):
            put_pair(part, x, at, mm(pair_rows(dqkv, x), wqkv[at, :], NT))

        tiles(D, tile)

    down(1 - p.x)
    scatter.far_to_core().start()
    scatter.send_over()
    down(p.x)
    scatter.near_to_core().start()
    load_all.wait()
    outer(other, stage, dqkv[...], tiles)
    keep_qkv = pltpu.make_async_copy(stage, dqkv_hbm, local.at[7])
    keep_qkv.start()
    cols_ref[...] = jnp.zeros_like(cols_ref)

    @pl.loop(0, n_tp * rows // ROW_CHUNK)
    def _(i):
        per = rows // ROW_CHUNK
        at = pl.ds(pl.multiple_of((i % per) * ROW_CHUNK, ROW_CHUNK), ROW_CHUNK)
        add_rows(cols_ref, 0, dqkv[i // per, at, :].astype(f32))

    scatter.wait()

    def final(at):
        dy = scatter.rows(at)
        dx, d_gain = norm_back(x_ref[at, :], dy, vec_ref[0:1, :])
        add_rows(sums_ref, 0, d_gain)
        add_rows(sums_ref, 1, dy)
        out_ref[at, :] = g_ref[at, :] + dx

    row_chunks(rows, final)
    gather.finish()
    scatter.finish()
    for micro in range(MICRO):
        reduce.finish(micro)
    keep_out.wait()
    keep_qkv.wait()
    background.finish()


def attn_bwd(grad, x, vecs, lse, all_rows, own, kv, mixed_all, w_a, w_out, out_width, n_tp, payload, collective_id):
    rows = x.shape[0]
    pieces = (MICRO, 4, 2, 2, PROMPT_DEV, WIDE)
    return pl.pallas_call(
        functools.partial(attn_bwd_kernel, tuple(kind for kind, _ in payload)),
        out_shape=(
            jax.ShapeDtypeStruct((rows, D), f32),
            jax.ShapeDtypeStruct((8, D), f32),
            jax.ShapeDtypeStruct((1, 3 * WIDE), f32),
            jax.ShapeDtypeStruct((D, 3 * WIDE), bf16),
            jax.ShapeDtypeStruct((D, out_width), bf16),
        )
        + sent_shapes(payload),
        in_specs=[IN_VMEM] * 4 + [ANY] * (6 + len(payload)),
        out_specs=(IN_VMEM, IN_VMEM, IN_VMEM) + (ANY,) * (2 + len(payload)),
        scratch_shapes=[
            pltpu.VMEM((D, 3 * WIDE), bf16),
            pltpu.VMEM((WIDE, D), bf16),
            pltpu.VMEM((n_tp, rows, D), bf16),
            pltpu.VMEM((n_tp, rows, D), bf16),
            pltpu.VMEM((3, MICRO, TOK_DEV, WIDE), bf16),
            pltpu.VMEM((GROUP, MICRO, 2, PROMPT_DEV, WIDE), bf16),
            pltpu.VMEM((MICRO, TOK_DEV, WIDE), bf16),
            pltpu.VMEM(pieces, bf16),
            pltpu.VMEM((MICRO, 4, 2, PROMPT_DEV, WIDE), bf16),
            pltpu.VMEM((MICRO, 4, 2, PROMPT_DEV, WIDE), bf16),
            pltpu.VMEM((MICRO, 3, 2, PROMPT_DEV, WIDE), bf16),
            pltpu.VMEM((2, CONT_LEN, WIDE), bf16),
            pltpu.VMEM((n_tp, rows, 3 * WIDE), bf16),
            pltpu.VMEM((D, 3 * WIDE), bf16),
            pltpu.VMEM((D, out_width), bf16),
            pltpu.VMEM((KEYS, TOK_DEV), f32),
            pltpu.VMEM((KEYS, TOK_DEV), f32),
            pltpu.VMEM((KEYS, TOK_DEV), bf16),
            pltpu.VMEM((2 * HEAD, TOK_DEV), f32),
        ]
        + scatter_scratch(n_tp, rows)
        + [
            pltpu.SemaphoreType.DMA((4 * MICRO,)),
            pltpu.SemaphoreType.DMA((4 * MICRO,)),
            pltpu.SemaphoreType.DMA((8,)),
        ]
        + sent_scratch(payload),
        compiler_params=params(collective_id),
        cost_estimate=pl.CostEstimate(flops=2 * 10**11, bytes_accessed=50 * 2**20, transcendentals=0),
    )(grad, x, vecs, lse, all_rows, own, kv, mixed_all, w_a, w_out, *(a for _, a in payload))


def send_kernel(kinds, *refs):
    n = len(kinds)
    p, g = Peers(), Group()
    background = Background(g, p, kinds, refs[:n], refs[n : 2 * n], refs[2 * n :])
    barrier = pltpu.get_barrier_semaphore()
    others = []
    if "y" in kinds:
        others += [g.at(g.z, 1 - g.y)]
    if "z" in kinds:
        others += [g.at(g.ahead(k), g.y) for k in (1, 2, 3)]
    for member in others:
        pl.semaphore_signal(barrier, inc=1, device_id=(g.base + member, g.t), device_id_type=MESH)
    near = [p.core, p.over] if "t" in kinds else []
    for t in near:
        pl.semaphore_signal(barrier, inc=1, device_id=(p.f, t), device_id_type=MESH)
    pl.semaphore_wait(barrier, len(others) + len(near))
    background.start()
    background.finish()


def send_only(payload, collective_id):
    return pl.pallas_call(
        functools.partial(send_kernel, tuple(kind for kind, _ in payload)),
        out_shape=sent_shapes(payload),
        in_specs=[ANY] * len(payload),
        out_specs=(ANY,) * len(payload),
        scratch_shapes=sent_scratch(payload),
        compiler_params=params(collective_id),
    )(*(a for _, a in payload))


def forward_layer(x, layer, fetch, vecs, fc_bias, cols, n_tp):
    width = D - HEADS // n_tp * HEAD * (n_tp - 1)
    query_bias, value_bias = (lax.dynamic_slice_in_dim(vecs[i], cols, width) for i in (2, 3))
    biases = widen(jnp.stack([query_bias, jnp.zeros_like(query_bias), value_bias]))
    w_a = fetch.weights[layer, "a"]
    x_mid, lse, all_rows, own, kv, mixed, w_out = fetch.during(
        (layer, "b"), lambda shard: attn_fwd(x, vecs, biases, w_a, n_tp, shard, 5 + layer)
    )
    w_b = fetch.weights[layer, "b"]
    x_next, second_all, hidden_pre, hidden = fetch.during(
        (layer + 1, "a"), lambda shard: ff_fwd(x_mid, vecs, fc_bias[None], w_b, n_tp, shard, 1 + layer)
    )
    mixed_all = heads_joined(lax.all_gather(mixed[:, :, :width], "tp"), n_tp)
    return x_next, (x, w_out, lse, all_rows, own, kv, mixed_all, x_mid, second_all, hidden_pre, hidden)


class Fetch:
    def __init__(self, shards):
        self.staged = lax.axis_size("fsdp") == GROUP
        self.shards, self.weights = shards, {}
        last = None
        for key, shard in shards.items():
            if self.staged:
                if last is None:
                    last = spread_only(shard, 8, 9)
                    self.weights[key] = last.reshape(-1, shard.shape[1])
                continue
            if last is not None:
                shard, _ = lax.optimization_barrier((shard, last))
            whole = lax.all_gather(shard, "fsdp", axis=0, tiled=True)
            self.weights[key] = whole
            last = whole[:8, :128]

    def during(self, key, kernel):
        if not self.staged or key not in self.shards:
            return kernel(None)
        *results, whole = kernel(self.shards[key])
        self.weights[key] = whole.reshape(-1, whole.shape[2])
        return results


def fsdp_sum(part):
    return lax.psum_scatter(part, "fsdp", scatter_dimension=0, tiled=True).astype(f32)


def heads_joined(parts, n_tp):
    step = HEADS // n_tp * HEAD
    return jnp.concatenate([parts[t][..., :step] for t in range(n_tp - 1)] + [parts[n_tp - 1]], axis=-1)


def widen(value, axis=-1):
    pads = [(0, 0)] * value.ndim
    pads[axis] = (0, WIDE - value.shape[axis])
    return jnp.pad(value, pads)


def to_y(part):
    return ("y", part.reshape(4, 2, -1, part.shape[1]))


def to_z(part, arrived):
    own = lax.dynamic_index_in_dim(part.reshape(4, 2, -1, part.shape[1]), lax.axis_index("fsdp") % 2, 1, False)
    return ("z", (own.astype(f32) + arrived.astype(f32)).astype(bf16))


def owned(summed, arrived):
    own = lax.dynamic_index_in_dim(summed[1], lax.axis_index("fsdp") // 2, 0, False)
    return own.astype(f32) + jnp.sum(arrived.astype(f32), 0)


def with_vectors(grad_out, ff_sums, attn_sums, col_sums, fc_bias_sums, cols):
    width = grad_out.shape[1]

    def placed(part):
        return lax.dynamic_update_slice_in_dim(jnp.zeros((1, D), f32), part, cols, 1)

    vector_grads = jnp.concatenate(
        [
            attn_sums[:2],
            placed(col_sums[:, :width]),
            placed(col_sums[:, 2 * WIDE : 2 * WIDE + width]),
            attn_sums[4:5],
            ff_sums[5:],
            fc_bias_sums,
        ]
    )
    return widen(jnp.concatenate([grad_out, vector_grads.astype(bf16).T], axis=1))


def backward(grad, weights, vecs, saves, cols, n_tp):
    width = D - HEADS // n_tp * HEAD * (n_tp - 1)
    staged = lax.axis_size("fsdp") == GROUP
    sums = [None] * LAYERS
    joined = [None] * LAYERS
    waiting_y, waiting_z, waiting_t, done = [], [], [], {}

    def load(limit_z, limit_y):
        chosen_z = [waiting_z.pop(0) for _ in range(min(limit_z, len(waiting_z)))]
        chosen_y = [waiting_y.pop(0) for _ in range(min(limit_y, len(waiting_y)))]
        return chosen_z, chosen_y, [item for _, item in chosen_z] + [to_y(part) for _, part in chosen_y]

    def unload(chosen_z, chosen_y, arrived):
        for (name, item), got in zip(chosen_z, arrived):
            done[name] = owned(item, got)
        for (name, part), got in zip(chosen_y, arrived[len(chosen_z) :]):
            waiting_z.append((name, to_z(part, got)))

    def produced(layer, names, values):
        for name, value in zip(names, values):
            if staged:
                waiting_y.append(((layer, name), value))
            else:
                done[layer, name] = fsdp_sum(value)

    plan = {(1, 0): (0, 0), (1, 1): (0, 2), (0, 0): (1, 2), (0, 1): (3, 2)}
    for layer in reversed(range(LAYERS)):
        w_a, w_b = weights[layer, "a"], weights[layer, "b"]
        x, w_out, lse, all_rows, own, kv, mixed_all, x_mid, second_all, hidden_pre, hidden = saves[layer]
        chosen_z, chosen_y, payload = load(*plan[layer, 0])
        grad, ff_sums, fc_bias_sums, grad_fc, grad_proj, *arrived = ff_bwd(
            grad, x_mid, vecs[layer], second_all, hidden_pre, hidden, w_b, n_tp, payload, 10 + layer
        )
        unload(chosen_z, chosen_y, arrived)
        produced(layer, ("proj", "fc"), (grad_proj, grad_fc))
        chosen_z, chosen_y, payload = load(*plan[layer, 1])
        grad, attn_sums, col_sums, grad_qkv, grad_out, *arrived = attn_bwd(
            grad, x, vecs[layer], lse, all_rows, own, kv, mixed_all, w_a, w_out, width, n_tp, payload, 20 + layer
        )
        unload(chosen_z, chosen_y, arrived)
        grad_out = with_vectors(grad_out, ff_sums, attn_sums, col_sums, fc_bias_sums, cols)
        produced(layer, ("qkv", "out"), (grad_qkv, grad_out))
    number = 30
    asked = set()
    while len(asked) < LAYERS or waiting_t:
        chosen_z, chosen_y, payload = load(9, 9)
        chosen_t, waiting_t = waiting_t, []
        arrived = []
        if payload or chosen_t:
            arrived = list(send_only(payload + [("t", part) for _, part in chosen_t], number))
            number += 1
        unload(chosen_z, chosen_y, arrived)
        for (layer, _), got in zip(chosen_t, arrived[len(payload) :]):
            joined[layer] = got
        for layer in range(LAYERS):
            if layer not in asked and (layer, "qkv") in done and (layer, "out") in done:
                asked.add(layer)
                both = jnp.concatenate([done[layer, "qkv"], done[layer, "out"]], axis=1).astype(bf16)
                waiting_t.append((layer, both))
    for layer in range(LAYERS):
        got = joined[layer]
        qkv_grad = jnp.concatenate(
            [heads_joined(got[:, :, i * WIDE : i * WIDE + width], n_tp) for i in range(3)], axis=1
        ).astype(f32)
        out_grad = heads_joined(got[:, :, 3 * WIDE : 3 * WIDE + width], n_tp).astype(f32)
        vector_sum = jnp.sum(got[:, :, 3 * WIDE + width : 3 * WIDE + width + 8].astype(f32), 0).T
        fc_bias_sum = done[layer, "out"][:, width + 8]
        sums[layer] = (qkv_grad, out_grad, done[layer, "fc"], done[layer, "proj"].T, fc_bias_sum, vector_sum)
    return grad, sums


def local(
    tokens,
    qkv_weight,
    query_bias,
    value_bias,
    out_weight,
    out_bias,
    fc_weight,
    fc_bias,
    proj_weight,
    proj_bias,
    first_gain,
    first_bias,
    second_gain,
    second_bias,
    out_grad,
):
    n_tp = lax.axis_size("tp")
    tp = lax.axis_index("tp")
    row_count = tokens.shape[1]
    step = HEADS // n_tp * HEAD
    width = D - step * (n_tp - 1)
    cols = tp * step

    vectors = jnp.stack(
        [first_gain, first_bias, query_bias, value_bias, out_bias, second_gain, second_bias, proj_bias, fc_bias[:, 0]]
    ).reshape(9 * LAYERS, -1)

    shards = {}
    for layer in range(LAYERS):
        sides = [widen(lax.dynamic_slice_in_dim(qkv_weight[layer], cols + i * D, width, 1)) for i in range(3)]
        sides.append(widen(lax.dynamic_slice_in_dim(out_weight[layer], cols, width, 1)))
        if layer == 0:
            sides.append(jnp.pad(vectors.T, ((0, 0), (0, 128 - 9 * LAYERS))))
        shards[layer, "a"] = jnp.concatenate(sides, axis=1)
        fc, proj = fc_weight[layer], proj_weight[layer].T
        more = ((0, 0), (0, lanes_up(fc.shape[1]) - fc.shape[1]))
        shards[layer, "b"] = jnp.concatenate([jnp.pad(fc, more), jnp.pad(proj, more)], axis=1)
    fetch = Fetch(shards)
    vectors = fetch.weights[0, "a"][:, 4 * WIDE : 4 * WIDE + 9 * LAYERS].T.astype(f32).reshape(9, LAYERS, D)

    state = tokens.astype(f32).reshape(MICRO * row_count, D)
    saves = []
    for layer in range(LAYERS):
        state, saved = forward_layer(state, layer, fetch, vectors[:8, layer], vectors[8, layer], cols, n_tp)
        saves.append(saved)
    out_tokens = state.astype(bf16).reshape(tokens.shape)
    grad = out_grad.astype(f32).reshape(MICRO * row_count, D)
    grad, sums = backward(
        grad, fetch.weights, [vectors[:8, layer] for layer in range(LAYERS)], saves, cols, n_tp
    )
    qkv_g, out_g, fc_g, proj_g, fc_bias_g, vec_g = (
        jnp.stack([sums[layer][i] for layer in range(LAYERS)]) for i in range(6)
    )
    return (
        out_tokens,
        grad.reshape(tokens.shape),
        qkv_g,
        vec_g[:, 2],
        vec_g[:, 3],
        out_g,
        vec_g[:, 4],
        fc_g,
        fc_bias_g[:, None],
        proj_g,
        vec_g[:, 7],
        vec_g[:, 0],
        vec_g[:, 1],
        vec_g[:, 5],
        vec_g[:, 6],
    )


def solution(mesh):
    rows = P(None, ("fsdp", "tp"), None)
    weight = P(None, "fsdp", None)
    vector = P(None, "fsdp")
    fc_in = P(None, "fsdp", "tp")
    hidden = P(None, "tp", "fsdp")
    in_specs = (
        rows, weight, vector, vector, weight, vector, fc_in, hidden, hidden,
        vector, vector, vector, vector, vector, rows,
    )
    out_specs = (
        rows, rows, weight, vector, vector, weight, vector, fc_in, hidden, hidden,
        vector, vector, vector, vector, vector,
    )
    return jax.shard_map(local, mesh=mesh, in_specs=in_specs, out_specs=out_specs, check_vma=False)
```

```python
import functools

import jax
import jax.numpy as jnp
from jax import lax
from jax.experimental import pallas as pl
from jax.experimental.pallas import tpu as pltpu
from jax.sharding import PartitionSpec as P

D = 1600
HEADS = 25
HEAD = 64
GROUP = 8
PROMPT_DEV = 128
CONT_LEN = 256
TOK_DEV = 384
MICRO = 2
LAYERS = 2
PROMPT = 1024
KEYS = PROMPT + CONT_LEN
CHUNK = 128

f32 = jnp.float32
bf16 = jnp.bfloat16
norm_eps = 1e-05
NN = (((1,), (0,)), ((), ()))
NT = (((1,), (1,)), ((), ()))
TN = (((0,), (0,)), ((), ()))


def mm(left, right, dims=NN):
    return lax.dot_general(left, right, dims, preferred_element_type=f32)


def gelu_tanh(value):
    return jax.nn.gelu(value, approximate=True)


MESH = pl.DeviceIdType.MESH
ANY = pl.BlockSpec(memory_space=pl.ANY)
IN_VMEM = pl.BlockSpec(memory_space=pltpu.VMEM)
TILE = 512
ROW_CHUNK = 32


class Peers:
    def __init__(self):
        self.f = lax.axis_index("fsdp")
        self.t = lax.axis_index("tp")
        x, c = self.t // 2, self.t % 2
        self.x = x
        self.core = 2 * x + 1 - c
        self.over = 2 * (1 - x) + c
        self.diag = 2 * (1 - x) + 1 - c

    def greet(self):
        barrier = pltpu.get_barrier_semaphore()
        for t in (self.core, self.over):
            pl.semaphore_signal(barrier, inc=1, device_id=(self.f, t), device_id_type=MESH)
        pl.semaphore_wait(barrier, 2)

    def copy(self, source, target, sems, index, t):
        return pltpu.make_async_remote_copy(
            src_ref=source,
            dst_ref=target,
            send_sem=sems[0].at[index],
            recv_sem=sems[1].at[index],
            device_id=(self.f, t),
            device_id_type=MESH,
        )


class Gather:
    def __init__(self, peers, buf, sems):
        self.p, self.buf, self.sems = peers, buf, sems

    def piece(self, slot, index, t):
        return self.p.copy(self.buf.at[slot], self.buf.at[slot], self.sems, index, t)

    def start(self):
        p = self.p
        self.piece(p.t, 1, p.over).start()
        self.piece(p.t, 0, p.core).start()

    def wait_chip(self):
        self.piece(self.p.core, 0, self.p.core).wait_recv()

    def relay(self):
        p = self.p
        self.piece(p.over, 1, p.over).wait_recv()
        self.piece(p.over, 2, p.core).start()

    def wait_diag(self):
        self.piece(self.p.diag, 2, self.p.core).wait_recv()

    def finish(self):
        p = self.p
        self.piece(p.t, 1, p.over).wait_send()
        self.piece(p.t, 0, p.core).wait_send()
        self.piece(p.over, 2, p.core).wait_send()


class Scatter:
    def __init__(self, peers, part, from_core, over_out, from_over, sems):
        self.p, self.part, self.sems = peers, part, sems
        self.from_core, self.over_out, self.from_over = from_core, over_out, from_over

    def far_to_core(self):
        return self.p.copy(self.part.at[self.p.diag], self.from_core.at[0], self.sems, 3, self.p.core)

    def near_to_core(self):
        return self.p.copy(self.part.at[self.p.core], self.from_core.at[1], self.sems, 4, self.p.core)

    def to_over(self):
        return self.p.copy(self.over_out, self.from_over, self.sems, 5, self.p.over)

    def send_over(self):
        self.far_to_core().wait_recv()

        @pl.loop(0, self.over_out.shape[0] // ROW_CHUNK)
        def _(i):
            at = pl.ds(pl.multiple_of(i * ROW_CHUNK, ROW_CHUNK), ROW_CHUNK)
            total = self.part[self.p.over, at, :].astype(f32) + self.from_core[0, at, :].astype(f32)
            self.over_out[at, :] = total.astype(bf16)

        self.to_over().start()

    def wait(self):
        self.near_to_core().wait_recv()
        self.to_over().wait_recv()

    def rows(self, at):
        return (
            self.part[self.p.t, at, :].astype(f32)
            + self.from_core[1, at, :].astype(f32)
            + self.from_over[at, :].astype(f32)
        )

    def finish(self):
        for copy in (self.far_to_core(), self.near_to_core(), self.to_over()):
            copy.wait_send()


class Group:
    def __init__(self):
        f = lax.axis_index("fsdp")
        self.t = lax.axis_index("tp")
        self.member = f % GROUP
        self.base = f - self.member
        self.z, self.y = self.member // 2, self.member % 2

    def at(self, z, y):
        return z * 2 + y

    def ahead(self, k):
        return (self.z + k) % 4

    def behind(self, k):
        return (self.z + 4 - k) % 4

    def greet_group(self):
        barrier = pltpu.get_barrier_semaphore()
        others = [self.at(self.z, 1 - self.y)] + [self.at(self.ahead(k), self.y) for k in (1, 2, 3)]
        for member in others:
            pl.semaphore_signal(
                barrier, inc=1, device_id=(self.base + member, self.t), device_id_type=MESH
            )
        pl.semaphore_wait(barrier, 4)

    def greet(self, peers, with_diag=False):
        barrier = pltpu.get_barrier_semaphore()
        others = [self.at(self.z, 1 - self.y)] + [self.at(self.ahead(k), self.y) for k in (1, 2, 3)]
        for member in others:
            pl.semaphore_signal(
                barrier, inc=1, device_id=(self.base + member, self.t), device_id_type=MESH
            )
        near = [peers.core, peers.over] + [peers.diag] * with_diag
        for t in near:
            pl.semaphore_signal(barrier, inc=1, device_id=(peers.f, t), device_id_type=MESH)
        pl.semaphore_wait(barrier, 4 + len(near))

    def copy(self, source, target, sems, index, member):
        return pltpu.make_async_remote_copy(
            src_ref=source,
            dst_ref=target,
            send_sem=sems[0].at[index],
            recv_sem=sems[1].at[index],
            device_id=(self.base + member, self.t),
            device_id_type=MESH,
        )


class Reduce:
    def __init__(self, group, source, from_y, from_z, sems, tiles):
        self.g, self.source, self.from_y, self.from_z, self.sems = group, source, from_y, from_z, sems
        self.own, self.got, self.gone, self.local = tiles

    def across(self, j):
        g = self.g
        z = g.ahead(j)
        return g.copy(
            self.source.at[z, 1 - g.y], self.from_y.at[z], self.sems, j, g.at(g.z, 1 - g.y)
        )

    def along(self, j):
        g = self.g
        return g.copy(self.gone.at[j - 1], self.from_z.at[j - 1], self.sems, 3 + j, g.at(g.ahead(j), g.y))

    def start(self):
        for j in (1, 2, 3, 0):
            self.across(j).start()

    def pump(self, j, before=None):
        g = self.g
        load_own = pltpu.make_async_copy(self.source.at[g.ahead(j), g.y], self.own, self.local.at[0])
        load_own.start()
        self.across(j).wait_recv()
        load_got = pltpu.make_async_copy(self.from_y.at[g.ahead(j)], self.got, self.local.at[1])
        load_got.start()
        load_own.wait()
        load_got.wait()
        if before is not None:
            before.along(j).wait_send()
        self.gone[j - 1] = self.own[...] + self.got[...]
        self.along(j).start()

    def finish(self, reused=False):
        self.across(0).wait_recv()
        for j in range(4):
            self.across(j).wait_send()
        for j in (1, 2, 3):
            self.along(j).wait_recv()
            if not reused:
                self.along(j).wait_send()


def reduce_parts(payload):
    results, scratch = (), []
    for part in payload:
        rows = part.shape[2:]
        results += (jax.ShapeDtypeStruct((4,) + rows, bf16), jax.ShapeDtypeStruct((3,) + rows, bf16))
        scratch += [pltpu.SemaphoreType.DMA((7,))] * 2
    if payload:
        scratch += [pltpu.VMEM(rows, bf16), pltpu.VMEM(rows, bf16), pltpu.VMEM((3,) + rows, bf16)]
        scratch += [pltpu.SemaphoreType.DMA((2,))]
    return tuple(payload), results, scratch


def reduces(group, sources, results, scratch):
    tiles = scratch[2 * len(sources) :]
    return [
        Reduce(group, source, results[2 * n], results[2 * n + 1], scratch[2 * n : 2 * n + 2], tiles)
        for n, source in enumerate(sources)
    ]


def reduce_kernel(source, from_y, from_z, *scratch):
    g = Group()
    g.greet_group()
    item = reduces(g, [source], [from_y, from_z], scratch)[0]
    item.start()
    for j in (1, 2, 3):
        item.pump(j)
    item.finish()


def reduce_only(part, collective_id):
    operands, results, scratch = reduce_parts([part])
    return pl.pallas_call(
        reduce_kernel,
        out_shape=results,
        in_specs=[ANY],
        out_specs=(ANY, ANY),
        scratch_shapes=scratch,
        compiler_params=params(collective_id),
    )(part)


def block_gather_kernel(n, *refs):
    p = Peers()
    p.greet()
    sources, targets, (send, recv, local) = refs[:n], refs[n : 2 * n], refs[2 * n :]
    keeps = []
    for i in range(n):
        keeps.append(pltpu.make_async_copy(sources[i], targets[i].at[p.t], local.at[i]))
        keeps[-1].start()
        p.copy(sources[i], targets[i].at[p.t], (send, recv), 3 * i + 1, p.over).start()
        p.copy(sources[i], targets[i].at[p.t], (send, recv), 3 * i, p.core).start()

    def relay(i):
        return p.copy(targets[i].at[p.over], targets[i].at[p.over], (send, recv), 3 * i + 2, p.core)

    for i in range(n):
        p.copy(sources[i], targets[i].at[p.over], (send, recv), 3 * i + 1, p.over).wait_recv()
        relay(i).start()
    for i in range(n):
        p.copy(sources[i], targets[i].at[p.core], (send, recv), 3 * i, p.core).wait()
        p.copy(sources[i], targets[i].at[p.diag], (send, recv), 3 * i + 2, p.core).wait_recv()
        p.copy(sources[i], targets[i].at[p.over], (send, recv), 3 * i + 1, p.over).wait_send()
        relay(i).wait_send()
        keeps[i].wait()


def block_gather(parts, n_tp, collective_id):
    n = len(parts)
    return pl.pallas_call(
        functools.partial(block_gather_kernel, n),
        out_shape=tuple(jax.ShapeDtypeStruct((n_tp,) + part.shape, part.dtype) for part in parts),
        in_specs=[ANY] * n,
        out_specs=(ANY,) * n,
        scratch_shapes=[pltpu.SemaphoreType.DMA((3 * n,))] * 2 + [pltpu.SemaphoreType.DMA((n,))],
        compiler_params=params(collective_id),
    )(*parts)


class Spread:
    def __init__(self, group, source, target, sems, chunks):
        self.g, self.source, self.target, self.sems = group, source, target, sems
        count = source.shape[1] // 128
        ends = [128 * (count * (c + 1) // chunks) for c in range(chunks)]
        self.columns = [slice(a, b) for a, b in zip([0] + ends, ends)]
        self.partner = group.at(group.z, 1 - group.y)

    def piece(self, member, c, index, to, own=False):
        target = self.target.at[member, :, self.columns[c]]
        source = self.source.at[:, self.columns[c]] if own else target
        return self.g.copy(source, target, self.sems, 7 * c + index, to)

    def own(self, c):
        g = self.g
        return [self.piece(g.member, c, k, g.at(g.ahead(k), g.y), True) for k in (1, 2, 3)] + [
            self.piece(g.member, c, 0, self.partner, True)
        ]

    def relayed(self, c):
        g = self.g
        return [self.piece(g.at(g.behind(k), g.y), c, 3 + k, self.partner) for k in (1, 2, 3)]

    def keep(self):
        return pltpu.make_async_copy(
            self.source, self.target.at[self.g.member], self.sems[0].at[7 * len(self.columns)]
        )

    def start(self, first=0, last=None):
        if first == 0:
            self.keep().start()
        for c in range(len(self.columns))[first:last]:
            for copy in self.own(c):
                copy.start()

    def relay(self, c):
        g = self.g
        for k, copy in zip((1, 2, 3), self.relayed(c)):
            self.piece(g.at(g.behind(k), g.y), c, k, self.partner).wait_recv()
            copy.start()

    def finish(self):
        g = self.g
        for c in range(len(self.columns)):
            self.piece(self.partner, c, 0, self.partner).wait_recv()
            for k in (1, 2, 3):
                self.piece(g.at(g.behind(k), 1 - g.y), c, 3 + k, self.partner).wait_recv()
            for copy in self.own(c) + self.relayed(c):
                copy.wait_send()
        self.keep().wait()


def spread_parts(shard, chunks):
    if shard is None:
        return (), (), []
    whole = jax.ShapeDtypeStruct((GROUP,) + shard.shape, shard.dtype)
    return (shard,), (whole,), [pltpu.SemaphoreType.DMA((7 * chunks + 1,))] * 2


def spread_kernel(chunks, source, target, send, recv):
    g = Group()
    g.greet_group()
    spread = Spread(g, source, target, (send, recv), chunks)
    spread.start()
    for c in range(chunks):
        spread.relay(c)
    spread.finish()


def spread_only(shard, chunks, collective_id):
    operands, results, scratch = spread_parts(shard, chunks)
    return pl.pallas_call(
        functools.partial(spread_kernel, chunks),
        out_shape=results[0],
        in_specs=[ANY],
        out_specs=ANY,
        scratch_shapes=scratch,
        compiler_params=params(collective_id),
    )(shard)


def row_chunks(rows, body):
    @pl.loop(0, rows // ROW_CHUNK)
    def _(i):
        body(pl.ds(pl.multiple_of(i * ROW_CHUNK, ROW_CHUNK), ROW_CHUNK))


def tiles(extent, body):
    whole = extent // TILE

    @pl.loop(0, whole)
    def _(i):
        body(pl.ds(pl.multiple_of(i * TILE, TILE), TILE))

    if extent % TILE:
        body(pl.ds(whole * TILE, extent % TILE))


def pair_rows(ref, x):
    both = ref[pl.ds(2 * x, 2)]
    return both.reshape(2 * both.shape[1], both.shape[2])


def put_pair(ref, x, at, value):
    ref[pl.ds(2 * x, 2), :, at] = value.reshape(2, value.shape[0] // 2, value.shape[1]).astype(ref.dtype)


def norm_stats(x):
    centred = x - jnp.mean(x, -1, keepdims=True)
    scale = lax.rsqrt(jnp.mean(centred * centred, -1, keepdims=True) + norm_eps)
    return centred * scale, scale


def lanes_up(width):
    return -(-width // 128) * 128


def proj_part(w_b, width):
    return w_b.at[:, lanes_up(width) :]


FF_CHUNKS = 3
ATTN_CHUNKS = 5


def ff_fwd_kernel(n, *refs):
    x_ref, vec_ref, fcb_ref, wb_hbm = refs[:4]
    shard, refs = refs[4 : 4 + n], refs[4 + n :]
    out_ref, all_hbm, pre_hbm, hid_hbm = refs[:4]
    whole, refs = refs[4 : 4 + n], refs[4 + n :]
    wfc, wproj, buf, pre, hid, part, from_core, over_out, from_over, send, recv, local = refs[:12]
    p, g = Peers(), Group()
    spread = Spread(g, shard[0], whole[0], refs[12:], FF_CHUNKS) if n else None
    rows = x_ref.shape[0]
    sems = (send, recv)
    gather = Gather(p, buf, sems)
    scatter = Scatter(p, part, from_core, over_out, from_over, sems)
    width = fcb_ref.shape[1]
    load_fc = pltpu.make_async_copy(wb_hbm.at[:, : wfc.shape[1]], wfc, local.at[0])
    load_proj = pltpu.make_async_copy(proj_part(wb_hbm, width), wproj, local.at[1])
    load_fc.start()
    load_proj.start()

    def norm(at):
        hat, _ = norm_stats(x_ref[at, :])
        buf[p.t, at, :] = (hat * vec_ref[5:6, :] + vec_ref[6:7, :]).astype(bf16)

    row_chunks(rows, norm)
    if n:
        g.greet(p)
    else:
        p.greet()
    gather.start()
    if n:
        spread.start()
    gather.wait_chip()
    load_fc.wait()

    def up(x):
        def tile(at):
            value = mm(pair_rows(buf, x), wfc[:, at]) + fcb_ref[:, at]
            put_pair(pre, x, at, value)
            put_pair(hid, x, at, gelu_tanh(value))

        tiles(width, tile)

    def down(x):
        def tile(at):
            put_pair(part, x, at, mm(pair_rows(hid, x), wproj[at, :width], NT))

        tiles(D, tile)

    up(p.x)
    if n:
        spread.relay(0)
    gather.relay()
    gather.wait_diag()
    keep_all = pltpu.make_async_copy(buf, all_hbm, local.at[2])
    keep_all.start()
    up(1 - p.x)
    keep_pre = pltpu.make_async_copy(pre, pre_hbm, local.at[3])
    keep_hid = pltpu.make_async_copy(hid, hid_hbm, local.at[4])
    keep_pre.start()
    keep_hid.start()
    load_proj.wait()
    down(1 - p.x)
    scatter.far_to_core().start()
    scatter.send_over()
    if n:
        spread.relay(1)
    down(p.x)
    scatter.near_to_core().start()
    if n:
        spread.relay(2)
    scatter.wait()

    def final(at):
        out_ref[at, :] = x_ref[at, :] + scatter.rows(at) + vec_ref[7:8, :]

    row_chunks(rows, final)
    gather.finish()
    scatter.finish()
    for copy in (keep_all, keep_pre, keep_hid):
        copy.wait()
    if n:
        spread.finish()


def scatter_scratch(n_tp, rows):
    return [
        pltpu.VMEM((n_tp, rows, D), bf16),
        pltpu.VMEM((2, rows, D), bf16),
        pltpu.VMEM((rows, D), bf16),
        pltpu.VMEM((rows, D), bf16),
        pltpu.SemaphoreType.DMA((6,)),
        pltpu.SemaphoreType.DMA((6,)),
    ]


def params(collective_id):
    return pltpu.CompilerParams(collective_id=collective_id, has_side_effects=True, vmem_limit_bytes=60 * 2**20)


def ff_fwd(x, vecs, fc_bias, w_b, n_tp, shard, collective_id):
    rows, width = x.shape[0], fc_bias.shape[1]
    block = (n_tp, rows)
    operands, results, sems = spread_parts(shard, FF_CHUNKS)
    return pl.pallas_call(
        functools.partial(ff_fwd_kernel, len(operands)),
        out_shape=(
            jax.ShapeDtypeStruct((rows, D), f32),
            jax.ShapeDtypeStruct(block + (D,), bf16),
            jax.ShapeDtypeStruct(block + (width,), f32),
            jax.ShapeDtypeStruct(block + (width,), bf16),
        )
        + results,
        in_specs=[IN_VMEM, IN_VMEM, IN_VMEM, ANY] + [ANY] * len(operands),
        out_specs=(IN_VMEM, ANY, ANY, ANY) + (ANY,) * len(operands),
        scratch_shapes=[
            pltpu.VMEM((D, lanes_up(width)), bf16),
            pltpu.VMEM((D, lanes_up(width)), bf16),
            pltpu.VMEM(block + (D,), bf16),
            pltpu.VMEM(block + (width,), f32),
            pltpu.VMEM(block + (width,), bf16),
        ]
        + scatter_scratch(n_tp, rows)
        + [pltpu.SemaphoreType.DMA((5,))]
        + sems,
        compiler_params=params(collective_id),
        cost_estimate=pl.CostEstimate(
            flops=4 * n_tp * rows * D * width, bytes_accessed=40 * 2**20, transcendentals=n_tp * rows * width
        ),
    )(x, vecs, fc_bias, w_b, *operands)


def gelu_slope(u):
    a = 0.7978845608028654
    square = u * u
    t = jnp.tanh(a * (u + 0.044715 * u * square))
    return 0.5 * (1.0 + t) + 0.5 * u * (1.0 - t * t) * (a * (1.0 + 3 * 0.044715 * square))


def norm_back(x, dy, gain):
    hat, scale = norm_stats(x)
    d_hat = dy * gain
    inner = d_hat - jnp.mean(d_hat, -1, keepdims=True) - hat * jnp.mean(d_hat * hat, -1, keepdims=True)
    return scale * inner, dy * hat


def add_rows(ref, row, value):
    ref[row : row + 1, :] += jnp.sum(value, axis=0, keepdims=True)


def ff_bwd_kernel(n, *refs):
    g_ref, x_ref, vec_ref, all_hbm, pre_hbm, hid_hbm, wb_hbm = refs[:7]
    sources, refs = refs[7 : 7 + n], refs[7 + n :]
    out_ref, sums_ref, fcb_ref, dfc_hbm, dproj_hbm = refs[:5]
    results, refs = refs[5 : 5 + 2 * n], refs[5 + 2 * n :]
    wfc, wproj, buf, other, pre, dpre, stage, part, from_core, over_out, from_over, send, recv, local = refs[:14]
    p, g = Peers(), Group()
    sums = reduces(g, sources, results, refs[14:])
    rows = x_ref.shape[0]
    n_tp, width = buf.shape[0], fcb_ref.shape[1]
    sems = (send, recv)
    gather = Gather(p, buf, sems)
    scatter = Scatter(p, part, from_core, over_out, from_over, sems)
    load_proj = pltpu.make_async_copy(proj_part(wb_hbm, width), wproj, local.at[0])
    load_pre = pltpu.make_async_copy(pre_hbm, pre, local.at[1])
    load_fc = pltpu.make_async_copy(wb_hbm.at[:, : wfc.shape[1]], wfc, local.at[2])
    load_other = pltpu.make_async_copy(hid_hbm, other, local.at[3])
    for copy in (load_proj, load_pre, load_fc, load_other):
        copy.start()
    sums_ref[...] = jnp.zeros_like(sums_ref)
    fcb_ref[...] = jnp.zeros_like(fcb_ref)

    def lower(at):
        low = g_ref[at, :].astype(bf16)
        buf[p.t, at, :] = low
        add_rows(sums_ref, 7, low.astype(f32))

    row_chunks(rows, lower)
    if n:
        g.greet(p)
    else:
        p.greet()
    gather.start()
    for item in sums:
        item.start()

    def pump(j):
        for item in sums:
            item.pump(j)

    gather.wait_chip()
    load_proj.wait()
    load_pre.wait()

    def through(x):
        def tile(at):
            d_hidden = mm(pair_rows(buf, x), wproj[:, at])
            u = pre[pl.ds(2 * x, 2), :, at].reshape(2 * rows, -1)
            low = (gelu_slope(u) * d_hidden).astype(bf16)
            put_pair(dpre, x, at, low)
            fcb_ref[:, at] += jnp.sum(low.astype(f32), axis=0, keepdims=True)

        tiles(width, tile)

    def down(x):
        def tile(at):
            put_pair(part, x, at, mm(pair_rows(dpre, x), wfc[at, :width], NT))

        tiles(D, tile)

    through(p.x)
    gather.relay()
    gather.wait_diag()
    through(1 - p.x)
    pump(1)
    load_fc.wait()
    down(1 - p.x)
    scatter.far_to_core().start()
    scatter.send_over()
    down(p.x)
    scatter.near_to_core().start()

    def outer(left, right, target, sem):
        whole = D // TILE
        rest = D - whole * TILE
        flat = right[...].reshape(n_tp * rows, width)

        def tile(i, size):
            at = pl.ds(pl.multiple_of(i * TILE, TILE), size)
            value = mm(left[:, :, at].reshape(n_tp * rows, size), flat, TN)
            stage[at, :] = value.astype(bf16)

        @pl.loop(0, whole)
        def _(i):
            tile(i, TILE)

        if rest:
            tile(whole, rest)
        return pltpu.make_async_copy(stage, target, sem)

    load_other.wait()
    pump(2)
    store = outer(buf, other, dproj_hbm, local.at[4])
    store.start()
    gather.finish()
    load_all = pltpu.make_async_copy(all_hbm, buf, local.at[5])
    load_all.start()
    scatter.wait()

    def final(at):
        dy = scatter.rows(at)
        dx, d_gain = norm_back(x_ref[at, :], dy, vec_ref[5:6, :])
        add_rows(sums_ref, 5, d_gain)
        add_rows(sums_ref, 6, dy)
        out_ref[at, :] = g_ref[at, :] + dx

    row_chunks(rows, final)
    load_all.wait()
    store.wait()
    store = outer(buf, dpre, dfc_hbm, local.at[6])
    store.start()
    pump(3)
    scatter.finish()
    store.wait()
    for item in sums:
        item.finish()


def ff_bwd(grad, x, vecs, all_rows, pre, hidden, w_b, n_tp, payload, collective_id):
    rows, width = x.shape[0], pre.shape[2]
    block = (n_tp, rows)
    operands, results, more = reduce_parts(payload)
    return pl.pallas_call(
        functools.partial(ff_bwd_kernel, len(payload)),
        out_shape=(
            jax.ShapeDtypeStruct((rows, D), f32),
            jax.ShapeDtypeStruct((8, D), f32),
            jax.ShapeDtypeStruct((1, width), f32),
            jax.ShapeDtypeStruct((D, width), bf16),
            jax.ShapeDtypeStruct((D, width), bf16),
        )
        + results,
        in_specs=[IN_VMEM] * 3 + [ANY] * (4 + len(payload)),
        out_specs=(IN_VMEM, IN_VMEM, IN_VMEM) + (ANY,) * (2 + 2 * len(payload)),
        scratch_shapes=[
            pltpu.VMEM((D, lanes_up(width)), bf16),
            pltpu.VMEM((D, lanes_up(width)), bf16),
            pltpu.VMEM(block + (D,), bf16),
            pltpu.VMEM(block + (width,), bf16),
            pltpu.VMEM(block + (width,), f32),
            pltpu.VMEM(block + (width,), bf16),
            pltpu.VMEM((D, width), bf16),
        ]
        + scatter_scratch(n_tp, rows)
        + [pltpu.SemaphoreType.DMA((7,))]
        + more,
        compiler_params=params(collective_id),
        cost_estimate=pl.CostEstimate(
            flops=8 * n_tp * rows * D * width, bytes_accessed=50 * 2**20, transcendentals=n_tp * rows * width
        ),
    )(grad, x, vecs, all_rows, pre, hidden, w_b, *operands)


class Share:
    def __init__(self, group, kv, sems):
        self.g, self.kv, self.sems = group, kv, sems
        self.partner = group.at(group.z, 1 - group.y)

    def piece(self, member, micro, index, to):
        ref = self.kv.at[member, micro]
        return self.g.copy(ref, ref, self.sems, micro * 7 + index, to)

    def own(self, micro):
        g = self.g
        return [self.piece(g.member, micro, 0, self.partner)] + [
            self.piece(g.member, micro, k, g.at(g.ahead(k), g.y)) for k in (1, 2, 3)
        ]

    def relayed(self, micro):
        g = self.g
        return [self.piece(g.at(g.behind(k), g.y), micro, 3 + k, self.partner) for k in (1, 2, 3)]

    def start(self, micro):
        for copy in self.own(micro):
            copy.start()

    def relay(self, micro):
        g = self.g
        for k, copy in zip((1, 2, 3), self.relayed(micro)):
            self.piece(g.at(g.behind(k), g.y), micro, k, self.partner).wait_recv()
            copy.start()

    def wait(self, micro):
        g = self.g
        self.piece(self.partner, micro, 0, self.partner).wait_recv()
        for k in (1, 2, 3):
            self.piece(g.at(g.behind(k), 1 - g.y), micro, 3 + k, self.partner).wait_recv()

    def finish(self, micro):
        for copy in self.own(micro) + self.relayed(micro):
            copy.wait_send()


class GroupSum:
    def __init__(self, group, parts, from_y, to_z, from_z, sems):
        self.g, self.parts, self.sems = group, parts, sems
        self.from_y, self.to_z, self.from_z = from_y, to_z, from_z

    def lanes(self, half):
        return slice(half * WIDE // 2, (half + 1) * WIDE // 2)

    def across(self, micro, half):
        g, lanes = self.g, self.lanes(half)
        return g.copy(
            self.parts.at[micro, :, 1 - g.y, :, :, lanes],
            self.from_y.at[micro, :, :, :, lanes],
            self.sems,
            (2 * micro + half) * 4,
            g.at(g.z, 1 - g.y),
        )

    def along(self, micro, half, k):
        g, lanes = self.g, self.lanes(half)
        to = g.ahead(k)
        return g.copy(
            self.to_z.at[micro, to, :, :, lanes],
            self.from_z.at[micro, k - 1, :, :, lanes],
            self.sems,
            (2 * micro + half) * 4 + k,
            g.at(to, g.y),
        )

    def start(self, micro, half):
        self.across(micro, half).start()

    def turn(self, micro, half):
        lanes = self.lanes(half)
        self.across(micro, half).wait_recv()

        @pl.loop(0, 4)
        def _(z):
            for kv in range(2):
                total = self.parts[micro, z, self.g.y, kv, :, lanes] + self.from_y[micro, z, kv, :, lanes]
                self.to_z[micro, z, kv, :, lanes] = total

        for k in (1, 2, 3):
            self.along(micro, half, k).start()

    def wait(self, micro):
        for half in range(2):
            for k in (1, 2, 3):
                self.along(micro, half, k).wait_recv()

    def total(self, micro, kv):
        g = self.g
        value = self.parts[micro, g.z, g.y, kv].astype(f32) + self.from_y[micro, g.z, kv].astype(f32)
        for k in range(3):
            value = value + self.from_z[micro, k, kv].astype(f32)
        return value.astype(bf16)

    def finish(self, micro):
        for half in range(2):
            self.across(micro, half).wait_send()
            for k in (1, 2, 3):
                self.along(micro, half, k).wait_send()


WIDE = 512
HEAD_PAIRS = WIDE // (2 * HEAD)
PROMPT_CHUNKS = PROMPT // CHUNK
CONT_CHUNKS = CONT_LEN // CHUNK


def chunk_at(c, base=0):
    return pl.ds(pl.multiple_of(base + c * CHUNK, CHUNK), CHUNK)


def key_limit(member):
    row = lax.broadcasted_iota(jnp.int32, (1, TOK_DEV), 1)
    return jnp.where(row < PROMPT_DEV, member * PROMPT_DEV + row, PROMPT - PROMPT_DEV + row)


def half_of(value, half):
    lane = lax.broadcasted_iota(jnp.int32, value.shape, 1)
    return jnp.where((lane >= HEAD * half) & (lane < HEAD * (half + 1)), value, jnp.zeros_like(value))


def fold(value, op):
    return op(value.reshape(value.shape[0] // 8, 8, value.shape[1]), axis=0)


def over_keys(body, prompt, own, carry):
    carry = lax.fori_loop(0, PROMPT_CHUNKS, lambda c, carry: body(c, lambda i: prompt(c, i), carry), carry)
    return lax.fori_loop(
        0, CONT_CHUNKS, lambda c, carry: body(PROMPT_CHUNKS + c, lambda i: own(c, i), carry), carry
    )


def head_pairs(head, finish):
    @pl.loop(0, HEAD_PAIRS)
    def _(pair):
        lanes = pl.ds(pl.multiple_of(pair * 2 * HEAD, 2 * HEAD), 2 * HEAD)
        head(pair, lanes, 0)

        @pl.when(pair < HEAD_PAIRS - 1)
        def _():
            head(pair, lanes, 1)

        finish(pair, lanes)


def to_slots(target, micro, first, value, lanes):
    per = target.shape[1] // MICRO
    row = first
    while row < first + value.shape[0]:
        slot, within = row // per, row % per
        count = min(per - within, first + value.shape[0] - row)
        target[slot, micro * per + within : micro * per + within + count, lanes] = value[
            row - first : row - first + count
        ]
        row += count


def pair_to_blocks(target, x, value):
    per = value.shape[0] // (2 * MICRO)
    for core in range(2):
        for micro in range(MICRO):
            at = pl.ds(pl.multiple_of((2 * x + core) * per, per), per)
            first = (core * MICRO + micro) * per
            target[micro, at, :] = value[first : first + per]


def attn_fwd_kernel(n, *refs):
    x_ref, vec_ref, bias_ref, wqkv_hbm = refs[:4]
    shard, refs = refs[4 : 4 + n], refs[4 + n :]
    out_ref, lse_ref, all_hbm, own_hbm, kv_hbm, mix_hbm, wout_hbm = refs[:7]
    whole, refs = refs[7 : 7 + n], refs[7 + n :]
    wqkv, wout, wparts, buf, own, kv, mix, s_ref, p_ref, o_ref = refs[:10]
    part, from_core, over_out, from_over, send, recv, gsend, grecv, wsend, wrecv, local = refs[10:21]
    p, g = Peers(), Group()
    spread = Spread(g, shard[0], whole[0], refs[21:], ATTN_CHUNKS) if n else None
    rows = x_ref.shape[0]
    n_tp = buf.shape[0]
    step = HEADS // n_tp * HEAD
    width = wparts.shape[1]
    sems = (send, recv)
    gather = Gather(p, buf, sems)
    scatter = Scatter(p, part, from_core, over_out, from_over, sems)
    share = Share(g, kv, (gsend, grecv))
    load_qkv = pltpu.make_async_copy(wqkv_hbm.at[:, : 3 * WIDE], wqkv, local.at[0])
    load_qkv.start()

    def rows_for(t):
        return wqkv_hbm.at[pl.ds(pl.multiple_of(t * step, 128), width), 3 * WIDE : 4 * WIDE]

    keep_part = pltpu.make_async_copy(rows_for(p.t), wparts.at[p.t], local.at[1])
    keep_part.start()
    give_parts = [
        p.copy(rows_for(t), wparts.at[p.t], (wsend, wrecv), i, t) for i, t in enumerate((p.core, p.over, p.diag))
    ]

    def norm(at):
        hat, _ = norm_stats(x_ref[at, :])
        buf[p.t, at, :] = (hat * vec_ref[0:1, :] + vec_ref[1:2, :]).astype(bf16)

    row_chunks(rows, norm)
    g.greet(p, True)
    gather.start()
    for copy in give_parts:
        copy.start()
    if n:
        spread.start(0, 1)
    gather.wait_chip()
    load_qkv.wait()

    def project(x):
        for i in range(3):
            value = mm(pair_rows(buf, x), wqkv[:, i * WIDE : (i + 1) * WIDE]) + bias_ref[i : i + 1, :]
            low = value.astype(bf16)
            if i == 0:
                low = low * HEAD ** (-0.5)
            pair_to_blocks(own.at[i], x, low)

    project(p.x)
    gather.relay()
    gather.wait_diag()
    project(1 - p.x)
    for micro in range(MICRO):
        for i in range(2):
            kv[g.member, micro, i] = own[1 + i, micro, :PROMPT_DEV, :]
        share.start(micro)
    if n:
        spread.start(1)
        spread.relay(0)
    keep_all = pltpu.make_async_copy(buf, all_hbm, local.at[2])
    keep_own = pltpu.make_async_copy(own, own_hbm, local.at[3])
    keep_all.start()
    keep_own.start()
    limit = key_limit(g.member)
    sub = lax.broadcasted_iota(jnp.int32, (CHUNK, TOK_DEV), 0)

    for micro in range(MICRO):
        if micro == 0:
            share.relay(0)
        share.wait(micro)

        def head(pair, lanes, half, micro=micro):
            if half == 0:

                @pl.when(pair == 1)
                def _():
                    if micro == 0:
                        share.relay(1)
                    elif n:
                        spread.relay(2)

                @pl.when(pair == HEAD_PAIRS - 1)
                def _():
                    if n:
                        spread.relay(1 + 2 * micro)

            qh = half_of(own[0, micro, :, lanes], half)

            def first(c, load, top):
                s = jnp.where(sub + c * CHUNK <= limit, mm(load(0), qh, NT), -1e30)
                s_ref[chunk_at(c), :] = s
                return jnp.maximum(top, fold(s, jnp.max))

            top = over_keys(
                first,
                lambda c, i: kv[c, micro, i, :, lanes],
                lambda c, i: own[1 + i, micro, chunk_at(c, PROMPT_DEV), lanes],
                jnp.full((8, TOK_DEV), -1e30, f32),
            )
            top = jnp.max(top, axis=0, keepdims=True)

            def second(c, total):
                e = jnp.exp(s_ref[chunk_at(c), :] - top)
                p_ref[chunk_at(c), :] = e.astype(bf16)
                return total + fold(e, jnp.sum)

            total = lax.fori_loop(0, KEYS // CHUNK, second, jnp.zeros((8, TOK_DEV), f32))
            total = jnp.sum(total, axis=0, keepdims=True)
            values = kv[:, micro, 1, :, lanes].reshape(PROMPT, 2 * HEAD)
            out = mm(values, p_ref[:PROMPT, :], TN) + mm(own[2, micro, PROMPT_DEV:, lanes], p_ref[PROMPT:, :], TN)
            at = slice(HEAD * half, HEAD * (half + 1))
            o_ref[at, :] = out[at, :] / total
            lse_ref[micro, pair, half : half + 1, :] = top + jnp.log(total)

        def finish(pair, lanes, micro=micro):
            @pl.when(pair == HEAD_PAIRS - 1)
            def _():
                o_ref[HEAD:, :] = jnp.zeros((HEAD, TOK_DEV), f32)

            to_slots(mix, micro, 0, o_ref[...].T.astype(bf16), lanes)

        head_pairs(head, finish)

    keep_kv = pltpu.make_async_copy(kv, kv_hbm, local.at[4])
    keep_mix = pltpu.make_async_copy(mix, mix_hbm, local.at[5])
    keep_kv.start()
    keep_mix.start()
    keep_part.wait()
    for i, t in enumerate((p.core, p.over, p.diag)):
        p.copy(rows_for(t), wparts.at[t], (wsend, wrecv), i, t).wait_recv()
    for t in range(n_tp):
        count = min(WIDE, D - t * step)
        wout[:width, t * step : t * step + count] = wparts[t, :, :count]
    wout[width:, :] = jnp.zeros((WIDE - width, D), bf16)

    @pl.when(p.t < n_tp - 1)
    def _():
        wout[step:width, :] = jnp.zeros((width - step, D), bf16)

    keep_out = pltpu.make_async_copy(wout, wout_hbm, local.at[6])
    keep_out.start()

    def down(x):
        def tile(at):
            put_pair(part, x, at, mm(pair_rows(mix, x), wout[:, at]))

        tiles(D, tile)

    down(1 - p.x)
    scatter.far_to_core().start()
    scatter.send_over()
    down(p.x)
    scatter.near_to_core().start()
    if n:
        spread.relay(4)
    scatter.wait()

    def final(at):
        out_ref[at, :] = x_ref[at, :] + (scatter.rows(at) + vec_ref[4:5, :])

    row_chunks(rows, final)
    gather.finish()
    scatter.finish()
    for micro in range(MICRO):
        share.finish(micro)
    for copy in give_parts:
        copy.wait_send()
    for copy in (keep_all, keep_own, keep_kv, keep_mix, keep_out):
        copy.wait()
    if n:
        spread.finish()


def attn_shapes(n_tp, rows):
    return (
        ((n_tp, rows, D), bf16),
        ((3, MICRO, TOK_DEV, WIDE), bf16),
        ((GROUP, MICRO, 2, PROMPT_DEV, WIDE), bf16),
        ((n_tp, rows, WIDE), bf16),
    )


def attn_fwd(x, vecs, biases, w_a, n_tp, shard, collective_id):
    rows = x.shape[0]
    width = D - HEADS // n_tp * HEAD * (n_tp - 1)
    saved = attn_shapes(n_tp, rows)
    operands, results, sems = spread_parts(shard, ATTN_CHUNKS)
    return pl.pallas_call(
        functools.partial(attn_fwd_kernel, len(operands)),
        out_shape=(
            jax.ShapeDtypeStruct((rows, D), f32),
            jax.ShapeDtypeStruct((MICRO, HEAD_PAIRS, 8, TOK_DEV), f32),
        )
        + tuple(jax.ShapeDtypeStruct(*s) for s in saved + (((WIDE, D), bf16),))
        + results,
        in_specs=[IN_VMEM, IN_VMEM, IN_VMEM, ANY] + [ANY] * len(operands),
        out_specs=(IN_VMEM, IN_VMEM) + (ANY,) * (5 + len(operands)),
        scratch_shapes=[pltpu.VMEM((D, 3 * WIDE), bf16), pltpu.VMEM((WIDE, D), bf16), pltpu.VMEM((n_tp, width, WIDE), bf16)]
        + [pltpu.VMEM(*s) for s in saved]
        + [
            pltpu.VMEM((KEYS, TOK_DEV), f32),
            pltpu.VMEM((KEYS, TOK_DEV), bf16),
            pltpu.VMEM((2 * HEAD, TOK_DEV), f32),
        ]
        + scatter_scratch(n_tp, rows)
        + [
            pltpu.SemaphoreType.DMA((7 * MICRO,)),
            pltpu.SemaphoreType.DMA((7 * MICRO,)),
            pltpu.SemaphoreType.DMA((3,)),
            pltpu.SemaphoreType.DMA((3,)),
            pltpu.SemaphoreType.DMA((7,)),
        ]
        + sems,
        compiler_params=params(collective_id),
        cost_estimate=pl.CostEstimate(flops=10**11, bytes_accessed=30 * 2**20, transcendentals=0),
    )(x, vecs, biases, w_a, *operands)


def attn_bwd_kernel(n, *refs):
    g_ref, x_ref, vec_ref, lse_ref, all_hbm, own_hbm, kv_hbm, mix_hbm, wqkv_hbm, wout_hbm = refs[:10]
    sources, refs = refs[10 : 10 + n], refs[10 + n :]
    out_ref, sums_ref, cols_ref, dqo_hbm = refs[:4]
    results, refs = refs[4 : 4 + 2 * n], refs[4 + 2 * n :]
    wqkv, wout, buf, other, own, kv, gm, dkv, from_y, to_z, from_z, dkc, dqkv, stage, stage_out = refs[:15]
    p_ref, dp_ref, ds_ref, o_ref = refs[15:19]
    part, from_core, over_out, from_over, send, recv, gsend, grecv, local = refs[19:28]
    p, g = Peers(), Group()
    sums = reduces(g, sources, results, refs[28:])
    rows = x_ref.shape[0]
    n_tp = buf.shape[0]
    out_step = HEADS // n_tp * HEAD
    out_width = D - out_step * (n_tp - 1)
    sems = (send, recv)
    gather = Gather(p, buf, sems)
    scatter = Scatter(p, part, from_core, over_out, from_over, sems)
    reduce = GroupSum(g, dkv, from_y, to_z, from_z, (gsend, grecv))
    load_out = pltpu.make_async_copy(wout_hbm, wout, local.at[0])
    load_own = pltpu.make_async_copy(own_hbm, own, local.at[1])
    load_kv = pltpu.make_async_copy(kv_hbm, kv, local.at[2])
    load_qkv = pltpu.make_async_copy(wqkv_hbm.at[:, : 3 * WIDE], wqkv, local.at[3])
    load_mix = pltpu.make_async_copy(mix_hbm, other, local.at[4])
    for copy in (load_out, load_own, load_kv, load_qkv, load_mix):
        copy.start()
    sums_ref[...] = jnp.zeros_like(sums_ref)

    def lower(at):
        low = g_ref[at, :].astype(bf16)
        buf[p.t, at, :] = low
        add_rows(sums_ref, 4, low.astype(f32))

    row_chunks(rows, lower)
    g.greet(p)
    gather.start()
    hooks = {(1, 0): [lambda: reduce.turn(0, 0)], (1, 1): [lambda: reduce.turn(0, 1)]}
    if n:
        first_sum, second_sum = sums
        first_sum.start()
        hooks[0, 1] = [lambda: first_sum.pump(2)]
        hooks[0, 2] = [lambda: first_sum.pump(3), second_sum.start]
        for k in range(3):
            hooks.setdefault((1, k), []).append(lambda k=k: second_sum.pump(k + 1, first_sum))
    gather.wait_chip()
    load_out.wait()

    def mixed_back(x):
        pair_to_blocks(gm, x, mm(pair_rows(buf, x), wout[...], NT).astype(bf16))

    mixed_back(p.x)
    gather.relay()
    gather.wait_diag()
    mixed_back(1 - p.x)
    load_own.wait()
    load_kv.wait()
    limit = key_limit(g.member)
    sub = lax.broadcasted_iota(jnp.int32, (CHUNK, TOK_DEV), 0)

    if n:
        first_sum.pump(1)

    for micro in range(MICRO):

        def head(pair, lanes, half, micro=micro):
            for at in range(HEAD_PAIRS):
                if half == 0 and (micro, at) in hooks:

                    @pl.when(pair == at)
                    def _(at=at):
                        for hook in hooks[micro, at]:
                            hook()

            qh = half_of(own[0, micro, :, lanes], half)
            gh = half_of(gm[micro, :, lanes], half)
            lse = lse_ref[micro, pair, half : half + 1, :]

            def first(c, load, inner):
                s = jnp.where(sub + c * CHUNK <= limit, mm(load(0), qh, NT), -1e30)
                e = jnp.exp(s - lse)
                dp = mm(load(1), gh, NT)
                p_ref[chunk_at(c), :] = e
                dp_ref[chunk_at(c), :] = dp
                return inner + fold(e * dp, jnp.sum)

            inner = over_keys(
                first,
                lambda c, i: kv[c, micro, i, :, lanes],
                lambda c, i: own[1 + i, micro, chunk_at(c, PROMPT_DEV), lanes],
                jnp.zeros((8, TOK_DEV), f32),
            )
            inner = jnp.sum(inner, axis=0, keepdims=True)

            def second(c, put):
                e = p_ref[chunk_at(c), :]
                ds = (e * (dp_ref[chunk_at(c), :] - inner)).astype(bf16)
                ds_ref[chunk_at(c), :] = ds
                put(0, mm(ds, qh))
                put(1, mm(e.astype(bf16), gh))

            @pl.loop(0, PROMPT_CHUNKS)
            def _(c):
                def put(i, value):
                    at = (micro, c // 2, c % 2, i, slice(None), lanes)
                    if half:
                        value = value + dkv[at].astype(f32)
                    dkv[at] = value.astype(bf16)

                second(c, put)

            @pl.loop(0, CONT_CHUNKS)
            def _(c):
                def put(i, value):
                    at = (i, chunk_at(c), lanes)
                    if half:
                        value = value + dkc[at].astype(f32)
                    dkc[at] = value.astype(bf16)

                second(PROMPT_CHUNKS + c, put)

            keys = kv[:, micro, 0, :, lanes].reshape(PROMPT, 2 * HEAD)
            dq = mm(keys, ds_ref[:PROMPT, :], TN) + mm(own[1, micro, PROMPT_DEV:, lanes], ds_ref[PROMPT:, :], TN)
            at = slice(HEAD * half, HEAD * (half + 1))
            o_ref[at, :] = dq[at, :] * HEAD ** (-0.5)

        def finish(pair, lanes, micro=micro):
            @pl.when(pair == HEAD_PAIRS - 1)
            def _():
                o_ref[HEAD:, :] = jnp.zeros((HEAD, TOK_DEV), f32)

            to_slots(dqkv, micro, 0, o_ref[...].T.astype(bf16), lanes)

            @pl.when(pair == HEAD_PAIRS // 2 - 1)
            def _():
                reduce.start(micro, 0)

        head_pairs(head, finish)
        reduce.start(micro, 1)
        for i in range(2):
            to_slots(dqkv, micro, PROMPT_DEV, dkc[i], slice((1 + i) * WIDE, (2 + i) * WIDE))

    load_mix.wait()
    columns = pl.ds(pl.multiple_of(p.t * out_step, 128), out_width)

    def outer(source, target, right, body):
        flat = right.reshape(n_tp * rows, right.shape[-1])

        def tile(at):
            left = source[:, :, at].reshape(n_tp * rows, -1)
            target[at, : flat.shape[1]] = mm(left, flat, TN).astype(bf16)

        body(D, tile)

    reduce.turn(1, 0)
    stage_out[:, out_width:] = jnp.zeros((D, WIDE - out_width), bf16)
    outer(other, stage_out, buf[:, :, columns], tiles)
    keep_out = pltpu.make_async_copy(stage_out, dqo_hbm.at[:, 3 * WIDE :], local.at[5])
    keep_out.start()
    load_all = pltpu.make_async_copy(all_hbm, other, local.at[6])
    load_all.start()
    reduce.turn(1, 1)
    for micro in range(MICRO):
        reduce.wait(micro)
        for i in range(2):
            to_slots(dqkv, micro, 0, reduce.total(micro, i), slice((1 + i) * WIDE, (2 + i) * WIDE))
    load_qkv.wait()

    def down(x):
        def tile(at):
            put_pair(part, x, at, mm(pair_rows(dqkv, x), wqkv[at, :], NT))

        tiles(D, tile)

    down(1 - p.x)
    scatter.far_to_core().start()
    scatter.send_over()
    down(p.x)
    scatter.near_to_core().start()
    load_all.wait()
    outer(other, stage, dqkv[...], tiles)
    keep_qkv = pltpu.make_async_copy(stage, dqo_hbm.at[:, : 3 * WIDE], local.at[7])
    keep_qkv.start()
    cols_ref[...] = jnp.zeros_like(cols_ref)

    @pl.loop(0, n_tp * rows // ROW_CHUNK)
    def _(i):
        per = rows // ROW_CHUNK
        at = pl.ds(pl.multiple_of((i % per) * ROW_CHUNK, ROW_CHUNK), ROW_CHUNK)
        add_rows(cols_ref, 0, dqkv[i // per, at, :].astype(f32))

    scatter.wait()

    def final(at):
        dy = scatter.rows(at)
        dx, d_gain = norm_back(x_ref[at, :], dy, vec_ref[0:1, :])
        add_rows(sums_ref, 0, d_gain)
        add_rows(sums_ref, 1, dy)
        out_ref[at, :] = g_ref[at, :] + dx

    row_chunks(rows, final)
    gather.finish()
    scatter.finish()
    for micro in range(MICRO):
        reduce.finish(micro)
    keep_out.wait()
    keep_qkv.wait()
    for i, item in enumerate(sums):
        item.finish(i < n - 1)


def attn_bwd(grad, x, vecs, lse, all_rows, own, kv, mixed_all, w_a, w_out, n_tp, payload, collective_id):
    rows = x.shape[0]
    operands, results, more = reduce_parts(payload)
    pieces = (MICRO, 4, 2, 2, PROMPT_DEV, WIDE)
    return pl.pallas_call(
        functools.partial(attn_bwd_kernel, len(payload)),
        out_shape=(
            jax.ShapeDtypeStruct((rows, D), f32),
            jax.ShapeDtypeStruct((8, D), f32),
            jax.ShapeDtypeStruct((1, 3 * WIDE), f32),
            jax.ShapeDtypeStruct((D, 4 * WIDE), bf16),
        )
        + results,
        in_specs=[IN_VMEM] * 4 + [ANY] * (6 + len(payload)),
        out_specs=(IN_VMEM, IN_VMEM, IN_VMEM) + (ANY,) * (1 + 2 * len(payload)),
        scratch_shapes=[
            pltpu.VMEM((D, 3 * WIDE), bf16),
            pltpu.VMEM((WIDE, D), bf16),
            pltpu.VMEM((n_tp, rows, D), bf16),
            pltpu.VMEM((n_tp, rows, D), bf16),
            pltpu.VMEM((3, MICRO, TOK_DEV, WIDE), bf16),
            pltpu.VMEM((GROUP, MICRO, 2, PROMPT_DEV, WIDE), bf16),
            pltpu.VMEM((MICRO, TOK_DEV, WIDE), bf16),
            pltpu.VMEM(pieces, bf16),
            pltpu.VMEM((MICRO, 4, 2, PROMPT_DEV, WIDE), bf16),
            pltpu.VMEM((MICRO, 4, 2, PROMPT_DEV, WIDE), bf16),
            pltpu.VMEM((MICRO, 3, 2, PROMPT_DEV, WIDE), bf16),
            pltpu.VMEM((2, CONT_LEN, WIDE), bf16),
            pltpu.VMEM((n_tp, rows, 3 * WIDE), bf16),
            pltpu.VMEM((D, 3 * WIDE), bf16),
            pltpu.VMEM((D, WIDE), bf16),
            pltpu.VMEM((KEYS, TOK_DEV), f32),
            pltpu.VMEM((KEYS, TOK_DEV), f32),
            pltpu.VMEM((KEYS, TOK_DEV), bf16),
            pltpu.VMEM((2 * HEAD, TOK_DEV), f32),
        ]
        + scatter_scratch(n_tp, rows)
        + [
            pltpu.SemaphoreType.DMA((8 * MICRO,)),
            pltpu.SemaphoreType.DMA((8 * MICRO,)),
            pltpu.SemaphoreType.DMA((8,)),
        ]
        + more,
        compiler_params=params(collective_id),
        cost_estimate=pl.CostEstimate(flops=2 * 10**11, bytes_accessed=50 * 2**20, transcendentals=0),
    )(grad, x, vecs, lse, all_rows, own, kv, mixed_all, w_a, w_out, *operands)


def forward_layer(x, layer, fetch, vecs, fc_bias, cols, n_tp):
    width = D - HEADS // n_tp * HEAD * (n_tp - 1)
    query_bias, value_bias = (lax.dynamic_slice_in_dim(vecs[i], cols, width) for i in (2, 3))
    biases = widen(jnp.stack([query_bias, jnp.zeros_like(query_bias), value_bias]))
    w_a = fetch.weights[layer, "a"]
    x_mid, lse, all_rows, own, kv, mixed, w_out = fetch.during(
        (layer, "b"), lambda shard: attn_fwd(x, vecs, biases, w_a, n_tp, shard, 5 + layer)
    )
    w_b = fetch.weights[layer, "b"]
    x_next, second_all, hidden_pre, hidden = fetch.during(
        (layer + 1, "a"), lambda shard: ff_fwd(x_mid, vecs, fc_bias[None], w_b, n_tp, shard, 1 + layer)
    )
    mixed_all = heads_joined(lax.all_gather(mixed[:, :, :width], "tp"), n_tp)
    return x_next, (x, w_out, lse, all_rows, own, kv, mixed_all, x_mid, second_all, hidden_pre, hidden)


class Fetch:
    def __init__(self, shards):
        self.staged = lax.axis_size("fsdp") == GROUP
        self.shards, self.weights = shards, {}
        last = None
        for key, shard in shards.items():
            if self.staged:
                if last is None:
                    last = spread_only(shard, 8, 9)
                    self.weights[key] = last.reshape(-1, shard.shape[1])
                continue
            if last is not None:
                shard, _ = lax.optimization_barrier((shard, last))
            whole = lax.all_gather(shard, "fsdp", axis=0, tiled=True)
            self.weights[key] = whole
            last = whole[:8, :128]

    def during(self, key, kernel):
        if not self.staged or key not in self.shards:
            return kernel(None)
        *results, whole = kernel(self.shards[key])
        self.weights[key] = whole.reshape(-1, whole.shape[2])
        return results


def fsdp_sum(part):
    return lax.psum_scatter(part, "fsdp", scatter_dimension=0, tiled=True).astype(f32)


def heads_joined(parts, n_tp):
    step = HEADS // n_tp * HEAD
    return jnp.concatenate([parts[t][..., :step] for t in range(n_tp - 1)] + [parts[n_tp - 1]], axis=-1)


def widen(value, axis=-1):
    pads = [(0, 0)] * value.ndim
    pads[axis] = (0, WIDE - value.shape[axis])
    return jnp.pad(value, pads)


def by_owner(part):
    return part.reshape(4, 2, -1, part.shape[1])


def owned(part, from_y, from_z):
    z, y = lax.axis_index("fsdp") // 2, lax.axis_index("fsdp") % 2
    own = lax.dynamic_index_in_dim(lax.dynamic_index_in_dim(part, z, 0, False), y, 0, False)
    near = lax.dynamic_index_in_dim(from_y, z, 0, False)
    return own.astype(f32) + near.astype(f32) + jnp.sum(from_z.astype(f32), 0)


def with_vectors(grad_qo, ff_sums, attn_sums, col_sums, fc_bias_sums, cols, width):
    def placed(part):
        return lax.dynamic_update_slice_in_dim(jnp.zeros((1, D), f32), part, cols, 1)

    vector_grads = jnp.concatenate(
        [
            attn_sums[:2],
            placed(col_sums[:, :width]),
            placed(col_sums[:, 2 * WIDE : 2 * WIDE + width]),
            attn_sums[4:5],
            ff_sums[5:],
            fc_bias_sums,
        ]
    )
    return lax.dynamic_update_slice(grad_qo, vector_grads.astype(bf16).T, (0, 3 * WIDE + width))


def backward(grad, weights, vecs, saves, cols, n_tp):
    width = D - HEADS // n_tp * HEAD * (n_tp - 1)
    staged = lax.axis_size("fsdp") == GROUP
    done, joined, waiting = {}, {}, {}

    def during(keys, kernel):
        payload = [waiting.pop(key) for key in keys if key in waiting]
        results = list(kernel(payload))
        if payload:
            arrived = results[-2 * len(payload) :]
            results = results[: -2 * len(payload)]
            for i, key in enumerate(keys):
                done[key] = owned(payload[i], arrived[2 * i], arrived[2 * i + 1])
        return results

    def produced(key, value):
        if staged:
            waiting[key] = by_owner(value)
        else:
            done[key] = fsdp_sum(value)

    for layer in reversed(range(LAYERS)):
        w_a, w_b = weights[layer, "a"], weights[layer, "b"]
        x, w_out, lse, all_rows, own, kv, mixed_all, x_mid, second_all, hidden_pre, hidden = saves[layer]
        grad, ff_sums, fc_bias_sums, grad_fc, grad_proj = during(
            [(layer + 1, "qo")],
            lambda payload: ff_bwd(
                grad, x_mid, vecs[layer], second_all, hidden_pre, hidden, w_b, n_tp, payload, 10 + layer
            ),
        )
        produced((layer, "proj"), grad_proj)
        produced((layer, "fc"), grad_fc)
        grad, attn_sums, col_sums, grad_qo = during(
            [(layer, "proj"), (layer, "fc")],
            lambda payload: attn_bwd(
                grad, x, vecs[layer], lse, all_rows, own, kv, mixed_all, w_a, w_out, n_tp, payload, 20 + layer
            ),
        )
        produced((layer, "qo"), with_vectors(grad_qo, ff_sums, attn_sums, col_sums, fc_bias_sums, cols, width))
    during([(0, "qo")] if staged else [], lambda payload: reduce_only(payload[0], 30) if payload else ())
    sums = []
    both = block_gather([done[layer, "qo"].astype(bf16) for layer in range(LAYERS)], n_tp, 31)
    for layer, got in enumerate(both):
        qkv_grad = jnp.concatenate(
            [heads_joined(got[:, :, i * WIDE : i * WIDE + width], n_tp) for i in range(3)], axis=1
        ).astype(f32)
        out_grad = heads_joined(got[:, :, 3 * WIDE : 3 * WIDE + width], n_tp).astype(f32)
        vector_sum = jnp.sum(got[:, :, 3 * WIDE + width : 3 * WIDE + width + 8].astype(f32), 0).T
        fc_bias_sum = done[layer, "qo"][:, 3 * WIDE + width + 8]
        sums.append((qkv_grad, out_grad, done[layer, "fc"], done[layer, "proj"].T, fc_bias_sum, vector_sum))
    return grad, sums


def local(
    tokens,
    qkv_weight,
    query_bias,
    value_bias,
    out_weight,
    out_bias,
    fc_weight,
    fc_bias,
    proj_weight,
    proj_bias,
    first_gain,
    first_bias,
    second_gain,
    second_bias,
    out_grad,
):
    n_tp = lax.axis_size("tp")
    tp = lax.axis_index("tp")
    row_count = tokens.shape[1]
    step = HEADS // n_tp * HEAD
    width = D - step * (n_tp - 1)
    cols = tp * step

    vectors = jnp.stack(
        [first_gain, first_bias, query_bias, value_bias, out_bias, second_gain, second_bias, proj_bias, fc_bias[:, 0]]
    ).reshape(9 * LAYERS, -1)

    shards = {}
    for layer in range(LAYERS):
        sides = [widen(lax.dynamic_slice_in_dim(qkv_weight[layer], cols + i * D, width, 1)) for i in range(3)]
        sides.append(widen(lax.dynamic_slice_in_dim(out_weight[layer], cols, width, 1)))
        if layer == 0:
            sides.append(jnp.pad(vectors.T, ((0, 0), (0, 128 - 9 * LAYERS))))
        shards[layer, "a"] = jnp.concatenate(sides, axis=1)
        fc, proj = fc_weight[layer], proj_weight[layer].T
        more = ((0, 0), (0, lanes_up(fc.shape[1]) - fc.shape[1]))
        shards[layer, "b"] = jnp.concatenate([jnp.pad(fc, more), jnp.pad(proj, more)], axis=1)
    fetch = Fetch(shards)
    vectors = fetch.weights[0, "a"][:, 4 * WIDE : 4 * WIDE + 9 * LAYERS].T.astype(f32).reshape(9, LAYERS, D)

    state = tokens.astype(f32).reshape(MICRO * row_count, D)
    saves = []
    for layer in range(LAYERS):
        state, saved = forward_layer(state, layer, fetch, vectors[:8, layer], vectors[8, layer], cols, n_tp)
        saves.append(saved)
    out_tokens = state.astype(bf16).reshape(tokens.shape)
    grad = out_grad.astype(f32).reshape(MICRO * row_count, D)
    grad, sums = backward(
        grad, fetch.weights, [vectors[:8, layer] for layer in range(LAYERS)], saves, cols, n_tp
    )
    qkv_g, out_g, fc_g, proj_g, fc_bias_g, vec_g = (
        jnp.stack([sums[layer][i] for layer in range(LAYERS)]) for i in range(6)
    )
    return (
        out_tokens,
        grad.reshape(tokens.shape),
        qkv_g,
        vec_g[:, 2],
        vec_g[:, 3],
        out_g,
        vec_g[:, 4],
        fc_g,
        fc_bias_g[:, None],
        proj_g,
        vec_g[:, 7],
        vec_g[:, 0],
        vec_g[:, 1],
        vec_g[:, 5],
        vec_g[:, 6],
    )


def solution(mesh):
    rows = P(None, ("fsdp", "tp"), None)
    weight = P(None, "fsdp", None)
    vector = P(None, "fsdp")
    fc_in = P(None, "fsdp", "tp")
    hidden = P(None, "tp", "fsdp")
    in_specs = (
        rows, weight, vector, vector, weight, vector, fc_in, hidden, hidden,
        vector, vector, vector, vector, vector, rows,
    )
    out_specs = (
        rows, rows, weight, vector, vector, weight, vector, fc_in, hidden, hidden,
        vector, vector, vector, vector, vector,
    )
    return jax.shard_map(local, mesh=mesh, in_specs=in_specs, out_specs=out_specs, check_vma=False)
```

```python
import functools

import jax
import jax.numpy as jnp
from jax import lax
from jax.experimental import pallas as pl
from jax.experimental.pallas import tpu as pltpu
from jax.sharding import PartitionSpec as P

D = 1600
HEADS = 25
HEAD = 64
GROUP = 8
PROMPT_DEV = 128
CONT_LEN = 256
TOK_DEV = 384
MICRO = 2
LAYERS = 2
PROMPT = 1024
KEYS = PROMPT + CONT_LEN
CHUNK = 128

f32 = jnp.float32
bf16 = jnp.bfloat16
norm_eps = 1e-05
NN = (((1,), (0,)), ((), ()))
NT = (((1,), (1,)), ((), ()))
TN = (((0,), (0,)), ((), ()))


def mm(left, right, dims=NN):
    return lax.dot_general(left, right, dims, preferred_element_type=f32)


def gelu_tanh(value):
    return jax.nn.gelu(value, approximate=True)


MESH = pl.DeviceIdType.MESH
ANY = pl.BlockSpec(memory_space=pl.ANY)
IN_VMEM = pl.BlockSpec(memory_space=pltpu.VMEM)
TILE = 512
ROW_CHUNK = 32


class Peers:
    def __init__(self):
        self.f = lax.axis_index("fsdp")
        self.t = lax.axis_index("tp")
        x, c = self.t // 2, self.t % 2
        self.x = x
        self.core = 2 * x + 1 - c
        self.over = 2 * (1 - x) + c
        self.diag = 2 * (1 - x) + 1 - c

    def greet(self):
        barrier = pltpu.get_barrier_semaphore()
        for t in (self.core, self.over):
            pl.semaphore_signal(barrier, inc=1, device_id=(self.f, t), device_id_type=MESH)
        pl.semaphore_wait(barrier, 2)

    def copy(self, source, target, sems, index, t):
        return pltpu.make_async_remote_copy(
            src_ref=source,
            dst_ref=target,
            send_sem=sems[0].at[index],
            recv_sem=sems[1].at[index],
            device_id=(self.f, t),
            device_id_type=MESH,
        )


class Gather:
    def __init__(self, peers, buf, sems):
        self.p, self.buf, self.sems = peers, buf, sems

    def piece(self, slot, index, t):
        return self.p.copy(self.buf.at[slot], self.buf.at[slot], self.sems, index, t)

    def start(self):
        p = self.p
        self.piece(p.t, 1, p.over).start()
        self.piece(p.t, 0, p.core).start()

    def wait_chip(self):
        self.piece(self.p.core, 0, self.p.core).wait_recv()

    def relay(self):
        p = self.p
        self.piece(p.over, 1, p.over).wait_recv()
        self.piece(p.over, 2, p.core).start()

    def wait_diag(self):
        self.piece(self.p.diag, 2, self.p.core).wait_recv()

    def finish(self):
        p = self.p
        self.piece(p.t, 1, p.over).wait_send()
        self.piece(p.t, 0, p.core).wait_send()
        self.piece(p.over, 2, p.core).wait_send()


class Scatter:
    def __init__(self, peers, part, from_core, over_out, from_over, sems):
        self.p, self.part, self.sems = peers, part, sems
        self.from_core, self.over_out, self.from_over = from_core, over_out, from_over

    def far_to_core(self):
        return self.p.copy(self.part.at[self.p.diag], self.from_core.at[0], self.sems, 3, self.p.core)

    def near_to_core(self):
        return self.p.copy(self.part.at[self.p.core], self.from_core.at[1], self.sems, 4, self.p.core)

    def to_over(self):
        return self.p.copy(self.over_out, self.from_over, self.sems, 5, self.p.over)

    def send_over(self):
        self.far_to_core().wait_recv()

        @pl.loop(0, self.over_out.shape[0] // ROW_CHUNK)
        def _(i):
            at = pl.ds(pl.multiple_of(i * ROW_CHUNK, ROW_CHUNK), ROW_CHUNK)
            total = self.part[self.p.over, at, :].astype(f32) + self.from_core[0, at, :].astype(f32)
            self.over_out[at, :] = total.astype(bf16)

        self.to_over().start()

    def wait(self):
        self.near_to_core().wait_recv()
        self.to_over().wait_recv()

    def rows(self, at):
        return (
            self.part[self.p.t, at, :].astype(f32)
            + self.from_core[1, at, :].astype(f32)
            + self.from_over[at, :].astype(f32)
        )

    def finish(self):
        for copy in (self.far_to_core(), self.near_to_core(), self.to_over()):
            copy.wait_send()


class Group:
    def __init__(self):
        f = lax.axis_index("fsdp")
        self.t = lax.axis_index("tp")
        self.member = f % GROUP
        self.base = f - self.member
        self.z, self.y = self.member // 2, self.member % 2

    def at(self, z, y):
        return z * 2 + y

    def ahead(self, k):
        return (self.z + k) % 4

    def behind(self, k):
        return (self.z + 4 - k) % 4

    def greet_group(self):
        barrier = pltpu.get_barrier_semaphore()
        others = [self.at(self.z, 1 - self.y)] + [self.at(self.ahead(k), self.y) for k in (1, 2, 3)]
        for member in others:
            pl.semaphore_signal(
                barrier, inc=1, device_id=(self.base + member, self.t), device_id_type=MESH
            )
        pl.semaphore_wait(barrier, 4)

    def greet(self, peers, with_diag=False):
        barrier = pltpu.get_barrier_semaphore()
        others = [self.at(self.z, 1 - self.y)] + [self.at(self.ahead(k), self.y) for k in (1, 2, 3)]
        for member in others:
            pl.semaphore_signal(
                barrier, inc=1, device_id=(self.base + member, self.t), device_id_type=MESH
            )
        near = [peers.core, peers.over] + [peers.diag] * with_diag
        for t in near:
            pl.semaphore_signal(barrier, inc=1, device_id=(peers.f, t), device_id_type=MESH)
        pl.semaphore_wait(barrier, 4 + len(near))

    def copy(self, source, target, sems, index, member):
        return pltpu.make_async_remote_copy(
            src_ref=source,
            dst_ref=target,
            send_sem=sems[0].at[index],
            recv_sem=sems[1].at[index],
            device_id=(self.base + member, self.t),
            device_id_type=MESH,
        )


class Reduce:
    def __init__(self, group, source, from_y, from_z, sems, tiles):
        self.g, self.source, self.from_y, self.from_z, self.sems = group, source, from_y, from_z, sems
        self.own, self.got, self.gone, self.local = tiles

    def across(self, j):
        g = self.g
        z = g.ahead(j)
        return g.copy(
            self.source.at[z, 1 - g.y], self.from_y.at[z], self.sems, j, g.at(g.z, 1 - g.y)
        )

    def along(self, j):
        g = self.g
        return g.copy(self.gone.at[j - 1], self.from_z.at[j - 1], self.sems, 3 + j, g.at(g.ahead(j), g.y))

    def start(self, *pieces):
        for j in pieces:
            self.across(j).start()

    def pump(self, j, before=None):
        g = self.g
        load_own = pltpu.make_async_copy(self.source.at[g.ahead(j), g.y], self.own, self.local.at[0])
        load_own.start()
        self.across(j).wait_recv()
        load_got = pltpu.make_async_copy(self.from_y.at[g.ahead(j)], self.got, self.local.at[1])
        load_got.start()
        load_own.wait()
        load_got.wait()
        if before is not None:
            before.along(j).wait_send()
        self.gone[j - 1] = self.own[...] + self.got[...]
        self.along(j).start()

    def finish(self, reused=False):
        self.across(0).wait_recv()
        for j in range(4):
            self.across(j).wait_send()
        for j in (1, 2, 3):
            self.along(j).wait_recv()
            if not reused:
                self.along(j).wait_send()


def reduce_parts(payload):
    results, scratch = (), []
    for part in payload:
        rows = part.shape[2:]
        results += (jax.ShapeDtypeStruct((4,) + rows, bf16), jax.ShapeDtypeStruct((3,) + rows, bf16))
        scratch += [pltpu.SemaphoreType.DMA((7,))] * 2
    if payload:
        scratch += [pltpu.VMEM(rows, bf16), pltpu.VMEM(rows, bf16), pltpu.VMEM((3,) + rows, bf16)]
        scratch += [pltpu.SemaphoreType.DMA((2,))]
    return tuple(payload), results, scratch


def reduces(group, sources, results, scratch):
    tiles = scratch[2 * len(sources) :]
    return [
        Reduce(group, source, results[2 * n], results[2 * n + 1], scratch[2 * n : 2 * n + 2], tiles)
        for n, source in enumerate(sources)
    ]


class BlockGather:
    def __init__(self, peers, source, target, sems, first, local):
        self.p, self.source, self.target, self.sems, self.first = peers, source, target, sems, first
        self.local = local

    def piece(self, slot, index, to, own=False):
        target = self.target.at[slot]
        return self.p.copy(self.source if own else target, target, self.sems, self.first + index, to)

    def keep(self):
        return pltpu.make_async_copy(self.source, self.target.at[self.p.t], self.local)

    def start(self):
        p = self.p
        self.piece(p.t, 1, p.over, True).start()
        self.piece(p.t, 0, p.core, True).start()
        self.keep().start()

    def relay(self):
        p = self.p
        self.piece(p.over, 1, p.over).wait_recv()
        self.piece(p.over, 2, p.core).start()

    def finish(self):
        p = self.p
        self.piece(p.core, 0, p.core).wait_recv()
        self.piece(p.diag, 2, p.core).wait_recv()
        self.piece(p.t, 1, p.over, True).wait_send()
        self.piece(p.t, 0, p.core, True).wait_send()
        self.piece(p.over, 2, p.core).wait_send()
        self.keep().wait()


def add_up(own, others, target):
    rows = own.shape[0]
    for first in range(0, rows, 40):
        at = slice(first, min(first + 40, rows))
        total = own[at, :].astype(f32)
        for other in others:
            total = total + other[at, :].astype(f32)
        target[at, :] = total.astype(target.dtype)


def last_sum_kernel(source, earlier, from_y, from_z, got, got_earlier, *scratch):
    p, g = Peers(), Group()
    scratch, (bsend, brecv, blocal, mine) = scratch[:-4], scratch[-4:]
    own, near, gone, local = scratch[2:]
    before = BlockGather(p, earlier, got_earlier, (bsend, brecv), 0, blocal.at[0])
    after = BlockGather(p, mine, got, (bsend, brecv), 3, blocal.at[1])
    item = reduces(g, [source], [from_y, from_z], scratch)[0]
    g.greet(p)
    item.start(1, 2)
    before.start()
    item.pump(1)
    item.start(3)
    before.relay()
    item.pump(2)
    item.start(0)
    item.pump(3)
    item.finish()
    loads = [
        pltpu.make_async_copy(source.at[g.z, g.y], own, local.at[0]),
        pltpu.make_async_copy(from_y.at[g.z], near, local.at[1]),
        pltpu.make_async_copy(from_z, gone, blocal.at[2]),
    ]
    for load in loads:
        load.start()
    for load in loads:
        load.wait()
    add_up(own, [near] + [gone.at[k] for k in range(3)], mine)
    after.start()
    before.finish()
    after.relay()
    after.finish()


def last_sum(part, earlier, n_tp, collective_id):
    operands, results, scratch = reduce_parts([part])
    whole = jax.ShapeDtypeStruct((n_tp,) + earlier.shape, bf16)
    _, _, got, got_earlier = pl.pallas_call(
        last_sum_kernel,
        out_shape=results + (whole, whole),
        in_specs=[ANY, ANY],
        out_specs=(ANY,) * 4,
        scratch_shapes=scratch
        + [pltpu.SemaphoreType.DMA((6,))] * 2
        + [pltpu.SemaphoreType.DMA((3,)), pltpu.VMEM(earlier.shape, bf16)],
        compiler_params=params(collective_id),
    )(part, earlier)
    return got, got_earlier


def assemble_kernel(*refs):
    inputs, refs = refs[: 7 * LAYERS], refs[7 * LAYERS :]
    qkv_ref, out_ref, fc_ref, proj_ref = refs[:4]
    vector_refs, (tiles, sems) = refs[4:13], refs[13:]
    t, f = lax.axis_index("tp"), lax.axis_index("fsdp")
    z, y = f // 2, f % 2
    loads = []
    for layer in range(LAYERS):
        for w in range(2):
            part, near, far = inputs[7 * layer + 1 + 3 * w : 7 * layer + 4 + 3 * w]
            n = 2 * layer + w
            loads.append(
                [
                    pltpu.make_async_copy(part.at[z, y], tiles.at[n, 0], sems.at[n, 0]),
                    pltpu.make_async_copy(near.at[z], tiles.at[n, 1], sems.at[n, 1]),
                    pltpu.make_async_copy(far, tiles.at[n, 2:5], sems.at[n, 2]),
                ]
            )
    for load in sum(loads, []):
        load.start()
    n_tp = inputs[0].shape[0]
    step = HEADS // n_tp * HEAD
    width = D - step * (n_tp - 1)
    counts = [step] * (n_tp - 1) + [width]
    for layer in range(LAYERS):
        got = inputs[7 * layer]
        for i in range(3):
            for k, count in enumerate(counts):
                value = got[k, :, i * WIDE : i * WIDE + count].astype(f32)
                qkv_ref[layer, :, i * D + k * step : i * D + k * step + count] = value
        for k, count in enumerate(counts):
            out_ref[layer, :, k * step : k * step + count] = got[k, :, 3 * WIDE : 3 * WIDE + count].astype(f32)
        extra = got[:, :, 3 * WIDE + step : 4 * WIDE].astype(f32)
        total = jnp.sum(extra, axis=0).T
        own = got[t, :, 3 * WIDE + step : 4 * WIDE].astype(f32).T
        skip = width - step
        for v in range(8):
            vector_refs[v][layer : layer + 1, :] = total[skip + v : skip + v + 1, :]
        vector_refs[8][layer : layer + 1, :] = own[skip + 8 : skip + 9, :]
        for w in range(2):
            n = 2 * layer + w
            for load in loads[n]:
                load.wait()
            total = tiles[n, 0].astype(f32)
            for k in range(1, 5):
                total = total + tiles[n, k].astype(f32)
            if w:
                fc_ref[layer] = total
            else:
                proj_ref[layer] = total.T


def assemble(layers):
    rows, width = layers[0][1].shape[2:]
    outs = [(LAYERS, rows, 3 * D), (LAYERS, rows, D), (LAYERS, rows, width), (LAYERS, width, rows)]
    outs += [(LAYERS, rows)] * 9
    return pl.pallas_call(
        assemble_kernel,
        out_shape=tuple(jax.ShapeDtypeStruct(o, f32) for o in outs),
        in_specs=([IN_VMEM] + [ANY] * 6) * LAYERS,
        out_specs=(IN_VMEM,) * len(outs),
        scratch_shapes=[
            pltpu.VMEM((2 * LAYERS, 5, rows, width), bf16),
            pltpu.SemaphoreType.DMA((2 * LAYERS, 3)),
        ],
        compiler_params=pltpu.CompilerParams(vmem_limit_bytes=60 * 2**20),
    )(*sum((list(layer) for layer in layers), []))


class Spread:
    def __init__(self, group, source, target, sems, chunks):
        self.g, self.source, self.target, self.sems = group, source, target, sems
        count = source.shape[1] // 128
        ends = [128 * (count * (c + 1) // chunks) for c in range(chunks)]
        self.columns = [slice(a, b) for a, b in zip([0] + ends, ends)]
        self.partner = group.at(group.z, 1 - group.y)

    def piece(self, member, c, index, to, own=False):
        target = self.target.at[member, :, self.columns[c]]
        source = self.source.at[:, self.columns[c]] if own else target
        return self.g.copy(source, target, self.sems, 7 * c + index, to)

    def own(self, c):
        g = self.g
        return [self.piece(g.member, c, k, g.at(g.ahead(k), g.y), True) for k in (1, 2, 3)] + [
            self.piece(g.member, c, 0, self.partner, True)
        ]

    def relayed(self, c):
        g = self.g
        return [self.piece(g.at(g.behind(k), g.y), c, 3 + k, self.partner) for k in (1, 2, 3)]

    def keep(self):
        return pltpu.make_async_copy(
            self.source, self.target.at[self.g.member], self.sems[0].at[7 * len(self.columns)]
        )

    def start(self, first=0, last=None):
        if first == 0:
            self.keep().start()
        for c in range(len(self.columns))[first:last]:
            for copy in self.own(c):
                copy.start()

    def relay(self, c):
        g = self.g
        for k, copy in zip((1, 2, 3), self.relayed(c)):
            self.piece(g.at(g.behind(k), g.y), c, k, self.partner).wait_recv()
            copy.start()

    def finish(self):
        g = self.g
        for c in range(len(self.columns)):
            self.piece(self.partner, c, 0, self.partner).wait_recv()
            for k in (1, 2, 3):
                self.piece(g.at(g.behind(k), 1 - g.y), c, 3 + k, self.partner).wait_recv()
            for copy in self.own(c) + self.relayed(c):
                copy.wait_send()
        self.keep().wait()


def spread_parts(shard, chunks):
    if shard is None:
        return (), (), []
    whole = jax.ShapeDtypeStruct((GROUP,) + shard.shape, shard.dtype)
    return (shard,), (whole,), [pltpu.SemaphoreType.DMA((7 * chunks + 1,))] * 2


def spread_kernel(chunks, source, target, send, recv):
    g = Group()
    g.greet_group()
    spread = Spread(g, source, target, (send, recv), chunks)
    spread.start()
    for c in range(chunks):
        spread.relay(c)
    spread.finish()


def spread_only(shard, chunks, collective_id):
    operands, results, scratch = spread_parts(shard, chunks)
    return pl.pallas_call(
        functools.partial(spread_kernel, chunks),
        out_shape=results[0],
        in_specs=[ANY],
        out_specs=ANY,
        scratch_shapes=scratch,
        compiler_params=params(collective_id),
    )(shard)


def row_chunks(rows, body):
    @pl.loop(0, rows // ROW_CHUNK)
    def _(i):
        body(pl.ds(pl.multiple_of(i * ROW_CHUNK, ROW_CHUNK), ROW_CHUNK))


def tiles(extent, body):
    whole = extent // TILE

    @pl.loop(0, whole)
    def _(i):
        body(pl.ds(pl.multiple_of(i * TILE, TILE), TILE))

    if extent % TILE:
        body(pl.ds(whole * TILE, extent % TILE))


def pair_rows(ref, x):
    both = ref[pl.ds(2 * x, 2)]
    return both.reshape(2 * both.shape[1], both.shape[2])


def put_pair(ref, x, at, value):
    ref[pl.ds(2 * x, 2), :, at] = value.reshape(2, value.shape[0] // 2, value.shape[1]).astype(ref.dtype)


def norm_stats(x):
    centred = x - jnp.mean(x, -1, keepdims=True)
    scale = lax.rsqrt(jnp.mean(centred * centred, -1, keepdims=True) + norm_eps)
    return centred * scale, scale


def lanes_up(width):
    return -(-width // 128) * 128


def proj_part(w_b, width):
    return w_b.at[:, lanes_up(width) :]


FF_CHUNKS = 3
ATTN_CHUNKS = 5


def ff_fwd_kernel(n, *refs):
    x_ref, vec_ref, fcb_ref, wb_hbm = refs[:4]
    shard, refs = refs[4 : 4 + n], refs[4 + n :]
    out_ref, all_hbm, pre_hbm, hid_hbm = refs[:4]
    whole, refs = refs[4 : 4 + n], refs[4 + n :]
    wfc, wproj, buf, pre, hid, part, from_core, over_out, from_over, send, recv, local = refs[:12]
    p, g = Peers(), Group()
    spread = Spread(g, shard[0], whole[0], refs[12:], FF_CHUNKS) if n else None
    rows = x_ref.shape[0]
    sems = (send, recv)
    gather = Gather(p, buf, sems)
    scatter = Scatter(p, part, from_core, over_out, from_over, sems)
    width = fcb_ref.shape[1]
    load_fc = pltpu.make_async_copy(wb_hbm.at[:, : wfc.shape[1]], wfc, local.at[0])
    load_proj = pltpu.make_async_copy(proj_part(wb_hbm, width), wproj, local.at[1])
    load_fc.start()
    load_proj.start()

    def norm(at):
        hat, _ = norm_stats(x_ref[at, :])
        buf[p.t, at, :] = (hat * vec_ref[5:6, :] + vec_ref[6:7, :]).astype(bf16)

    row_chunks(rows, norm)
    if n:
        g.greet(p)
    else:
        p.greet()
    gather.start()
    if n:
        spread.start()
    gather.wait_chip()
    load_fc.wait()

    def up(x):
        def tile(at):
            value = mm(pair_rows(buf, x), wfc[:, at]) + fcb_ref[:, at]
            put_pair(pre, x, at, value)
            put_pair(hid, x, at, gelu_tanh(value))

        tiles(width, tile)

    def down(x):
        def tile(at):
            put_pair(part, x, at, mm(pair_rows(hid, x), wproj[at, :width], NT))

        tiles(D, tile)

    up(p.x)
    if n:
        spread.relay(0)
    gather.relay()
    gather.wait_diag()
    keep_all = pltpu.make_async_copy(buf, all_hbm, local.at[2])
    keep_all.start()
    up(1 - p.x)
    keep_pre = pltpu.make_async_copy(pre, pre_hbm, local.at[3])
    keep_hid = pltpu.make_async_copy(hid, hid_hbm, local.at[4])
    keep_pre.start()
    keep_hid.start()
    load_proj.wait()
    down(1 - p.x)
    scatter.far_to_core().start()
    scatter.send_over()
    if n:
        spread.relay(1)
    down(p.x)
    scatter.near_to_core().start()
    if n:
        spread.relay(2)
    scatter.wait()

    def final(at):
        out_ref[at, :] = x_ref[at, :] + scatter.rows(at) + vec_ref[7:8, :]

    row_chunks(rows, final)
    gather.finish()
    scatter.finish()
    for copy in (keep_all, keep_pre, keep_hid):
        copy.wait()
    if n:
        spread.finish()


def scatter_scratch(n_tp, rows):
    return [
        pltpu.VMEM((n_tp, rows, D), bf16),
        pltpu.VMEM((2, rows, D), bf16),
        pltpu.VMEM((rows, D), bf16),
        pltpu.VMEM((rows, D), bf16),
        pltpu.SemaphoreType.DMA((6,)),
        pltpu.SemaphoreType.DMA((6,)),
    ]


def params(collective_id):
    return pltpu.CompilerParams(collective_id=collective_id, has_side_effects=True, vmem_limit_bytes=60 * 2**20)


def ff_fwd(x, vecs, fc_bias, w_b, n_tp, shard, collective_id):
    rows, width = x.shape[0], fc_bias.shape[1]
    block = (n_tp, rows)
    operands, results, sems = spread_parts(shard, FF_CHUNKS)
    return pl.pallas_call(
        functools.partial(ff_fwd_kernel, len(operands)),
        out_shape=(
            jax.ShapeDtypeStruct((rows, D), f32),
            jax.ShapeDtypeStruct(block + (D,), bf16),
            jax.ShapeDtypeStruct(block + (width,), f32),
            jax.ShapeDtypeStruct(block + (width,), bf16),
        )
        + results,
        in_specs=[IN_VMEM, IN_VMEM, IN_VMEM, ANY] + [ANY] * len(operands),
        out_specs=(IN_VMEM, ANY, ANY, ANY) + (ANY,) * len(operands),
        scratch_shapes=[
            pltpu.VMEM((D, lanes_up(width)), bf16),
            pltpu.VMEM((D, lanes_up(width)), bf16),
            pltpu.VMEM(block + (D,), bf16),
            pltpu.VMEM(block + (width,), f32),
            pltpu.VMEM(block + (width,), bf16),
        ]
        + scatter_scratch(n_tp, rows)
        + [pltpu.SemaphoreType.DMA((5,))]
        + sems,
        compiler_params=params(collective_id),
        cost_estimate=pl.CostEstimate(
            flops=4 * n_tp * rows * D * width, bytes_accessed=40 * 2**20, transcendentals=n_tp * rows * width
        ),
    )(x, vecs, fc_bias, w_b, *operands)


def gelu_slope(u):
    a = 0.7978845608028654
    square = u * u
    t = jnp.tanh(a * (u + 0.044715 * u * square))
    return 0.5 * (1.0 + t) + 0.5 * u * (1.0 - t * t) * (a * (1.0 + 3 * 0.044715 * square))


def norm_back(x, dy, gain):
    hat, scale = norm_stats(x)
    d_hat = dy * gain
    inner = d_hat - jnp.mean(d_hat, -1, keepdims=True) - hat * jnp.mean(d_hat * hat, -1, keepdims=True)
    return scale * inner, dy * hat


def add_rows(ref, row, value):
    ref[row : row + 1, :] += jnp.sum(value, axis=0, keepdims=True)


def ff_bwd_kernel(n, *refs):
    g_ref, x_ref, vec_ref, all_hbm, pre_hbm, hid_hbm, wb_hbm = refs[:7]
    sources, refs = refs[7 : 7 + n], refs[7 + n :]
    out_ref, sums_ref, fcb_ref, dfc_hbm, dproj_hbm = refs[:5]
    results, refs = refs[5 : 5 + 2 * n], refs[5 + 2 * n :]
    wfc, wproj, buf, other, pre, dpre, stage, part, from_core, over_out, from_over, send, recv, local = refs[:14]
    p, g = Peers(), Group()
    sums = reduces(g, sources, results, refs[14:])
    rows = x_ref.shape[0]
    n_tp, width = buf.shape[0], fcb_ref.shape[1]
    sems = (send, recv)
    gather = Gather(p, buf, sems)
    scatter = Scatter(p, part, from_core, over_out, from_over, sems)
    load_proj = pltpu.make_async_copy(proj_part(wb_hbm, width), wproj, local.at[0])
    load_pre = pltpu.make_async_copy(pre_hbm, pre, local.at[1])
    load_fc = pltpu.make_async_copy(wb_hbm.at[:, : wfc.shape[1]], wfc, local.at[2])
    load_other = pltpu.make_async_copy(hid_hbm, other, local.at[3])
    for copy in (load_proj, load_pre, load_fc, load_other):
        copy.start()
    sums_ref[...] = jnp.zeros_like(sums_ref)
    fcb_ref[...] = jnp.zeros_like(fcb_ref)

    def lower(at):
        low = g_ref[at, :].astype(bf16)
        buf[p.t, at, :] = low
        add_rows(sums_ref, 7, low.astype(f32))

    row_chunks(rows, lower)
    if n:
        g.greet(p)
    else:
        p.greet()
    gather.start()
    for item in sums:
        item.start(1)

    def pump(j):
        for item in sums:
            item.pump(j)
            if j == 2:
                item.start(0)

    gather.wait_chip()
    load_proj.wait()
    load_pre.wait()

    def through(x):
        def tile(at):
            d_hidden = mm(pair_rows(buf, x), wproj[:, at])
            u = pre[pl.ds(2 * x, 2), :, at].reshape(2 * rows, -1)
            low = (gelu_slope(u) * d_hidden).astype(bf16)
            put_pair(dpre, x, at, low)
            fcb_ref[:, at] += jnp.sum(low.astype(f32), axis=0, keepdims=True)

        tiles(width, tile)

    def down(x):
        def tile(at):
            put_pair(part, x, at, mm(pair_rows(dpre, x), wfc[at, :width], NT))

        tiles(D, tile)

    through(p.x)
    for item in sums:
        item.start(2)
    gather.relay()
    gather.wait_diag()
    through(1 - p.x)
    pump(1)
    load_fc.wait()
    down(1 - p.x)
    scatter.far_to_core().start()
    scatter.send_over()
    for item in sums:
        item.start(3)
    down(p.x)
    scatter.near_to_core().start()

    def outer(left, right, target, sem):
        whole = D // TILE
        rest = D - whole * TILE
        flat = right[...].reshape(n_tp * rows, width)

        def tile(i, size):
            at = pl.ds(pl.multiple_of(i * TILE, TILE), size)
            value = mm(left[:, :, at].reshape(n_tp * rows, size), flat, TN)
            stage[at, :] = value.astype(bf16)

        @pl.loop(0, whole)
        def _(i):
            tile(i, TILE)

        if rest:
            tile(whole, rest)
        return pltpu.make_async_copy(stage, target, sem)

    load_other.wait()
    pump(2)
    store = outer(buf, other, dproj_hbm, local.at[4])
    store.start()
    gather.finish()
    load_all = pltpu.make_async_copy(all_hbm, buf, local.at[5])
    load_all.start()
    scatter.wait()

    def final(at):
        dy = scatter.rows(at)
        dx, d_gain = norm_back(x_ref[at, :], dy, vec_ref[5:6, :])
        add_rows(sums_ref, 5, d_gain)
        add_rows(sums_ref, 6, dy)
        out_ref[at, :] = g_ref[at, :] + dx

    row_chunks(rows, final)
    load_all.wait()
    store.wait()
    store = outer(buf, dpre, dfc_hbm, local.at[6])
    store.start()
    pump(3)
    scatter.finish()
    store.wait()
    for item in sums:
        item.finish()


def ff_bwd(grad, x, vecs, all_rows, pre, hidden, w_b, n_tp, payload, collective_id):
    rows, width = x.shape[0], pre.shape[2]
    block = (n_tp, rows)
    operands, results, more = reduce_parts(payload)
    return pl.pallas_call(
        functools.partial(ff_bwd_kernel, len(payload)),
        out_shape=(
            jax.ShapeDtypeStruct((rows, D), f32),
            jax.ShapeDtypeStruct((8, D), f32),
            jax.ShapeDtypeStruct((1, width), f32),
            jax.ShapeDtypeStruct((D, width), bf16),
            jax.ShapeDtypeStruct((D, width), bf16),
        )
        + results,
        in_specs=[IN_VMEM] * 3 + [ANY] * (4 + len(payload)),
        out_specs=(IN_VMEM, IN_VMEM, IN_VMEM) + (ANY,) * (2 + 2 * len(payload)),
        scratch_shapes=[
            pltpu.VMEM((D, lanes_up(width)), bf16),
            pltpu.VMEM((D, lanes_up(width)), bf16),
            pltpu.VMEM(block + (D,), bf16),
            pltpu.VMEM(block + (width,), bf16),
            pltpu.VMEM(block + (width,), f32),
            pltpu.VMEM(block + (width,), bf16),
            pltpu.VMEM((D, width), bf16),
        ]
        + scatter_scratch(n_tp, rows)
        + [pltpu.SemaphoreType.DMA((7,))]
        + more,
        compiler_params=params(collective_id),
        cost_estimate=pl.CostEstimate(
            flops=8 * n_tp * rows * D * width, bytes_accessed=50 * 2**20, transcendentals=n_tp * rows * width
        ),
    )(grad, x, vecs, all_rows, pre, hidden, w_b, *operands)


HALVES = [(micro, half) for micro in range(MICRO) for half in range(2)]


def half_lanes(half):
    return slice(half * WIDE // 2, (half + 1) * WIDE // 2)


class Share:
    def __init__(self, group, kv, sems):
        self.g, self.kv, self.sems = group, kv, sems
        self.partner = group.at(group.z, 1 - group.y)

    def piece(self, member, part, index, to):
        micro, half = part
        ref = self.kv.at[member, micro, :, :, half_lanes(half)]
        return self.g.copy(ref, ref, self.sems, (2 * micro + half) * 7 + index, to)

    def own(self, part):
        g = self.g
        return [self.piece(g.member, part, 0, self.partner)] + [
            self.piece(g.member, part, k, g.at(g.ahead(k), g.y)) for k in (1, 2, 3)
        ]

    def relayed(self, part):
        g = self.g
        return [self.piece(g.at(g.behind(k), g.y), part, 3 + k, self.partner) for k in (1, 2, 3)]

    def start(self, *part):
        for copy in self.own(part):
            copy.start()

    def relay(self, *part):
        g = self.g
        for k, copy in zip((1, 2, 3), self.relayed(part)):
            self.piece(g.at(g.behind(k), g.y), part, k, self.partner).wait_recv()
            copy.start()

    def wait(self, *part):
        g = self.g
        self.piece(self.partner, part, 0, self.partner).wait_recv()
        for k in (1, 2, 3):
            self.piece(g.at(g.behind(k), 1 - g.y), part, 3 + k, self.partner).wait_recv()

    def finish(self):
        for part in HALVES:
            for copy in self.own(part) + self.relayed(part):
                copy.wait_send()


class GroupSum:
    def __init__(self, group, parts, from_y, to_z, from_z, sems):
        self.g, self.parts, self.sems = group, parts, sems
        self.from_y, self.to_z, self.from_z = from_y, to_z, from_z

    def across(self, micro, half):
        g, lanes = self.g, half_lanes(half)
        return g.copy(
            self.parts.at[micro, :, 1 - g.y, :, :, lanes],
            self.from_y.at[micro, :, :, :, lanes],
            self.sems,
            (2 * micro + half) * 4,
            g.at(g.z, 1 - g.y),
        )

    def along(self, micro, half, k):
        g, lanes = self.g, half_lanes(half)
        to = g.ahead(k)
        return g.copy(
            self.to_z.at[micro, to, :, :, lanes],
            self.from_z.at[micro, k - 1, :, :, lanes],
            self.sems,
            (2 * micro + half) * 4 + k,
            g.at(to, g.y),
        )

    def start(self, micro, half):
        self.across(micro, half).start()

    def turn(self, micro, half):
        lanes = half_lanes(half)
        self.across(micro, half).wait_recv()

        @pl.loop(0, 4)
        def _(z):
            for kv in range(2):
                total = self.parts[micro, z, self.g.y, kv, :, lanes] + self.from_y[micro, z, kv, :, lanes]
                self.to_z[micro, z, kv, :, lanes] = total

        for k in (1, 2, 3):
            self.along(micro, half, k).start()

    def wait(self, micro):
        for half in range(2):
            for k in (1, 2, 3):
                self.along(micro, half, k).wait_recv()

    def total(self, micro, kv):
        g = self.g
        value = self.parts[micro, g.z, g.y, kv].astype(f32) + self.from_y[micro, g.z, kv].astype(f32)
        for k in range(3):
            value = value + self.from_z[micro, k, kv].astype(f32)
        return value.astype(bf16)

    def finish(self, micro):
        for half in range(2):
            self.across(micro, half).wait_send()
            for k in (1, 2, 3):
                self.along(micro, half, k).wait_send()


WIDE = 512
HEAD_PAIRS = WIDE // (2 * HEAD)
PROMPT_CHUNKS = PROMPT // CHUNK
CONT_CHUNKS = CONT_LEN // CHUNK


def chunk_at(c, base=0):
    return pl.ds(pl.multiple_of(base + c * CHUNK, CHUNK), CHUNK)


def key_limit(member):
    row = lax.broadcasted_iota(jnp.int32, (1, TOK_DEV), 1)
    return jnp.where(row < PROMPT_DEV, member * PROMPT_DEV + row, PROMPT - PROMPT_DEV + row)


def half_of(value, half):
    lane = lax.broadcasted_iota(jnp.int32, value.shape, 1)
    return jnp.where((lane >= HEAD * half) & (lane < HEAD * (half + 1)), value, jnp.zeros_like(value))


def fold(value, op):
    return op(value.reshape(value.shape[0] // 8, 8, value.shape[1]), axis=0)


def over_keys(body, prompt, own, carry):
    carry = lax.fori_loop(0, PROMPT_CHUNKS, lambda c, carry: body(c, lambda i: prompt(c, i), carry), carry)
    return lax.fori_loop(
        0, CONT_CHUNKS, lambda c, carry: body(PROMPT_CHUNKS + c, lambda i: own(c, i), carry), carry
    )


def head_pairs(head, finish):
    @pl.loop(0, HEAD_PAIRS)
    def _(pair):
        lanes = pl.ds(pl.multiple_of(pair * 2 * HEAD, 2 * HEAD), 2 * HEAD)
        head(pair, lanes, 0)

        @pl.when(pair < HEAD_PAIRS - 1)
        def _():
            head(pair, lanes, 1)

        finish(pair, lanes)


def run_hooks(hooks, micro, pair, half):
    for at in range(HEAD_PAIRS):
        if half == 0 and (micro, at) in hooks:

            @pl.when(pair == at)
            def _(at=at):
                for hook in hooks[micro, at]:
                    hook()


def to_slots(target, micro, first, value, lanes):
    per = target.shape[1] // MICRO
    row = first
    while row < first + value.shape[0]:
        slot, within = row // per, row % per
        count = min(per - within, first + value.shape[0] - row)
        target[slot, micro * per + within : micro * per + within + count, lanes] = value[
            row - first : row - first + count
        ]
        row += count


def pair_to_blocks(target, x, value):
    per = value.shape[0] // (2 * MICRO)
    for core in range(2):
        for micro in range(MICRO):
            at = pl.ds(pl.multiple_of((2 * x + core) * per, per), per)
            first = (core * MICRO + micro) * per
            target[micro, at, :] = value[first : first + per]


def attn_fwd_kernel(n, *refs):
    x_ref, vec_ref, bias_ref, wqkv_hbm = refs[:4]
    shard, refs = refs[4 : 4 + n], refs[4 + n :]
    out_ref, lse_ref, all_hbm, own_hbm, kv_hbm, mix_hbm, wout_hbm = refs[:7]
    whole, refs = refs[7 : 7 + n], refs[7 + n :]
    wqkv, wout, wparts, buf, own, kv, mix, s_ref, p_ref, o_ref = refs[:10]
    part, from_core, over_out, from_over, send, recv, gsend, grecv, wsend, wrecv, local = refs[10:21]
    p, g = Peers(), Group()
    spread = Spread(g, shard[0], whole[0], refs[21:], ATTN_CHUNKS) if n else None
    rows = x_ref.shape[0]
    n_tp = buf.shape[0]
    step = HEADS // n_tp * HEAD
    width = wparts.shape[1]
    sems = (send, recv)
    gather = Gather(p, buf, sems)
    scatter = Scatter(p, part, from_core, over_out, from_over, sems)
    share = Share(g, kv, (gsend, grecv))
    load_qkv = pltpu.make_async_copy(wqkv_hbm.at[:, : 3 * WIDE], wqkv, local.at[0])
    load_qkv.start()

    def rows_for(t):
        return wqkv_hbm.at[pl.ds(pl.multiple_of(t * step, 128), width), 3 * WIDE : 4 * WIDE]

    keep_part = pltpu.make_async_copy(rows_for(p.t), wparts.at[p.t], local.at[1])
    keep_part.start()
    give_parts = [
        p.copy(rows_for(t), wparts.at[p.t], (wsend, wrecv), i, t) for i, t in enumerate((p.core, p.over, p.diag))
    ]

    def norm(at):
        hat, _ = norm_stats(x_ref[at, :])
        buf[p.t, at, :] = (hat * vec_ref[0:1, :] + vec_ref[1:2, :]).astype(bf16)

    row_chunks(rows, norm)
    g.greet(p, True)
    gather.start()
    for copy in give_parts:
        copy.start()
    if n:
        spread.start(0, 1)
    gather.wait_chip()
    load_qkv.wait()

    def project(x):
        for i in range(3):
            value = mm(pair_rows(buf, x), wqkv[:, i * WIDE : (i + 1) * WIDE]) + bias_ref[i : i + 1, :]
            low = value.astype(bf16)
            if i == 0:
                low = low * HEAD ** (-0.5)
            pair_to_blocks(own.at[i], x, low)

    project(p.x)
    gather.relay()
    gather.wait_diag()
    project(1 - p.x)
    for micro in range(MICRO):
        for i in range(2):
            kv[g.member, micro, i] = own[1 + i, micro, :PROMPT_DEV, :]
    share.start(0, 0)
    if n:
        spread.relay(0)
    hooks = {
        (0, 1): [lambda: share.relay(0, 1), lambda: share.start(1, 0)],
        (0, 2): [lambda: share.wait(0, 1)],
        (0, 3): [lambda: share.relay(1, 0), lambda: share.start(1, 1)],
        (1, 0): [lambda: share.wait(1, 0)],
        (1, 1): [lambda: share.relay(1, 1)],
        (1, 2): [lambda: share.wait(1, 1)],
    }
    if n:
        hooks[1, 1].append(lambda: spread.start(1, 2))
    keep_all = pltpu.make_async_copy(buf, all_hbm, local.at[2])
    keep_own = pltpu.make_async_copy(own, own_hbm, local.at[3])
    keep_all.start()
    keep_own.start()
    limit = key_limit(g.member)
    sub = lax.broadcasted_iota(jnp.int32, (CHUNK, TOK_DEV), 0)

    share.relay(0, 0)
    share.start(0, 1)
    share.wait(0, 0)

    for micro in range(MICRO):

        def head(pair, lanes, half, micro=micro):
            run_hooks(hooks, micro, pair, half)
            qh = half_of(own[0, micro, :, lanes], half)

            def first(c, load, top):
                s = jnp.where(sub + c * CHUNK <= limit, mm(load(0), qh, NT), -1e30)
                s_ref[chunk_at(c), :] = s
                return jnp.maximum(top, fold(s, jnp.max))

            top = over_keys(
                first,
                lambda c, i: kv[c, micro, i, :, lanes],
                lambda c, i: own[1 + i, micro, chunk_at(c, PROMPT_DEV), lanes],
                jnp.full((8, TOK_DEV), -1e30, f32),
            )
            top = jnp.max(top, axis=0, keepdims=True)

            def second(c, total):
                e = jnp.exp(s_ref[chunk_at(c), :] - top)
                p_ref[chunk_at(c), :] = e.astype(bf16)
                return total + fold(e, jnp.sum)

            total = lax.fori_loop(0, KEYS // CHUNK, second, jnp.zeros((8, TOK_DEV), f32))
            total = jnp.sum(total, axis=0, keepdims=True)
            values = kv[:, micro, 1, :, lanes].reshape(PROMPT, 2 * HEAD)
            out = mm(values, p_ref[:PROMPT, :], TN) + mm(own[2, micro, PROMPT_DEV:, lanes], p_ref[PROMPT:, :], TN)
            at = slice(HEAD * half, HEAD * (half + 1))
            o_ref[at, :] = out[at, :] / total
            lse_ref[micro, pair, half : half + 1, :] = top + jnp.log(total)

        def finish(pair, lanes, micro=micro):
            @pl.when(pair == HEAD_PAIRS - 1)
            def _():
                o_ref[HEAD:, :] = jnp.zeros((HEAD, TOK_DEV), f32)

            to_slots(mix, micro, 0, o_ref[...].T.astype(bf16), lanes)

        head_pairs(head, finish)

    keep_kv = pltpu.make_async_copy(kv, kv_hbm, local.at[4])
    keep_mix = pltpu.make_async_copy(mix, mix_hbm, local.at[5])
    keep_kv.start()
    keep_mix.start()
    keep_part.wait()
    for i, t in enumerate((p.core, p.over, p.diag)):
        p.copy(rows_for(t), wparts.at[t], (wsend, wrecv), i, t).wait_recv()
    for t in range(n_tp):
        count = min(WIDE, D - t * step)
        wout[:width, t * step : t * step + count] = wparts[t, :, :count]
    wout[width:, :] = jnp.zeros((WIDE - width, D), bf16)

    @pl.when(p.t < n_tp - 1)
    def _():
        wout[step:width, :] = jnp.zeros((width - step, D), bf16)

    keep_out = pltpu.make_async_copy(wout, wout_hbm, local.at[6])
    keep_out.start()

    def down(x):
        def tile(at):
            put_pair(part, x, at, mm(pair_rows(mix, x), wout[:, at]))

        tiles(D, tile)

    if n:
        spread.start(2, 3)
    down(1 - p.x)
    scatter.far_to_core().start()
    scatter.send_over()
    down(p.x)
    scatter.near_to_core().start()
    if n:
        spread.relay(1)
        spread.start(3, 4)
    scatter.wait()

    def final(at):
        out_ref[at, :] = x_ref[at, :] + (scatter.rows(at) + vec_ref[4:5, :])

    row_chunks(rows, final)
    if n:
        spread.relay(2)
        spread.start(4)
        spread.relay(3)
        spread.relay(4)
    gather.finish()
    scatter.finish()
    share.finish()
    for copy in give_parts:
        copy.wait_send()
    for copy in (keep_all, keep_own, keep_kv, keep_mix, keep_out):
        copy.wait()
    if n:
        spread.finish()


def attn_shapes(n_tp, rows):
    return (
        ((n_tp, rows, D), bf16),
        ((3, MICRO, TOK_DEV, WIDE), bf16),
        ((GROUP, MICRO, 2, PROMPT_DEV, WIDE), bf16),
        ((n_tp, rows, WIDE), bf16),
    )


def attn_fwd(x, vecs, biases, w_a, n_tp, shard, collective_id):
    rows = x.shape[0]
    width = D - HEADS // n_tp * HEAD * (n_tp - 1)
    saved = attn_shapes(n_tp, rows)
    operands, results, sems = spread_parts(shard, ATTN_CHUNKS)
    return pl.pallas_call(
        functools.partial(attn_fwd_kernel, len(operands)),
        out_shape=(
            jax.ShapeDtypeStruct((rows, D), f32),
            jax.ShapeDtypeStruct((MICRO, HEAD_PAIRS, 8, TOK_DEV), f32),
        )
        + tuple(jax.ShapeDtypeStruct(*s) for s in saved + (((WIDE, D), bf16),))
        + results,
        in_specs=[IN_VMEM, IN_VMEM, IN_VMEM, ANY] + [ANY] * len(operands),
        out_specs=(IN_VMEM, IN_VMEM) + (ANY,) * (5 + len(operands)),
        scratch_shapes=[pltpu.VMEM((D, 3 * WIDE), bf16), pltpu.VMEM((WIDE, D), bf16), pltpu.VMEM((n_tp, width, WIDE), bf16)]
        + [pltpu.VMEM(*s) for s in saved]
        + [
            pltpu.VMEM((KEYS, TOK_DEV), f32),
            pltpu.VMEM((KEYS, TOK_DEV), bf16),
            pltpu.VMEM((2 * HEAD, TOK_DEV), f32),
        ]
        + scatter_scratch(n_tp, rows)
        + [
            pltpu.SemaphoreType.DMA((14 * MICRO,)),
            pltpu.SemaphoreType.DMA((14 * MICRO,)),
            pltpu.SemaphoreType.DMA((3,)),
            pltpu.SemaphoreType.DMA((3,)),
            pltpu.SemaphoreType.DMA((7,)),
        ]
        + sems,
        compiler_params=params(collective_id),
        cost_estimate=pl.CostEstimate(flops=10**11, bytes_accessed=30 * 2**20, transcendentals=0),
    )(x, vecs, biases, w_a, *operands)


def attn_bwd_kernel(n, *refs):
    g_ref, x_ref, vec_ref, lse_ref, all_hbm, own_hbm, kv_hbm, mix_hbm, wqkv_hbm, wout_hbm = refs[:10]
    sources, refs = refs[10 : 10 + n], refs[10 + n :]
    out_ref, sums_ref, cols_ref, dqo_hbm = refs[:4]
    results, refs = refs[4 : 4 + 2 * n], refs[4 + 2 * n :]
    wqkv, wout, buf, other, own, kv, gm, dkv, from_y, to_z, from_z, dkc, dqkv, stage, stage_out = refs[:15]
    p_ref, dp_ref, ds_ref, o_ref = refs[15:19]
    part, from_core, over_out, from_over, send, recv, gsend, grecv, local = refs[19:28]
    p, g = Peers(), Group()
    sums = reduces(g, sources, results, refs[28:])
    rows = x_ref.shape[0]
    n_tp = buf.shape[0]
    out_step = HEADS // n_tp * HEAD
    out_width = D - out_step * (n_tp - 1)
    sems = (send, recv)
    gather = Gather(p, buf, sems)
    scatter = Scatter(p, part, from_core, over_out, from_over, sems)
    reduce = GroupSum(g, dkv, from_y, to_z, from_z, (gsend, grecv))
    load_out = pltpu.make_async_copy(wout_hbm, wout, local.at[0])
    load_own = pltpu.make_async_copy(own_hbm, own, local.at[1])
    load_kv = pltpu.make_async_copy(kv_hbm, kv, local.at[2])
    load_qkv = pltpu.make_async_copy(wqkv_hbm.at[:, : 3 * WIDE], wqkv, local.at[3])
    load_mix = pltpu.make_async_copy(mix_hbm, other, local.at[4])
    for copy in (load_out, load_own, load_kv, load_qkv, load_mix):
        copy.start()
    sums_ref[...] = jnp.zeros_like(sums_ref)

    def lower(at):
        low = g_ref[at, :].astype(bf16)
        buf[p.t, at, :] = low
        add_rows(sums_ref, 4, low.astype(f32))

    row_chunks(rows, lower)
    g.greet(p)
    gather.start()
    hooks = {(1, 0): [lambda: reduce.turn(0, 0)], (1, 1): [lambda: reduce.turn(0, 1)]}
    if n:
        first_sum, second_sum = sums
        first_sum.start(1)
        hooks[0, 1] = [lambda: first_sum.start(0), lambda: first_sum.pump(2)]
        hooks[0, 2] = [lambda: second_sum.start(1), lambda: first_sum.pump(3)]
        hooks[0, 3] = [lambda: second_sum.start(2)]
        hooks[1, 1] += [lambda: second_sum.pump(1, first_sum), lambda: second_sum.start(3)]
    gather.wait_chip()
    load_out.wait()

    def mixed_back(x):
        pair_to_blocks(gm, x, mm(pair_rows(buf, x), wout[...], NT).astype(bf16))

    mixed_back(p.x)
    if n:
        first_sum.start(2)
    gather.relay()
    gather.wait_diag()
    mixed_back(1 - p.x)
    load_own.wait()
    load_kv.wait()
    limit = key_limit(g.member)
    sub = lax.broadcasted_iota(jnp.int32, (CHUNK, TOK_DEV), 0)

    if n:
        first_sum.start(3)
        first_sum.pump(1)

    for micro in range(MICRO):

        def head(pair, lanes, half, micro=micro):
            run_hooks(hooks, micro, pair, half)
            qh = half_of(own[0, micro, :, lanes], half)
            gh = half_of(gm[micro, :, lanes], half)
            lse = lse_ref[micro, pair, half : half + 1, :]

            def first(c, load, inner):
                s = jnp.where(sub + c * CHUNK <= limit, mm(load(0), qh, NT), -1e30)
                e = jnp.exp(s - lse)
                dp = mm(load(1), gh, NT)
                p_ref[chunk_at(c), :] = e
                dp_ref[chunk_at(c), :] = dp
                return inner + fold(e * dp, jnp.sum)

            inner = over_keys(
                first,
                lambda c, i: kv[c, micro, i, :, lanes],
                lambda c, i: own[1 + i, micro, chunk_at(c, PROMPT_DEV), lanes],
                jnp.zeros((8, TOK_DEV), f32),
            )
            inner = jnp.sum(inner, axis=0, keepdims=True)

            def second(c, put):
                e = p_ref[chunk_at(c), :]
                ds = (e * (dp_ref[chunk_at(c), :] - inner)).astype(bf16)
                ds_ref[chunk_at(c), :] = ds
                put(0, mm(ds, qh))
                put(1, mm(e.astype(bf16), gh))

            @pl.loop(0, PROMPT_CHUNKS)
            def _(c):
                def put(i, value):
                    at = (micro, c // 2, c % 2, i, slice(None), lanes)
                    if half:
                        value = value + dkv[at].astype(f32)
                    dkv[at] = value.astype(bf16)

                second(c, put)

            @pl.loop(0, CONT_CHUNKS)
            def _(c):
                def put(i, value):
                    at = (i, chunk_at(c), lanes)
                    if half:
                        value = value + dkc[at].astype(f32)
                    dkc[at] = value.astype(bf16)

                second(PROMPT_CHUNKS + c, put)

            keys = kv[:, micro, 0, :, lanes].reshape(PROMPT, 2 * HEAD)
            dq = mm(keys, ds_ref[:PROMPT, :], TN) + mm(own[1, micro, PROMPT_DEV:, lanes], ds_ref[PROMPT:, :], TN)
            at = slice(HEAD * half, HEAD * (half + 1))
            o_ref[at, :] = dq[at, :] * HEAD ** (-0.5)

        def finish(pair, lanes, micro=micro):
            @pl.when(pair == HEAD_PAIRS - 1)
            def _():
                o_ref[HEAD:, :] = jnp.zeros((HEAD, TOK_DEV), f32)

            to_slots(dqkv, micro, 0, o_ref[...].T.astype(bf16), lanes)

            @pl.when(pair == HEAD_PAIRS // 2 - 1)
            def _():
                reduce.start(micro, 0)

        head_pairs(head, finish)
        reduce.start(micro, 1)
        for i in range(2):
            to_slots(dqkv, micro, PROMPT_DEV, dkc[i], slice((1 + i) * WIDE, (2 + i) * WIDE))

    load_mix.wait()
    columns = pl.ds(pl.multiple_of(p.t * out_step, 128), out_width)

    def outer(source, target, right, body):
        flat = right.reshape(n_tp * rows, right.shape[-1])

        def tile(at):
            left = source[:, :, at].reshape(n_tp * rows, -1)
            target[at, : flat.shape[1]] = mm(left, flat, TN).astype(bf16)

        body(D, tile)

    reduce.turn(1, 0)
    stage_out[:, out_width:] = jnp.zeros((D, WIDE - out_width), bf16)
    outer(other, stage_out, buf[:, :, columns], tiles)
    keep_out = pltpu.make_async_copy(stage_out, dqo_hbm.at[:, 3 * WIDE :], local.at[5])
    keep_out.start()
    load_all = pltpu.make_async_copy(all_hbm, other, local.at[6])
    load_all.start()
    reduce.turn(1, 1)
    if n:
        second_sum.start(0)
    for micro in range(MICRO):
        reduce.wait(micro)
        for i in range(2):
            to_slots(dqkv, micro, 0, reduce.total(micro, i), slice((1 + i) * WIDE, (2 + i) * WIDE))
    if n:
        second_sum.pump(2, first_sum)
        second_sum.pump(3, first_sum)
    load_qkv.wait()

    def down(x):
        def tile(at):
            put_pair(part, x, at, mm(pair_rows(dqkv, x), wqkv[at, :], NT))

        tiles(D, tile)

    down(1 - p.x)
    scatter.far_to_core().start()
    scatter.send_over()
    down(p.x)
    scatter.near_to_core().start()
    load_all.wait()
    outer(other, stage, dqkv[...], tiles)
    keep_qkv = pltpu.make_async_copy(stage, dqo_hbm.at[:, : 3 * WIDE], local.at[7])
    keep_qkv.start()
    cols_ref[...] = jnp.zeros_like(cols_ref)

    @pl.loop(0, n_tp * rows // ROW_CHUNK)
    def _(i):
        per = rows // ROW_CHUNK
        at = pl.ds(pl.multiple_of((i % per) * ROW_CHUNK, ROW_CHUNK), ROW_CHUNK)
        add_rows(cols_ref, 0, dqkv[i // per, at, :].astype(f32))

    scatter.wait()

    def final(at):
        dy = scatter.rows(at)
        dx, d_gain = norm_back(x_ref[at, :], dy, vec_ref[0:1, :])
        add_rows(sums_ref, 0, d_gain)
        add_rows(sums_ref, 1, dy)
        out_ref[at, :] = g_ref[at, :] + dx

    row_chunks(rows, final)
    gather.finish()
    scatter.finish()
    for micro in range(MICRO):
        reduce.finish(micro)
    keep_out.wait()
    keep_qkv.wait()
    for i, item in enumerate(sums):
        item.finish(i < n - 1)


def attn_bwd(grad, x, vecs, lse, all_rows, own, kv, mixed_all, w_a, w_out, n_tp, payload, collective_id):
    rows = x.shape[0]
    operands, results, more = reduce_parts(payload)
    pieces = (MICRO, 4, 2, 2, PROMPT_DEV, WIDE)
    return pl.pallas_call(
        functools.partial(attn_bwd_kernel, len(payload)),
        out_shape=(
            jax.ShapeDtypeStruct((rows, D), f32),
            jax.ShapeDtypeStruct((8, D), f32),
            jax.ShapeDtypeStruct((1, 3 * WIDE), f32),
            jax.ShapeDtypeStruct((D, 4 * WIDE), bf16),
        )
        + results,
        in_specs=[IN_VMEM] * 4 + [ANY] * (6 + len(payload)),
        out_specs=(IN_VMEM, IN_VMEM, IN_VMEM) + (ANY,) * (1 + 2 * len(payload)),
        scratch_shapes=[
            pltpu.VMEM((D, 3 * WIDE), bf16),
            pltpu.VMEM((WIDE, D), bf16),
            pltpu.VMEM((n_tp, rows, D), bf16),
            pltpu.VMEM((n_tp, rows, D), bf16),
            pltpu.VMEM((3, MICRO, TOK_DEV, WIDE), bf16),
            pltpu.VMEM((GROUP, MICRO, 2, PROMPT_DEV, WIDE), bf16),
            pltpu.VMEM((MICRO, TOK_DEV, WIDE), bf16),
            pltpu.VMEM(pieces, bf16),
            pltpu.VMEM((MICRO, 4, 2, PROMPT_DEV, WIDE), bf16),
            pltpu.VMEM((MICRO, 4, 2, PROMPT_DEV, WIDE), bf16),
            pltpu.VMEM((MICRO, 3, 2, PROMPT_DEV, WIDE), bf16),
            pltpu.VMEM((2, CONT_LEN, WIDE), bf16),
            pltpu.VMEM((n_tp, rows, 3 * WIDE), bf16),
            pltpu.VMEM((D, 3 * WIDE), bf16),
            pltpu.VMEM((D, WIDE), bf16),
            pltpu.VMEM((KEYS, TOK_DEV), f32),
            pltpu.VMEM((KEYS, TOK_DEV), f32),
            pltpu.VMEM((KEYS, TOK_DEV), bf16),
            pltpu.VMEM((2 * HEAD, TOK_DEV), f32),
        ]
        + scatter_scratch(n_tp, rows)
        + [
            pltpu.SemaphoreType.DMA((8 * MICRO,)),
            pltpu.SemaphoreType.DMA((8 * MICRO,)),
            pltpu.SemaphoreType.DMA((8,)),
        ]
        + more,
        compiler_params=params(collective_id),
        cost_estimate=pl.CostEstimate(flops=2 * 10**11, bytes_accessed=50 * 2**20, transcendentals=0),
    )(grad, x, vecs, lse, all_rows, own, kv, mixed_all, w_a, w_out, *operands)


def forward_layer(x, layer, fetch, vecs, fc_bias, cols, n_tp):
    width = D - HEADS // n_tp * HEAD * (n_tp - 1)
    query_bias, value_bias = (lax.dynamic_slice_in_dim(vecs[i], cols, width) for i in (2, 3))
    biases = widen(jnp.stack([query_bias, jnp.zeros_like(query_bias), value_bias]))
    w_a = fetch.weights[layer, "a"]
    x_mid, lse, all_rows, own, kv, mixed, w_out = fetch.during(
        (layer, "b"), lambda shard: attn_fwd(x, vecs, biases, w_a, n_tp, shard, 5 + layer)
    )
    w_b = fetch.weights[layer, "b"]
    x_next, second_all, hidden_pre, hidden = fetch.during(
        (layer + 1, "a"), lambda shard: ff_fwd(x_mid, vecs, fc_bias[None], w_b, n_tp, shard, 1 + layer)
    )
    mixed_all = heads_joined(lax.all_gather(mixed[:, :, :width], "tp"), n_tp)
    return x_next, (x, w_out, lse, all_rows, own, kv, mixed_all, x_mid, second_all, hidden_pre, hidden)


class Fetch:
    def __init__(self, shards):
        self.staged = lax.axis_size("fsdp") == GROUP
        self.shards, self.weights = shards, {}
        last = None
        for key, shard in shards.items():
            if self.staged:
                if last is None:
                    last = spread_only(shard, 8, 9)
                    self.weights[key] = last.reshape(-1, shard.shape[1])
                continue
            if last is not None:
                shard, _ = lax.optimization_barrier((shard, last))
            whole = lax.all_gather(shard, "fsdp", axis=0, tiled=True)
            self.weights[key] = whole
            last = whole[:8, :128]

    def during(self, key, kernel):
        if not self.staged or key not in self.shards:
            return kernel(None)
        *results, whole = kernel(self.shards[key])
        self.weights[key] = whole.reshape(-1, whole.shape[2])
        return results


def fsdp_sum(part):
    return lax.psum_scatter(part, "fsdp", scatter_dimension=0, tiled=True).astype(f32)


def heads_joined(parts, n_tp):
    step = HEADS // n_tp * HEAD
    return jnp.concatenate([parts[t][..., :step] for t in range(n_tp - 1)] + [parts[n_tp - 1]], axis=-1)


def widen(value, axis=-1):
    pads = [(0, 0)] * value.ndim
    pads[axis] = (0, WIDE - value.shape[axis])
    return jnp.pad(value, pads)


def by_owner(part):
    return part.reshape(4, 2, -1, part.shape[1])


def owned(part, from_y, from_z):
    z, y = lax.axis_index("fsdp") // 2, lax.axis_index("fsdp") % 2
    own = lax.dynamic_index_in_dim(lax.dynamic_index_in_dim(part, z, 0, False), y, 0, False)
    near = lax.dynamic_index_in_dim(from_y, z, 0, False)
    return own.astype(f32) + near.astype(f32) + jnp.sum(from_z.astype(f32), 0)


def with_vectors(grad_qo, ff_sums, attn_sums, col_sums, fc_bias_sums, cols, width):
    def placed(part):
        return lax.dynamic_update_slice_in_dim(jnp.zeros((1, D), f32), part, cols, 1)

    vector_grads = jnp.concatenate(
        [
            attn_sums[:2],
            placed(col_sums[:, :width]),
            placed(col_sums[:, 2 * WIDE : 2 * WIDE + width]),
            attn_sums[4:5],
            ff_sums[5:],
            fc_bias_sums,
        ]
    )
    return lax.dynamic_update_slice(grad_qo, vector_grads.astype(bf16).T, (0, 3 * WIDE + width))


def backward(grad, weights, vecs, saves, cols, n_tp):
    width = D - HEADS // n_tp * HEAD * (n_tp - 1)
    staged = lax.axis_size("fsdp") == GROUP
    done, waiting = {}, {}

    def during(keys, kernel):
        keys = [key for key in keys if key in waiting]
        payload = [waiting.pop(key) for key in keys]
        results = list(kernel(payload))
        if payload:
            arrived = results[-2 * len(payload) :]
            results = results[: -2 * len(payload)]
            for i, key in enumerate(keys):
                done[key] = (payload[i], arrived[2 * i], arrived[2 * i + 1])
        return results

    def produced(key, value):
        if staged:
            waiting[key] = by_owner(value)
        else:
            done[key] = fsdp_sum(value)

    for layer in reversed(range(LAYERS)):
        w_a, w_b = weights[layer, "a"], weights[layer, "b"]
        x, w_out, lse, all_rows, own, kv, mixed_all, x_mid, second_all, hidden_pre, hidden = saves[layer]
        grad, ff_sums, fc_bias_sums, grad_fc, grad_proj = during(
            [(layer + 1, "qo")],
            lambda payload: ff_bwd(
                grad, x_mid, vecs[layer], second_all, hidden_pre, hidden, w_b, n_tp, payload, 10 + layer
            ),
        )
        produced((layer, "proj"), grad_proj)
        produced((layer, "fc"), grad_fc)
        grad, attn_sums, col_sums, grad_qo = during(
            [(layer, "proj"), (layer, "fc")],
            lambda payload: attn_bwd(
                grad, x, vecs[layer], lse, all_rows, own, kv, mixed_all, w_a, w_out, n_tp, payload, 20 + layer
            ),
        )
        produced((layer, "qo"), with_vectors(grad_qo, ff_sums, attn_sums, col_sums, fc_bias_sums, cols, width))
    if staged:
        got = last_sum(waiting[0, "qo"], owned(*done[1, "qo"]).astype(bf16), n_tp, 30)
        return grad, assemble([(got[k],) + done[k, "proj"] + done[k, "fc"] for k in range(LAYERS)])
    outs = []
    for layer in range(LAYERS):
        qo = done[layer, "qo"]
        got = lax.all_gather(qo.astype(bf16), "tp")
        qkv_grad = jnp.concatenate(
            [heads_joined(got[:, :, i * WIDE : i * WIDE + width], n_tp) for i in range(3)], axis=1
        )
        out_grad = heads_joined(got[:, :, 3 * WIDE : 3 * WIDE + width], n_tp)
        vector_sum = jnp.sum(got[:, :, 3 * WIDE + width : 3 * WIDE + width + 8].astype(f32), 0).T
        rest = (vector_sum[v] for v in range(8))
        outs.append((qkv_grad, out_grad, done[layer, "fc"], done[layer, "proj"].T, *rest, qo[:, 3 * WIDE + width + 8]))
    return grad, tuple(jnp.stack(pair).astype(f32) for pair in zip(*outs))


def local(
    tokens,
    qkv_weight,
    query_bias,
    value_bias,
    out_weight,
    out_bias,
    fc_weight,
    fc_bias,
    proj_weight,
    proj_bias,
    first_gain,
    first_bias,
    second_gain,
    second_bias,
    out_grad,
):
    n_tp = lax.axis_size("tp")
    tp = lax.axis_index("tp")
    row_count = tokens.shape[1]
    step = HEADS // n_tp * HEAD
    width = D - step * (n_tp - 1)
    cols = tp * step

    vectors = jnp.stack(
        [first_gain, first_bias, query_bias, value_bias, out_bias, second_gain, second_bias, proj_bias, fc_bias[:, 0]]
    ).reshape(9 * LAYERS, -1)

    shards = {}
    for layer in range(LAYERS):
        sides = [widen(lax.dynamic_slice_in_dim(qkv_weight[layer], cols + i * D, width, 1)) for i in range(3)]
        sides.append(widen(lax.dynamic_slice_in_dim(out_weight[layer], cols, width, 1)))
        if layer == 0:
            sides.append(jnp.pad(vectors.T, ((0, 0), (0, 128 - 9 * LAYERS))))
        shards[layer, "a"] = jnp.concatenate(sides, axis=1)
        fc, proj = fc_weight[layer], proj_weight[layer].T
        more = ((0, 0), (0, lanes_up(fc.shape[1]) - fc.shape[1]))
        shards[layer, "b"] = jnp.concatenate([jnp.pad(fc, more), jnp.pad(proj, more)], axis=1)
    fetch = Fetch(shards)
    vectors = fetch.weights[0, "a"][:, 4 * WIDE : 4 * WIDE + 9 * LAYERS].T.astype(f32).reshape(9, LAYERS, D)

    state = tokens.astype(f32).reshape(MICRO * row_count, D)
    saves = []
    for layer in range(LAYERS):
        state, saved = forward_layer(state, layer, fetch, vectors[:8, layer], vectors[8, layer], cols, n_tp)
        saves.append(saved)
    out_tokens = state.astype(bf16).reshape(tokens.shape)
    grad = out_grad.astype(f32).reshape(MICRO * row_count, D)
    grad, (qkv_g, out_g, fc_g, proj_g, *vec_g) = backward(
        grad, fetch.weights, [vectors[:8, layer] for layer in range(LAYERS)], saves, cols, n_tp
    )
    return (
        out_tokens,
        grad.reshape(tokens.shape),
        qkv_g,
        vec_g[2],
        vec_g[3],
        out_g,
        vec_g[4],
        fc_g,
        vec_g[8][:, None],
        proj_g,
        vec_g[7],
        vec_g[0],
        vec_g[1],
        vec_g[5],
        vec_g[6],
    )


def solution(mesh):
    rows = P(None, ("fsdp", "tp"), None)
    weight = P(None, "fsdp", None)
    vector = P(None, "fsdp")
    fc_in = P(None, "fsdp", "tp")
    hidden = P(None, "tp", "fsdp")
    in_specs = (
        rows, weight, vector, vector, weight, vector, fc_in, hidden, hidden,
        vector, vector, vector, vector, vector, rows,
    )
    out_specs = (
        rows, rows, weight, vector, vector, weight, vector, fc_in, hidden, hidden,
        vector, vector, vector, vector, vector,
    )
    return jax.shard_map(local, mesh=mesh, in_specs=in_specs, out_specs=out_specs, check_vma=False)
```

```python
import functools

import jax
import jax.numpy as jnp
from jax import lax
from jax.experimental import pallas as pl
from jax.experimental.pallas import tpu as pltpu
from jax.sharding import PartitionSpec as P

D = 1600
HEADS = 25
HEAD = 64
GROUP = 8
PROMPT_DEV = 128
CONT_LEN = 256
TOK_DEV = 384
MICRO = 2
LAYERS = 2
PROMPT = 1024
KEYS = PROMPT + CONT_LEN
CHUNK = 128

f32 = jnp.float32
bf16 = jnp.bfloat16
norm_eps = 1e-05
NN = (((1,), (0,)), ((), ()))
NT = (((1,), (1,)), ((), ()))
TN = (((0,), (0,)), ((), ()))


def mm(left, right, dims=NN):
    return lax.dot_general(left, right, dims, preferred_element_type=f32)


def gelu_tanh(value):
    return jax.nn.gelu(value, approximate=True)


MESH = pl.DeviceIdType.MESH
ANY = pl.BlockSpec(memory_space=pl.ANY)
IN_VMEM = pl.BlockSpec(memory_space=pltpu.VMEM)
TILE = 512
ROW_CHUNK = 32


class Peers:
    def __init__(self):
        self.f = lax.axis_index("fsdp")
        self.t = lax.axis_index("tp")
        x, c = self.t // 2, self.t % 2
        self.x = x
        self.core = 2 * x + 1 - c
        self.over = 2 * (1 - x) + c
        self.diag = 2 * (1 - x) + 1 - c

    def greet(self):
        barrier = pltpu.get_barrier_semaphore()
        for t in (self.core, self.over):
            pl.semaphore_signal(barrier, inc=1, device_id=(self.f, t), device_id_type=MESH)
        pl.semaphore_wait(barrier, 2)

    def copy(self, source, target, sems, index, t):
        return pltpu.make_async_remote_copy(
            src_ref=source,
            dst_ref=target,
            send_sem=sems[0].at[index],
            recv_sem=sems[1].at[index],
            device_id=(self.f, t),
            device_id_type=MESH,
        )


class Gather:
    def __init__(self, peers, buf, sems):
        self.p, self.buf, self.sems = peers, buf, sems

    def piece(self, slot, index, t):
        return self.p.copy(self.buf.at[slot], self.buf.at[slot], self.sems, index, t)

    def start(self):
        p = self.p
        self.piece(p.t, 1, p.over).start()
        self.piece(p.t, 0, p.core).start()

    def wait_chip(self):
        self.piece(self.p.core, 0, self.p.core).wait_recv()

    def relay(self):
        p = self.p
        self.piece(p.over, 1, p.over).wait_recv()
        self.piece(p.over, 2, p.core).start()

    def wait_diag(self):
        self.piece(self.p.diag, 2, self.p.core).wait_recv()

    def finish(self):
        p = self.p
        self.piece(p.t, 1, p.over).wait_send()
        self.piece(p.t, 0, p.core).wait_send()
        self.piece(p.over, 2, p.core).wait_send()


class Scatter:
    def __init__(self, peers, part, from_core, over_out, from_over, sems):
        self.p, self.part, self.sems = peers, part, sems
        self.from_core, self.over_out, self.from_over = from_core, over_out, from_over

    def far_to_core(self):
        return self.p.copy(self.part.at[self.p.diag], self.from_core.at[0], self.sems, 3, self.p.core)

    def near_to_core(self):
        return self.p.copy(self.part.at[self.p.core], self.from_core.at[1], self.sems, 4, self.p.core)

    def to_over(self):
        return self.p.copy(self.over_out, self.from_over, self.sems, 5, self.p.over)

    def send_over(self):
        self.far_to_core().wait_recv()

        @pl.loop(0, self.over_out.shape[0] // ROW_CHUNK)
        def _(i):
            at = pl.ds(pl.multiple_of(i * ROW_CHUNK, ROW_CHUNK), ROW_CHUNK)
            total = self.part[self.p.over, at, :].astype(f32) + self.from_core[0, at, :].astype(f32)
            self.over_out[at, :] = total.astype(bf16)

        self.to_over().start()

    def wait(self):
        self.near_to_core().wait_recv()
        self.to_over().wait_recv()

    def rows(self, at):
        return (
            self.part[self.p.t, at, :].astype(f32)
            + self.from_core[1, at, :].astype(f32)
            + self.from_over[at, :].astype(f32)
        )

    def finish(self):
        for copy in (self.far_to_core(), self.near_to_core(), self.to_over()):
            copy.wait_send()


class Group:
    def __init__(self):
        f = lax.axis_index("fsdp")
        self.t = lax.axis_index("tp")
        self.member = f % GROUP
        self.base = f - self.member
        self.z, self.y = self.member // 2, self.member % 2

    def at(self, z, y):
        return z * 2 + y

    def ahead(self, k):
        return (self.z + k) % 4

    def behind(self, k):
        return (self.z + 4 - k) % 4

    def greet_group(self):
        barrier = pltpu.get_barrier_semaphore()
        others = [self.at(self.z, 1 - self.y)] + [self.at(self.ahead(k), self.y) for k in (1, 2, 3)]
        for member in others:
            pl.semaphore_signal(
                barrier, inc=1, device_id=(self.base + member, self.t), device_id_type=MESH
            )
        pl.semaphore_wait(barrier, 4)

    def greet(self, peers, with_diag=False):
        barrier = pltpu.get_barrier_semaphore()
        others = [self.at(self.z, 1 - self.y)] + [self.at(self.ahead(k), self.y) for k in (1, 2, 3)]
        for member in others:
            pl.semaphore_signal(
                barrier, inc=1, device_id=(self.base + member, self.t), device_id_type=MESH
            )
        near = [peers.core, peers.over] + [peers.diag] * with_diag
        for t in near:
            pl.semaphore_signal(barrier, inc=1, device_id=(peers.f, t), device_id_type=MESH)
        pl.semaphore_wait(barrier, 4 + len(near))

    def copy(self, source, target, sems, index, member):
        return pltpu.make_async_remote_copy(
            src_ref=source,
            dst_ref=target,
            send_sem=sems[0].at[index],
            recv_sem=sems[1].at[index],
            device_id=(self.base + member, self.t),
            device_id_type=MESH,
        )


class Reduce:
    def __init__(self, group, source, from_y, from_z, sems, tiles, columns=None):
        self.g, self.sems, self.columns = group, sems, columns
        self.source, self.from_y, self.from_z = source, from_y, from_z
        self.own, self.got, self.gone, self.local = tiles

    def cut(self, ref, *index):
        if self.columns is None:
            return ref.at[index]
        return ref.at[index + (slice(None), self.columns)]

    def across(self, j):
        g = self.g
        z = g.ahead(j)
        return g.copy(
            self.cut(self.source, z, 1 - g.y), self.cut(self.from_y, z), self.sems, j, g.at(g.z, 1 - g.y)
        )

    def along(self, j):
        g = self.g
        source, target = self.cut(self.gone, j - 1), self.cut(self.from_z, j - 1)
        return g.copy(source, target, self.sems, 3 + j, g.at(g.ahead(j), g.y))

    def start(self, *pieces):
        for j in pieces:
            self.across(j).start()

    def pump(self, j, before=None, then=None):
        g = self.g
        own, got = (self.own, self.got) if self.columns is None else (self.cut(self.own), self.cut(self.got))
        load_own = pltpu.make_async_copy(self.cut(self.source, g.ahead(j), g.y), own, self.local.at[0])
        load_own.start()
        self.across(j).wait_recv()
        if then is not None:
            then()
        load_got = pltpu.make_async_copy(self.cut(self.from_y, g.ahead(j)), got, self.local.at[1])
        load_got.start()
        load_own.wait()
        load_got.wait()
        if before is not None:
            before.along(j).wait_send()
        columns = slice(None) if self.columns is None else self.columns
        self.gone[j - 1, :, columns] = self.own[:, columns] + self.got[:, columns]
        self.along(j).start()

    def finish(self, reused=False):
        self.across(0).wait_recv()
        for j in range(4):
            self.across(j).wait_send()
        for j in (1, 2, 3):
            self.along(j).wait_recv()
            if not reused:
                self.along(j).wait_send()


def reduce_parts(payload):
    results, scratch = (), []
    for part in payload:
        rows = part.shape[2:]
        results += (jax.ShapeDtypeStruct((4,) + rows, bf16), jax.ShapeDtypeStruct((3,) + rows, bf16))
    scratch += [pltpu.SemaphoreType.DMA((7,))] * (2 * max(2, len(payload)) if payload else 0)
    if payload:
        scratch += [pltpu.VMEM(rows, bf16), pltpu.VMEM(rows, bf16), pltpu.VMEM((3,) + rows, bf16)]
        scratch += [pltpu.SemaphoreType.DMA((2,))]
    return tuple(payload), results, scratch


def reduces(group, sources, results, scratch):
    tiles = scratch[4:]
    if len(sources) == 1:
        middle, end = sources[0].shape[3] // 2, sources[0].shape[3]
        halves = (slice(0, middle), slice(middle, end))
        return [
            Reduce(group, sources[0], *results, scratch[2 * n : 2 * n + 2], tiles, columns)
            for n, columns in enumerate(halves)
        ]
    return [
        Reduce(group, source, results[2 * n], results[2 * n + 1], scratch[2 * n : 2 * n + 2], tiles)
        for n, source in enumerate(sources)
    ]


def in_turn(items):
    order = [(item, j) for item in items for j in (1, 2, 3)] + [(item, 0) for item in items]

    def step(n):
        item, j = order[n]
        item.pump(j, then=lambda: order[n + 1][0].start(order[n + 1][1]))

    steps = [functools.partial(step, n) for n in range(3 * len(items))]
    return [lambda: items[0].start(1)] + steps + [lambda item=item: item.start(0) for item in items[1:]]


class BlockGather:
    def __init__(self, peers, source, target, sems, first, local):
        self.p, self.source, self.target, self.sems, self.first = peers, source, target, sems, first
        self.local = local

    def piece(self, slot, index, to, own=False):
        target = self.target.at[slot]
        return self.p.copy(self.source if own else target, target, self.sems, self.first + index, to)

    def keep(self):
        return pltpu.make_async_copy(self.source, self.target.at[self.p.t], self.local)

    def start(self):
        p = self.p
        self.piece(p.t, 1, p.over, True).start()
        self.piece(p.t, 0, p.core, True).start()
        self.keep().start()

    def relay(self):
        p = self.p
        self.piece(p.over, 1, p.over).wait_recv()
        self.piece(p.over, 2, p.core).start()

    def finish(self):
        p = self.p
        self.piece(p.core, 0, p.core).wait_recv()
        self.piece(p.diag, 2, p.core).wait_recv()
        self.piece(p.t, 1, p.over, True).wait_send()
        self.piece(p.t, 0, p.core, True).wait_send()
        self.piece(p.over, 2, p.core).wait_send()
        self.keep().wait()


def add_up(own, others, target):
    rows = own.shape[0]
    for first in range(0, rows, 40):
        at = slice(first, min(first + 40, rows))
        total = own[at, :].astype(f32)
        for other in others:
            total = total + other[at, :].astype(f32)
        target[at, :] = total.astype(target.dtype)


def last_sum_kernel(source, earlier, from_y, from_z, got, got_earlier, *scratch):
    p, g = Peers(), Group()
    scratch, (bsend, brecv, blocal, mine) = scratch[:-4], scratch[-4:]
    own, near, gone, local = scratch[4:]
    before = BlockGather(p, earlier, got_earlier, (bsend, brecv), 0, blocal.at[0])
    after = BlockGather(p, mine, got, (bsend, brecv), 3, blocal.at[1])
    items = reduces(g, [source], [from_y, from_z], scratch)
    steps = in_turn(items)
    g.greet(p)
    steps[0]()
    before.start()
    for n, step in enumerate(steps[1:]):
        if n == 3:
            before.relay()
        step()
    for item in items:
        item.finish()
    loads = [
        pltpu.make_async_copy(source.at[g.z, g.y], own, local.at[0]),
        pltpu.make_async_copy(from_y.at[g.z], near, local.at[1]),
        pltpu.make_async_copy(from_z, gone, blocal.at[2]),
    ]
    for load in loads:
        load.start()
    for load in loads:
        load.wait()
    add_up(own, [near] + [gone.at[k] for k in range(3)], mine)
    after.start()
    before.finish()
    after.relay()
    after.finish()


def last_sum(part, earlier, n_tp, collective_id):
    operands, results, scratch = reduce_parts([part])
    whole = jax.ShapeDtypeStruct((n_tp,) + earlier.shape, bf16)
    _, _, got, got_earlier = pl.pallas_call(
        last_sum_kernel,
        out_shape=results + (whole, whole),
        in_specs=[ANY, ANY],
        out_specs=(ANY,) * 4,
        scratch_shapes=scratch
        + [pltpu.SemaphoreType.DMA((6,))] * 2
        + [pltpu.SemaphoreType.DMA((3,)), pltpu.VMEM(earlier.shape, bf16)],
        compiler_params=params(collective_id),
    )(part, earlier)
    return got, got_earlier


def assemble_kernel(*refs):
    inputs, refs = refs[: 7 * LAYERS], refs[7 * LAYERS :]
    qkv_ref, out_ref, fc_ref, proj_ref = refs[:4]
    vector_refs, (tiles, sems) = refs[4:13], refs[13:]
    t, f = lax.axis_index("tp"), lax.axis_index("fsdp")
    z, y = f // 2, f % 2
    loads = []
    for layer in range(LAYERS):
        for w in range(2):
            part, near, far = inputs[7 * layer + 1 + 3 * w : 7 * layer + 4 + 3 * w]
            n = 2 * layer + w
            loads.append(
                [
                    pltpu.make_async_copy(part.at[z, y], tiles.at[n, 0], sems.at[n, 0]),
                    pltpu.make_async_copy(near.at[z], tiles.at[n, 1], sems.at[n, 1]),
                    pltpu.make_async_copy(far, tiles.at[n, 2:5], sems.at[n, 2]),
                ]
            )
    for load in sum(loads, []):
        load.start()
    n_tp = inputs[0].shape[0]
    step = HEADS // n_tp * HEAD
    width = D - step * (n_tp - 1)
    counts = [step] * (n_tp - 1) + [width]
    for layer in range(LAYERS):
        got = inputs[7 * layer]
        for i in range(3):
            for k, count in enumerate(counts):
                value = got[k, :, i * WIDE : i * WIDE + count].astype(f32)
                qkv_ref[layer, :, i * D + k * step : i * D + k * step + count] = value
        for k, count in enumerate(counts):
            out_ref[layer, :, k * step : k * step + count] = got[k, :, 3 * WIDE : 3 * WIDE + count].astype(f32)
        extra = got[:, :, 3 * WIDE + step : 4 * WIDE].astype(f32)
        total = jnp.sum(extra, axis=0).T
        own = got[t, :, 3 * WIDE + step : 4 * WIDE].astype(f32).T
        skip = width - step
        for v in range(8):
            vector_refs[v][layer : layer + 1, :] = total[skip + v : skip + v + 1, :]
        vector_refs[8][layer : layer + 1, :] = own[skip + 8 : skip + 9, :]
        for w in range(2):
            n = 2 * layer + w
            for load in loads[n]:
                load.wait()
            total = tiles[n, 0].astype(f32)
            for k in range(1, 5):
                total = total + tiles[n, k].astype(f32)
            if w:
                fc_ref[layer] = total
            else:
                proj_ref[layer] = total.T


def assemble(layers):
    rows, width = layers[0][1].shape[2:]
    outs = [(LAYERS, rows, 3 * D), (LAYERS, rows, D), (LAYERS, rows, width), (LAYERS, width, rows)]
    outs += [(LAYERS, rows)] * 9
    return pl.pallas_call(
        assemble_kernel,
        out_shape=tuple(jax.ShapeDtypeStruct(o, f32) for o in outs),
        in_specs=([IN_VMEM] + [ANY] * 6) * LAYERS,
        out_specs=(IN_VMEM,) * len(outs),
        scratch_shapes=[
            pltpu.VMEM((2 * LAYERS, 5, rows, width), bf16),
            pltpu.SemaphoreType.DMA((2 * LAYERS, 3)),
        ],
        compiler_params=pltpu.CompilerParams(vmem_limit_bytes=60 * 2**20),
    )(*sum((list(layer) for layer in layers), []))


class Spread:
    def __init__(self, group, source, target, sems, chunks):
        self.g, self.source, self.target, self.sems = group, source, target, sems
        count = source.shape[1] // 128
        ends = [128 * (count * sum(chunks[: c + 1]) // sum(chunks)) for c in range(len(chunks))]
        self.columns = [slice(a, b) for a, b in zip([0] + ends, ends)]
        self.partner = group.at(group.z, 1 - group.y)

    def piece(self, member, c, index, to, own=False):
        target = self.target.at[member, :, self.columns[c]]
        source = self.source.at[:, self.columns[c]] if own else target
        return self.g.copy(source, target, self.sems, 7 * c + index, to)

    def own(self, c):
        g = self.g
        return [self.piece(g.member, c, k, g.at(g.ahead(k), g.y), True) for k in (1, 2, 3)] + [
            self.piece(g.member, c, 0, self.partner, True)
        ]

    def relayed(self, c):
        g = self.g
        return [self.piece(g.at(g.behind(k), g.y), c, 3 + k, self.partner) for k in (1, 2, 3)]

    def keep(self):
        return pltpu.make_async_copy(
            self.source, self.target.at[self.g.member], self.sems[0].at[7 * len(self.columns)]
        )

    def start(self, first=0, last=None):
        if first == 0:
            self.keep().start()
        for c in range(len(self.columns))[first:last]:
            for copy in self.own(c):
                copy.start()

    def relay(self, c):
        g = self.g
        for k, copy in zip((1, 2, 3), self.relayed(c)):
            self.piece(g.at(g.behind(k), g.y), c, k, self.partner).wait_recv()
            copy.start()

    def finish(self):
        g = self.g
        for c in range(len(self.columns)):
            self.piece(self.partner, c, 0, self.partner).wait_recv()
            for k in (1, 2, 3):
                self.piece(g.at(g.behind(k), 1 - g.y), c, 3 + k, self.partner).wait_recv()
            for copy in self.own(c) + self.relayed(c):
                copy.wait_send()
        self.keep().wait()


def spread_parts(shard, chunks):
    if shard is None:
        return (), (), []
    whole = jax.ShapeDtypeStruct((GROUP,) + shard.shape, shard.dtype)
    return (shard,), (whole,), [pltpu.SemaphoreType.DMA((7 * len(chunks) + 1,))] * 2


def spread_kernel(chunks, source, target, send, recv):
    g = Group()
    g.greet_group()
    spread = Spread(g, source, target, (send, recv), chunks)
    spread.start(0, 2)
    for c in range(len(chunks)):
        spread.relay(c)
        spread.start(c + 2, c + 3)
    spread.finish()


def spread_only(shard, chunks, collective_id):
    operands, results, scratch = spread_parts(shard, chunks)
    return pl.pallas_call(
        functools.partial(spread_kernel, chunks),
        out_shape=results[0],
        in_specs=[ANY],
        out_specs=ANY,
        scratch_shapes=scratch,
        compiler_params=params(collective_id),
    )(shard)


def row_chunks(rows, body):
    @pl.loop(0, rows // ROW_CHUNK)
    def _(i):
        body(pl.ds(pl.multiple_of(i * ROW_CHUNK, ROW_CHUNK), ROW_CHUNK))


def tiles(extent, body):
    whole = extent // TILE

    @pl.loop(0, whole)
    def _(i):
        body(pl.ds(pl.multiple_of(i * TILE, TILE), TILE))

    if extent % TILE:
        body(pl.ds(whole * TILE, extent % TILE))


def pair_rows(ref, x):
    both = ref[pl.ds(2 * x, 2)]
    return both.reshape(2 * both.shape[1], both.shape[2])


def put_pair(ref, x, at, value):
    ref[pl.ds(2 * x, 2), :, at] = value.reshape(2, value.shape[0] // 2, value.shape[1]).astype(ref.dtype)


def norm_stats(x):
    centred = x - jnp.mean(x, -1, keepdims=True)
    scale = lax.rsqrt(jnp.mean(centred * centred, -1, keepdims=True) + norm_eps)
    return centred * scale, scale


def lanes_up(width):
    return -(-width // 128) * 128


def proj_part(w_b, width):
    return w_b.at[:, lanes_up(width) :]


FIRST_CHUNKS = (3, 3, 3, 3, 3, 2)
FF_CHUNKS = (5, 5, 4, 2)
ATTN_CHUNKS = (5, 6, 6, 5, 4)


def ff_fwd_kernel(n, *refs):
    x_ref, vec_ref, fcb_ref, wb_hbm = refs[:4]
    shard, refs = refs[4 : 4 + n], refs[4 + n :]
    out_ref, all_hbm, pre_hbm, hid_hbm = refs[:4]
    whole, refs = refs[4 : 4 + n], refs[4 + n :]
    wfc, wproj, buf, pre, hid, part, from_core, over_out, from_over, send, recv, local = refs[:12]
    p, g = Peers(), Group()
    spread = Spread(g, shard[0], whole[0], refs[12:], FF_CHUNKS) if n else None
    rows = x_ref.shape[0]
    sems = (send, recv)
    gather = Gather(p, buf, sems)
    scatter = Scatter(p, part, from_core, over_out, from_over, sems)
    width = fcb_ref.shape[1]
    load_fc = pltpu.make_async_copy(wb_hbm.at[:, : wfc.shape[1]], wfc, local.at[0])
    load_proj = pltpu.make_async_copy(proj_part(wb_hbm, width), wproj, local.at[1])
    load_fc.start()
    load_proj.start()

    def norm(at):
        hat, _ = norm_stats(x_ref[at, :])
        buf[p.t, at, :] = (hat * vec_ref[5:6, :] + vec_ref[6:7, :]).astype(bf16)

    row_chunks(rows, norm)
    if n:
        g.greet(p)
    else:
        p.greet()
    gather.start()
    if n:
        spread.start(0, 1)
    gather.wait_chip()
    load_fc.wait()

    def up(x):
        def tile(at):
            value = mm(pair_rows(buf, x), wfc[:, at]) + fcb_ref[:, at]
            put_pair(pre, x, at, value)
            put_pair(hid, x, at, gelu_tanh(value))

        tiles(width, tile)

    def down(x):
        def tile(at):
            put_pair(part, x, at, mm(pair_rows(hid, x), wproj[at, :width], NT))

        tiles(D, tile)

    up(p.x)
    if n:
        spread.start(1, 2)
    gather.relay()
    gather.wait_diag()
    if n:
        spread.relay(0)
    keep_all = pltpu.make_async_copy(buf, all_hbm, local.at[2])
    keep_all.start()
    up(1 - p.x)
    keep_pre = pltpu.make_async_copy(pre, pre_hbm, local.at[3])
    keep_hid = pltpu.make_async_copy(hid, hid_hbm, local.at[4])
    keep_pre.start()
    keep_hid.start()
    load_proj.wait()
    down(1 - p.x)
    scatter.far_to_core().start()
    scatter.send_over()
    if n:
        spread.start(2, 3)
    down(p.x)
    scatter.near_to_core().start()
    if n:
        spread.relay(1)
        spread.start(3)
    scatter.wait()

    def final(at):
        out_ref[at, :] = x_ref[at, :] + scatter.rows(at) + vec_ref[7:8, :]

    row_chunks(rows, final)
    if n:
        spread.relay(2)
        spread.relay(3)
    gather.finish()
    scatter.finish()
    for copy in (keep_all, keep_pre, keep_hid):
        copy.wait()
    if n:
        spread.finish()


def scatter_scratch(n_tp, rows):
    return [
        pltpu.VMEM((n_tp, rows, D), bf16),
        pltpu.VMEM((2, rows, D), bf16),
        pltpu.VMEM((rows, D), bf16),
        pltpu.VMEM((rows, D), bf16),
        pltpu.SemaphoreType.DMA((6,)),
        pltpu.SemaphoreType.DMA((6,)),
    ]


def params(collective_id):
    return pltpu.CompilerParams(collective_id=collective_id, has_side_effects=True, vmem_limit_bytes=60 * 2**20)


def ff_fwd(x, vecs, fc_bias, w_b, n_tp, shard, collective_id):
    rows, width = x.shape[0], fc_bias.shape[1]
    block = (n_tp, rows)
    operands, results, sems = spread_parts(shard, FF_CHUNKS)
    return pl.pallas_call(
        functools.partial(ff_fwd_kernel, len(operands)),
        out_shape=(
            jax.ShapeDtypeStruct((rows, D), f32),
            jax.ShapeDtypeStruct(block + (D,), bf16),
            jax.ShapeDtypeStruct(block + (width,), f32),
            jax.ShapeDtypeStruct(block + (width,), bf16),
        )
        + results,
        in_specs=[IN_VMEM, IN_VMEM, IN_VMEM, ANY] + [ANY] * len(operands),
        out_specs=(IN_VMEM, ANY, ANY, ANY) + (ANY,) * len(operands),
        scratch_shapes=[
            pltpu.VMEM((D, lanes_up(width)), bf16),
            pltpu.VMEM((D, lanes_up(width)), bf16),
            pltpu.VMEM(block + (D,), bf16),
            pltpu.VMEM(block + (width,), f32),
            pltpu.VMEM(block + (width,), bf16),
        ]
        + scatter_scratch(n_tp, rows)
        + [pltpu.SemaphoreType.DMA((5,))]
        + sems,
        compiler_params=params(collective_id),
        cost_estimate=pl.CostEstimate(
            flops=4 * n_tp * rows * D * width, bytes_accessed=40 * 2**20, transcendentals=n_tp * rows * width
        ),
    )(x, vecs, fc_bias, w_b, *operands)


def gelu_slope(u):
    a = 0.7978845608028654
    square = u * u
    t = jnp.tanh(a * (u + 0.044715 * u * square))
    return 0.5 * (1.0 + t) + 0.5 * u * (1.0 - t * t) * (a * (1.0 + 3 * 0.044715 * square))


def norm_back(x, dy, gain):
    hat, scale = norm_stats(x)
    d_hat = dy * gain
    inner = d_hat - jnp.mean(d_hat, -1, keepdims=True) - hat * jnp.mean(d_hat * hat, -1, keepdims=True)
    return scale * inner, dy * hat


def add_rows(ref, row, value):
    ref[row : row + 1, :] += jnp.sum(value, axis=0, keepdims=True)


def ff_bwd_kernel(n, *refs):
    g_ref, x_ref, vec_ref, all_hbm, pre_hbm, hid_hbm, wb_hbm = refs[:7]
    sources, refs = refs[7 : 7 + n], refs[7 + n :]
    out_ref, sums_ref, fcb_ref, dfc_hbm, dproj_hbm = refs[:5]
    results, refs = refs[5 : 5 + 2 * n], refs[5 + 2 * n :]
    wfc, wproj, buf, other, pre, dpre, stage, part, from_core, over_out, from_over, send, recv, local = refs[:14]
    p, g = Peers(), Group()
    sums = reduces(g, sources, results, refs[14:])
    rows = x_ref.shape[0]
    n_tp, width = buf.shape[0], fcb_ref.shape[1]
    sems = (send, recv)
    gather = Gather(p, buf, sems)
    scatter = Scatter(p, part, from_core, over_out, from_over, sems)
    load_proj = pltpu.make_async_copy(proj_part(wb_hbm, width), wproj, local.at[0])
    load_pre = pltpu.make_async_copy(pre_hbm, pre, local.at[1])
    load_fc = pltpu.make_async_copy(wb_hbm.at[:, : wfc.shape[1]], wfc, local.at[2])
    load_other = pltpu.make_async_copy(hid_hbm, other, local.at[3])
    for copy in (load_proj, load_pre, load_fc, load_other):
        copy.start()
    sums_ref[...] = jnp.zeros_like(sums_ref)
    fcb_ref[...] = jnp.zeros_like(fcb_ref)

    def lower(at):
        low = g_ref[at, :].astype(bf16)
        buf[p.t, at, :] = low
        add_rows(sums_ref, 7, low.astype(f32))

    row_chunks(rows, lower)
    if n:
        g.greet(p)
    else:
        p.greet()
    gather.start()
    steps = in_turn(sums) if n else []

    def advance():
        if steps:
            steps.pop(0)()

    advance()
    gather.wait_chip()
    load_proj.wait()
    load_pre.wait()

    def through(x):
        def tile(at):
            d_hidden = mm(pair_rows(buf, x), wproj[:, at])
            u = pre[pl.ds(2 * x, 2), :, at].reshape(2 * rows, -1)
            low = (gelu_slope(u) * d_hidden).astype(bf16)
            put_pair(dpre, x, at, low)
            fcb_ref[:, at] += jnp.sum(low.astype(f32), axis=0, keepdims=True)

        tiles(width, tile)

    def down(x):
        def tile(at):
            put_pair(part, x, at, mm(pair_rows(dpre, x), wfc[at, :width], NT))

        tiles(D, tile)

    through(p.x)
    gather.relay()
    advance()
    gather.wait_diag()
    through(1 - p.x)
    advance()
    load_fc.wait()
    down(1 - p.x)
    scatter.far_to_core().start()
    scatter.send_over()
    advance()
    down(p.x)
    scatter.near_to_core().start()
    advance()

    def outer(left, right, target, sem):
        whole = D // TILE
        rest = D - whole * TILE
        flat = right[...].reshape(n_tp * rows, width)

        def tile(i, size):
            at = pl.ds(pl.multiple_of(i * TILE, TILE), size)
            value = mm(left[:, :, at].reshape(n_tp * rows, size), flat, TN)
            stage[at, :] = value.astype(bf16)

        @pl.loop(0, whole)
        def _(i):
            tile(i, TILE)

        if rest:
            tile(whole, rest)
        return pltpu.make_async_copy(stage, target, sem)

    load_other.wait()
    store = outer(buf, other, dproj_hbm, local.at[4])
    store.start()
    gather.finish()
    load_all = pltpu.make_async_copy(all_hbm, buf, local.at[5])
    load_all.start()
    advance()
    scatter.wait()

    def final(at):
        dy = scatter.rows(at)
        dx, d_gain = norm_back(x_ref[at, :], dy, vec_ref[5:6, :])
        add_rows(sums_ref, 5, d_gain)
        add_rows(sums_ref, 6, dy)
        out_ref[at, :] = g_ref[at, :] + dx

    row_chunks(rows, final)
    load_all.wait()
    store.wait()
    store = outer(buf, dpre, dfc_hbm, local.at[6])
    store.start()
    while steps:
        advance()
    scatter.finish()
    store.wait()
    for item in sums:
        item.finish()


def ff_bwd(grad, x, vecs, all_rows, pre, hidden, w_b, n_tp, payload, collective_id):
    rows, width = x.shape[0], pre.shape[2]
    block = (n_tp, rows)
    operands, results, more = reduce_parts(payload)
    return pl.pallas_call(
        functools.partial(ff_bwd_kernel, len(payload)),
        out_shape=(
            jax.ShapeDtypeStruct((rows, D), f32),
            jax.ShapeDtypeStruct((8, D), f32),
            jax.ShapeDtypeStruct((1, width), f32),
            jax.ShapeDtypeStruct((D, width), bf16),
            jax.ShapeDtypeStruct((D, width), bf16),
        )
        + results,
        in_specs=[IN_VMEM] * 3 + [ANY] * (4 + len(payload)),
        out_specs=(IN_VMEM, IN_VMEM, IN_VMEM) + (ANY,) * (2 + 2 * len(payload)),
        scratch_shapes=[
            pltpu.VMEM((D, lanes_up(width)), bf16),
            pltpu.VMEM((D, lanes_up(width)), bf16),
            pltpu.VMEM(block + (D,), bf16),
            pltpu.VMEM(block + (width,), bf16),
            pltpu.VMEM(block + (width,), f32),
            pltpu.VMEM(block + (width,), bf16),
            pltpu.VMEM((D, width), bf16),
        ]
        + scatter_scratch(n_tp, rows)
        + [pltpu.SemaphoreType.DMA((7,))]
        + more,
        compiler_params=params(collective_id),
        cost_estimate=pl.CostEstimate(
            flops=8 * n_tp * rows * D * width, bytes_accessed=50 * 2**20, transcendentals=n_tp * rows * width
        ),
    )(grad, x, vecs, all_rows, pre, hidden, w_b, *operands)


HALVES = [(micro, half) for micro in range(MICRO) for half in range(2)]


def half_lanes(half):
    return slice(half * WIDE // 2, (half + 1) * WIDE // 2)


class Share:
    def __init__(self, group, kv, sems):
        self.g, self.kv, self.sems = group, kv, sems
        self.partner = group.at(group.z, 1 - group.y)

    def piece(self, member, part, index, to):
        micro, half = part
        ref = self.kv.at[member, micro, :, :, half_lanes(half)]
        return self.g.copy(ref, ref, self.sems, (2 * micro + half) * 7 + index, to)

    def own(self, part):
        g = self.g
        return [self.piece(g.member, part, 0, self.partner)] + [
            self.piece(g.member, part, k, g.at(g.ahead(k), g.y)) for k in (1, 2, 3)
        ]

    def relayed(self, part):
        g = self.g
        return [self.piece(g.at(g.behind(k), g.y), part, 3 + k, self.partner) for k in (1, 2, 3)]

    def start(self, *part):
        for copy in self.own(part):
            copy.start()

    def relay(self, *part):
        g = self.g
        for k, copy in zip((1, 2, 3), self.relayed(part)):
            self.piece(g.at(g.behind(k), g.y), part, k, self.partner).wait_recv()
            copy.start()

    def wait(self, *part):
        g = self.g
        self.piece(self.partner, part, 0, self.partner).wait_recv()
        for k in (1, 2, 3):
            self.piece(g.at(g.behind(k), 1 - g.y), part, 3 + k, self.partner).wait_recv()

    def finish(self):
        for part in HALVES:
            for copy in self.own(part) + self.relayed(part):
                copy.wait_send()


class GroupSum:
    def __init__(self, group, parts, from_y, to_z, from_z, sems):
        self.g, self.parts, self.sems = group, parts, sems
        self.from_y, self.to_z, self.from_z = from_y, to_z, from_z

    def across(self, micro, half):
        g, lanes = self.g, half_lanes(half)
        return g.copy(
            self.parts.at[micro, :, 1 - g.y, :, :, lanes],
            self.from_y.at[micro, :, :, :, lanes],
            self.sems,
            (2 * micro + half) * 4,
            g.at(g.z, 1 - g.y),
        )

    def along(self, micro, half, k):
        g, lanes = self.g, half_lanes(half)
        to = g.ahead(k)
        return g.copy(
            self.to_z.at[micro, to, :, :, lanes],
            self.from_z.at[micro, k - 1, :, :, lanes],
            self.sems,
            (2 * micro + half) * 4 + k,
            g.at(to, g.y),
        )

    def start(self, micro, half):
        self.across(micro, half).start()

    def turn(self, micro, half):
        lanes = half_lanes(half)
        self.across(micro, half).wait_recv()

        @pl.loop(0, 4)
        def _(z):
            for kv in range(2):
                total = self.parts[micro, z, self.g.y, kv, :, lanes] + self.from_y[micro, z, kv, :, lanes]
                self.to_z[micro, z, kv, :, lanes] = total

        for k in (1, 2, 3):
            self.along(micro, half, k).start()

    def wait(self, micro):
        for half in range(2):
            for k in (1, 2, 3):
                self.along(micro, half, k).wait_recv()

    def total(self, micro, kv):
        g = self.g
        value = self.parts[micro, g.z, g.y, kv].astype(f32) + self.from_y[micro, g.z, kv].astype(f32)
        for k in range(3):
            value = value + self.from_z[micro, k, kv].astype(f32)
        return value.astype(bf16)

    def finish(self, micro):
        for half in range(2):
            self.across(micro, half).wait_send()
            for k in (1, 2, 3):
                self.along(micro, half, k).wait_send()


WIDE = 512
HEAD_PAIRS = WIDE // (2 * HEAD)
PROMPT_CHUNKS = PROMPT // CHUNK
CONT_CHUNKS = CONT_LEN // CHUNK


def chunk_at(c, base=0):
    return pl.ds(pl.multiple_of(base + c * CHUNK, CHUNK), CHUNK)


def key_limit(member):
    row = lax.broadcasted_iota(jnp.int32, (1, TOK_DEV), 1)
    return jnp.where(row < PROMPT_DEV, member * PROMPT_DEV + row, PROMPT - PROMPT_DEV + row)


def half_of(value, half):
    lane = lax.broadcasted_iota(jnp.int32, value.shape, 1)
    return jnp.where((lane >= HEAD * half) & (lane < HEAD * (half + 1)), value, jnp.zeros_like(value))


def fold(value, op):
    return op(value.reshape(value.shape[0] // 8, 8, value.shape[1]), axis=0)


def over_keys(body, prompt, own, carry):
    carry = lax.fori_loop(0, PROMPT_CHUNKS, lambda c, carry: body(c, lambda i: prompt(c, i), carry), carry)
    return lax.fori_loop(
        0, CONT_CHUNKS, lambda c, carry: body(PROMPT_CHUNKS + c, lambda i: own(c, i), carry), carry
    )


def head_pairs(head, finish):
    @pl.loop(0, HEAD_PAIRS)
    def _(pair):
        lanes = pl.ds(pl.multiple_of(pair * 2 * HEAD, 2 * HEAD), 2 * HEAD)
        head(pair, lanes, 0)

        @pl.when(pair < HEAD_PAIRS - 1)
        def _():
            head(pair, lanes, 1)

        finish(pair, lanes)


def run_hooks(hooks, micro, pair, half):
    for at in range(HEAD_PAIRS):
        if half == 0 and (micro, at) in hooks:

            @pl.when(pair == at)
            def _(at=at):
                for hook in hooks[micro, at]:
                    hook()


def to_slots(target, micro, first, value, lanes):
    per = target.shape[1] // MICRO
    row = first
    while row < first + value.shape[0]:
        slot, within = row // per, row % per
        count = min(per - within, first + value.shape[0] - row)
        target[slot, micro * per + within : micro * per + within + count, lanes] = value[
            row - first : row - first + count
        ]
        row += count


def pair_to_blocks(target, x, value):
    per = value.shape[0] // (2 * MICRO)
    for core in range(2):
        for micro in range(MICRO):
            at = pl.ds(pl.multiple_of((2 * x + core) * per, per), per)
            first = (core * MICRO + micro) * per
            target[micro, at, :] = value[first : first + per]


def attn_fwd_kernel(n, *refs):
    x_ref, vec_ref, bias_ref, wqkv_hbm = refs[:4]
    shard, refs = refs[4 : 4 + n], refs[4 + n :]
    out_ref, lse_ref, all_hbm, own_hbm, kv_hbm, mix_hbm, wout_hbm = refs[:7]
    whole, refs = refs[7 : 7 + n], refs[7 + n :]
    wqkv, wout, wparts, buf, own, kv, mix, s_ref, p_ref, o_ref = refs[:10]
    part, from_core, over_out, from_over, send, recv, gsend, grecv, wsend, wrecv, local = refs[10:21]
    msend, mrecv = refs[21:23]
    p, g = Peers(), Group()
    spread = Spread(g, shard[0], whole[0], refs[23:], ATTN_CHUNKS) if n else None
    mixes = BlockGather(p, mix, mix_hbm, (msend, mrecv), 0, local.at[5])
    rows = x_ref.shape[0]
    n_tp = buf.shape[0]
    step = HEADS // n_tp * HEAD
    width = wparts.shape[1]
    sems = (send, recv)
    gather = Gather(p, buf, sems)
    scatter = Scatter(p, part, from_core, over_out, from_over, sems)
    share = Share(g, kv, (gsend, grecv))
    load_qkv = pltpu.make_async_copy(wqkv_hbm.at[:, : 3 * WIDE], wqkv, local.at[0])
    load_qkv.start()

    def rows_for(t):
        return wqkv_hbm.at[pl.ds(pl.multiple_of(t * step, 128), width), 3 * WIDE : 4 * WIDE]

    keep_part = pltpu.make_async_copy(rows_for(p.t), wparts.at[p.t], local.at[1])
    keep_part.start()
    give_parts = [
        p.copy(rows_for(t), wparts.at[p.t], (wsend, wrecv), i, t) for i, t in enumerate((p.core, p.over, p.diag))
    ]

    def norm(at):
        hat, _ = norm_stats(x_ref[at, :])
        buf[p.t, at, :] = (hat * vec_ref[0:1, :] + vec_ref[1:2, :]).astype(bf16)

    row_chunks(rows, norm)
    g.greet(p, True)
    gather.start()
    for copy in give_parts:
        copy.start()
    if n:
        spread.start(0, 1)
    gather.wait_chip()
    load_qkv.wait()

    def project(x):
        for i in range(3):
            value = mm(pair_rows(buf, x), wqkv[:, i * WIDE : (i + 1) * WIDE]) + bias_ref[i : i + 1, :]
            low = value.astype(bf16)
            if i == 0:
                low = low * HEAD ** (-0.5)
            pair_to_blocks(own.at[i], x, low)

    project(p.x)
    gather.relay()
    gather.wait_diag()
    project(1 - p.x)
    for micro in range(MICRO):
        for i in range(2):
            kv[g.member, micro, i] = own[1 + i, micro, :PROMPT_DEV, :]
    share.start(0, 0)
    if n:
        spread.relay(0)
        spread.start(1, 2)
    hooks = {
        (0, 1): [lambda: share.relay(0, 1), lambda: share.start(1, 0)],
        (0, 2): [lambda: share.wait(0, 1)],
        (0, 3): [lambda: share.relay(1, 0), lambda: share.start(1, 1)],
        (1, 0): [lambda: share.wait(1, 0)],
        (1, 1): [lambda: share.relay(1, 1)],
        (1, 2): [lambda: share.wait(1, 1)],
    }
    if n:
        hooks[0, 1] += [lambda: spread.start(2, 3), lambda: spread.relay(1)]
        hooks[1, 1] += [lambda: spread.start(3, 4), lambda: spread.relay(2)]
        hooks[1, 3] = [lambda: spread.start(4)]
    keep_all = pltpu.make_async_copy(buf, all_hbm, local.at[2])
    keep_own = pltpu.make_async_copy(own, own_hbm, local.at[3])
    keep_all.start()
    keep_own.start()
    limit = key_limit(g.member)
    sub = lax.broadcasted_iota(jnp.int32, (CHUNK, TOK_DEV), 0)

    share.relay(0, 0)
    share.start(0, 1)
    share.wait(0, 0)

    for micro in range(MICRO):

        def head(pair, lanes, half, micro=micro):
            run_hooks(hooks, micro, pair, half)
            qh = half_of(own[0, micro, :, lanes], half)

            def first(c, load, top):
                s = jnp.where(sub + c * CHUNK <= limit, mm(load(0), qh, NT), -1e30)
                s_ref[chunk_at(c), :] = s
                return jnp.maximum(top, fold(s, jnp.max))

            top = over_keys(
                first,
                lambda c, i: kv[c, micro, i, :, lanes],
                lambda c, i: own[1 + i, micro, chunk_at(c, PROMPT_DEV), lanes],
                jnp.full((8, TOK_DEV), -1e30, f32),
            )
            top = jnp.max(top, axis=0, keepdims=True)

            def second(c, total):
                e = jnp.exp(s_ref[chunk_at(c), :] - top)
                p_ref[chunk_at(c), :] = e.astype(bf16)
                return total + fold(e, jnp.sum)

            total = lax.fori_loop(0, KEYS // CHUNK, second, jnp.zeros((8, TOK_DEV), f32))
            total = jnp.sum(total, axis=0, keepdims=True)
            values = kv[:, micro, 1, :, lanes].reshape(PROMPT, 2 * HEAD)
            out = mm(values, p_ref[:PROMPT, :], TN) + mm(own[2, micro, PROMPT_DEV:, lanes], p_ref[PROMPT:, :], TN)
            at = slice(HEAD * half, HEAD * (half + 1))
            o_ref[at, :] = out[at, :] / total
            lse_ref[micro, pair, half : half + 1, :] = top + jnp.log(total)

        def finish(pair, lanes, micro=micro):
            @pl.when(pair == HEAD_PAIRS - 1)
            def _():
                o_ref[HEAD:, :] = jnp.zeros((HEAD, TOK_DEV), f32)

            to_slots(mix, micro, 0, o_ref[...].T.astype(bf16), lanes)

        head_pairs(head, finish)

    keep_kv = pltpu.make_async_copy(kv, kv_hbm, local.at[4])
    keep_kv.start()
    keep_part.wait()
    for i, t in enumerate((p.core, p.over, p.diag)):
        p.copy(rows_for(t), wparts.at[t], (wsend, wrecv), i, t).wait_recv()
    for t in range(n_tp):
        count = min(WIDE, D - t * step)
        wout[:width, t * step : t * step + count] = wparts[t, :, :count]
    wout[width:, :] = jnp.zeros((WIDE - width, D), bf16)

    @pl.when(p.t < n_tp - 1)
    def _():
        wout[step:width, :] = jnp.zeros((width - step, D), bf16)

    keep_out = pltpu.make_async_copy(wout, wout_hbm, local.at[6])
    keep_out.start()

    def down(x):
        def tile(at):
            put_pair(part, x, at, mm(pair_rows(mix, x), wout[:, at]))

        tiles(D, tile)

    down(1 - p.x)
    scatter.far_to_core().start()
    scatter.send_over()
    down(p.x)
    scatter.near_to_core().start()
    if n:
        spread.relay(3)
    scatter.wait()
    mixes.start()

    def final(at):
        out_ref[at, :] = x_ref[at, :] + (scatter.rows(at) + vec_ref[4:5, :])

    row_chunks(rows, final)
    mixes.relay()
    if n:
        spread.relay(4)
    gather.finish()
    scatter.finish()
    share.finish()
    for copy in give_parts:
        copy.wait_send()
    for copy in (keep_all, keep_own, keep_kv, keep_out):
        copy.wait()
    mixes.finish()
    if n:
        spread.finish()


def attn_shapes(n_tp, rows):
    return (
        ((n_tp, rows, D), bf16),
        ((3, MICRO, TOK_DEV, WIDE), bf16),
        ((GROUP, MICRO, 2, PROMPT_DEV, WIDE), bf16),
        ((n_tp, rows, WIDE), bf16),
    )


def attn_fwd(x, vecs, biases, w_a, n_tp, shard, collective_id):
    rows = x.shape[0]
    width = D - HEADS // n_tp * HEAD * (n_tp - 1)
    saved = attn_shapes(n_tp, rows)
    operands, results, sems = spread_parts(shard, ATTN_CHUNKS)
    return pl.pallas_call(
        functools.partial(attn_fwd_kernel, len(operands)),
        out_shape=(
            jax.ShapeDtypeStruct((rows, D), f32),
            jax.ShapeDtypeStruct((MICRO, HEAD_PAIRS, 8, TOK_DEV), f32),
        )
        + tuple(jax.ShapeDtypeStruct(*s) for s in saved[:3])
        + (jax.ShapeDtypeStruct((n_tp,) + saved[3][0], bf16), jax.ShapeDtypeStruct((WIDE, D), bf16))
        + results,
        in_specs=[IN_VMEM, IN_VMEM, IN_VMEM, ANY] + [ANY] * len(operands),
        out_specs=(IN_VMEM, IN_VMEM) + (ANY,) * (5 + len(operands)),
        scratch_shapes=[pltpu.VMEM((D, 3 * WIDE), bf16), pltpu.VMEM((WIDE, D), bf16), pltpu.VMEM((n_tp, width, WIDE), bf16)]
        + [pltpu.VMEM(*s) for s in saved]
        + [
            pltpu.VMEM((KEYS, TOK_DEV), f32),
            pltpu.VMEM((KEYS, TOK_DEV), bf16),
            pltpu.VMEM((2 * HEAD, TOK_DEV), f32),
        ]
        + scatter_scratch(n_tp, rows)
        + [
            pltpu.SemaphoreType.DMA((14 * MICRO,)),
            pltpu.SemaphoreType.DMA((14 * MICRO,)),
            pltpu.SemaphoreType.DMA((3,)),
            pltpu.SemaphoreType.DMA((3,)),
            pltpu.SemaphoreType.DMA((7,)),
            pltpu.SemaphoreType.DMA((3,)),
            pltpu.SemaphoreType.DMA((3,)),
        ]
        + sems,
        compiler_params=params(collective_id),
        cost_estimate=pl.CostEstimate(flops=10**11, bytes_accessed=30 * 2**20, transcendentals=0),
    )(x, vecs, biases, w_a, *operands)


def attn_bwd_kernel(n, *refs):
    g_ref, x_ref, vec_ref, lse_ref, all_hbm, own_hbm, kv_hbm, mix_hbm, wqkv_hbm, wout_hbm = refs[:10]
    sources, refs = refs[10 : 10 + n], refs[10 + n :]
    out_ref, sums_ref, cols_ref, dqo_hbm = refs[:4]
    results, refs = refs[4 : 4 + 2 * n], refs[4 + 2 * n :]
    wqkv, wout, buf, other, mixed, own, kv, gm, dkv, from_y, to_z, from_z, dkc, dqkv, stage, stage_out = refs[:16]
    p_ref, dp_ref, ds_ref, o_ref = refs[16:20]
    part, from_core, over_out, from_over, send, recv, gsend, grecv, local = refs[20:29]
    p, g = Peers(), Group()
    sums = reduces(g, sources, results, refs[29:])
    rows = x_ref.shape[0]
    n_tp = buf.shape[0]
    out_step = HEADS // n_tp * HEAD
    out_width = D - out_step * (n_tp - 1)
    sems = (send, recv)
    gather = Gather(p, buf, sems)
    scatter = Scatter(p, part, from_core, over_out, from_over, sems)
    reduce = GroupSum(g, dkv, from_y, to_z, from_z, (gsend, grecv))
    load_out = pltpu.make_async_copy(wout_hbm, wout, local.at[0])
    load_own = pltpu.make_async_copy(own_hbm, own, local.at[1])
    load_kv = pltpu.make_async_copy(kv_hbm, kv, local.at[2])
    load_qkv = pltpu.make_async_copy(wqkv_hbm.at[:, : 3 * WIDE], wqkv, local.at[3])
    load_mix = pltpu.make_async_copy(mix_hbm, mixed, local.at[4])
    load_all = pltpu.make_async_copy(all_hbm, other, local.at[6])
    for copy in (load_out, load_own, load_kv, load_qkv, load_mix, load_all):
        copy.start()
    sums_ref[...] = jnp.zeros_like(sums_ref)

    def lower(at):
        low = g_ref[at, :].astype(bf16)
        buf[p.t, at, :] = low
        add_rows(sums_ref, 4, low.astype(f32))

    row_chunks(rows, lower)
    g.greet(p)
    gather.start()
    hooks = {(1, 0): [lambda: reduce.turn(0, 0)], (1, 1): [lambda: reduce.turn(0, 1)]}
    if n:
        first_sum, second_sum = sums
        first_sum.start(1)
        hooks[0, 1] = [lambda: first_sum.start(0), lambda: first_sum.pump(2)]
        hooks[0, 2] = [lambda: second_sum.start(1), lambda: first_sum.pump(3)]
        hooks[0, 3] = [lambda: second_sum.start(2)]
        hooks[1, 1] += [lambda: second_sum.pump(1, first_sum), lambda: second_sum.start(3)]
    gather.wait_chip()
    load_out.wait()

    def mixed_back(x):
        pair_to_blocks(gm, x, mm(pair_rows(buf, x), wout[...], NT).astype(bf16))

    mixed_back(p.x)
    if n:
        first_sum.start(2)
    gather.relay()
    gather.wait_diag()
    mixed_back(1 - p.x)
    load_own.wait()
    load_kv.wait()
    limit = key_limit(g.member)
    sub = lax.broadcasted_iota(jnp.int32, (CHUNK, TOK_DEV), 0)

    if n:
        first_sum.start(3)
        first_sum.pump(1)

    for micro in range(MICRO):

        def head(pair, lanes, half, micro=micro):
            run_hooks(hooks, micro, pair, half)
            qh = half_of(own[0, micro, :, lanes], half)
            gh = half_of(gm[micro, :, lanes], half)
            lse = lse_ref[micro, pair, half : half + 1, :]

            def first(c, load, inner):
                s = jnp.where(sub + c * CHUNK <= limit, mm(load(0), qh, NT), -1e30)
                e = jnp.exp(s - lse)
                dp = mm(load(1), gh, NT)
                p_ref[chunk_at(c), :] = e
                dp_ref[chunk_at(c), :] = dp
                return inner + fold(e * dp, jnp.sum)

            inner = over_keys(
                first,
                lambda c, i: kv[c, micro, i, :, lanes],
                lambda c, i: own[1 + i, micro, chunk_at(c, PROMPT_DEV), lanes],
                jnp.zeros((8, TOK_DEV), f32),
            )
            inner = jnp.sum(inner, axis=0, keepdims=True)

            def second(c, put):
                e = p_ref[chunk_at(c), :]
                ds = (e * (dp_ref[chunk_at(c), :] - inner)).astype(bf16)
                ds_ref[chunk_at(c), :] = ds
                put(0, mm(ds, qh))
                put(1, mm(e.astype(bf16), gh))

            @pl.loop(0, PROMPT_CHUNKS)
            def _(c):
                def put(i, value):
                    at = (micro, c // 2, c % 2, i, slice(None), lanes)
                    if half:
                        value = value + dkv[at].astype(f32)
                    dkv[at] = value.astype(bf16)

                second(c, put)

            @pl.loop(0, CONT_CHUNKS)
            def _(c):
                def put(i, value):
                    at = (i, chunk_at(c), lanes)
                    if half:
                        value = value + dkc[at].astype(f32)
                    dkc[at] = value.astype(bf16)

                second(PROMPT_CHUNKS + c, put)

            keys = kv[:, micro, 0, :, lanes].reshape(PROMPT, 2 * HEAD)
            dq = mm(keys, ds_ref[:PROMPT, :], TN) + mm(own[1, micro, PROMPT_DEV:, lanes], ds_ref[PROMPT:, :], TN)
            at = slice(HEAD * half, HEAD * (half + 1))
            o_ref[at, :] = dq[at, :] * HEAD ** (-0.5)

        def finish(pair, lanes, micro=micro):
            @pl.when(pair == HEAD_PAIRS - 1)
            def _():
                o_ref[HEAD:, :] = jnp.zeros((HEAD, TOK_DEV), f32)

            to_slots(dqkv, micro, 0, o_ref[...].T.astype(bf16), lanes)

            @pl.when(pair == HEAD_PAIRS // 2 - 1)
            def _():
                reduce.start(micro, 0)

        head_pairs(head, finish)
        reduce.start(micro, 1)
        for i in range(2):
            to_slots(dqkv, micro, PROMPT_DEV, dkc[i], slice((1 + i) * WIDE, (2 + i) * WIDE))

    load_mix.wait()
    columns = pl.ds(pl.multiple_of(p.t * out_step, 128), out_width)

    def outer(source, target, right, body):
        flat = right.reshape(n_tp * rows, right.shape[-1])

        def tile(at):
            left = source[:, :, at].reshape(n_tp * rows, -1)
            target[at, : flat.shape[1]] = mm(left, flat, TN).astype(bf16)

        body(D, tile)

    reduce.turn(1, 0)
    stage_out[:, out_width:] = jnp.zeros((D, WIDE - out_width), bf16)
    low = buf[:, :, columns].reshape(n_tp * rows, out_width)
    for t in range(n_tp):
        count = out_step if t < n_tp - 1 else out_width
        value = mm(mixed[t].reshape(n_tp * rows, WIDE), low, TN).astype(bf16)
        stage_out[t * out_step : t * out_step + count, :out_width] = value[:count, :]
    keep_out = pltpu.make_async_copy(stage_out, dqo_hbm.at[:, 3 * WIDE :], local.at[5])
    keep_out.start()
    reduce.turn(1, 1)
    if n:
        second_sum.start(0)
    for micro in range(MICRO):
        reduce.wait(micro)
        for i in range(2):
            to_slots(dqkv, micro, 0, reduce.total(micro, i), slice((1 + i) * WIDE, (2 + i) * WIDE))
    if n:
        second_sum.pump(2, first_sum)
        second_sum.pump(3, first_sum)
    load_qkv.wait()

    def down(x):
        def tile(at):
            put_pair(part, x, at, mm(pair_rows(dqkv, x), wqkv[at, :], NT))

        tiles(D, tile)

    down(1 - p.x)
    scatter.far_to_core().start()
    scatter.send_over()
    down(p.x)
    scatter.near_to_core().start()
    load_all.wait()
    outer(other, stage, dqkv[...], tiles)
    keep_qkv = pltpu.make_async_copy(stage, dqo_hbm.at[:, : 3 * WIDE], local.at[7])
    keep_qkv.start()
    cols_ref[...] = jnp.zeros_like(cols_ref)

    @pl.loop(0, n_tp * rows // ROW_CHUNK)
    def _(i):
        per = rows // ROW_CHUNK
        at = pl.ds(pl.multiple_of((i % per) * ROW_CHUNK, ROW_CHUNK), ROW_CHUNK)
        add_rows(cols_ref, 0, dqkv[i // per, at, :].astype(f32))

    scatter.wait()

    def final(at):
        dy = scatter.rows(at)
        dx, d_gain = norm_back(x_ref[at, :], dy, vec_ref[0:1, :])
        add_rows(sums_ref, 0, d_gain)
        add_rows(sums_ref, 1, dy)
        out_ref[at, :] = g_ref[at, :] + dx

    row_chunks(rows, final)
    gather.finish()
    scatter.finish()
    for micro in range(MICRO):
        reduce.finish(micro)
    keep_out.wait()
    keep_qkv.wait()
    for i, item in enumerate(sums):
        item.finish(i < n - 1)


def attn_bwd(grad, x, vecs, lse, all_rows, own, kv, mixed_all, w_a, w_out, n_tp, payload, collective_id):
    rows = x.shape[0]
    operands, results, more = reduce_parts(payload)
    pieces = (MICRO, 4, 2, 2, PROMPT_DEV, WIDE)
    return pl.pallas_call(
        functools.partial(attn_bwd_kernel, len(payload)),
        out_shape=(
            jax.ShapeDtypeStruct((rows, D), f32),
            jax.ShapeDtypeStruct((8, D), f32),
            jax.ShapeDtypeStruct((1, 3 * WIDE), f32),
            jax.ShapeDtypeStruct((D, 4 * WIDE), bf16),
        )
        + results,
        in_specs=[IN_VMEM] * 4 + [ANY] * (6 + len(payload)),
        out_specs=(IN_VMEM, IN_VMEM, IN_VMEM) + (ANY,) * (1 + 2 * len(payload)),
        scratch_shapes=[
            pltpu.VMEM((D, 3 * WIDE), bf16),
            pltpu.VMEM((WIDE, D), bf16),
            pltpu.VMEM((n_tp, rows, D), bf16),
            pltpu.VMEM((n_tp, rows, D), bf16),
            pltpu.VMEM((n_tp, n_tp, rows, WIDE), bf16),
            pltpu.VMEM((3, MICRO, TOK_DEV, WIDE), bf16),
            pltpu.VMEM((GROUP, MICRO, 2, PROMPT_DEV, WIDE), bf16),
            pltpu.VMEM((MICRO, TOK_DEV, WIDE), bf16),
            pltpu.VMEM(pieces, bf16),
            pltpu.VMEM((MICRO, 4, 2, PROMPT_DEV, WIDE), bf16),
            pltpu.VMEM((MICRO, 4, 2, PROMPT_DEV, WIDE), bf16),
            pltpu.VMEM((MICRO, 3, 2, PROMPT_DEV, WIDE), bf16),
            pltpu.VMEM((2, CONT_LEN, WIDE), bf16),
            pltpu.VMEM((n_tp, rows, 3 * WIDE), bf16),
            pltpu.VMEM((D, 3 * WIDE), bf16),
            pltpu.VMEM((D, WIDE), bf16),
            pltpu.VMEM((KEYS, TOK_DEV), f32),
            pltpu.VMEM((KEYS, TOK_DEV), f32),
            pltpu.VMEM((KEYS, TOK_DEV), bf16),
            pltpu.VMEM((2 * HEAD, TOK_DEV), f32),
        ]
        + scatter_scratch(n_tp, rows)
        + [
            pltpu.SemaphoreType.DMA((8 * MICRO,)),
            pltpu.SemaphoreType.DMA((8 * MICRO,)),
            pltpu.SemaphoreType.DMA((8,)),
        ]
        + more,
        compiler_params=params(collective_id),
        cost_estimate=pl.CostEstimate(flops=2 * 10**11, bytes_accessed=50 * 2**20, transcendentals=0),
    )(grad, x, vecs, lse, all_rows, own, kv, mixed_all, w_a, w_out, *operands)


def forward_layer(x, layer, fetch, vecs, fc_bias, cols, n_tp):
    width = D - HEADS // n_tp * HEAD * (n_tp - 1)
    query_bias, value_bias = (lax.dynamic_slice_in_dim(vecs[i], cols, width) for i in (2, 3))
    biases = widen(jnp.stack([query_bias, jnp.zeros_like(query_bias), value_bias]))
    w_a = fetch.weights[layer, "a"]
    x_mid, lse, all_rows, own, kv, mixed, w_out = fetch.during(
        (layer, "b"), lambda shard: attn_fwd(x, vecs, biases, w_a, n_tp, shard, 5 + layer)
    )
    w_b = fetch.weights[layer, "b"]
    x_next, second_all, hidden_pre, hidden = fetch.during(
        (layer + 1, "a"), lambda shard: ff_fwd(x_mid, vecs, fc_bias[None], w_b, n_tp, shard, 1 + layer)
    )
    return x_next, (x, w_out, lse, all_rows, own, kv, mixed, x_mid, second_all, hidden_pre, hidden)


class Fetch:
    def __init__(self, shards):
        self.staged = lax.axis_size("fsdp") == GROUP
        self.shards, self.weights = shards, {}
        last = None
        for key, shard in shards.items():
            if self.staged:
                if last is None:
                    last = spread_only(shard, FIRST_CHUNKS, 9)
                    self.weights[key] = last.reshape(-1, shard.shape[1])
                continue
            if last is not None:
                shard, _ = lax.optimization_barrier((shard, last))
            whole = lax.all_gather(shard, "fsdp", axis=0, tiled=True)
            self.weights[key] = whole
            last = whole[:8, :128]

    def during(self, key, kernel):
        if not self.staged or key not in self.shards:
            return kernel(None)
        *results, whole = kernel(self.shards[key])
        self.weights[key] = whole.reshape(-1, whole.shape[2])
        return results


def fsdp_sum(part):
    return lax.psum_scatter(part, "fsdp", scatter_dimension=0, tiled=True).astype(f32)


def heads_joined(parts, n_tp):
    step = HEADS // n_tp * HEAD
    return jnp.concatenate([parts[t][..., :step] for t in range(n_tp - 1)] + [parts[n_tp - 1]], axis=-1)


def widen(value, axis=-1):
    pads = [(0, 0)] * value.ndim
    pads[axis] = (0, WIDE - value.shape[axis])
    return jnp.pad(value, pads)


def by_owner(part):
    return part.reshape(4, 2, -1, part.shape[1])


def owned(part, from_y, from_z):
    z, y = lax.axis_index("fsdp") // 2, lax.axis_index("fsdp") % 2
    own = lax.dynamic_index_in_dim(lax.dynamic_index_in_dim(part, z, 0, False), y, 0, False)
    near = lax.dynamic_index_in_dim(from_y, z, 0, False)
    return own.astype(f32) + near.astype(f32) + jnp.sum(from_z.astype(f32), 0)


def with_vectors(grad_qo, ff_sums, attn_sums, col_sums, fc_bias_sums, cols, width):
    def placed(part):
        return lax.dynamic_update_slice_in_dim(jnp.zeros((1, D), f32), part, cols, 1)

    vector_grads = jnp.concatenate(
        [
            attn_sums[:2],
            placed(col_sums[:, :width]),
            placed(col_sums[:, 2 * WIDE : 2 * WIDE + width]),
            attn_sums[4:5],
            ff_sums[5:],
            fc_bias_sums,
        ]
    )
    return lax.dynamic_update_slice(grad_qo, vector_grads.astype(bf16).T, (0, 3 * WIDE + width))


def backward(grad, weights, vecs, saves, cols, n_tp):
    width = D - HEADS // n_tp * HEAD * (n_tp - 1)
    staged = lax.axis_size("fsdp") == GROUP
    done, waiting = {}, {}

    def during(keys, kernel):
        keys = [key for key in keys if key in waiting]
        payload = [waiting.pop(key) for key in keys]
        results = list(kernel(payload))
        if payload:
            arrived = results[-2 * len(payload) :]
            results = results[: -2 * len(payload)]
            for i, key in enumerate(keys):
                done[key] = (payload[i], arrived[2 * i], arrived[2 * i + 1])
        return results

    def produced(key, value):
        if staged:
            waiting[key] = by_owner(value)
        else:
            done[key] = fsdp_sum(value)

    for layer in reversed(range(LAYERS)):
        w_a, w_b = weights[layer, "a"], weights[layer, "b"]
        x, w_out, lse, all_rows, own, kv, mixed_all, x_mid, second_all, hidden_pre, hidden = saves[layer]
        grad, ff_sums, fc_bias_sums, grad_fc, grad_proj = during(
            [(layer + 1, "qo")],
            lambda payload: ff_bwd(
                grad, x_mid, vecs[layer], second_all, hidden_pre, hidden, w_b, n_tp, payload, 10 + layer
            ),
        )
        produced((layer, "proj"), grad_proj)
        produced((layer, "fc"), grad_fc)
        grad, attn_sums, col_sums, grad_qo = during(
            [(layer, "proj"), (layer, "fc")],
            lambda payload: attn_bwd(
                grad, x, vecs[layer], lse, all_rows, own, kv, mixed_all, w_a, w_out, n_tp, payload, 20 + layer
            ),
        )
        produced((layer, "qo"), with_vectors(grad_qo, ff_sums, attn_sums, col_sums, fc_bias_sums, cols, width))
    if staged:
        got = last_sum(waiting[0, "qo"], owned(*done[1, "qo"]).astype(bf16), n_tp, 30)
        return grad, assemble([(got[k],) + done[k, "proj"] + done[k, "fc"] for k in range(LAYERS)])
    outs = []
    for layer in range(LAYERS):
        qo = done[layer, "qo"]
        got = lax.all_gather(qo.astype(bf16), "tp")
        qkv_grad = jnp.concatenate(
            [heads_joined(got[:, :, i * WIDE : i * WIDE + width], n_tp) for i in range(3)], axis=1
        )
        out_grad = heads_joined(got[:, :, 3 * WIDE : 3 * WIDE + width], n_tp)
        vector_sum = jnp.sum(got[:, :, 3 * WIDE + width : 3 * WIDE + width + 8].astype(f32), 0).T
        rest = (vector_sum[v] for v in range(8))
        outs.append((qkv_grad, out_grad, done[layer, "fc"], done[layer, "proj"].T, *rest, qo[:, 3 * WIDE + width + 8]))
    return grad, tuple(jnp.stack(pair).astype(f32) for pair in zip(*outs))


def local(
    tokens,
    qkv_weight,
    query_bias,
    value_bias,
    out_weight,
    out_bias,
    fc_weight,
    fc_bias,
    proj_weight,
    proj_bias,
    first_gain,
    first_bias,
    second_gain,
    second_bias,
    out_grad,
):
    n_tp = lax.axis_size("tp")
    tp = lax.axis_index("tp")
    row_count = tokens.shape[1]
    step = HEADS // n_tp * HEAD
    width = D - step * (n_tp - 1)
    cols = tp * step

    vectors = jnp.stack(
        [first_gain, first_bias, query_bias, value_bias, out_bias, second_gain, second_bias, proj_bias, fc_bias[:, 0]]
    ).reshape(9 * LAYERS, -1)

    shards = {}
    for layer in range(LAYERS):
        sides = [widen(lax.dynamic_slice_in_dim(qkv_weight[layer], cols + i * D, width, 1)) for i in range(3)]
        sides.append(widen(lax.dynamic_slice_in_dim(out_weight[layer], cols, width, 1)))
        if layer == 0:
            sides.append(jnp.pad(vectors.T, ((0, 0), (0, 128 - 9 * LAYERS))))
        shards[layer, "a"] = jnp.concatenate(sides, axis=1)
        fc, proj = fc_weight[layer], proj_weight[layer].T
        more = ((0, 0), (0, lanes_up(fc.shape[1]) - fc.shape[1]))
        shards[layer, "b"] = jnp.concatenate([jnp.pad(fc, more), jnp.pad(proj, more)], axis=1)
    fetch = Fetch(shards)
    vectors = fetch.weights[0, "a"][:, 4 * WIDE : 4 * WIDE + 9 * LAYERS].T.astype(f32).reshape(9, LAYERS, D)

    state = tokens.astype(f32).reshape(MICRO * row_count, D)
    saves = []
    for layer in range(LAYERS):
        state, saved = forward_layer(state, layer, fetch, vectors[:8, layer], vectors[8, layer], cols, n_tp)
        saves.append(saved)
    out_tokens = state.astype(bf16).reshape(tokens.shape)
    grad = out_grad.astype(f32).reshape(MICRO * row_count, D)
    grad, (qkv_g, out_g, fc_g, proj_g, *vec_g) = backward(
        grad, fetch.weights, [vectors[:8, layer] for layer in range(LAYERS)], saves, cols, n_tp
    )
    return (
        out_tokens,
        grad.reshape(tokens.shape),
        qkv_g,
        vec_g[2],
        vec_g[3],
        out_g,
        vec_g[4],
        fc_g,
        vec_g[8][:, None],
        proj_g,
        vec_g[7],
        vec_g[0],
        vec_g[1],
        vec_g[5],
        vec_g[6],
    )


def solution(mesh):
    rows = P(None, ("fsdp", "tp"), None)
    weight = P(None, "fsdp", None)
    vector = P(None, "fsdp")
    fc_in = P(None, "fsdp", "tp")
    hidden = P(None, "tp", "fsdp")
    in_specs = (
        rows, weight, vector, vector, weight, vector, fc_in, hidden, hidden,
        vector, vector, vector, vector, vector, rows,
    )
    out_specs = (
        rows, rows, weight, vector, vector, weight, vector, fc_in, hidden, hidden,
        vector, vector, vector, vector, vector,
    )
    return jax.shard_map(local, mesh=mesh, in_specs=in_specs, out_specs=out_specs, check_vma=False)
```

```python
import functools

import jax
import jax.numpy as jnp
from jax import lax
from jax.experimental import pallas as pl
from jax.experimental.pallas import tpu as pltpu
from jax.sharding import PartitionSpec as P

D = 1600
HEADS = 25
HEAD = 64
GROUP = 8
PROMPT_DEV = 128
CONT_LEN = 256
TOK_DEV = 384
MICRO = 2
LAYERS = 2
PROMPT = 1024
KEYS = PROMPT + CONT_LEN
CHUNK = 128

f32 = jnp.float32
bf16 = jnp.bfloat16
norm_eps = 1e-05
NN = (((1,), (0,)), ((), ()))
NT = (((1,), (1,)), ((), ()))
TN = (((0,), (0,)), ((), ()))


def mm(left, right, dims=NN):
    return lax.dot_general(left, right, dims, preferred_element_type=f32)


def gelu_tanh(value):
    return jax.nn.gelu(value, approximate=True)


MESH = pl.DeviceIdType.MESH
ANY = pl.BlockSpec(memory_space=pl.ANY)
IN_VMEM = pl.BlockSpec(memory_space=pltpu.VMEM)
TILE = 512
ROW_CHUNK = 32


class Peers:
    def __init__(self):
        self.f = lax.axis_index("fsdp")
        self.t = lax.axis_index("tp")
        x, c = self.t // 2, self.t % 2
        self.x = x
        self.core = 2 * x + 1 - c
        self.over = 2 * (1 - x) + c
        self.diag = 2 * (1 - x) + 1 - c

    def greet(self):
        barrier = pltpu.get_barrier_semaphore()
        for t in (self.core, self.over):
            pl.semaphore_signal(barrier, inc=1, device_id=(self.f, t), device_id_type=MESH)
        pl.semaphore_wait(barrier, 2)

    def copy(self, source, target, sems, index, t):
        return pltpu.make_async_remote_copy(
            src_ref=source,
            dst_ref=target,
            send_sem=sems[0].at[index],
            recv_sem=sems[1].at[index],
            device_id=(self.f, t),
            device_id_type=MESH,
        )


class Gather:
    def __init__(self, peers, buf, sems):
        self.p, self.buf, self.sems = peers, buf, sems

    def piece(self, slot, index, t):
        return self.p.copy(self.buf.at[slot], self.buf.at[slot], self.sems, index, t)

    def start(self):
        p = self.p
        self.piece(p.t, 1, p.over).start()
        self.piece(p.t, 0, p.core).start()

    def wait_chip(self):
        self.piece(self.p.core, 0, self.p.core).wait_recv()

    def relay(self):
        p = self.p
        self.piece(p.over, 1, p.over).wait_recv()
        self.piece(p.over, 2, p.core).start()

    def wait_diag(self):
        self.piece(self.p.diag, 2, self.p.core).wait_recv()

    def finish(self):
        p = self.p
        self.piece(p.t, 1, p.over).wait_send()
        self.piece(p.t, 0, p.core).wait_send()
        self.piece(p.over, 2, p.core).wait_send()


class Scatter:
    def __init__(self, peers, part, from_core, over_out, from_over, sems):
        self.p, self.part, self.sems = peers, part, sems
        self.from_core, self.over_out, self.from_over = from_core, over_out, from_over

    def far_to_core(self):
        return self.p.copy(self.part.at[self.p.diag], self.from_core.at[0], self.sems, 3, self.p.core)

    def near_to_core(self):
        return self.p.copy(self.part.at[self.p.core], self.from_core.at[1], self.sems, 4, self.p.core)

    def to_over(self):
        return self.p.copy(self.over_out, self.from_over, self.sems, 5, self.p.over)

    def send_over(self):
        self.far_to_core().wait_recv()

        @pl.loop(0, self.over_out.shape[0] // ROW_CHUNK)
        def _(i):
            at = pl.ds(pl.multiple_of(i * ROW_CHUNK, ROW_CHUNK), ROW_CHUNK)
            total = self.part[self.p.over, at, :].astype(f32) + self.from_core[0, at, :].astype(f32)
            self.over_out[at, :] = total.astype(bf16)

        self.to_over().start()

    def wait(self):
        self.near_to_core().wait_recv()
        self.to_over().wait_recv()

    def rows(self, at):
        return (
            self.part[self.p.t, at, :].astype(f32)
            + self.from_core[1, at, :].astype(f32)
            + self.from_over[at, :].astype(f32)
        )

    def finish(self):
        for copy in (self.far_to_core(), self.near_to_core(), self.to_over()):
            copy.wait_send()


class Group:
    def __init__(self):
        f = lax.axis_index("fsdp")
        self.t = lax.axis_index("tp")
        self.member = f % GROUP
        self.base = f - self.member
        self.z, self.y = self.member // 2, self.member % 2

        half = self.z // 2
        self.inner = (self.z + half) % 2 == 1
        self.mate = 2 * half + 1 - self.z % 2
        self.far_inner, self.far_end = 2 - half, 3 - 3 * half

    def at(self, z, y):
        return z * 2 + y

    def ahead(self, k):
        return (self.z + k) % 4

    def behind(self, k):
        return (self.z + 4 - k) % 4

    def greet_group(self):
        barrier = pltpu.get_barrier_semaphore()
        others = [self.at(self.z, 1 - self.y)] + [self.at(self.ahead(k), self.y) for k in (1, 2, 3)]
        for member in others:
            pl.semaphore_signal(
                barrier, inc=1, device_id=(self.base + member, self.t), device_id_type=MESH
            )
        pl.semaphore_wait(barrier, 4)

    def greet(self, peers, with_diag=False):
        barrier = pltpu.get_barrier_semaphore()
        others = [self.at(self.z, 1 - self.y)] + [self.at(self.ahead(k), self.y) for k in (1, 2, 3)]
        for member in others:
            pl.semaphore_signal(
                barrier, inc=1, device_id=(self.base + member, self.t), device_id_type=MESH
            )
        near = [peers.core, peers.over] + [peers.diag] * with_diag
        for t in near:
            pl.semaphore_signal(barrier, inc=1, device_id=(peers.f, t), device_id_type=MESH)
        pl.semaphore_wait(barrier, 4 + len(near))

    def copy(self, source, target, sems, index, member, send_index=None):
        return pltpu.make_async_remote_copy(
            src_ref=source,
            dst_ref=target,
            send_sem=sems[0].at[index if send_index is None else send_index],
            recv_sem=sems[1].at[index],
            device_id=(self.base + member, self.t),
            device_id_type=MESH,
        )


class Reduce:
    def __init__(self, group, source, from_y, from_z, sems, tiles, columns=None):
        self.g, self.sems, self.columns = group, sems, columns
        self.source, self.from_y, self.from_z = source, from_y, from_z
        self.own, self.got, self.gone, self.local = tiles

    def cut(self, ref, *index):
        if self.columns is None:
            return ref.at[index]
        return ref.at[index + (slice(None), self.columns)]

    def across(self, j):
        g = self.g
        z = g.ahead(j)
        return g.copy(
            self.cut(self.source, z, 1 - g.y), self.cut(self.from_y, z), self.sems, j, g.at(g.z, 1 - g.y)
        )

    def along(self, j):
        g = self.g
        source, target = self.cut(self.gone, j - 1), self.cut(self.from_z, j - 1)
        return g.copy(source, target, self.sems, 3 + j, g.at(g.ahead(j), g.y))

    def start(self, *pieces):
        for j in pieces:
            self.across(j).start()

    def pump(self, j, before=None, then=None):
        g = self.g
        own, got = (self.own, self.got) if self.columns is None else (self.cut(self.own), self.cut(self.got))
        load_own = pltpu.make_async_copy(self.cut(self.source, g.ahead(j), g.y), own, self.local.at[0])
        load_own.start()
        self.across(j).wait_recv()
        if then is not None:
            then()
        load_got = pltpu.make_async_copy(self.cut(self.from_y, g.ahead(j)), got, self.local.at[1])
        load_got.start()
        load_own.wait()
        load_got.wait()
        if before is not None:
            before.along(j).wait_send()
        columns = slice(None) if self.columns is None else self.columns
        self.gone[j - 1, :, columns] = self.own[:, columns] + self.got[:, columns]
        self.along(j).start()

    def finish(self, reused=False, arrived=False):
        if not arrived:
            self.across(0).wait_recv()
        for j in range(4):
            self.across(j).wait_send()
        for j in (1, 2, 3):
            self.along(j).wait_recv()
            if not reused:
                self.along(j).wait_send()


def reduce_parts(payload):
    results, scratch = (), []
    for part in payload:
        rows = part.shape[2:]
        results += (jax.ShapeDtypeStruct((4,) + rows, bf16), jax.ShapeDtypeStruct((3,) + rows, bf16))
    scratch += [pltpu.SemaphoreType.DMA((7,))] * (2 * max(2, len(payload)) if payload else 0)
    if payload:
        scratch += [pltpu.VMEM(rows, bf16), pltpu.VMEM(rows, bf16), pltpu.VMEM((3,) + rows, bf16)]
        scratch += [pltpu.SemaphoreType.DMA((2,))]
    return tuple(payload), results, scratch


def reduces(group, sources, results, scratch):
    tiles = scratch[4:]
    if len(sources) == 1:
        middle, end = sources[0].shape[3] // 2, sources[0].shape[3]
        halves = (slice(0, middle), slice(middle, end))
        return [
            Reduce(group, sources[0], *results, scratch[2 * n : 2 * n + 2], tiles, columns)
            for n, columns in enumerate(halves)
        ]
    return [
        Reduce(group, source, results[2 * n], results[2 * n + 1], scratch[2 * n : 2 * n + 2], tiles)
        for n, source in enumerate(sources)
    ]


def in_turn(items):
    order = [(item, j) for item in items for j in (1, 2, 3, 0)]

    def step(n):
        def following():
            item, j = order[n + 1]
            item.start(j)

        item, j = order[n]
        if j:
            item.pump(j, then=following)
        else:
            item.across(0).wait_recv()
            following()

    return [lambda: items[0].start(1)] + [functools.partial(step, n) for n in range(len(order) - 1)]


class BlockGather:
    def __init__(self, peers, source, target, sems, first, local, columns=None):
        self.p, self.sems, self.first, self.local = peers, sems, first, local
        self.source = source if columns is None else source.at[:, columns]
        self.slot = lambda t: target.at[t] if columns is None else target.at[t, :, columns]

    def piece(self, slot, index, to, own=False):
        target = self.slot(slot)
        return self.p.copy(self.source if own else target, target, self.sems, self.first + index, to)

    def keep(self):
        return pltpu.make_async_copy(self.source, self.slot(self.p.t), self.local)

    def start(self):
        p = self.p
        self.piece(p.t, 1, p.over, True).start()
        self.piece(p.t, 0, p.core, True).start()
        self.keep().start()

    def relay(self):
        p = self.p
        self.piece(p.over, 1, p.over).wait_recv()
        self.piece(p.over, 2, p.core).start()

    def finish(self):
        p = self.p
        self.piece(p.core, 0, p.core).wait_recv()
        self.piece(p.diag, 2, p.core).wait_recv()
        self.piece(p.t, 1, p.over, True).wait_send()
        self.piece(p.t, 0, p.core, True).wait_send()
        self.piece(p.over, 2, p.core).wait_send()
        self.keep().wait()


def add_up(own, others, target, columns):
    rows = own.shape[0]
    for first in range(0, rows, 40):
        at = (slice(first, min(first + 40, rows)), columns)
        total = own[at].astype(f32)
        for other in others:
            total = total + other[at].astype(f32)
        target[at] = total.astype(target.dtype)


def last_sum_kernel(source, earlier, from_y, from_z, got, got_earlier, *scratch):
    p, g = Peers(), Group()
    scratch, (bsend, brecv, blocal, terms, mine) = scratch[:-5], scratch[-5:]
    before = BlockGather(p, earlier, got_earlier, (bsend, brecv), 0, blocal.at[0])
    items = reduces(g, [source], [from_y, from_z], scratch)
    after = [
        BlockGather(p, mine, got, (bsend, brecv), 3 + 3 * n, blocal.at[1 + n], item.columns)
        for n, item in enumerate(items)
    ]
    steps = in_turn(items)
    g.greet(p)
    steps[0]()
    before.start()

    def total(n):
        item = items[n]
        item.finish(arrived=n == 0)
        loads = [
            pltpu.make_async_copy(item.cut(source, g.z, g.y), item.cut(terms, 0), blocal.at[3]),
            pltpu.make_async_copy(item.cut(from_y, g.z), item.cut(terms, 1), blocal.at[4]),
        ]
        for k in range(3):
            loads.append(pltpu.make_async_copy(item.cut(from_z, k), item.cut(terms, 2 + k), blocal.at[5 + k]))
        for load in loads:
            load.start()
        for load in loads:
            load.wait()
        add_up(terms.at[0], [terms.at[k] for k in range(1, 5)], mine, item.columns)
        after[n].start()

    for n, step in enumerate(steps[1:]):
        if n == 3:
            before.relay()
        step()
    total(0)
    after[0].relay()
    total(1)
    before.finish()
    after[0].finish()
    after[1].relay()
    after[1].finish()


def last_sum(part, earlier, n_tp, collective_id):
    operands, results, scratch = reduce_parts([part])
    whole = jax.ShapeDtypeStruct((n_tp,) + earlier.shape, bf16)
    _, _, got, got_earlier = pl.pallas_call(
        last_sum_kernel,
        out_shape=results + (whole, whole),
        in_specs=[ANY, ANY],
        out_specs=(ANY,) * 4,
        scratch_shapes=scratch
        + [pltpu.SemaphoreType.DMA((9,))] * 2
        + [pltpu.SemaphoreType.DMA((8,)), pltpu.VMEM((5,) + earlier.shape, bf16), pltpu.VMEM(earlier.shape, bf16)],
        compiler_params=params(collective_id),
    )(part, earlier)
    return got, got_earlier


def assemble_kernel(*refs):
    inputs, refs = refs[: 7 * LAYERS], refs[7 * LAYERS :]
    qkv_ref, out_ref, fc_ref, proj_ref = refs[:4]
    vector_refs, (tiles, sems) = refs[4:13], refs[13:]
    t, f = lax.axis_index("tp"), lax.axis_index("fsdp")
    z, y = f // 2, f % 2
    loads = []
    for layer in range(LAYERS):
        for w in range(2):
            part, near, far = inputs[7 * layer + 1 + 3 * w : 7 * layer + 4 + 3 * w]
            n = 2 * layer + w
            loads.append(
                [
                    pltpu.make_async_copy(part.at[z, y], tiles.at[n, 0], sems.at[n, 0]),
                    pltpu.make_async_copy(near.at[z], tiles.at[n, 1], sems.at[n, 1]),
                    pltpu.make_async_copy(far, tiles.at[n, 2:5], sems.at[n, 2]),
                ]
            )
    for load in sum(loads, []):
        load.start()
    n_tp = inputs[0].shape[0]
    step = HEADS // n_tp * HEAD
    width = D - step * (n_tp - 1)
    counts = [step] * (n_tp - 1) + [width]
    for layer in range(LAYERS):
        got = inputs[7 * layer]
        for i in range(3):
            for k, count in enumerate(counts):
                value = got[k, :, i * WIDE : i * WIDE + count].astype(f32)
                qkv_ref[layer, :, i * D + k * step : i * D + k * step + count] = value
        for k, count in enumerate(counts):
            out_ref[layer, :, k * step : k * step + count] = got[k, :, 3 * WIDE : 3 * WIDE + count].astype(f32)
        extra = got[:, :, 3 * WIDE + step : 4 * WIDE].astype(f32)
        total = jnp.sum(extra, axis=0).T
        own = got[t, :, 3 * WIDE + step : 4 * WIDE].astype(f32).T
        skip = width - step
        for v in range(8):
            vector_refs[v][layer : layer + 1, :] = total[skip + v : skip + v + 1, :]
        vector_refs[8][layer : layer + 1, :] = own[skip + 8 : skip + 9, :]
        for w in range(2):
            n = 2 * layer + w
            for load in loads[n]:
                load.wait()
            total = tiles[n, 0].astype(f32)
            for k in range(1, 5):
                total = total + tiles[n, k].astype(f32)
            if w:
                fc_ref[layer] = total
            else:
                proj_ref[layer] = total.T


def assemble(layers):
    rows, width = layers[0][1].shape[2:]
    outs = [(LAYERS, rows, 3 * D), (LAYERS, rows, D), (LAYERS, rows, width), (LAYERS, width, rows)]
    outs += [(LAYERS, rows)] * 9
    return pl.pallas_call(
        assemble_kernel,
        out_shape=tuple(jax.ShapeDtypeStruct(o, f32) for o in outs),
        in_specs=([IN_VMEM] + [ANY] * 6) * LAYERS,
        out_specs=(IN_VMEM,) * len(outs),
        scratch_shapes=[
            pltpu.VMEM((2 * LAYERS, 5, rows, width), bf16),
            pltpu.SemaphoreType.DMA((2 * LAYERS, 3)),
        ],
        compiler_params=pltpu.CompilerParams(vmem_limit_bytes=60 * 2**20),
    )(*sum((list(layer) for layer in layers), []))


class Spread:
    def __init__(self, group, source, target, sems, chunks):
        self.g, self.source, self.target, self.sems = group, source, target, sems
        count = source.shape[1] // 128
        ends = [128 * (count * sum(chunks[: c + 1]) // sum(chunks)) for c in range(len(chunks))]
        self.columns = [slice(a, b) for a, b in zip([0] + ends, ends)]
        self.partner = group.at(group.z, 1 - group.y)
        self.origins = (group.mate, group.far_inner, group.far_end)

    def piece(self, member, c, index, to, own=False, send_index=None):
        target = self.target.at[member, :, self.columns[c]]
        source = self.source.at[:, self.columns[c]] if own else target
        send = None if send_index is None else 9 * c + send_index
        return self.g.copy(source, target, self.sems, 9 * c + index, to, send)

    def own(self, c):
        g = self.g
        arrives = jnp.where(g.inner, 2, 3)
        return [
            self.piece(g.member, c, arrives, g.at(g.far_inner, g.y), True, 2),
            self.piece(g.member, c, 1, g.at(g.mate, g.y), True),
            self.piece(g.member, c, 0, self.partner, True),
        ]

    def relayed(self, c, k):
        g = self.g
        return self.piece(g.at(self.origins[k - 1], g.y), c, 3 + k, self.partner)

    def passed(self, c, k):
        g = self.g
        return self.piece(g.at(self.origins[k - 1], g.y), c, k, g.at(g.mate, g.y), send_index=5 + k)

    def keep(self):
        return pltpu.make_async_copy(
            self.source, self.target.at[self.g.member], self.sems[0].at[9 * len(self.columns)]
        )

    def start(self, first=0, last=None):
        if first == 0:
            self.keep().start()
        for c in range(len(self.columns))[first:last]:
            for copy in self.own(c):
                copy.start()

    def relay(self, c):
        g = self.g
        for k in (1, 2, 3):
            self.piece(g.at(self.origins[k - 1], g.y), c, k, self.partner).wait_recv()
            if k > 1:

                @pl.when(g.inner)
                def _(k=k):
                    self.passed(c, k).start()

            self.relayed(c, k).start()

    def finish(self):
        g = self.g
        for c in range(len(self.columns)):
            self.piece(self.partner, c, 0, self.partner).wait_recv()
            for k in (1, 2, 3):
                self.piece(g.at(self.origins[k - 1], 1 - g.y), c, 3 + k, self.partner).wait_recv()
                self.relayed(c, k).wait_send()
            for copy in self.own(c):
                copy.wait_send()

            @pl.when(g.inner)
            def _(c=c):
                self.passed(c, 2).wait_send()
                self.passed(c, 3).wait_send()

        self.keep().wait()


def spread_parts(shard, chunks):
    if shard is None:
        return (), (), []
    whole = jax.ShapeDtypeStruct((GROUP,) + shard.shape, shard.dtype)
    return (shard,), (whole,), [pltpu.SemaphoreType.DMA((9 * len(chunks) + 1,))] * 2


def spread_kernel(chunks, source, target, send, recv):
    g = Group()
    g.greet_group()
    spread = Spread(g, source, target, (send, recv), chunks)
    spread.start(0, 2)
    for c in range(len(chunks)):
        spread.relay(c)
        spread.start(c + 2, c + 3)
    spread.finish()


def spread_only(shard, chunks, collective_id):
    operands, results, scratch = spread_parts(shard, chunks)
    return pl.pallas_call(
        functools.partial(spread_kernel, chunks),
        out_shape=results[0],
        in_specs=[ANY],
        out_specs=ANY,
        scratch_shapes=scratch,
        compiler_params=params(collective_id),
    )(shard)


def row_chunks(rows, body):
    @pl.loop(0, rows // ROW_CHUNK)
    def _(i):
        body(pl.ds(pl.multiple_of(i * ROW_CHUNK, ROW_CHUNK), ROW_CHUNK))


def tiles(extent, body):
    whole = extent // TILE

    @pl.loop(0, whole)
    def _(i):
        body(pl.ds(pl.multiple_of(i * TILE, TILE), TILE))

    if extent % TILE:
        body(pl.ds(whole * TILE, extent % TILE))


def pair_rows(ref, x):
    both = ref[pl.ds(2 * x, 2)]
    return both.reshape(2 * both.shape[1], both.shape[2])


def put_pair(ref, x, at, value):
    ref[pl.ds(2 * x, 2), :, at] = value.reshape(2, value.shape[0] // 2, value.shape[1]).astype(ref.dtype)


def norm_stats(x):
    centred = x - jnp.mean(x, -1, keepdims=True)
    scale = lax.rsqrt(jnp.mean(centred * centred, -1, keepdims=True) + norm_eps)
    return centred * scale, scale


def lanes_up(width):
    return -(-width // 128) * 128


def proj_part(w_b, width):
    return w_b.at[:, lanes_up(width) :]


FIRST_CHUNKS = (3, 3, 3, 3, 3, 2)
FF_CHUNKS = (5, 5, 4, 2)
ATTN_CHUNKS = (5, 6, 6, 5, 4)


def ff_fwd_kernel(n, *refs):
    x_ref, vec_ref, fcb_ref, wb_hbm = refs[:4]
    shard, refs = refs[4 : 4 + n], refs[4 + n :]
    out_ref, all_hbm, pre_hbm, hid_hbm = refs[:4]
    whole, refs = refs[4 : 4 + n], refs[4 + n :]
    wfc, wproj, buf, pre, hid, part, from_core, over_out, from_over, send, recv, local = refs[:12]
    p, g = Peers(), Group()
    spread = Spread(g, shard[0], whole[0], refs[12:], FF_CHUNKS) if n else None
    rows = x_ref.shape[0]
    sems = (send, recv)
    gather = Gather(p, buf, sems)
    scatter = Scatter(p, part, from_core, over_out, from_over, sems)
    width = fcb_ref.shape[1]
    load_fc = pltpu.make_async_copy(wb_hbm.at[:, : wfc.shape[1]], wfc, local.at[0])
    load_proj = pltpu.make_async_copy(proj_part(wb_hbm, width), wproj, local.at[1])
    load_fc.start()
    load_proj.start()

    def norm(at):
        hat, _ = norm_stats(x_ref[at, :])
        buf[p.t, at, :] = (hat * vec_ref[5:6, :] + vec_ref[6:7, :]).astype(bf16)

    row_chunks(rows, norm)
    if n:
        g.greet(p)
    else:
        p.greet()
    gather.start()
    if n:
        spread.start(0, 1)
    gather.wait_chip()
    load_fc.wait()

    def up(x):
        def tile(at):
            value = mm(pair_rows(buf, x), wfc[:, at]) + fcb_ref[:, at]
            put_pair(pre, x, at, value)
            put_pair(hid, x, at, gelu_tanh(value))

        tiles(width, tile)

    def down(x):
        def tile(at):
            put_pair(part, x, at, mm(pair_rows(hid, x), wproj[at, :width], NT))

        tiles(D, tile)

    up(p.x)
    if n:
        spread.start(1, 2)
    gather.relay()
    gather.wait_diag()
    if n:
        spread.relay(0)
    keep_all = pltpu.make_async_copy(buf, all_hbm, local.at[2])
    keep_all.start()
    up(1 - p.x)
    keep_pre = pltpu.make_async_copy(pre, pre_hbm, local.at[3])
    keep_hid = pltpu.make_async_copy(hid, hid_hbm, local.at[4])
    keep_pre.start()
    keep_hid.start()
    load_proj.wait()
    down(1 - p.x)
    scatter.far_to_core().start()
    scatter.send_over()
    if n:
        spread.start(2, 3)
    down(p.x)
    scatter.near_to_core().start()
    if n:
        spread.relay(1)
        spread.start(3)
    scatter.wait()

    def final(at):
        out_ref[at, :] = x_ref[at, :] + scatter.rows(at) + vec_ref[7:8, :]

    row_chunks(rows, final)
    if n:
        spread.relay(2)
        spread.relay(3)
    gather.finish()
    scatter.finish()
    for copy in (keep_all, keep_pre, keep_hid):
        copy.wait()
    if n:
        spread.finish()


def scatter_scratch(n_tp, rows):
    return [
        pltpu.VMEM((n_tp, rows, D), bf16),
        pltpu.VMEM((2, rows, D), bf16),
        pltpu.VMEM((rows, D), bf16),
        pltpu.VMEM((rows, D), bf16),
        pltpu.SemaphoreType.DMA((6,)),
        pltpu.SemaphoreType.DMA((6,)),
    ]


def params(collective_id):
    return pltpu.CompilerParams(collective_id=collective_id, has_side_effects=True, vmem_limit_bytes=60 * 2**20)


def ff_fwd(x, vecs, fc_bias, w_b, n_tp, shard, collective_id):
    rows, width = x.shape[0], fc_bias.shape[1]
    block = (n_tp, rows)
    operands, results, sems = spread_parts(shard, FF_CHUNKS)
    return pl.pallas_call(
        functools.partial(ff_fwd_kernel, len(operands)),
        out_shape=(
            jax.ShapeDtypeStruct((rows, D), f32),
            jax.ShapeDtypeStruct(block + (D,), bf16),
            jax.ShapeDtypeStruct(block + (width,), f32),
            jax.ShapeDtypeStruct(block + (width,), bf16),
        )
        + results,
        in_specs=[IN_VMEM, IN_VMEM, IN_VMEM, ANY] + [ANY] * len(operands),
        out_specs=(IN_VMEM, ANY, ANY, ANY) + (ANY,) * len(operands),
        scratch_shapes=[
            pltpu.VMEM((D, lanes_up(width)), bf16),
            pltpu.VMEM((D, lanes_up(width)), bf16),
            pltpu.VMEM(block + (D,), bf16),
            pltpu.VMEM(block + (width,), f32),
            pltpu.VMEM(block + (width,), bf16),
        ]
        + scatter_scratch(n_tp, rows)
        + [pltpu.SemaphoreType.DMA((5,))]
        + sems,
        compiler_params=params(collective_id),
        cost_estimate=pl.CostEstimate(
            flops=4 * n_tp * rows * D * width, bytes_accessed=40 * 2**20, transcendentals=n_tp * rows * width
        ),
    )(x, vecs, fc_bias, w_b, *operands)


def gelu_slope(u):
    a = 0.7978845608028654
    square = u * u
    t = jnp.tanh(a * (u + 0.044715 * u * square))
    return 0.5 * (1.0 + t) + 0.5 * u * (1.0 - t * t) * (a * (1.0 + 3 * 0.044715 * square))


def norm_back(x, dy, gain):
    hat, scale = norm_stats(x)
    d_hat = dy * gain
    inner = d_hat - jnp.mean(d_hat, -1, keepdims=True) - hat * jnp.mean(d_hat * hat, -1, keepdims=True)
    return scale * inner, dy * hat


def add_rows(ref, row, value):
    ref[row : row + 1, :] += jnp.sum(value, axis=0, keepdims=True)


def ff_bwd_kernel(n, *refs):
    g_ref, x_ref, vec_ref, all_hbm, pre_hbm, hid_hbm, wb_hbm = refs[:7]
    sources, refs = refs[7 : 7 + n], refs[7 + n :]
    out_ref, sums_ref, fcb_ref, dfc_hbm, dproj_hbm = refs[:5]
    results, refs = refs[5 : 5 + 2 * n], refs[5 + 2 * n :]
    wfc, wproj, buf, other, pre, dpre, stage, part, from_core, over_out, from_over, send, recv, local = refs[:14]
    p, g = Peers(), Group()
    sums = reduces(g, sources, results, refs[14:])
    rows = x_ref.shape[0]
    n_tp, width = buf.shape[0], fcb_ref.shape[1]
    sems = (send, recv)
    gather = Gather(p, buf, sems)
    scatter = Scatter(p, part, from_core, over_out, from_over, sems)
    load_proj = pltpu.make_async_copy(proj_part(wb_hbm, width), wproj, local.at[0])
    load_pre = pltpu.make_async_copy(pre_hbm, pre, local.at[1])
    load_fc = pltpu.make_async_copy(wb_hbm.at[:, : wfc.shape[1]], wfc, local.at[2])
    load_other = pltpu.make_async_copy(hid_hbm, other, local.at[3])
    for copy in (load_proj, load_pre, load_fc, load_other):
        copy.start()
    sums_ref[...] = jnp.zeros_like(sums_ref)
    fcb_ref[...] = jnp.zeros_like(fcb_ref)

    def lower(at):
        low = g_ref[at, :].astype(bf16)
        buf[p.t, at, :] = low
        add_rows(sums_ref, 7, low.astype(f32))

    row_chunks(rows, lower)
    if n:
        g.greet(p)
    else:
        p.greet()
    gather.start()
    steps = in_turn(sums) if n else []

    def advance():
        if steps:
            steps.pop(0)()

    advance()
    gather.wait_chip()
    load_proj.wait()
    load_pre.wait()

    def through(x):
        def tile(at):
            d_hidden = mm(pair_rows(buf, x), wproj[:, at])
            u = pre[pl.ds(2 * x, 2), :, at].reshape(2 * rows, -1)
            low = (gelu_slope(u) * d_hidden).astype(bf16)
            put_pair(dpre, x, at, low)
            fcb_ref[:, at] += jnp.sum(low.astype(f32), axis=0, keepdims=True)

        tiles(width, tile)

    def down(x):
        def tile(at):
            put_pair(part, x, at, mm(pair_rows(dpre, x), wfc[at, :width], NT))

        tiles(D, tile)

    through(p.x)
    gather.relay()
    advance()
    gather.wait_diag()
    through(1 - p.x)
    advance()
    load_fc.wait()
    down(1 - p.x)
    scatter.far_to_core().start()
    scatter.send_over()
    advance()
    down(p.x)
    scatter.near_to_core().start()
    advance()

    def outer(left, right, target, sem):
        whole = D // TILE
        rest = D - whole * TILE
        flat = right[...].reshape(n_tp * rows, width)

        def tile(i, size):
            at = pl.ds(pl.multiple_of(i * TILE, TILE), size)
            value = mm(left[:, :, at].reshape(n_tp * rows, size), flat, TN)
            stage[at, :] = value.astype(bf16)

        @pl.loop(0, whole)
        def _(i):
            tile(i, TILE)

        if rest:
            tile(whole, rest)
        return pltpu.make_async_copy(stage, target, sem)

    load_other.wait()
    store = outer(buf, other, dproj_hbm, local.at[4])
    store.start()
    gather.finish()
    load_all = pltpu.make_async_copy(all_hbm, buf, local.at[5])
    load_all.start()
    advance()
    scatter.wait()

    def final(at):
        dy = scatter.rows(at)
        dx, d_gain = norm_back(x_ref[at, :], dy, vec_ref[5:6, :])
        add_rows(sums_ref, 5, d_gain)
        add_rows(sums_ref, 6, dy)
        out_ref[at, :] = g_ref[at, :] + dx

    row_chunks(rows, final)
    load_all.wait()
    store.wait()
    store = outer(buf, dpre, dfc_hbm, local.at[6])
    store.start()
    while steps:
        advance()
    scatter.finish()
    store.wait()
    for i, item in enumerate(sums):
        item.finish(arrived=i == 0)


def ff_bwd(grad, x, vecs, all_rows, pre, hidden, w_b, n_tp, payload, collective_id):
    rows, width = x.shape[0], pre.shape[2]
    block = (n_tp, rows)
    operands, results, more = reduce_parts(payload)
    return pl.pallas_call(
        functools.partial(ff_bwd_kernel, len(payload)),
        out_shape=(
            jax.ShapeDtypeStruct((rows, D), f32),
            jax.ShapeDtypeStruct((8, D), f32),
            jax.ShapeDtypeStruct((1, width), f32),
            jax.ShapeDtypeStruct((D, width), bf16),
            jax.ShapeDtypeStruct((D, width), bf16),
        )
        + results,
        in_specs=[IN_VMEM] * 3 + [ANY] * (4 + len(payload)),
        out_specs=(IN_VMEM, IN_VMEM, IN_VMEM) + (ANY,) * (2 + 2 * len(payload)),
        scratch_shapes=[
            pltpu.VMEM((D, lanes_up(width)), bf16),
            pltpu.VMEM((D, lanes_up(width)), bf16),
            pltpu.VMEM(block + (D,), bf16),
            pltpu.VMEM(block + (width,), bf16),
            pltpu.VMEM(block + (width,), f32),
            pltpu.VMEM(block + (width,), bf16),
            pltpu.VMEM((D, width), bf16),
        ]
        + scatter_scratch(n_tp, rows)
        + [pltpu.SemaphoreType.DMA((7,))]
        + more,
        compiler_params=params(collective_id),
        cost_estimate=pl.CostEstimate(
            flops=8 * n_tp * rows * D * width, bytes_accessed=50 * 2**20, transcendentals=n_tp * rows * width
        ),
    )(grad, x, vecs, all_rows, pre, hidden, w_b, *operands)


HALVES = [(micro, half) for micro in range(MICRO) for half in range(2)]


def half_lanes(half):
    return slice(half * WIDE // 2, (half + 1) * WIDE // 2)


class Share:
    def __init__(self, group, kv, sems):
        self.g, self.kv, self.sems = group, kv, sems
        self.partner = group.at(group.z, 1 - group.y)

    def piece(self, member, part, index, to):
        micro, half = part
        ref = self.kv.at[member, micro, :, :, half_lanes(half)]
        return self.g.copy(ref, ref, self.sems, (2 * micro + half) * 7 + index, to)

    def own(self, part):
        g = self.g
        return [self.piece(g.member, part, 0, self.partner)] + [
            self.piece(g.member, part, k, g.at(g.ahead(k), g.y)) for k in (1, 2, 3)
        ]

    def relayed(self, part):
        g = self.g
        return [self.piece(g.at(g.behind(k), g.y), part, 3 + k, self.partner) for k in (1, 2, 3)]

    def start(self, *part):
        for copy in self.own(part):
            copy.start()

    def relay(self, *part):
        g = self.g
        for k, copy in zip((1, 2, 3), self.relayed(part)):
            self.piece(g.at(g.behind(k), g.y), part, k, self.partner).wait_recv()
            copy.start()

    def wait(self, *part):
        g = self.g
        self.piece(self.partner, part, 0, self.partner).wait_recv()
        for k in (1, 2, 3):
            self.piece(g.at(g.behind(k), 1 - g.y), part, 3 + k, self.partner).wait_recv()

    def finish(self):
        for part in HALVES:
            for copy in self.own(part) + self.relayed(part):
                copy.wait_send()


class GroupSum:
    def __init__(self, group, parts, from_y, to_z, from_z, sems):
        self.g, self.parts, self.sems = group, parts, sems
        self.from_y, self.to_z, self.from_z = from_y, to_z, from_z

    def across(self, micro, half):
        g, lanes = self.g, half_lanes(half)
        return g.copy(
            self.parts.at[micro, :, 1 - g.y, :, :, lanes],
            self.from_y.at[micro, :, :, :, lanes],
            self.sems,
            (2 * micro + half) * 4,
            g.at(g.z, 1 - g.y),
        )

    def along(self, micro, half, k):
        g, lanes = self.g, half_lanes(half)
        to = g.ahead(k)
        return g.copy(
            self.to_z.at[micro, to, :, :, lanes],
            self.from_z.at[micro, k - 1, :, :, lanes],
            self.sems,
            (2 * micro + half) * 4 + k,
            g.at(to, g.y),
        )

    def start(self, micro, half):
        self.across(micro, half).start()

    def turn(self, micro, half):
        lanes = half_lanes(half)
        self.across(micro, half).wait_recv()

        @pl.loop(0, 4)
        def _(z):
            for kv in range(2):
                total = self.parts[micro, z, self.g.y, kv, :, lanes] + self.from_y[micro, z, kv, :, lanes]
                self.to_z[micro, z, kv, :, lanes] = total

        for k in (1, 2, 3):
            self.along(micro, half, k).start()

    def wait(self, micro):
        for half in range(2):
            for k in (1, 2, 3):
                self.along(micro, half, k).wait_recv()

    def total(self, micro, kv):
        g = self.g
        value = self.parts[micro, g.z, g.y, kv].astype(f32) + self.from_y[micro, g.z, kv].astype(f32)
        for k in range(3):
            value = value + self.from_z[micro, k, kv].astype(f32)
        return value.astype(bf16)

    def finish(self, micro):
        for half in range(2):
            self.across(micro, half).wait_send()
            for k in (1, 2, 3):
                self.along(micro, half, k).wait_send()


WIDE = 512
HEAD_PAIRS = WIDE // (2 * HEAD)
PROMPT_CHUNKS = PROMPT // CHUNK
CONT_CHUNKS = CONT_LEN // CHUNK


def chunk_at(c, base=0):
    return pl.ds(pl.multiple_of(base + c * CHUNK, CHUNK), CHUNK)


def key_limit(member):
    row = lax.broadcasted_iota(jnp.int32, (1, TOK_DEV), 1)
    return jnp.where(row < PROMPT_DEV, member * PROMPT_DEV + row, PROMPT - PROMPT_DEV + row)


def half_of(value, half):
    lane = lax.broadcasted_iota(jnp.int32, value.shape, 1)
    return jnp.where((lane >= HEAD * half) & (lane < HEAD * (half + 1)), value, jnp.zeros_like(value))


def fold(value, op):
    return op(value.reshape(value.shape[0] // 8, 8, value.shape[1]), axis=0)


def over_keys(body, prompt, own, carry):
    carry = lax.fori_loop(0, PROMPT_CHUNKS, lambda c, carry: body(c, lambda i: prompt(c, i), carry), carry)
    return lax.fori_loop(
        0, CONT_CHUNKS, lambda c, carry: body(PROMPT_CHUNKS + c, lambda i: own(c, i), carry), carry
    )


def head_pairs(head, finish):
    @pl.loop(0, HEAD_PAIRS)
    def _(pair):
        lanes = pl.ds(pl.multiple_of(pair * 2 * HEAD, 2 * HEAD), 2 * HEAD)
        head(pair, lanes, 0)

        @pl.when(pair < HEAD_PAIRS - 1)
        def _():
            head(pair, lanes, 1)

        finish(pair, lanes)


def run_hooks(hooks, micro, pair, half):
    for at in range(HEAD_PAIRS):
        if half == 0 and (micro, at) in hooks:

            @pl.when(pair == at)
            def _(at=at):
                for hook in hooks[micro, at]:
                    hook()


def to_slots(target, micro, first, value, lanes):
    per = target.shape[1] // MICRO
    row = first
    while row < first + value.shape[0]:
        slot, within = row // per, row % per
        count = min(per - within, first + value.shape[0] - row)
        target[slot, micro * per + within : micro * per + within + count, lanes] = value[
            row - first : row - first + count
        ]
        row += count


def pair_to_blocks(target, x, value):
    per = value.shape[0] // (2 * MICRO)
    for core in range(2):
        for micro in range(MICRO):
            at = pl.ds(pl.multiple_of((2 * x + core) * per, per), per)
            first = (core * MICRO + micro) * per
            target[micro, at, :] = value[first : first + per]


def attn_fwd_kernel(n, *refs):
    x_ref, vec_ref, bias_ref, wqkv_hbm = refs[:4]
    shard, refs = refs[4 : 4 + n], refs[4 + n :]
    out_ref, lse_ref, all_hbm, own_hbm, kv_hbm, mix_hbm, wout_hbm = refs[:7]
    whole, refs = refs[7 : 7 + n], refs[7 + n :]
    wqkv, wout, wparts, buf, own, kv, mix, s_ref, p_ref, o_ref = refs[:10]
    part, from_core, over_out, from_over, send, recv, gsend, grecv, wsend, wrecv, local = refs[10:21]
    msend, mrecv = refs[21:23]
    p, g = Peers(), Group()
    spread = Spread(g, shard[0], whole[0], refs[23:], ATTN_CHUNKS) if n else None
    mixes = BlockGather(p, mix, mix_hbm, (msend, mrecv), 0, local.at[5])
    rows = x_ref.shape[0]
    n_tp = buf.shape[0]
    step = HEADS // n_tp * HEAD
    width = wparts.shape[1]
    sems = (send, recv)
    gather = Gather(p, buf, sems)
    scatter = Scatter(p, part, from_core, over_out, from_over, sems)
    share = Share(g, kv, (gsend, grecv))
    load_qkv = pltpu.make_async_copy(wqkv_hbm.at[:, : 3 * WIDE], wqkv, local.at[0])
    load_qkv.start()

    def rows_for(t):
        return wqkv_hbm.at[pl.ds(pl.multiple_of(t * step, 128), width), 3 * WIDE : 4 * WIDE]

    keep_part = pltpu.make_async_copy(rows_for(p.t), wparts.at[p.t], local.at[1])
    keep_part.start()
    give_parts = [
        p.copy(rows_for(t), wparts.at[p.t], (wsend, wrecv), i, t) for i, t in enumerate((p.core, p.over, p.diag))
    ]

    def norm(at):
        hat, _ = norm_stats(x_ref[at, :])
        buf[p.t, at, :] = (hat * vec_ref[0:1, :] + vec_ref[1:2, :]).astype(bf16)

    row_chunks(rows, norm)
    g.greet(p, True)
    gather.start()
    for copy in give_parts:
        copy.start()
    if n:
        spread.start(0, 1)
    gather.wait_chip()
    load_qkv.wait()

    def project(x):
        for i in range(3):
            value = mm(pair_rows(buf, x), wqkv[:, i * WIDE : (i + 1) * WIDE]) + bias_ref[i : i + 1, :]
            low = value.astype(bf16)
            if i == 0:
                low = low * HEAD ** (-0.5)
            pair_to_blocks(own.at[i], x, low)

    project(p.x)
    gather.relay()
    gather.wait_diag()
    project(1 - p.x)
    for micro in range(MICRO):
        for i in range(2):
            kv[g.member, micro, i] = own[1 + i, micro, :PROMPT_DEV, :]
    share.start(0, 0)
    if n:
        spread.start(1, 2)
    hooks = {
        (0, 1): [lambda: share.relay(0, 1), lambda: share.start(1, 0)],
        (0, 2): [lambda: share.wait(0, 1)],
        (0, 3): [lambda: share.relay(1, 0), lambda: share.start(1, 1)],
        (1, 0): [lambda: share.wait(1, 0)],
        (1, 1): [lambda: share.relay(1, 1)],
        (1, 2): [lambda: share.wait(1, 1)],
    }
    if n:
        hooks[0, 0] = [lambda: spread.start(2, 3)]
        hooks[0, 2] += [lambda: spread.relay(1)]
        hooks[0, 3] += [lambda: spread.start(3, 4)]
        hooks[1, 1] += [lambda: spread.relay(2), lambda: spread.start(4)]
    keep_all = pltpu.make_async_copy(buf, all_hbm, local.at[2])
    keep_own = pltpu.make_async_copy(own, own_hbm, local.at[3])
    keep_all.start()
    keep_own.start()
    limit = key_limit(g.member)
    sub = lax.broadcasted_iota(jnp.int32, (CHUNK, TOK_DEV), 0)

    share.relay(0, 0)
    share.start(0, 1)
    if n:
        spread.relay(0)
    share.wait(0, 0)

    for micro in range(MICRO):

        def head(pair, lanes, half, micro=micro):
            run_hooks(hooks, micro, pair, half)
            qh = half_of(own[0, micro, :, lanes], half)

            def first(c, load, top):
                s = jnp.where(sub + c * CHUNK <= limit, mm(load(0), qh, NT), -1e30)
                s_ref[chunk_at(c), :] = s
                return jnp.maximum(top, fold(s, jnp.max))

            top = over_keys(
                first,
                lambda c, i: kv[c, micro, i, :, lanes],
                lambda c, i: own[1 + i, micro, chunk_at(c, PROMPT_DEV), lanes],
                jnp.full((8, TOK_DEV), -1e30, f32),
            )
            top = jnp.max(top, axis=0, keepdims=True)

            def second(c, total):
                e = jnp.exp(s_ref[chunk_at(c), :] - top)
                p_ref[chunk_at(c), :] = e.astype(bf16)
                return total + fold(e, jnp.sum)

            total = lax.fori_loop(0, KEYS // CHUNK, second, jnp.zeros((8, TOK_DEV), f32))
            total = jnp.sum(total, axis=0, keepdims=True)
            values = kv[:, micro, 1, :, lanes].reshape(PROMPT, 2 * HEAD)
            out = mm(values, p_ref[:PROMPT, :], TN) + mm(own[2, micro, PROMPT_DEV:, lanes], p_ref[PROMPT:, :], TN)
            at = slice(HEAD * half, HEAD * (half + 1))
            o_ref[at, :] = out[at, :] / total
            lse_ref[micro, pair, half : half + 1, :] = top + jnp.log(total)

        def finish(pair, lanes, micro=micro):
            @pl.when(pair == HEAD_PAIRS - 1)
            def _():
                o_ref[HEAD:, :] = jnp.zeros((HEAD, TOK_DEV), f32)

            to_slots(mix, micro, 0, o_ref[...].T.astype(bf16), lanes)

        head_pairs(head, finish)

    keep_kv = pltpu.make_async_copy(kv, kv_hbm, local.at[4])
    keep_kv.start()
    keep_part.wait()
    for i, t in enumerate((p.core, p.over, p.diag)):
        p.copy(rows_for(t), wparts.at[t], (wsend, wrecv), i, t).wait_recv()
    for t in range(n_tp):
        count = min(WIDE, D - t * step)
        wout[:width, t * step : t * step + count] = wparts[t, :, :count]
    wout[width:, :] = jnp.zeros((WIDE - width, D), bf16)

    @pl.when(p.t < n_tp - 1)
    def _():
        wout[step:width, :] = jnp.zeros((width - step, D), bf16)

    keep_out = pltpu.make_async_copy(wout, wout_hbm, local.at[6])
    keep_out.start()

    def down(x):
        def tile(at):
            put_pair(part, x, at, mm(pair_rows(mix, x), wout[:, at]))

        tiles(D, tile)

    down(1 - p.x)
    scatter.far_to_core().start()
    scatter.send_over()
    down(p.x)
    scatter.near_to_core().start()
    if n:
        spread.relay(3)
    scatter.wait()
    mixes.start()

    def final(at):
        out_ref[at, :] = x_ref[at, :] + (scatter.rows(at) + vec_ref[4:5, :])

    row_chunks(rows, final)
    mixes.relay()
    if n:
        spread.relay(4)
    gather.finish()
    scatter.finish()
    share.finish()
    for copy in give_parts:
        copy.wait_send()
    for copy in (keep_all, keep_own, keep_kv, keep_out):
        copy.wait()
    mixes.finish()
    if n:
        spread.finish()


def attn_shapes(n_tp, rows):
    return (
        ((n_tp, rows, D), bf16),
        ((3, MICRO, TOK_DEV, WIDE), bf16),
        ((GROUP, MICRO, 2, PROMPT_DEV, WIDE), bf16),
        ((n_tp, rows, WIDE), bf16),
    )


def attn_fwd(x, vecs, biases, w_a, n_tp, shard, collective_id):
    rows = x.shape[0]
    width = D - HEADS // n_tp * HEAD * (n_tp - 1)
    saved = attn_shapes(n_tp, rows)
    operands, results, sems = spread_parts(shard, ATTN_CHUNKS)
    return pl.pallas_call(
        functools.partial(attn_fwd_kernel, len(operands)),
        out_shape=(
            jax.ShapeDtypeStruct((rows, D), f32),
            jax.ShapeDtypeStruct((MICRO, HEAD_PAIRS, 8, TOK_DEV), f32),
        )
        + tuple(jax.ShapeDtypeStruct(*s) for s in saved[:3])
        + (jax.ShapeDtypeStruct((n_tp,) + saved[3][0], bf16), jax.ShapeDtypeStruct((WIDE, D), bf16))
        + results,
        in_specs=[IN_VMEM, IN_VMEM, IN_VMEM, ANY] + [ANY] * len(operands),
        out_specs=(IN_VMEM, IN_VMEM) + (ANY,) * (5 + len(operands)),
        scratch_shapes=[pltpu.VMEM((D, 3 * WIDE), bf16), pltpu.VMEM((WIDE, D), bf16), pltpu.VMEM((n_tp, width, WIDE), bf16)]
        + [pltpu.VMEM(*s) for s in saved]
        + [
            pltpu.VMEM((KEYS, TOK_DEV), f32),
            pltpu.VMEM((KEYS, TOK_DEV), bf16),
            pltpu.VMEM((2 * HEAD, TOK_DEV), f32),
        ]
        + scatter_scratch(n_tp, rows)
        + [
            pltpu.SemaphoreType.DMA((14 * MICRO,)),
            pltpu.SemaphoreType.DMA((14 * MICRO,)),
            pltpu.SemaphoreType.DMA((3,)),
            pltpu.SemaphoreType.DMA((3,)),
            pltpu.SemaphoreType.DMA((7,)),
            pltpu.SemaphoreType.DMA((3,)),
            pltpu.SemaphoreType.DMA((3,)),
        ]
        + sems,
        compiler_params=params(collective_id),
        cost_estimate=pl.CostEstimate(flops=10**11, bytes_accessed=30 * 2**20, transcendentals=0),
    )(x, vecs, biases, w_a, *operands)


def attn_bwd_kernel(n, *refs):
    g_ref, x_ref, vec_ref, lse_ref, all_hbm, own_hbm, kv_hbm, mix_hbm, wqkv_hbm, wout_hbm = refs[:10]
    sources, refs = refs[10 : 10 + n], refs[10 + n :]
    out_ref, sums_ref, cols_ref, dqo_hbm = refs[:4]
    results, refs = refs[4 : 4 + 2 * n], refs[4 + 2 * n :]
    wqkv, wout, buf, other, mixed, own, kv, gm, dkv, from_y, to_z, from_z, dkc, dqkv, stage, stage_out = refs[:16]
    p_ref, dp_ref, ds_ref, o_ref = refs[16:20]
    part, from_core, over_out, from_over, send, recv, gsend, grecv, local = refs[20:29]
    p, g = Peers(), Group()
    sums = reduces(g, sources, results, refs[29:])
    rows = x_ref.shape[0]
    n_tp = buf.shape[0]
    out_step = HEADS // n_tp * HEAD
    out_width = D - out_step * (n_tp - 1)
    sems = (send, recv)
    gather = Gather(p, buf, sems)
    scatter = Scatter(p, part, from_core, over_out, from_over, sems)
    reduce = GroupSum(g, dkv, from_y, to_z, from_z, (gsend, grecv))
    load_out = pltpu.make_async_copy(wout_hbm, wout, local.at[0])
    load_own = pltpu.make_async_copy(own_hbm, own, local.at[1])
    load_kv = pltpu.make_async_copy(kv_hbm, kv, local.at[2])
    load_qkv = pltpu.make_async_copy(wqkv_hbm.at[:, : 3 * WIDE], wqkv, local.at[3])
    load_mix = pltpu.make_async_copy(mix_hbm, mixed, local.at[4])
    load_all = pltpu.make_async_copy(all_hbm, other, local.at[6])
    for copy in (load_out, load_own, load_kv, load_qkv, load_mix, load_all):
        copy.start()
    sums_ref[...] = jnp.zeros_like(sums_ref)

    def lower(at):
        low = g_ref[at, :].astype(bf16)
        buf[p.t, at, :] = low
        add_rows(sums_ref, 4, low.astype(f32))

    row_chunks(rows, lower)
    g.greet(p)
    gather.start()
    hooks = {(1, 1): [lambda: reduce.turn(0, 0)], (1, 2): [lambda: reduce.turn(0, 1)]}
    if n:
        first_sum, second_sum = sums
        first_sum.start(1)
        hooks[0, 1] = [lambda: first_sum.pump(2)]
        hooks[0, 2] = [lambda: first_sum.pump(3)]
        hooks[1, 1] += [lambda: second_sum.start(1)]
        hooks[1, 3] = [lambda: second_sum.pump(1, first_sum)]
    gather.wait_chip()
    load_out.wait()

    def mixed_back(x):
        pair_to_blocks(gm, x, mm(pair_rows(buf, x), wout[...], NT).astype(bf16))

    mixed_back(p.x)
    if n:
        first_sum.start(2)
    gather.relay()
    gather.wait_diag()
    mixed_back(1 - p.x)
    load_own.wait()
    load_kv.wait()
    limit = key_limit(g.member)
    sub = lax.broadcasted_iota(jnp.int32, (CHUNK, TOK_DEV), 0)

    if n:
        first_sum.pump(1, then=lambda: first_sum.start(3))

    for micro in range(MICRO):

        def head(pair, lanes, half, micro=micro):
            run_hooks(hooks, micro, pair, half)
            qh = half_of(own[0, micro, :, lanes], half)
            gh = half_of(gm[micro, :, lanes], half)
            lse = lse_ref[micro, pair, half : half + 1, :]

            def first(c, load, inner):
                s = jnp.where(sub + c * CHUNK <= limit, mm(load(0), qh, NT), -1e30)
                e = jnp.exp(s - lse)
                dp = mm(load(1), gh, NT)
                p_ref[chunk_at(c), :] = e
                dp_ref[chunk_at(c), :] = dp
                return inner + fold(e * dp, jnp.sum)

            inner = over_keys(
                first,
                lambda c, i: kv[c, micro, i, :, lanes],
                lambda c, i: own[1 + i, micro, chunk_at(c, PROMPT_DEV), lanes],
                jnp.zeros((8, TOK_DEV), f32),
            )
            inner = jnp.sum(inner, axis=0, keepdims=True)

            def second(c, put):
                e = p_ref[chunk_at(c), :]
                ds = (e * (dp_ref[chunk_at(c), :] - inner)).astype(bf16)
                ds_ref[chunk_at(c), :] = ds
                put(0, mm(ds, qh))
                put(1, mm(e.astype(bf16), gh))

            @pl.loop(0, PROMPT_CHUNKS)
            def _(c):
                def put(i, value):
                    at = (micro, c // 2, c % 2, i, slice(None), lanes)
                    if half:
                        value = value + dkv[at].astype(f32)
                    dkv[at] = value.astype(bf16)

                second(c, put)

            @pl.loop(0, CONT_CHUNKS)
            def _(c):
                def put(i, value):
                    at = (i, chunk_at(c), lanes)
                    if half:
                        value = value + dkc[at].astype(f32)
                    dkc[at] = value.astype(bf16)

                second(PROMPT_CHUNKS + c, put)

            keys = kv[:, micro, 0, :, lanes].reshape(PROMPT, 2 * HEAD)
            dq = mm(keys, ds_ref[:PROMPT, :], TN) + mm(own[1, micro, PROMPT_DEV:, lanes], ds_ref[PROMPT:, :], TN)
            at = slice(HEAD * half, HEAD * (half + 1))
            o_ref[at, :] = dq[at, :] * HEAD ** (-0.5)

        def finish(pair, lanes, micro=micro):
            @pl.when(pair == HEAD_PAIRS - 1)
            def _():
                o_ref[HEAD:, :] = jnp.zeros((HEAD, TOK_DEV), f32)

            to_slots(dqkv, micro, 0, o_ref[...].T.astype(bf16), lanes)

            @pl.when(pair == HEAD_PAIRS // 2 - 1)
            def _():
                reduce.start(micro, 0)

        head_pairs(head, finish)
        reduce.start(micro, 1)
        for i in range(2):
            to_slots(dqkv, micro, PROMPT_DEV, dkc[i], slice((1 + i) * WIDE, (2 + i) * WIDE))

    load_mix.wait()
    columns = pl.ds(pl.multiple_of(p.t * out_step, 128), out_width)

    def outer(source, target, right, body):
        flat = right.reshape(n_tp * rows, right.shape[-1])

        def tile(at):
            left = source[:, :, at].reshape(n_tp * rows, -1)
            target[at, : flat.shape[1]] = mm(left, flat, TN).astype(bf16)

        body(D, tile)

    reduce.turn(1, 0)
    stage_out[:, out_width:] = jnp.zeros((D, WIDE - out_width), bf16)
    low = buf[:, :, columns].reshape(n_tp * rows, out_width)
    for t in range(n_tp):
        count = out_step if t < n_tp - 1 else out_width
        value = mm(mixed[t].reshape(n_tp * rows, WIDE), low, TN).astype(bf16)
        stage_out[t * out_step : t * out_step + count, :out_width] = value[:count, :]
    keep_out = pltpu.make_async_copy(stage_out, dqo_hbm.at[:, 3 * WIDE :], local.at[5])
    keep_out.start()
    reduce.turn(1, 1)
    if n:
        second_sum.start(2)
    for micro in range(MICRO):
        reduce.wait(micro)
        for i in range(2):
            to_slots(dqkv, micro, 0, reduce.total(micro, i), slice((1 + i) * WIDE, (2 + i) * WIDE))
    if n:
        second_sum.pump(2, first_sum, lambda: second_sum.start(3))
    load_qkv.wait()

    def down(x):
        def tile(at):
            put_pair(part, x, at, mm(pair_rows(dqkv, x), wqkv[at, :], NT))

        tiles(D, tile)

    down(1 - p.x)
    scatter.far_to_core().start()
    scatter.send_over()
    down(p.x)
    scatter.near_to_core().start()
    if n:
        second_sum.pump(3, first_sum, lambda: second_sum.start(0))
        first_sum.start(0)
    load_all.wait()
    outer(other, stage, dqkv[...], tiles)
    keep_qkv = pltpu.make_async_copy(stage, dqo_hbm.at[:, : 3 * WIDE], local.at[7])
    keep_qkv.start()
    cols_ref[...] = jnp.zeros_like(cols_ref)

    @pl.loop(0, n_tp * rows // ROW_CHUNK)
    def _(i):
        per = rows // ROW_CHUNK
        at = pl.ds(pl.multiple_of((i % per) * ROW_CHUNK, ROW_CHUNK), ROW_CHUNK)
        add_rows(cols_ref, 0, dqkv[i // per, at, :].astype(f32))

    scatter.wait()

    def final(at):
        dy = scatter.rows(at)
        dx, d_gain = norm_back(x_ref[at, :], dy, vec_ref[0:1, :])
        add_rows(sums_ref, 0, d_gain)
        add_rows(sums_ref, 1, dy)
        out_ref[at, :] = g_ref[at, :] + dx

    row_chunks(rows, final)
    gather.finish()
    scatter.finish()
    for micro in range(MICRO):
        reduce.finish(micro)
    keep_out.wait()
    keep_qkv.wait()
    for i, item in enumerate(sums):
        item.finish(i < n - 1)


def attn_bwd(grad, x, vecs, lse, all_rows, own, kv, mixed_all, w_a, w_out, n_tp, payload, collective_id):
    rows = x.shape[0]
    operands, results, more = reduce_parts(payload)
    pieces = (MICRO, 4, 2, 2, PROMPT_DEV, WIDE)
    return pl.pallas_call(
        functools.partial(attn_bwd_kernel, len(payload)),
        out_shape=(
            jax.ShapeDtypeStruct((rows, D), f32),
            jax.ShapeDtypeStruct((8, D), f32),
            jax.ShapeDtypeStruct((1, 3 * WIDE), f32),
            jax.ShapeDtypeStruct((D, 4 * WIDE), bf16),
        )
        + results,
        in_specs=[IN_VMEM] * 4 + [ANY] * (6 + len(payload)),
        out_specs=(IN_VMEM, IN_VMEM, IN_VMEM) + (ANY,) * (1 + 2 * len(payload)),
        scratch_shapes=[
            pltpu.VMEM((D, 3 * WIDE), bf16),
            pltpu.VMEM((WIDE, D), bf16),
            pltpu.VMEM((n_tp, rows, D), bf16),
            pltpu.VMEM((n_tp, rows, D), bf16),
            pltpu.VMEM((n_tp, n_tp, rows, WIDE), bf16),
            pltpu.VMEM((3, MICRO, TOK_DEV, WIDE), bf16),
            pltpu.VMEM((GROUP, MICRO, 2, PROMPT_DEV, WIDE), bf16),
            pltpu.VMEM((MICRO, TOK_DEV, WIDE), bf16),
            pltpu.VMEM(pieces, bf16),
            pltpu.VMEM((MICRO, 4, 2, PROMPT_DEV, WIDE), bf16),
            pltpu.VMEM((MICRO, 4, 2, PROMPT_DEV, WIDE), bf16),
            pltpu.VMEM((MICRO, 3, 2, PROMPT_DEV, WIDE), bf16),
            pltpu.VMEM((2, CONT_LEN, WIDE), bf16),
            pltpu.VMEM((n_tp, rows, 3 * WIDE), bf16),
            pltpu.VMEM((D, 3 * WIDE), bf16),
            pltpu.VMEM((D, WIDE), bf16),
            pltpu.VMEM((KEYS, TOK_DEV), f32),
            pltpu.VMEM((KEYS, TOK_DEV), f32),
            pltpu.VMEM((KEYS, TOK_DEV), bf16),
            pltpu.VMEM((2 * HEAD, TOK_DEV), f32),
        ]
        + scatter_scratch(n_tp, rows)
        + [
            pltpu.SemaphoreType.DMA((8 * MICRO,)),
            pltpu.SemaphoreType.DMA((8 * MICRO,)),
            pltpu.SemaphoreType.DMA((8,)),
        ]
        + more,
        compiler_params=params(collective_id),
        cost_estimate=pl.CostEstimate(flops=2 * 10**11, bytes_accessed=50 * 2**20, transcendentals=0),
    )(grad, x, vecs, lse, all_rows, own, kv, mixed_all, w_a, w_out, *operands)


def forward_layer(x, layer, fetch, vecs, fc_bias, cols, n_tp):
    width = D - HEADS // n_tp * HEAD * (n_tp - 1)
    query_bias, value_bias = (lax.dynamic_slice_in_dim(vecs[i], cols, width) for i in (2, 3))
    biases = widen(jnp.stack([query_bias, jnp.zeros_like(query_bias), value_bias]))
    w_a = fetch.weights[layer, "a"]
    x_mid, lse, all_rows, own, kv, mixed, w_out = fetch.during(
        (layer, "b"), lambda shard: attn_fwd(x, vecs, biases, w_a, n_tp, shard, 5 + layer)
    )
    w_b = fetch.weights[layer, "b"]
    x_next, second_all, hidden_pre, hidden = fetch.during(
        (layer + 1, "a"), lambda shard: ff_fwd(x_mid, vecs, fc_bias[None], w_b, n_tp, shard, 1 + layer)
    )
    return x_next, (x, w_out, lse, all_rows, own, kv, mixed, x_mid, second_all, hidden_pre, hidden)


class Fetch:
    def __init__(self, shards):
        self.staged = lax.axis_size("fsdp") == GROUP
        self.shards, self.weights = shards, {}
        last = None
        for key, shard in shards.items():
            if self.staged:
                if last is None:
                    last = spread_only(shard, FIRST_CHUNKS, 9)
                    self.weights[key] = last.reshape(-1, shard.shape[1])
                continue
            if last is not None:
                shard, _ = lax.optimization_barrier((shard, last))
            whole = lax.all_gather(shard, "fsdp", axis=0, tiled=True)
            self.weights[key] = whole
            last = whole[:8, :128]

    def during(self, key, kernel):
        if not self.staged or key not in self.shards:
            return kernel(None)
        *results, whole = kernel(self.shards[key])
        self.weights[key] = whole.reshape(-1, whole.shape[2])
        return results


def fsdp_sum(part):
    return lax.psum_scatter(part, "fsdp", scatter_dimension=0, tiled=True).astype(f32)


def heads_joined(parts, n_tp):
    step = HEADS // n_tp * HEAD
    return jnp.concatenate([parts[t][..., :step] for t in range(n_tp - 1)] + [parts[n_tp - 1]], axis=-1)


def widen(value, axis=-1):
    pads = [(0, 0)] * value.ndim
    pads[axis] = (0, WIDE - value.shape[axis])
    return jnp.pad(value, pads)


def by_owner(part):
    return part.reshape(4, 2, -1, part.shape[1])


def owned(part, from_y, from_z):
    z, y = lax.axis_index("fsdp") // 2, lax.axis_index("fsdp") % 2
    own = lax.dynamic_index_in_dim(lax.dynamic_index_in_dim(part, z, 0, False), y, 0, False)
    near = lax.dynamic_index_in_dim(from_y, z, 0, False)
    return own.astype(f32) + near.astype(f32) + jnp.sum(from_z.astype(f32), 0)


def with_vectors(grad_qo, ff_sums, attn_sums, col_sums, fc_bias_sums, cols, width):
    def placed(part):
        return lax.dynamic_update_slice_in_dim(jnp.zeros((1, D), f32), part, cols, 1)

    vector_grads = jnp.concatenate(
        [
            attn_sums[:2],
            placed(col_sums[:, :width]),
            placed(col_sums[:, 2 * WIDE : 2 * WIDE + width]),
            attn_sums[4:5],
            ff_sums[5:],
            fc_bias_sums,
        ]
    )
    return lax.dynamic_update_slice(grad_qo, vector_grads.astype(bf16).T, (0, 3 * WIDE + width))


def backward(grad, weights, vecs, saves, cols, n_tp):
    width = D - HEADS // n_tp * HEAD * (n_tp - 1)
    staged = lax.axis_size("fsdp") == GROUP
    done, waiting = {}, {}

    def during(keys, kernel):
        keys = [key for key in keys if key in waiting]
        payload = [waiting.pop(key) for key in keys]
        results = list(kernel(payload))
        if payload:
            arrived = results[-2 * len(payload) :]
            results = results[: -2 * len(payload)]
            for i, key in enumerate(keys):
                done[key] = (payload[i], arrived[2 * i], arrived[2 * i + 1])
        return results

    def produced(key, value):
        if staged:
            waiting[key] = by_owner(value)
        else:
            done[key] = fsdp_sum(value)

    for layer in reversed(range(LAYERS)):
        w_a, w_b = weights[layer, "a"], weights[layer, "b"]
        x, w_out, lse, all_rows, own, kv, mixed_all, x_mid, second_all, hidden_pre, hidden = saves[layer]
        grad, ff_sums, fc_bias_sums, grad_fc, grad_proj = during(
            [(layer + 1, "qo")],
            lambda payload: ff_bwd(
                grad, x_mid, vecs[layer], second_all, hidden_pre, hidden, w_b, n_tp, payload, 10 + layer
            ),
        )
        produced((layer, "proj"), grad_proj)
        produced((layer, "fc"), grad_fc)
        grad, attn_sums, col_sums, grad_qo = during(
            [(layer, "proj"), (layer, "fc")],
            lambda payload: attn_bwd(
                grad, x, vecs[layer], lse, all_rows, own, kv, mixed_all, w_a, w_out, n_tp, payload, 20 + layer
            ),
        )
        produced((layer, "qo"), with_vectors(grad_qo, ff_sums, attn_sums, col_sums, fc_bias_sums, cols, width))
    if staged:
        got = last_sum(waiting[0, "qo"], owned(*done[1, "qo"]).astype(bf16), n_tp, 30)
        return grad, assemble([(got[k],) + done[k, "proj"] + done[k, "fc"] for k in range(LAYERS)])
    outs = []
    for layer in range(LAYERS):
        qo = done[layer, "qo"]
        got = lax.all_gather(qo.astype(bf16), "tp")
        qkv_grad = jnp.concatenate(
            [heads_joined(got[:, :, i * WIDE : i * WIDE + width], n_tp) for i in range(3)], axis=1
        )
        out_grad = heads_joined(got[:, :, 3 * WIDE : 3 * WIDE + width], n_tp)
        vector_sum = jnp.sum(got[:, :, 3 * WIDE + width : 3 * WIDE + width + 8].astype(f32), 0).T
        rest = (vector_sum[v] for v in range(8))
        outs.append((qkv_grad, out_grad, done[layer, "fc"], done[layer, "proj"].T, *rest, qo[:, 3 * WIDE + width + 8]))
    return grad, tuple(jnp.stack(pair).astype(f32) for pair in zip(*outs))


def local(
    tokens,
    qkv_weight,
    query_bias,
    value_bias,
    out_weight,
    out_bias,
    fc_weight,
    fc_bias,
    proj_weight,
    proj_bias,
    first_gain,
    first_bias,
    second_gain,
    second_bias,
    out_grad,
):
    n_tp = lax.axis_size("tp")
    tp = lax.axis_index("tp")
    row_count = tokens.shape[1]
    step = HEADS // n_tp * HEAD
    width = D - step * (n_tp - 1)
    cols = tp * step

    vectors = jnp.stack(
        [first_gain, first_bias, query_bias, value_bias, out_bias, second_gain, second_bias, proj_bias, fc_bias[:, 0]]
    ).reshape(9 * LAYERS, -1)

    shards = {}
    for layer in range(LAYERS):
        sides = [widen(lax.dynamic_slice_in_dim(qkv_weight[layer], cols + i * D, width, 1)) for i in range(3)]
        sides.append(widen(lax.dynamic_slice_in_dim(out_weight[layer], cols, width, 1)))
        if layer == 0:
            sides.append(jnp.pad(vectors.T, ((0, 0), (0, 128 - 9 * LAYERS))))
        shards[layer, "a"] = jnp.concatenate(sides, axis=1)
        fc, proj = fc_weight[layer], proj_weight[layer].T
        more = ((0, 0), (0, lanes_up(fc.shape[1]) - fc.shape[1]))
        shards[layer, "b"] = jnp.concatenate([jnp.pad(fc, more), jnp.pad(proj, more)], axis=1)
    fetch = Fetch(shards)
    vectors = fetch.weights[0, "a"][:, 4 * WIDE : 4 * WIDE + 9 * LAYERS].T.astype(f32).reshape(9, LAYERS, D)

    state = tokens.astype(f32).reshape(MICRO * row_count, D)
    saves = []
    for layer in range(LAYERS):
        state, saved = forward_layer(state, layer, fetch, vectors[:8, layer], vectors[8, layer], cols, n_tp)
        saves.append(saved)
    out_tokens = state.astype(bf16).reshape(tokens.shape)
    grad = out_grad.astype(f32).reshape(MICRO * row_count, D)
    grad, (qkv_g, out_g, fc_g, proj_g, *vec_g) = backward(
        grad, fetch.weights, [vectors[:8, layer] for layer in range(LAYERS)], saves, cols, n_tp
    )
    return (
        out_tokens,
        grad.reshape(tokens.shape),
        qkv_g,
        vec_g[2],
        vec_g[3],
        out_g,
        vec_g[4],
        fc_g,
        vec_g[8][:, None],
        proj_g,
        vec_g[7],
        vec_g[0],
        vec_g[1],
        vec_g[5],
        vec_g[6],
    )


def solution(mesh):
    rows = P(None, ("fsdp", "tp"), None)
    weight = P(None, "fsdp", None)
    vector = P(None, "fsdp")
    fc_in = P(None, "fsdp", "tp")
    hidden = P(None, "tp", "fsdp")
    in_specs = (
        rows, weight, vector, vector, weight, vector, fc_in, hidden, hidden,
        vector, vector, vector, vector, vector, rows,
    )
    out_specs = (
        rows, rows, weight, vector, vector, weight, vector, fc_in, hidden, hidden,
        vector, vector, vector, vector, vector,
    )
    return jax.shard_map(local, mesh=mesh, in_specs=in_specs, out_specs=out_specs, check_vma=False)
```

```python
import functools

import jax
import jax.numpy as jnp
from jax import lax
from jax.experimental import pallas as pl
from jax.experimental.pallas import tpu as pltpu
from jax.sharding import PartitionSpec as P

D = 1600
HEADS = 25
HEAD = 64
GROUP = 8
PROMPT_DEV = 128
CONT_LEN = 256
TOK_DEV = 384
MICRO = 2
LAYERS = 2
PROMPT = 1024
KEYS = PROMPT + CONT_LEN
CHUNK = 128

f32 = jnp.float32
bf16 = jnp.bfloat16
norm_eps = 1e-05
NN = (((1,), (0,)), ((), ()))
NT = (((1,), (1,)), ((), ()))
TN = (((0,), (0,)), ((), ()))


def mm(left, right, dims=NN):
    return lax.dot_general(left, right, dims, preferred_element_type=f32)


def gelu_tanh(value):
    return jax.nn.gelu(value, approximate=True)


MESH = pl.DeviceIdType.MESH
ANY = pl.BlockSpec(memory_space=pl.ANY)
IN_VMEM = pl.BlockSpec(memory_space=pltpu.VMEM)
TILE = 512
ROW_CHUNK = 32


class Peers:
    def __init__(self):
        self.f = lax.axis_index("fsdp")
        self.t = lax.axis_index("tp")
        x, c = self.t // 2, self.t % 2
        self.x = x
        self.core = 2 * x + 1 - c
        self.over = 2 * (1 - x) + c
        self.diag = 2 * (1 - x) + 1 - c

    def greet(self):
        barrier = pltpu.get_barrier_semaphore()
        for t in (self.core, self.over):
            pl.semaphore_signal(barrier, inc=1, device_id=(self.f, t), device_id_type=MESH)
        pl.semaphore_wait(barrier, 2)

    def copy(self, source, target, sems, index, t):
        return pltpu.make_async_remote_copy(
            src_ref=source,
            dst_ref=target,
            send_sem=sems[0].at[index],
            recv_sem=sems[1].at[index],
            device_id=(self.f, t),
            device_id_type=MESH,
        )


class Gather:
    def __init__(self, peers, buf, sems):
        self.p, self.buf, self.sems = peers, buf, sems

    def piece(self, slot, index, t):
        return self.p.copy(self.buf.at[slot], self.buf.at[slot], self.sems, index, t)

    def start(self):
        p = self.p
        self.piece(p.t, 1, p.over).start()
        self.piece(p.t, 0, p.core).start()

    def wait_chip(self):
        self.piece(self.p.core, 0, self.p.core).wait_recv()

    def relay(self):
        p = self.p
        self.piece(p.over, 1, p.over).wait_recv()
        self.piece(p.over, 2, p.core).start()

    def wait_diag(self):
        self.piece(self.p.diag, 2, self.p.core).wait_recv()

    def finish(self):
        p = self.p
        self.piece(p.t, 1, p.over).wait_send()
        self.piece(p.t, 0, p.core).wait_send()
        self.piece(p.over, 2, p.core).wait_send()


class Scatter:
    def __init__(self, peers, part, from_core, over_out, from_over, sems):
        self.p, self.part, self.sems = peers, part, sems
        self.from_core, self.over_out, self.from_over = from_core, over_out, from_over

    def far_to_core(self):
        return self.p.copy(self.part.at[self.p.diag], self.from_core.at[0], self.sems, 3, self.p.core)

    def near_to_core(self):
        return self.p.copy(self.part.at[self.p.core], self.from_core.at[1], self.sems, 4, self.p.core)

    def to_over(self):
        return self.p.copy(self.over_out, self.from_over, self.sems, 5, self.p.over)

    def send_over(self):
        self.far_to_core().wait_recv()

        @pl.loop(0, self.over_out.shape[0] // ROW_CHUNK)
        def _(i):
            at = pl.ds(pl.multiple_of(i * ROW_CHUNK, ROW_CHUNK), ROW_CHUNK)
            total = self.part[self.p.over, at, :].astype(f32) + self.from_core[0, at, :].astype(f32)
            self.over_out[at, :] = total.astype(bf16)

        self.to_over().start()

    def wait(self):
        self.near_to_core().wait_recv()
        self.to_over().wait_recv()

    def rows(self, at):
        return (
            self.part[self.p.t, at, :].astype(f32)
            + self.from_core[1, at, :].astype(f32)
            + self.from_over[at, :].astype(f32)
        )

    def finish(self):
        for copy in (self.far_to_core(), self.near_to_core(), self.to_over()):
            copy.wait_send()


class Group:
    def __init__(self):
        f = lax.axis_index("fsdp")
        self.t = lax.axis_index("tp")
        self.member = f % GROUP
        self.base = f - self.member
        self.z, self.y = self.member // 2, self.member % 2

        half = self.z // 2
        self.inner = (self.z + half) % 2 == 1
        self.mate = 2 * half + 1 - self.z % 2
        self.far_inner, self.far_end = 2 - half, 3 - 3 * half

    def at(self, z, y):
        return z * 2 + y

    def ahead(self, k):
        return (self.z + k) % 4

    def behind(self, k):
        return (self.z + 4 - k) % 4

    def greet_group(self):
        barrier = pltpu.get_barrier_semaphore()
        others = [self.at(self.z, 1 - self.y)] + [self.at(self.ahead(k), self.y) for k in (1, 2, 3)]
        for member in others:
            pl.semaphore_signal(
                barrier, inc=1, device_id=(self.base + member, self.t), device_id_type=MESH
            )
        pl.semaphore_wait(barrier, 4)

    def greet(self, peers, with_diag=False):
        barrier = pltpu.get_barrier_semaphore()
        others = [self.at(self.z, 1 - self.y)] + [self.at(self.ahead(k), self.y) for k in (1, 2, 3)]
        for member in others:
            pl.semaphore_signal(
                barrier, inc=1, device_id=(self.base + member, self.t), device_id_type=MESH
            )
        near = [peers.core, peers.over] + [peers.diag] * with_diag
        for t in near:
            pl.semaphore_signal(barrier, inc=1, device_id=(peers.f, t), device_id_type=MESH)
        pl.semaphore_wait(barrier, 4 + len(near))

    def copy(self, source, target, sems, index, member, send_index=None):
        return pltpu.make_async_remote_copy(
            src_ref=source,
            dst_ref=target,
            send_sem=sems[0].at[index if send_index is None else send_index],
            recv_sem=sems[1].at[index],
            device_id=(self.base + member, self.t),
            device_id_type=MESH,
        )


class Reduce:
    def __init__(self, group, source, from_y, from_z, sems, tiles, columns=None):
        self.g, self.sems, self.columns = group, sems, columns
        self.source, self.from_y, self.from_z = source, from_y, from_z
        self.own, self.got, self.gone, self.local = tiles

    def cut(self, ref, *index):
        if self.columns is None:
            return ref.at[index]
        return ref.at[index + (slice(None), self.columns)]

    def across(self, j):
        g = self.g
        z = g.ahead(j)
        return g.copy(
            self.cut(self.source, z, 1 - g.y), self.cut(self.from_y, z), self.sems, j, g.at(g.z, 1 - g.y)
        )

    def along(self, j):
        g = self.g
        source, target = self.cut(self.gone, j - 1), self.cut(self.from_z, j - 1)
        return g.copy(source, target, self.sems, 3 + j, g.at(g.ahead(j), g.y))

    def start(self, *pieces):
        for j in pieces:
            self.across(j).start()

    def pump(self, j, before=None, then=None):
        g = self.g
        own, got = (self.own, self.got) if self.columns is None else (self.cut(self.own), self.cut(self.got))
        load_own = pltpu.make_async_copy(self.cut(self.source, g.ahead(j), g.y), own, self.local.at[0])
        load_own.start()
        self.across(j).wait_recv()
        if then is not None:
            then()
        load_got = pltpu.make_async_copy(self.cut(self.from_y, g.ahead(j)), got, self.local.at[1])
        load_got.start()
        load_own.wait()
        load_got.wait()
        if before is not None:
            before.along(j).wait_send()
        columns = slice(None) if self.columns is None else self.columns
        self.gone[j - 1, :, columns] = self.own[:, columns] + self.got[:, columns]
        self.along(j).start()

    def finish(self, reused=False, arrived=False):
        if not arrived:
            self.across(0).wait_recv()
        for j in range(4):
            self.across(j).wait_send()
        for j in (1, 2, 3):
            self.along(j).wait_recv()
            if not reused:
                self.along(j).wait_send()


def reduce_parts(payload):
    results, scratch = (), []
    for part in payload:
        rows = part.shape[2:]
        results += (jax.ShapeDtypeStruct((4,) + rows, bf16), jax.ShapeDtypeStruct((3,) + rows, bf16))
    scratch += [pltpu.SemaphoreType.DMA((7,))] * (2 * max(2, len(payload)) if payload else 0)
    if payload:
        scratch += [pltpu.VMEM(rows, bf16), pltpu.VMEM(rows, bf16), pltpu.VMEM((3,) + rows, bf16)]
        scratch += [pltpu.SemaphoreType.DMA((2,))]
    return tuple(payload), results, scratch


def reduces(group, sources, results, scratch):
    tiles = scratch[4:]
    if len(sources) == 1:
        middle, end = sources[0].shape[3] // 2, sources[0].shape[3]
        halves = (slice(0, middle), slice(middle, end))
        return [
            Reduce(group, sources[0], *results, scratch[2 * n : 2 * n + 2], tiles, columns)
            for n, columns in enumerate(halves)
        ]
    return [
        Reduce(group, source, results[2 * n], results[2 * n + 1], scratch[2 * n : 2 * n + 2], tiles)
        for n, source in enumerate(sources)
    ]


def in_turn(items):
    order = [(item, j) for item in items for j in (1, 2, 3, 0)]

    def step(n):
        def following():
            item, j = order[n + 1]
            item.start(j)

        item, j = order[n]
        if j:
            item.pump(j, then=following)
        else:
            item.across(0).wait_recv()
            following()

    return [lambda: items[0].start(1)] + [functools.partial(step, n) for n in range(len(order) - 1)]


class BlockGather:
    def __init__(self, peers, source, target, sems, first, local, columns=None):
        self.p, self.sems, self.first, self.local = peers, sems, first, local
        self.source = source if columns is None else source.at[:, columns]
        self.slot = lambda t: target.at[t] if columns is None else target.at[t, :, columns]

    def piece(self, slot, index, to, own=False):
        target = self.slot(slot)
        return self.p.copy(self.source if own else target, target, self.sems, self.first + index, to)

    def keep(self):
        return pltpu.make_async_copy(self.source, self.slot(self.p.t), self.local)

    def start(self):
        p = self.p
        self.piece(p.t, 1, p.over, True).start()
        self.piece(p.t, 0, p.core, True).start()
        self.keep().start()

    def relay(self):
        p = self.p
        self.piece(p.over, 1, p.over).wait_recv()
        self.piece(p.over, 2, p.core).start()

    def finish(self):
        p = self.p
        self.piece(p.core, 0, p.core).wait_recv()
        self.piece(p.diag, 2, p.core).wait_recv()
        self.piece(p.t, 1, p.over, True).wait_send()
        self.piece(p.t, 0, p.core, True).wait_send()
        self.piece(p.over, 2, p.core).wait_send()
        self.keep().wait()


def add_up(own, others, target, columns):
    rows = own.shape[0]
    for first in range(0, rows, 40):
        at = (slice(first, min(first + 40, rows)), columns)
        total = own[at].astype(f32)
        for other in others:
            total = total + other[at].astype(f32)
        target[at] = total.astype(target.dtype)


def last_sum_kernel(source, earlier, from_y, from_z, got, got_earlier, *scratch):
    p, g = Peers(), Group()
    scratch, (bsend, brecv, blocal, terms, mine) = scratch[:-5], scratch[-5:]
    before = BlockGather(p, earlier, got_earlier, (bsend, brecv), 0, blocal.at[0])
    items = reduces(g, [source], [from_y, from_z], scratch)
    after = [
        BlockGather(p, mine, got, (bsend, brecv), 3 + 3 * n, blocal.at[1 + n], item.columns)
        for n, item in enumerate(items)
    ]
    steps = in_turn(items)
    g.greet(p)
    steps[0]()
    before.start()

    def total(n):
        item = items[n]
        item.finish(arrived=n == 0)
        loads = [
            pltpu.make_async_copy(item.cut(source, g.z, g.y), item.cut(terms, 0), blocal.at[3]),
            pltpu.make_async_copy(item.cut(from_y, g.z), item.cut(terms, 1), blocal.at[4]),
        ]
        for k in range(3):
            loads.append(pltpu.make_async_copy(item.cut(from_z, k), item.cut(terms, 2 + k), blocal.at[5 + k]))
        for load in loads:
            load.start()
        for load in loads:
            load.wait()
        add_up(terms.at[0], [terms.at[k] for k in range(1, 5)], mine, item.columns)
        after[n].start()

    for n, step in enumerate(steps[1:]):
        if n == 3:
            before.relay()
        step()
    total(0)
    after[0].relay()
    total(1)
    before.finish()
    after[0].finish()
    after[1].relay()
    after[1].finish()


def last_sum(part, earlier, n_tp, collective_id):
    operands, results, scratch = reduce_parts([part])
    whole = jax.ShapeDtypeStruct((n_tp,) + earlier.shape, bf16)
    _, _, got, got_earlier = pl.pallas_call(
        last_sum_kernel,
        out_shape=results + (whole, whole),
        in_specs=[ANY, ANY],
        out_specs=(ANY,) * 4,
        scratch_shapes=scratch
        + [pltpu.SemaphoreType.DMA((9,))] * 2
        + [pltpu.SemaphoreType.DMA((8,)), pltpu.VMEM((5,) + earlier.shape, bf16), pltpu.VMEM(earlier.shape, bf16)],
        compiler_params=params(collective_id),
    )(part, earlier)
    return got, got_earlier


def assemble_kernel(*refs):
    inputs, refs = refs[: 7 * LAYERS], refs[7 * LAYERS :]
    qkv_ref, out_ref, fc_ref, proj_ref = refs[:4]
    vector_refs, (tiles, sems) = refs[4:13], refs[13:]
    t, f = lax.axis_index("tp"), lax.axis_index("fsdp")
    z, y = f // 2, f % 2
    loads = []
    for layer in range(LAYERS):
        for w in range(2):
            part, near, far = inputs[7 * layer + 1 + 3 * w : 7 * layer + 4 + 3 * w]
            n = 2 * layer + w
            loads.append(
                [
                    pltpu.make_async_copy(part.at[z, y], tiles.at[n, 0], sems.at[n, 0]),
                    pltpu.make_async_copy(near.at[z], tiles.at[n, 1], sems.at[n, 1]),
                    pltpu.make_async_copy(far, tiles.at[n, 2:5], sems.at[n, 2]),
                ]
            )
    for load in sum(loads, []):
        load.start()
    n_tp = inputs[0].shape[0]
    step = HEADS // n_tp * HEAD
    width = D - step * (n_tp - 1)
    counts = [step] * (n_tp - 1) + [width]
    for layer in range(LAYERS):
        got = inputs[7 * layer]
        for i in range(3):
            for k, count in enumerate(counts):
                value = got[k, :, i * WIDE : i * WIDE + count].astype(f32)
                qkv_ref[layer, :, i * D + k * step : i * D + k * step + count] = value
        for k, count in enumerate(counts):
            out_ref[layer, :, k * step : k * step + count] = got[k, :, 3 * WIDE : 3 * WIDE + count].astype(f32)
        extra = got[:, :, 3 * WIDE + step : 4 * WIDE].astype(f32)
        total = jnp.sum(extra, axis=0).T
        own = got[t, :, 3 * WIDE + step : 4 * WIDE].astype(f32).T
        skip = width - step
        for v in range(8):
            vector_refs[v][layer : layer + 1, :] = total[skip + v : skip + v + 1, :]
        vector_refs[8][layer : layer + 1, :] = own[skip + 8 : skip + 9, :]
        for w in range(2):
            n = 2 * layer + w
            for load in loads[n]:
                load.wait()
            total = tiles[n, 0].astype(f32)
            for k in range(1, 5):
                total = total + tiles[n, k].astype(f32)
            if w:
                fc_ref[layer] = total
            else:
                proj_ref[layer] = total.T


def assemble(layers):
    rows, width = layers[0][1].shape[2:]
    outs = [(LAYERS, rows, 3 * D), (LAYERS, rows, D), (LAYERS, rows, width), (LAYERS, width, rows)]
    outs += [(LAYERS, rows)] * 9
    return pl.pallas_call(
        assemble_kernel,
        out_shape=tuple(jax.ShapeDtypeStruct(o, f32) for o in outs),
        in_specs=([IN_VMEM] + [ANY] * 6) * LAYERS,
        out_specs=(IN_VMEM,) * len(outs),
        scratch_shapes=[
            pltpu.VMEM((2 * LAYERS, 5, rows, width), bf16),
            pltpu.SemaphoreType.DMA((2 * LAYERS, 3)),
        ],
        compiler_params=pltpu.CompilerParams(vmem_limit_bytes=60 * 2**20),
    )(*sum((list(layer) for layer in layers), []))


class Spread:
    def __init__(self, group, source, target, sems, chunks):
        self.g, self.source, self.target, self.sems = group, source, target, sems
        count = source.shape[1] // 128
        ends = [128 * (count * sum(chunks[: c + 1]) // sum(chunks)) for c in range(len(chunks))]
        self.columns = [slice(a, b) for a, b in zip([0] + ends, ends)]
        self.partner = group.at(group.z, 1 - group.y)
        self.origins = (group.mate, group.far_inner, group.far_end)

    def piece(self, member, c, index, to, own=False, send_index=None):
        target = self.target.at[member, :, self.columns[c]]
        source = self.source.at[:, self.columns[c]] if own else target
        send = None if send_index is None else 9 * c + send_index
        return self.g.copy(source, target, self.sems, 9 * c + index, to, send)

    def own(self, c):
        g = self.g
        arrives = jnp.where(g.inner, 2, 3)
        return [
            self.piece(g.member, c, arrives, g.at(g.far_inner, g.y), True, 2),
            self.piece(g.member, c, 1, g.at(g.mate, g.y), True),
        ]

    def own_across(self, c):
        return self.piece(self.g.member, c, 0, self.partner, True)

    def relayed(self, c, k):
        g = self.g
        return self.piece(g.at(self.origins[k - 1], g.y), c, 3 + k, self.partner)

    def passed(self, c, k):
        g = self.g
        return self.piece(g.at(self.origins[k - 1], g.y), c, k, g.at(g.mate, g.y), send_index=5 + k)

    def keep(self):
        return pltpu.make_async_copy(
            self.source, self.target.at[self.g.member], self.sems[0].at[9 * len(self.columns)]
        )

    def start(self, first=0, last=None):
        if first == 0:
            self.keep().start()
            for c in range(len(self.columns)):
                self.own_across(c).start()
        for c in range(len(self.columns))[first:last]:
            for copy in self.own(c):
                copy.start()

    def arrival(self, c, k):
        g = self.g
        self.piece(g.at(self.origins[k - 1], g.y), c, k, self.partner).wait_recv()

    def relay(self, c):
        self.arrival(c, 1)
        self.relayed(c, 1).start()

        @pl.when(self.g.inner)
        def _():
            for k in (2, 3):
                self.arrival(c, k)
                self.passed(c, k).start()
                self.relayed(c, k).start()

    def relay_late(self, c):
        @pl.when(jnp.logical_not(self.g.inner))
        def _():
            for k in (2, 3):
                self.arrival(c, k)
                self.relayed(c, k).start()

    def finish(self):
        g = self.g
        for c in range(len(self.columns)):
            self.piece(self.partner, c, 0, self.partner).wait_recv()
            for k in (1, 2, 3):
                self.piece(g.at(self.origins[k - 1], 1 - g.y), c, 3 + k, self.partner).wait_recv()
                self.relayed(c, k).wait_send()
            for copy in self.own(c) + [self.own_across(c)]:
                copy.wait_send()

            @pl.when(g.inner)
            def _(c=c):
                self.passed(c, 2).wait_send()
                self.passed(c, 3).wait_send()

        self.keep().wait()


def spread_parts(shard, chunks):
    if shard is None:
        return (), (), []
    whole = jax.ShapeDtypeStruct((GROUP,) + shard.shape, shard.dtype)
    return (shard,), (whole,), [pltpu.SemaphoreType.DMA((9 * len(chunks) + 1,))] * 2


def spread_kernel(chunks, source, target, send, recv):
    g = Group()
    g.greet_group()
    spread = Spread(g, source, target, (send, recv), chunks)
    spread.start(0, 2)
    for c in range(len(chunks)):
        spread.relay(c)
        spread.start(c + 2, c + 3)
        if c:
            spread.relay_late(c - 1)
    spread.relay_late(len(chunks) - 1)
    spread.finish()


def spread_only(shard, chunks, collective_id):
    operands, results, scratch = spread_parts(shard, chunks)
    return pl.pallas_call(
        functools.partial(spread_kernel, chunks),
        out_shape=results[0],
        in_specs=[ANY],
        out_specs=ANY,
        scratch_shapes=scratch,
        compiler_params=params(collective_id),
    )(shard)


def row_chunks(rows, body):
    @pl.loop(0, rows // ROW_CHUNK)
    def _(i):
        body(pl.ds(pl.multiple_of(i * ROW_CHUNK, ROW_CHUNK), ROW_CHUNK))


def tiles(extent, body):
    whole = extent // TILE

    @pl.loop(0, whole)
    def _(i):
        body(pl.ds(pl.multiple_of(i * TILE, TILE), TILE))

    if extent % TILE:
        body(pl.ds(whole * TILE, extent % TILE))


def pair_rows(ref, x):
    both = ref[pl.ds(2 * x, 2)]
    return both.reshape(2 * both.shape[1], both.shape[2])


def put_pair(ref, x, at, value):
    ref[pl.ds(2 * x, 2), :, at] = value.reshape(2, value.shape[0] // 2, value.shape[1]).astype(ref.dtype)


def norm_stats(x):
    centred = x - jnp.mean(x, -1, keepdims=True)
    scale = lax.rsqrt(jnp.mean(centred * centred, -1, keepdims=True) + norm_eps)
    return centred * scale, scale


def lanes_up(width):
    return -(-width // 128) * 128


def proj_part(w_b, width):
    return w_b.at[:, lanes_up(width) :]


FIRST_CHUNKS = (3, 3, 3, 3, 3, 2)
FF_CHUNKS = (5, 5, 4, 2)
ATTN_CHUNKS = (5, 6, 6, 5, 4)


def ff_fwd_kernel(n, *refs):
    x_ref, vec_ref, fcb_ref, wb_hbm = refs[:4]
    shard, refs = refs[4 : 4 + n], refs[4 + n :]
    out_ref, all_hbm, pre_hbm, hid_hbm = refs[:4]
    whole, refs = refs[4 : 4 + n], refs[4 + n :]
    wfc, wproj, buf, pre, hid, part, from_core, over_out, from_over, send, recv, local = refs[:12]
    p, g = Peers(), Group()
    spread = Spread(g, shard[0], whole[0], refs[12:], FF_CHUNKS) if n else None
    rows = x_ref.shape[0]
    sems = (send, recv)
    gather = Gather(p, buf, sems)
    scatter = Scatter(p, part, from_core, over_out, from_over, sems)
    width = fcb_ref.shape[1]
    load_fc = pltpu.make_async_copy(wb_hbm.at[:, : wfc.shape[1]], wfc, local.at[0])
    load_proj = pltpu.make_async_copy(proj_part(wb_hbm, width), wproj, local.at[1])
    load_fc.start()
    load_proj.start()

    def norm(at):
        hat, _ = norm_stats(x_ref[at, :])
        buf[p.t, at, :] = (hat * vec_ref[5:6, :] + vec_ref[6:7, :]).astype(bf16)

    row_chunks(rows, norm)
    if n:
        g.greet(p)
    else:
        p.greet()
    gather.start()
    if n:
        spread.start(0, 1)
    gather.wait_chip()
    load_fc.wait()

    def up(x):
        def tile(at):
            value = mm(pair_rows(buf, x), wfc[:, at]) + fcb_ref[:, at]
            put_pair(pre, x, at, value)
            put_pair(hid, x, at, gelu_tanh(value))

        tiles(width, tile)

    def down(x):
        def tile(at):
            put_pair(part, x, at, mm(pair_rows(hid, x), wproj[at, :width], NT))

        tiles(D, tile)

    up(p.x)
    if n:
        spread.start(1, 2)
    gather.relay()
    gather.wait_diag()
    if n:
        spread.relay(0)
    keep_all = pltpu.make_async_copy(buf, all_hbm, local.at[2])
    keep_all.start()
    up(1 - p.x)
    keep_pre = pltpu.make_async_copy(pre, pre_hbm, local.at[3])
    keep_hid = pltpu.make_async_copy(hid, hid_hbm, local.at[4])
    keep_pre.start()
    keep_hid.start()
    load_proj.wait()
    down(1 - p.x)
    scatter.far_to_core().start()
    scatter.send_over()
    if n:
        spread.start(2, 3)
        spread.relay_late(0)
    down(p.x)
    scatter.near_to_core().start()
    if n:
        spread.relay(1)
        spread.start(3)
    scatter.wait()

    def final(at):
        out_ref[at, :] = x_ref[at, :] + scatter.rows(at) + vec_ref[7:8, :]

    row_chunks(rows, final)
    if n:
        spread.relay(2)
        spread.relay_late(1)
        spread.relay(3)
        spread.relay_late(2)
        spread.relay_late(3)
    gather.finish()
    scatter.finish()
    for copy in (keep_all, keep_pre, keep_hid):
        copy.wait()
    if n:
        spread.finish()


def scatter_scratch(n_tp, rows):
    return [
        pltpu.VMEM((n_tp, rows, D), bf16),
        pltpu.VMEM((2, rows, D), bf16),
        pltpu.VMEM((rows, D), bf16),
        pltpu.VMEM((rows, D), bf16),
        pltpu.SemaphoreType.DMA((6,)),
        pltpu.SemaphoreType.DMA((6,)),
    ]


def params(collective_id):
    return pltpu.CompilerParams(collective_id=collective_id, has_side_effects=True, vmem_limit_bytes=60 * 2**20)


def ff_fwd(x, vecs, fc_bias, w_b, n_tp, shard, collective_id):
    rows, width = x.shape[0], fc_bias.shape[1]
    block = (n_tp, rows)
    operands, results, sems = spread_parts(shard, FF_CHUNKS)
    return pl.pallas_call(
        functools.partial(ff_fwd_kernel, len(operands)),
        out_shape=(
            jax.ShapeDtypeStruct((rows, D), f32),
            jax.ShapeDtypeStruct(block + (D,), bf16),
            jax.ShapeDtypeStruct(block + (width,), f32),
            jax.ShapeDtypeStruct(block + (width,), bf16),
        )
        + results,
        in_specs=[IN_VMEM, IN_VMEM, IN_VMEM, ANY] + [ANY] * len(operands),
        out_specs=(IN_VMEM, ANY, ANY, ANY) + (ANY,) * len(operands),
        scratch_shapes=[
            pltpu.VMEM((D, lanes_up(width)), bf16),
            pltpu.VMEM((D, lanes_up(width)), bf16),
            pltpu.VMEM(block + (D,), bf16),
            pltpu.VMEM(block + (width,), f32),
            pltpu.VMEM(block + (width,), bf16),
        ]
        + scatter_scratch(n_tp, rows)
        + [pltpu.SemaphoreType.DMA((5,))]
        + sems,
        compiler_params=params(collective_id),
        cost_estimate=pl.CostEstimate(
            flops=4 * n_tp * rows * D * width, bytes_accessed=40 * 2**20, transcendentals=n_tp * rows * width
        ),
    )(x, vecs, fc_bias, w_b, *operands)


def gelu_slope(u):
    a = 0.7978845608028654
    square = u * u
    t = jnp.tanh(a * (u + 0.044715 * u * square))
    return 0.5 * (1.0 + t) + 0.5 * u * (1.0 - t * t) * (a * (1.0 + 3 * 0.044715 * square))


def norm_back(x, dy, gain):
    hat, scale = norm_stats(x)
    d_hat = dy * gain
    inner = d_hat - jnp.mean(d_hat, -1, keepdims=True) - hat * jnp.mean(d_hat * hat, -1, keepdims=True)
    return scale * inner, dy * hat


def add_rows(ref, row, value):
    ref[row : row + 1, :] += jnp.sum(value, axis=0, keepdims=True)


def ff_bwd_kernel(n, *refs):
    g_ref, x_ref, vec_ref, all_hbm, pre_hbm, hid_hbm, wb_hbm = refs[:7]
    sources, refs = refs[7 : 7 + n], refs[7 + n :]
    out_ref, sums_ref, fcb_ref, dfc_hbm, dproj_hbm = refs[:5]
    results, refs = refs[5 : 5 + 2 * n], refs[5 + 2 * n :]
    wfc, wproj, buf, other, pre, dpre, stage, part, from_core, over_out, from_over, send, recv, local = refs[:14]
    p, g = Peers(), Group()
    sums = reduces(g, sources, results, refs[14:])
    rows = x_ref.shape[0]
    n_tp, width = buf.shape[0], fcb_ref.shape[1]
    sems = (send, recv)
    gather = Gather(p, buf, sems)
    scatter = Scatter(p, part, from_core, over_out, from_over, sems)
    load_proj = pltpu.make_async_copy(proj_part(wb_hbm, width), wproj, local.at[0])
    load_pre = pltpu.make_async_copy(pre_hbm, pre, local.at[1])
    load_fc = pltpu.make_async_copy(wb_hbm.at[:, : wfc.shape[1]], wfc, local.at[2])
    load_other = pltpu.make_async_copy(hid_hbm, other, local.at[3])
    for copy in (load_proj, load_pre, load_fc, load_other):
        copy.start()
    sums_ref[...] = jnp.zeros_like(sums_ref)
    fcb_ref[...] = jnp.zeros_like(fcb_ref)

    def lower(at):
        low = g_ref[at, :].astype(bf16)
        buf[p.t, at, :] = low
        add_rows(sums_ref, 7, low.astype(f32))

    row_chunks(rows, lower)
    if n:
        g.greet(p)
    else:
        p.greet()
    gather.start()
    steps = in_turn(sums) if n else []

    def advance():
        if steps:
            steps.pop(0)()

    advance()
    gather.wait_chip()
    load_proj.wait()
    load_pre.wait()

    def through(x):
        def tile(at):
            d_hidden = mm(pair_rows(buf, x), wproj[:, at])
            u = pre[pl.ds(2 * x, 2), :, at].reshape(2 * rows, -1)
            low = (gelu_slope(u) * d_hidden).astype(bf16)
            put_pair(dpre, x, at, low)
            fcb_ref[:, at] += jnp.sum(low.astype(f32), axis=0, keepdims=True)

        tiles(width, tile)

    def down(x):
        def tile(at):
            put_pair(part, x, at, mm(pair_rows(dpre, x), wfc[at, :width], NT))

        tiles(D, tile)

    through(p.x)
    gather.relay()
    advance()
    gather.wait_diag()
    through(1 - p.x)
    advance()
    load_fc.wait()
    down(1 - p.x)
    scatter.far_to_core().start()
    scatter.send_over()
    advance()
    down(p.x)
    scatter.near_to_core().start()
    advance()

    def outer(left, right, target, sem):
        whole = D // TILE
        rest = D - whole * TILE
        flat = right[...].reshape(n_tp * rows, width)

        def tile(i, size):
            at = pl.ds(pl.multiple_of(i * TILE, TILE), size)
            value = mm(left[:, :, at].reshape(n_tp * rows, size), flat, TN)
            stage[at, :] = value.astype(bf16)

        @pl.loop(0, whole)
        def _(i):
            tile(i, TILE)

        if rest:
            tile(whole, rest)
        return pltpu.make_async_copy(stage, target, sem)

    load_other.wait()
    store = outer(buf, other, dproj_hbm, local.at[4])
    store.start()
    gather.finish()
    load_all = pltpu.make_async_copy(all_hbm, buf, local.at[5])
    load_all.start()
    advance()
    scatter.wait()

    def final(at):
        dy = scatter.rows(at)
        dx, d_gain = norm_back(x_ref[at, :], dy, vec_ref[5:6, :])
        add_rows(sums_ref, 5, d_gain)
        add_rows(sums_ref, 6, dy)
        out_ref[at, :] = g_ref[at, :] + dx

    row_chunks(rows, final)
    load_all.wait()
    store.wait()
    store = outer(buf, dpre, dfc_hbm, local.at[6])
    store.start()
    while steps:
        advance()
    scatter.finish()
    store.wait()
    for i, item in enumerate(sums):
        item.finish(arrived=i == 0)


def ff_bwd(grad, x, vecs, all_rows, pre, hidden, w_b, n_tp, payload, collective_id):
    rows, width = x.shape[0], pre.shape[2]
    block = (n_tp, rows)
    operands, results, more = reduce_parts(payload)
    return pl.pallas_call(
        functools.partial(ff_bwd_kernel, len(payload)),
        out_shape=(
            jax.ShapeDtypeStruct((rows, D), f32),
            jax.ShapeDtypeStruct((8, D), f32),
            jax.ShapeDtypeStruct((1, width), f32),
            jax.ShapeDtypeStruct((D, width), bf16),
            jax.ShapeDtypeStruct((D, width), bf16),
        )
        + results,
        in_specs=[IN_VMEM] * 3 + [ANY] * (4 + len(payload)),
        out_specs=(IN_VMEM, IN_VMEM, IN_VMEM) + (ANY,) * (2 + 2 * len(payload)),
        scratch_shapes=[
            pltpu.VMEM((D, lanes_up(width)), bf16),
            pltpu.VMEM((D, lanes_up(width)), bf16),
            pltpu.VMEM(block + (D,), bf16),
            pltpu.VMEM(block + (width,), bf16),
            pltpu.VMEM(block + (width,), f32),
            pltpu.VMEM(block + (width,), bf16),
            pltpu.VMEM((D, width), bf16),
        ]
        + scatter_scratch(n_tp, rows)
        + [pltpu.SemaphoreType.DMA((7,))]
        + more,
        compiler_params=params(collective_id),
        cost_estimate=pl.CostEstimate(
            flops=8 * n_tp * rows * D * width, bytes_accessed=50 * 2**20, transcendentals=n_tp * rows * width
        ),
    )(grad, x, vecs, all_rows, pre, hidden, w_b, *operands)


HALVES = [(micro, half) for micro in range(MICRO) for half in range(2)]


def half_lanes(half):
    return slice(half * WIDE // 2, (half + 1) * WIDE // 2)


class Share:
    def __init__(self, group, kv, sems):
        self.g, self.kv, self.sems = group, kv, sems
        self.partner = group.at(group.z, 1 - group.y)

    def piece(self, member, part, index, to):
        micro, half = part
        ref = self.kv.at[member, micro, :, :, half_lanes(half)]
        return self.g.copy(ref, ref, self.sems, (2 * micro + half) * 7 + index, to)

    def own(self, part):
        g = self.g
        return [self.piece(g.member, part, 0, self.partner)] + [
            self.piece(g.member, part, k, g.at(g.ahead(k), g.y)) for k in (1, 2, 3)
        ]

    def relayed(self, part):
        g = self.g
        return [self.piece(g.at(g.behind(k), g.y), part, 3 + k, self.partner) for k in (1, 2, 3)]

    def start(self, *part):
        for copy in self.own(part):
            copy.start()

    def relay(self, *part):
        g = self.g
        for k, copy in zip((1, 2, 3), self.relayed(part)):
            self.piece(g.at(g.behind(k), g.y), part, k, self.partner).wait_recv()
            copy.start()

    def wait(self, *part):
        g = self.g
        self.piece(self.partner, part, 0, self.partner).wait_recv()
        for k in (1, 2, 3):
            self.piece(g.at(g.behind(k), 1 - g.y), part, 3 + k, self.partner).wait_recv()

    def finish(self):
        for part in HALVES:
            for copy in self.own(part) + self.relayed(part):
                copy.wait_send()


class GroupSum:
    def __init__(self, group, parts, from_y, to_z, from_z, sems):
        self.g, self.parts, self.sems = group, parts, sems
        self.from_y, self.to_z, self.from_z = from_y, to_z, from_z

    def across(self, micro, half):
        g, lanes = self.g, half_lanes(half)
        return g.copy(
            self.parts.at[micro, :, 1 - g.y, :, :, lanes],
            self.from_y.at[micro, :, :, :, lanes],
            self.sems,
            (2 * micro + half) * 4,
            g.at(g.z, 1 - g.y),
        )

    def along(self, micro, half, k):
        g, lanes = self.g, half_lanes(half)
        to = g.ahead(k)
        return g.copy(
            self.to_z.at[micro, to, :, :, lanes],
            self.from_z.at[micro, k - 1, :, :, lanes],
            self.sems,
            (2 * micro + half) * 4 + k,
            g.at(to, g.y),
        )

    def start(self, micro, half):
        self.across(micro, half).start()

    def turn(self, micro, half):
        lanes = half_lanes(half)
        self.across(micro, half).wait_recv()

        @pl.loop(0, 4)
        def _(z):
            for kv in range(2):
                total = self.parts[micro, z, self.g.y, kv, :, lanes] + self.from_y[micro, z, kv, :, lanes]
                self.to_z[micro, z, kv, :, lanes] = total

        for k in (1, 2, 3):
            self.along(micro, half, k).start()

    def wait(self, micro):
        for half in range(2):
            for k in (1, 2, 3):
                self.along(micro, half, k).wait_recv()

    def total(self, micro, kv):
        g = self.g
        value = self.parts[micro, g.z, g.y, kv].astype(f32) + self.from_y[micro, g.z, kv].astype(f32)
        for k in range(3):
            value = value + self.from_z[micro, k, kv].astype(f32)
        return value.astype(bf16)

    def finish(self, micro):
        for half in range(2):
            self.across(micro, half).wait_send()
            for k in (1, 2, 3):
                self.along(micro, half, k).wait_send()


WIDE = 512
HEAD_PAIRS = WIDE // (2 * HEAD)
PROMPT_CHUNKS = PROMPT // CHUNK
CONT_CHUNKS = CONT_LEN // CHUNK


def chunk_at(c, base=0):
    return pl.ds(pl.multiple_of(base + c * CHUNK, CHUNK), CHUNK)


def key_limit(member):
    row = lax.broadcasted_iota(jnp.int32, (1, TOK_DEV), 1)
    return jnp.where(row < PROMPT_DEV, member * PROMPT_DEV + row, PROMPT - PROMPT_DEV + row)


def half_of(value, half):
    lane = lax.broadcasted_iota(jnp.int32, value.shape, 1)
    return jnp.where((lane >= HEAD * half) & (lane < HEAD * (half + 1)), value, jnp.zeros_like(value))


def fold(value, op):
    return op(value.reshape(value.shape[0] // 8, 8, value.shape[1]), axis=0)


def over_keys(body, prompt, own, carry):
    carry = lax.fori_loop(0, PROMPT_CHUNKS, lambda c, carry: body(c, lambda i: prompt(c, i), carry), carry)
    return lax.fori_loop(
        0, CONT_CHUNKS, lambda c, carry: body(PROMPT_CHUNKS + c, lambda i: own(c, i), carry), carry
    )


def head_pairs(head, finish):
    @pl.loop(0, HEAD_PAIRS)
    def _(pair):
        lanes = pl.ds(pl.multiple_of(pair * 2 * HEAD, 2 * HEAD), 2 * HEAD)
        head(pair, lanes, 0)

        @pl.when(pair < HEAD_PAIRS - 1)
        def _():
            head(pair, lanes, 1)

        finish(pair, lanes)


def run_hooks(hooks, micro, pair, half):
    for at in range(HEAD_PAIRS):
        if half == 0 and (micro, at) in hooks:

            @pl.when(pair == at)
            def _(at=at):
                for hook in hooks[micro, at]:
                    hook()


def to_slots(target, micro, first, value, lanes):
    per = target.shape[1] // MICRO
    row = first
    while row < first + value.shape[0]:
        slot, within = row // per, row % per
        count = min(per - within, first + value.shape[0] - row)
        target[slot, micro * per + within : micro * per + within + count, lanes] = value[
            row - first : row - first + count
        ]
        row += count


def pair_to_blocks(target, x, value):
    per = value.shape[0] // (2 * MICRO)
    for core in range(2):
        for micro in range(MICRO):
            at = pl.ds(pl.multiple_of((2 * x + core) * per, per), per)
            first = (core * MICRO + micro) * per
            target[micro, at, :] = value[first : first + per]


def attn_fwd_kernel(n, *refs):
    x_ref, vec_ref, bias_ref, wqkv_hbm = refs[:4]
    shard, refs = refs[4 : 4 + n], refs[4 + n :]
    out_ref, lse_ref, all_hbm, own_hbm, kv_hbm, mix_hbm, wout_hbm = refs[:7]
    whole, refs = refs[7 : 7 + n], refs[7 + n :]
    wqkv, wout, wparts, buf, own, kv, mix, s_ref, p_ref, o_ref = refs[:10]
    part, from_core, over_out, from_over, send, recv, gsend, grecv, wsend, wrecv, local = refs[10:21]
    msend, mrecv = refs[21:23]
    p, g = Peers(), Group()
    spread = Spread(g, shard[0], whole[0], refs[23:], ATTN_CHUNKS) if n else None
    mixes = BlockGather(p, mix, mix_hbm, (msend, mrecv), 0, local.at[5])
    rows = x_ref.shape[0]
    n_tp = buf.shape[0]
    step = HEADS // n_tp * HEAD
    width = wparts.shape[1]
    sems = (send, recv)
    gather = Gather(p, buf, sems)
    scatter = Scatter(p, part, from_core, over_out, from_over, sems)
    share = Share(g, kv, (gsend, grecv))
    load_qkv = pltpu.make_async_copy(wqkv_hbm.at[:, : 3 * WIDE], wqkv, local.at[0])
    load_qkv.start()

    def rows_for(t):
        return wqkv_hbm.at[pl.ds(pl.multiple_of(t * step, 128), width), 3 * WIDE : 4 * WIDE]

    keep_part = pltpu.make_async_copy(rows_for(p.t), wparts.at[p.t], local.at[1])
    keep_part.start()
    give_parts = [
        p.copy(rows_for(t), wparts.at[p.t], (wsend, wrecv), i, t) for i, t in enumerate((p.core, p.over, p.diag))
    ]

    def norm(at):
        hat, _ = norm_stats(x_ref[at, :])
        buf[p.t, at, :] = (hat * vec_ref[0:1, :] + vec_ref[1:2, :]).astype(bf16)

    row_chunks(rows, norm)
    g.greet(p, True)
    gather.start()
    for copy in give_parts:
        copy.start()
    if n:
        spread.start(0, 1)
    gather.wait_chip()
    load_qkv.wait()

    def project(x):
        for i in range(3):
            value = mm(pair_rows(buf, x), wqkv[:, i * WIDE : (i + 1) * WIDE]) + bias_ref[i : i + 1, :]
            low = value.astype(bf16)
            if i == 0:
                low = low * HEAD ** (-0.5)
            pair_to_blocks(own.at[i], x, low)

    project(p.x)
    gather.relay()
    gather.wait_diag()
    project(1 - p.x)
    for micro in range(MICRO):
        for i in range(2):
            kv[g.member, micro, i] = own[1 + i, micro, :PROMPT_DEV, :]
    share.start(0, 0)
    if n:
        spread.start(1, 2)
    hooks = {
        (0, 1): [lambda: share.relay(0, 1), lambda: share.start(1, 0)],
        (0, 2): [lambda: share.wait(0, 1)],
        (0, 3): [lambda: share.relay(1, 0), lambda: share.start(1, 1)],
        (1, 0): [lambda: share.wait(1, 0)],
        (1, 1): [lambda: share.relay(1, 1)],
        (1, 2): [lambda: share.wait(1, 1)],
    }
    if n:
        hooks[0, 0] = [lambda: spread.start(2, 3)]
        hooks[0, 2] += [lambda: spread.relay(1), lambda: spread.relay_late(1)]
        hooks[0, 3] += [lambda: spread.start(3, 4)]
        hooks[1, 1] += [lambda: spread.relay(2), lambda: spread.relay_late(2), lambda: spread.start(4)]
    keep_all = pltpu.make_async_copy(buf, all_hbm, local.at[2])
    keep_own = pltpu.make_async_copy(own, own_hbm, local.at[3])
    keep_all.start()
    keep_own.start()
    limit = key_limit(g.member)
    sub = lax.broadcasted_iota(jnp.int32, (CHUNK, TOK_DEV), 0)

    share.relay(0, 0)
    share.start(0, 1)
    if n:
        spread.relay(0)
        spread.relay_late(0)
    share.wait(0, 0)

    for micro in range(MICRO):

        def head(pair, lanes, half, micro=micro):
            run_hooks(hooks, micro, pair, half)
            qh = half_of(own[0, micro, :, lanes], half)

            def first(c, load, top):
                s = jnp.where(sub + c * CHUNK <= limit, mm(load(0), qh, NT), -1e30)
                s_ref[chunk_at(c), :] = s
                return jnp.maximum(top, fold(s, jnp.max))

            top = over_keys(
                first,
                lambda c, i: kv[c, micro, i, :, lanes],
                lambda c, i: own[1 + i, micro, chunk_at(c, PROMPT_DEV), lanes],
                jnp.full((8, TOK_DEV), -1e30, f32),
            )
            top = jnp.max(top, axis=0, keepdims=True)

            def second(c, total):
                e = jnp.exp(s_ref[chunk_at(c), :] - top)
                p_ref[chunk_at(c), :] = e.astype(bf16)
                return total + fold(e, jnp.sum)

            total = lax.fori_loop(0, KEYS // CHUNK, second, jnp.zeros((8, TOK_DEV), f32))
            total = jnp.sum(total, axis=0, keepdims=True)
            values = kv[:, micro, 1, :, lanes].reshape(PROMPT, 2 * HEAD)
            out = mm(values, p_ref[:PROMPT, :], TN) + mm(own[2, micro, PROMPT_DEV:, lanes], p_ref[PROMPT:, :], TN)
            at = slice(HEAD * half, HEAD * (half + 1))
            o_ref[at, :] = out[at, :] / total
            lse_ref[micro, pair, half : half + 1, :] = top + jnp.log(total)

        def finish(pair, lanes, micro=micro):
            @pl.when(pair == HEAD_PAIRS - 1)
            def _():
                o_ref[HEAD:, :] = jnp.zeros((HEAD, TOK_DEV), f32)

            to_slots(mix, micro, 0, o_ref[...].T.astype(bf16), lanes)

        head_pairs(head, finish)

    keep_kv = pltpu.make_async_copy(kv, kv_hbm, local.at[4])
    keep_kv.start()
    keep_part.wait()
    for i, t in enumerate((p.core, p.over, p.diag)):
        p.copy(rows_for(t), wparts.at[t], (wsend, wrecv), i, t).wait_recv()
    for t in range(n_tp):
        count = min(WIDE, D - t * step)
        wout[:width, t * step : t * step + count] = wparts[t, :, :count]
    wout[width:, :] = jnp.zeros((WIDE - width, D), bf16)

    @pl.when(p.t < n_tp - 1)
    def _():
        wout[step:width, :] = jnp.zeros((width - step, D), bf16)

    keep_out = pltpu.make_async_copy(wout, wout_hbm, local.at[6])
    keep_out.start()

    def down(x):
        def tile(at):
            put_pair(part, x, at, mm(pair_rows(mix, x), wout[:, at]))

        tiles(D, tile)

    down(1 - p.x)
    scatter.far_to_core().start()
    scatter.send_over()
    down(p.x)
    scatter.near_to_core().start()
    if n:
        spread.relay(3)
        spread.relay_late(3)
    scatter.wait()
    mixes.start()

    def final(at):
        out_ref[at, :] = x_ref[at, :] + (scatter.rows(at) + vec_ref[4:5, :])

    row_chunks(rows, final)
    mixes.relay()
    if n:
        spread.relay(4)
        spread.relay_late(4)
    gather.finish()
    scatter.finish()
    share.finish()
    for copy in give_parts:
        copy.wait_send()
    for copy in (keep_all, keep_own, keep_kv, keep_out):
        copy.wait()
    mixes.finish()
    if n:
        spread.finish()


def attn_shapes(n_tp, rows):
    return (
        ((n_tp, rows, D), bf16),
        ((3, MICRO, TOK_DEV, WIDE), bf16),
        ((GROUP, MICRO, 2, PROMPT_DEV, WIDE), bf16),
        ((n_tp, rows, WIDE), bf16),
    )


def attn_fwd(x, vecs, biases, w_a, n_tp, shard, collective_id):
    rows = x.shape[0]
    width = D - HEADS // n_tp * HEAD * (n_tp - 1)
    saved = attn_shapes(n_tp, rows)
    operands, results, sems = spread_parts(shard, ATTN_CHUNKS)
    return pl.pallas_call(
        functools.partial(attn_fwd_kernel, len(operands)),
        out_shape=(
            jax.ShapeDtypeStruct((rows, D), f32),
            jax.ShapeDtypeStruct((MICRO, HEAD_PAIRS, 8, TOK_DEV), f32),
        )
        + tuple(jax.ShapeDtypeStruct(*s) for s in saved[:3])
        + (jax.ShapeDtypeStruct((n_tp,) + saved[3][0], bf16), jax.ShapeDtypeStruct((WIDE, D), bf16))
        + results,
        in_specs=[IN_VMEM, IN_VMEM, IN_VMEM, ANY] + [ANY] * len(operands),
        out_specs=(IN_VMEM, IN_VMEM) + (ANY,) * (5 + len(operands)),
        scratch_shapes=[pltpu.VMEM((D, 3 * WIDE), bf16), pltpu.VMEM((WIDE, D), bf16), pltpu.VMEM((n_tp, width, WIDE), bf16)]
        + [pltpu.VMEM(*s) for s in saved]
        + [
            pltpu.VMEM((KEYS, TOK_DEV), f32),
            pltpu.VMEM((KEYS, TOK_DEV), bf16),
            pltpu.VMEM((2 * HEAD, TOK_DEV), f32),
        ]
        + scatter_scratch(n_tp, rows)
        + [
            pltpu.SemaphoreType.DMA((14 * MICRO,)),
            pltpu.SemaphoreType.DMA((14 * MICRO,)),
            pltpu.SemaphoreType.DMA((3,)),
            pltpu.SemaphoreType.DMA((3,)),
            pltpu.SemaphoreType.DMA((7,)),
            pltpu.SemaphoreType.DMA((3,)),
            pltpu.SemaphoreType.DMA((3,)),
        ]
        + sems,
        compiler_params=params(collective_id),
        cost_estimate=pl.CostEstimate(flops=10**11, bytes_accessed=30 * 2**20, transcendentals=0),
    )(x, vecs, biases, w_a, *operands)


def attn_bwd_kernel(n, *refs):
    g_ref, x_ref, vec_ref, lse_ref, ff_ref, fcb_ref, all_hbm, own_hbm, kv_hbm, mix_hbm, wqkv_hbm, wout_hbm = refs[:12]
    sources, refs = refs[12 : 12 + n], refs[12 + n :]
    out_ref, dqo_hbm = refs[:2]
    results, refs = refs[2 : 2 + 2 * n], refs[2 + 2 * n :]
    (sums_ref, cols_ref, vectors), refs = refs[:3], refs[3:]
    wqkv, wout, buf, other, mixed, own, kv, gm, dkv, from_y, to_z, from_z, dkc, dqkv, stage, stage_out = refs[:16]
    p_ref, dp_ref, ds_ref, o_ref = refs[16:20]
    part, from_core, over_out, from_over, send, recv, gsend, grecv, local = refs[20:29]
    p, g = Peers(), Group()
    sums = reduces(g, sources, results, refs[29:])
    rows = x_ref.shape[0]
    n_tp = buf.shape[0]
    out_step = HEADS // n_tp * HEAD
    out_width = D - out_step * (n_tp - 1)
    sems = (send, recv)
    gather = Gather(p, buf, sems)
    scatter = Scatter(p, part, from_core, over_out, from_over, sems)
    reduce = GroupSum(g, dkv, from_y, to_z, from_z, (gsend, grecv))
    load_out = pltpu.make_async_copy(wout_hbm, wout, local.at[0])
    load_own = pltpu.make_async_copy(own_hbm, own, local.at[1])
    load_kv = pltpu.make_async_copy(kv_hbm, kv, local.at[2])
    load_qkv = pltpu.make_async_copy(wqkv_hbm.at[:, : 3 * WIDE], wqkv, local.at[3])
    load_mix = pltpu.make_async_copy(mix_hbm, mixed, local.at[4])
    load_all = pltpu.make_async_copy(all_hbm, other, local.at[6])
    for copy in (load_out, load_own, load_kv, load_qkv, load_mix, load_all):
        copy.start()
    sums_ref[...] = jnp.zeros_like(sums_ref)

    def lower(at):
        low = g_ref[at, :].astype(bf16)
        buf[p.t, at, :] = low
        add_rows(sums_ref, 4, low.astype(f32))

    row_chunks(rows, lower)
    g.greet(p)
    gather.start()
    hooks = {(1, 1): [lambda: reduce.turn(0, 0)], (1, 2): [lambda: reduce.turn(0, 1)]}
    if n:
        first_sum, second_sum = sums
        first_sum.start(1)
        hooks[0, 1] = [lambda: first_sum.pump(2)]
        hooks[0, 2] = [lambda: first_sum.pump(3)]
        hooks[1, 1] += [lambda: second_sum.start(1)]
        hooks[1, 3] = [lambda: second_sum.pump(1, first_sum)]
    gather.wait_chip()
    load_out.wait()

    def mixed_back(x):
        pair_to_blocks(gm, x, mm(pair_rows(buf, x), wout[...], NT).astype(bf16))

    mixed_back(p.x)
    if n:
        first_sum.start(2)
    gather.relay()
    gather.wait_diag()
    mixed_back(1 - p.x)
    load_own.wait()
    load_kv.wait()
    limit = key_limit(g.member)
    sub = lax.broadcasted_iota(jnp.int32, (CHUNK, TOK_DEV), 0)

    if n:
        first_sum.pump(1, then=lambda: first_sum.start(3))

    for micro in range(MICRO):

        def head(pair, lanes, half, micro=micro):
            run_hooks(hooks, micro, pair, half)
            qh = half_of(own[0, micro, :, lanes], half)
            gh = half_of(gm[micro, :, lanes], half)
            lse = lse_ref[micro, pair, half : half + 1, :]

            def first(c, load, inner):
                s = jnp.where(sub + c * CHUNK <= limit, mm(load(0), qh, NT), -1e30)
                e = jnp.exp(s - lse)
                dp = mm(load(1), gh, NT)
                p_ref[chunk_at(c), :] = e
                dp_ref[chunk_at(c), :] = dp
                return inner + fold(e * dp, jnp.sum)

            inner = over_keys(
                first,
                lambda c, i: kv[c, micro, i, :, lanes],
                lambda c, i: own[1 + i, micro, chunk_at(c, PROMPT_DEV), lanes],
                jnp.zeros((8, TOK_DEV), f32),
            )
            inner = jnp.sum(inner, axis=0, keepdims=True)

            def second(c, put):
                e = p_ref[chunk_at(c), :]
                ds = (e * (dp_ref[chunk_at(c), :] - inner)).astype(bf16)
                ds_ref[chunk_at(c), :] = ds
                put(0, mm(ds, qh))
                put(1, mm(e.astype(bf16), gh))

            @pl.loop(0, PROMPT_CHUNKS)
            def _(c):
                def put(i, value):
                    at = (micro, c // 2, c % 2, i, slice(None), lanes)
                    if half:
                        value = value + dkv[at].astype(f32)
                    dkv[at] = value.astype(bf16)

                second(c, put)

            @pl.loop(0, CONT_CHUNKS)
            def _(c):
                def put(i, value):
                    at = (i, chunk_at(c), lanes)
                    if half:
                        value = value + dkc[at].astype(f32)
                    dkc[at] = value.astype(bf16)

                second(PROMPT_CHUNKS + c, put)

            keys = kv[:, micro, 0, :, lanes].reshape(PROMPT, 2 * HEAD)
            dq = mm(keys, ds_ref[:PROMPT, :], TN) + mm(own[1, micro, PROMPT_DEV:, lanes], ds_ref[PROMPT:, :], TN)
            at = slice(HEAD * half, HEAD * (half + 1))
            o_ref[at, :] = dq[at, :] * HEAD ** (-0.5)

        def finish(pair, lanes, micro=micro):
            @pl.when(pair == HEAD_PAIRS - 1)
            def _():
                o_ref[HEAD:, :] = jnp.zeros((HEAD, TOK_DEV), f32)

            to_slots(dqkv, micro, 0, o_ref[...].T.astype(bf16), lanes)

            @pl.when(pair == HEAD_PAIRS // 2 - 1)
            def _():
                reduce.start(micro, 0)

        head_pairs(head, finish)
        reduce.start(micro, 1)
        for i in range(2):
            to_slots(dqkv, micro, PROMPT_DEV, dkc[i], slice((1 + i) * WIDE, (2 + i) * WIDE))

    load_mix.wait()
    columns = pl.ds(pl.multiple_of(p.t * out_step, 128), out_width)

    def outer(source, target, right, body):
        flat = right.reshape(n_tp * rows, right.shape[-1])

        def tile(at):
            left = source[:, :, at].reshape(n_tp * rows, -1)
            target[at, : flat.shape[1]] = mm(left, flat, TN).astype(bf16)

        body(D, tile)

    reduce.turn(1, 0)
    stage_out[:, out_width:] = jnp.zeros((D, WIDE - out_width), bf16)
    low = buf[:, :, columns].reshape(n_tp * rows, out_width)
    for t in range(n_tp):
        count = out_step if t < n_tp - 1 else out_width
        value = mm(mixed[t].reshape(n_tp * rows, WIDE), low, TN).astype(bf16)
        stage_out[t * out_step : t * out_step + count, :out_width] = value[:count, :]
    keep_out = pltpu.make_async_copy(
        stage_out.at[:, :out_step], dqo_hbm.at[:, 3 * WIDE : 3 * WIDE + out_step], local.at[5]
    )
    keep_out.start()
    reduce.turn(1, 1)
    if n:
        second_sum.start(2)
    for micro in range(MICRO):
        reduce.wait(micro)
        for i in range(2):
            to_slots(dqkv, micro, 0, reduce.total(micro, i), slice((1 + i) * WIDE, (2 + i) * WIDE))
    if n:
        second_sum.pump(2, first_sum, lambda: second_sum.start(3))
    load_qkv.wait()

    def down(x):
        def tile(at):
            put_pair(part, x, at, mm(pair_rows(dqkv, x), wqkv[at, :], NT))

        tiles(D, tile)

    down(1 - p.x)
    scatter.far_to_core().start()
    scatter.send_over()
    down(p.x)
    scatter.near_to_core().start()
    if n:
        second_sum.pump(3, first_sum, lambda: second_sum.start(0))
        first_sum.start(0)
    load_all.wait()
    outer(other, stage, dqkv[...], tiles)
    keep_qkv = pltpu.make_async_copy(stage, dqo_hbm.at[:, : 3 * WIDE], local.at[7])
    keep_qkv.start()
    cols_ref[...] = jnp.zeros_like(cols_ref)

    @pl.loop(0, n_tp * rows // ROW_CHUNK)
    def _(i):
        per = rows // ROW_CHUNK
        at = pl.ds(pl.multiple_of((i % per) * ROW_CHUNK, ROW_CHUNK), ROW_CHUNK)
        add_rows(cols_ref, 0, dqkv[i // per, at, :].astype(f32))

    scatter.wait()

    def final(at):
        dy = scatter.rows(at)
        dx, d_gain = norm_back(x_ref[at, :], dy, vec_ref[0:1, :])
        add_rows(sums_ref, 0, d_gain)
        add_rows(sums_ref, 1, dy)
        out_ref[at, :] = g_ref[at, :] + dx

    row_chunks(rows, final)
    vectors[...] = jnp.zeros_like(vectors)
    vectors[0:2, :] = sums_ref[0:2, :]
    vectors[2:3, columns] = cols_ref[:, :out_width]
    vectors[3:4, columns] = cols_ref[:, 2 * WIDE : 2 * WIDE + out_width]
    vectors[4:5, :] = sums_ref[4:5, :]
    vectors[5:8, :] = ff_ref[5:8, :]
    vectors[8:9, :] = fcb_ref[...]
    stage_out[:, out_width : out_width + 16] = vectors[...].T.astype(bf16)
    keep_rest = pltpu.make_async_copy(
        stage_out.at[:, out_step:], dqo_hbm.at[:, 3 * WIDE + out_step :], local.at[8]
    )
    keep_rest.start()
    gather.finish()
    scatter.finish()
    for micro in range(MICRO):
        reduce.finish(micro)
    keep_out.wait()
    keep_rest.wait()
    keep_qkv.wait()
    for i, item in enumerate(sums):
        item.finish(i < n - 1)


def attn_bwd(grad, x, vecs, lse, ff_sums, fc_bias_sums, all_rows, own, kv, mixed_all, w_a, w_out, n_tp, payload, collective_id):
    rows = x.shape[0]
    operands, results, more = reduce_parts(payload)
    pieces = (MICRO, 4, 2, 2, PROMPT_DEV, WIDE)
    return pl.pallas_call(
        functools.partial(attn_bwd_kernel, len(payload)),
        out_shape=(
            jax.ShapeDtypeStruct((rows, D), f32),
            jax.ShapeDtypeStruct((D, 4 * WIDE), bf16),
        )
        + results,
        in_specs=[IN_VMEM] * 6 + [ANY] * (6 + len(payload)),
        out_specs=(IN_VMEM,) + (ANY,) * (1 + 2 * len(payload)),
        scratch_shapes=[
            pltpu.VMEM((8, D), f32),
            pltpu.VMEM((1, 3 * WIDE), f32),
            pltpu.VMEM((16, D), f32),
            pltpu.VMEM((D, 3 * WIDE), bf16),
            pltpu.VMEM((WIDE, D), bf16),
            pltpu.VMEM((n_tp, rows, D), bf16),
            pltpu.VMEM((n_tp, rows, D), bf16),
            pltpu.VMEM((n_tp, n_tp, rows, WIDE), bf16),
            pltpu.VMEM((3, MICRO, TOK_DEV, WIDE), bf16),
            pltpu.VMEM((GROUP, MICRO, 2, PROMPT_DEV, WIDE), bf16),
            pltpu.VMEM((MICRO, TOK_DEV, WIDE), bf16),
            pltpu.VMEM(pieces, bf16),
            pltpu.VMEM((MICRO, 4, 2, PROMPT_DEV, WIDE), bf16),
            pltpu.VMEM((MICRO, 4, 2, PROMPT_DEV, WIDE), bf16),
            pltpu.VMEM((MICRO, 3, 2, PROMPT_DEV, WIDE), bf16),
            pltpu.VMEM((2, CONT_LEN, WIDE), bf16),
            pltpu.VMEM((n_tp, rows, 3 * WIDE), bf16),
            pltpu.VMEM((D, 3 * WIDE), bf16),
            pltpu.VMEM((D, WIDE), bf16),
            pltpu.VMEM((KEYS, TOK_DEV), f32),
            pltpu.VMEM((KEYS, TOK_DEV), f32),
            pltpu.VMEM((KEYS, TOK_DEV), bf16),
            pltpu.VMEM((2 * HEAD, TOK_DEV), f32),
        ]
        + scatter_scratch(n_tp, rows)
        + [
            pltpu.SemaphoreType.DMA((8 * MICRO,)),
            pltpu.SemaphoreType.DMA((8 * MICRO,)),
            pltpu.SemaphoreType.DMA((9,)),
        ]
        + more,
        compiler_params=params(collective_id),
        cost_estimate=pl.CostEstimate(flops=2 * 10**11, bytes_accessed=50 * 2**20, transcendentals=0),
    )(grad, x, vecs, lse, ff_sums, fc_bias_sums, all_rows, own, kv, mixed_all, w_a, w_out, *operands)


def forward_layer(x, layer, fetch, vecs, fc_bias, cols, n_tp):
    width = D - HEADS // n_tp * HEAD * (n_tp - 1)
    query_bias, value_bias = (lax.dynamic_slice_in_dim(vecs[i], cols, width) for i in (2, 3))
    biases = widen(jnp.stack([query_bias, jnp.zeros_like(query_bias), value_bias]))
    w_a = fetch.weights[layer, "a"]
    x_mid, lse, all_rows, own, kv, mixed, w_out = fetch.during(
        (layer, "b"), lambda shard: attn_fwd(x, vecs, biases, w_a, n_tp, shard, 5 + layer)
    )
    w_b = fetch.weights[layer, "b"]
    x_next, second_all, hidden_pre, hidden = fetch.during(
        (layer + 1, "a"), lambda shard: ff_fwd(x_mid, vecs, fc_bias[None], w_b, n_tp, shard, 1 + layer)
    )
    return x_next, (x, w_out, lse, all_rows, own, kv, mixed, x_mid, second_all, hidden_pre, hidden)


class Fetch:
    def __init__(self, shards):
        self.staged = lax.axis_size("fsdp") == GROUP
        self.shards, self.weights = shards, {}
        last = None
        for key, shard in shards.items():
            if self.staged:
                if last is None:
                    last = spread_only(shard, FIRST_CHUNKS, 9)
                    self.weights[key] = last.reshape(-1, shard.shape[1])
                continue
            if last is not None:
                shard, _ = lax.optimization_barrier((shard, last))
            whole = lax.all_gather(shard, "fsdp", axis=0, tiled=True)
            self.weights[key] = whole
            last = whole[:8, :128]

    def during(self, key, kernel):
        if not self.staged or key not in self.shards:
            return kernel(None)
        *results, whole = kernel(self.shards[key])
        self.weights[key] = whole.reshape(-1, whole.shape[2])
        return results


def fsdp_sum(part):
    return lax.psum_scatter(part, "fsdp", scatter_dimension=0, tiled=True).astype(f32)


def heads_joined(parts, n_tp):
    step = HEADS // n_tp * HEAD
    return jnp.concatenate([parts[t][..., :step] for t in range(n_tp - 1)] + [parts[n_tp - 1]], axis=-1)


def widen(value, axis=-1):
    pads = [(0, 0)] * value.ndim
    pads[axis] = (0, WIDE - value.shape[axis])
    return jnp.pad(value, pads)


def by_owner(part):
    return part.reshape(4, 2, -1, part.shape[1])


def owned(part, from_y, from_z):
    z, y = lax.axis_index("fsdp") // 2, lax.axis_index("fsdp") % 2
    own = lax.dynamic_index_in_dim(lax.dynamic_index_in_dim(part, z, 0, False), y, 0, False)
    near = lax.dynamic_index_in_dim(from_y, z, 0, False)
    return own.astype(f32) + near.astype(f32) + jnp.sum(from_z.astype(f32), 0)


def backward(grad, weights, vecs, saves, n_tp):
    width = D - HEADS // n_tp * HEAD * (n_tp - 1)
    staged = lax.axis_size("fsdp") == GROUP
    done, waiting = {}, {}

    def during(keys, kernel):
        keys = [key for key in keys if key in waiting]
        payload = [waiting.pop(key) for key in keys]
        results = list(kernel(payload))
        if payload:
            arrived = results[-2 * len(payload) :]
            results = results[: -2 * len(payload)]
            for i, key in enumerate(keys):
                done[key] = (payload[i], arrived[2 * i], arrived[2 * i + 1])
        return results

    def produced(key, value):
        if staged:
            waiting[key] = by_owner(value)
        else:
            done[key] = fsdp_sum(value)

    for layer in reversed(range(LAYERS)):
        w_a, w_b = weights[layer, "a"], weights[layer, "b"]
        x, w_out, lse, all_rows, own, kv, mixed_all, x_mid, second_all, hidden_pre, hidden = saves[layer]
        grad, ff_sums, fc_bias_sums, grad_fc, grad_proj = during(
            [(layer + 1, "qo")],
            lambda payload: ff_bwd(
                grad, x_mid, vecs[layer], second_all, hidden_pre, hidden, w_b, n_tp, payload, 10 + layer
            ),
        )
        produced((layer, "proj"), grad_proj)
        produced((layer, "fc"), grad_fc)
        grad, grad_qo = during(
            [(layer, "proj"), (layer, "fc")],
            lambda payload: attn_bwd(
                grad, x, vecs[layer], lse, ff_sums, fc_bias_sums, all_rows, own, kv, mixed_all,
                w_a, w_out, n_tp, payload, 20 + layer,
            ),
        )
        produced((layer, "qo"), grad_qo)
    if staged:
        got = last_sum(waiting[0, "qo"], owned(*done[1, "qo"]).astype(bf16), n_tp, 30)
        return grad, assemble([(got[k],) + done[k, "proj"] + done[k, "fc"] for k in range(LAYERS)])
    outs = []
    for layer in range(LAYERS):
        qo = done[layer, "qo"]
        got = lax.all_gather(qo.astype(bf16), "tp")
        qkv_grad = jnp.concatenate(
            [heads_joined(got[:, :, i * WIDE : i * WIDE + width], n_tp) for i in range(3)], axis=1
        )
        out_grad = heads_joined(got[:, :, 3 * WIDE : 3 * WIDE + width], n_tp)
        vector_sum = jnp.sum(got[:, :, 3 * WIDE + width : 3 * WIDE + width + 8].astype(f32), 0).T
        rest = (vector_sum[v] for v in range(8))
        outs.append((qkv_grad, out_grad, done[layer, "fc"], done[layer, "proj"].T, *rest, qo[:, 3 * WIDE + width + 8]))
    return grad, tuple(jnp.stack(pair).astype(f32) for pair in zip(*outs))


def local(
    tokens,
    qkv_weight,
    query_bias,
    value_bias,
    out_weight,
    out_bias,
    fc_weight,
    fc_bias,
    proj_weight,
    proj_bias,
    first_gain,
    first_bias,
    second_gain,
    second_bias,
    out_grad,
):
    n_tp = lax.axis_size("tp")
    tp = lax.axis_index("tp")
    row_count = tokens.shape[1]
    step = HEADS // n_tp * HEAD
    width = D - step * (n_tp - 1)
    cols = tp * step

    vectors = jnp.stack(
        [first_gain, first_bias, query_bias, value_bias, out_bias, second_gain, second_bias, proj_bias, fc_bias[:, 0]]
    ).reshape(9 * LAYERS, -1)

    shards = {}
    for layer in range(LAYERS):
        sides = [widen(lax.dynamic_slice_in_dim(qkv_weight[layer], cols + i * D, width, 1)) for i in range(3)]
        sides.append(widen(lax.dynamic_slice_in_dim(out_weight[layer], cols, width, 1)))
        if layer == 0:
            sides.append(jnp.pad(vectors.T, ((0, 0), (0, 128 - 9 * LAYERS))))
        shards[layer, "a"] = jnp.concatenate(sides, axis=1)
        fc, proj = fc_weight[layer], proj_weight[layer].T
        more = ((0, 0), (0, lanes_up(fc.shape[1]) - fc.shape[1]))
        shards[layer, "b"] = jnp.concatenate([jnp.pad(fc, more), jnp.pad(proj, more)], axis=1)
    fetch = Fetch(shards)
    vectors = fetch.weights[0, "a"][:, 4 * WIDE : 4 * WIDE + 9 * LAYERS].T.astype(f32).reshape(9, LAYERS, D)

    state = tokens.astype(f32).reshape(MICRO * row_count, D)
    saves = []
    for layer in range(LAYERS):
        state, saved = forward_layer(state, layer, fetch, vectors[:8, layer], vectors[8, layer], cols, n_tp)
        saves.append(saved)
    out_tokens = state.astype(bf16).reshape(tokens.shape)
    grad = out_grad.astype(f32).reshape(MICRO * row_count, D)
    grad, (qkv_g, out_g, fc_g, proj_g, *vec_g) = backward(
        grad, fetch.weights, [vectors[:8, layer] for layer in range(LAYERS)], saves, n_tp
    )
    return (
        out_tokens,
        grad.reshape(tokens.shape),
        qkv_g,
        vec_g[2],
        vec_g[3],
        out_g,
        vec_g[4],
        fc_g,
        vec_g[8][:, None],
        proj_g,
        vec_g[7],
        vec_g[0],
        vec_g[1],
        vec_g[5],
        vec_g[6],
    )


def solution(mesh):
    rows = P(None, ("fsdp", "tp"), None)
    weight = P(None, "fsdp", None)
    vector = P(None, "fsdp")
    fc_in = P(None, "fsdp", "tp")
    hidden = P(None, "tp", "fsdp")
    in_specs = (
        rows, weight, vector, vector, weight, vector, fc_in, hidden, hidden,
        vector, vector, vector, vector, vector, rows,
    )
    out_specs = (
        rows, rows, weight, vector, vector, weight, vector, fc_in, hidden, hidden,
        vector, vector, vector, vector, vector,
    )
    return jax.shard_map(local, mesh=mesh, in_specs=in_specs, out_specs=out_specs, check_vma=False)
```

```python
import functools

import jax
import jax.numpy as jnp
from jax import lax
from jax.experimental import pallas as pl
from jax.experimental.pallas import tpu as pltpu
from jax.sharding import PartitionSpec as P

D = 1600
HEADS = 25
HEAD = 64
GROUP = 8
PROMPT_DEV = 128
CONT_LEN = 256
TOK_DEV = 384
MICRO = 2
LAYERS = 2
PROMPT = 1024
KEYS = PROMPT + CONT_LEN
CHUNK = 128

f32 = jnp.float32
bf16 = jnp.bfloat16
norm_eps = 1e-05
NN = (((1,), (0,)), ((), ()))
NT = (((1,), (1,)), ((), ()))
TN = (((0,), (0,)), ((), ()))


def mm(left, right, dims=NN):
    return lax.dot_general(left, right, dims, preferred_element_type=f32)


def gelu_tanh(value):
    return jax.nn.gelu(value, approximate=True)


MESH = pl.DeviceIdType.MESH
ANY = pl.BlockSpec(memory_space=pl.ANY)
IN_VMEM = pl.BlockSpec(memory_space=pltpu.VMEM)
TILE = 512
ROW_CHUNK = 32


class Peers:
    def __init__(self):
        self.f = lax.axis_index("fsdp")
        self.t = lax.axis_index("tp")
        x, c = self.t // 2, self.t % 2
        self.x = x
        self.core = 2 * x + 1 - c
        self.over = 2 * (1 - x) + c
        self.diag = 2 * (1 - x) + 1 - c

    def greet(self):
        barrier = pltpu.get_barrier_semaphore()
        for t in (self.core, self.over):
            pl.semaphore_signal(barrier, inc=1, device_id=(self.f, t), device_id_type=MESH)
        pl.semaphore_wait(barrier, 2)

    def copy(self, source, target, sems, index, t):
        return pltpu.make_async_remote_copy(
            src_ref=source,
            dst_ref=target,
            send_sem=sems[0].at[index],
            recv_sem=sems[1].at[index],
            device_id=(self.f, t),
            device_id_type=MESH,
        )


class Gather:
    def __init__(self, peers, buf, sems):
        self.p, self.buf, self.sems = peers, buf, sems

    def piece(self, slot, index, t):
        return self.p.copy(self.buf.at[slot], self.buf.at[slot], self.sems, index, t)

    def start(self):
        p = self.p
        self.piece(p.t, 1, p.over).start()
        self.piece(p.t, 0, p.core).start()

    def wait_chip(self):
        self.piece(self.p.core, 0, self.p.core).wait_recv()

    def relay(self):
        p = self.p
        self.piece(p.over, 1, p.over).wait_recv()
        self.piece(p.over, 2, p.core).start()

    def wait_diag(self):
        self.piece(self.p.diag, 2, self.p.core).wait_recv()

    def finish(self):
        p = self.p
        self.piece(p.t, 1, p.over).wait_send()
        self.piece(p.t, 0, p.core).wait_send()
        self.piece(p.over, 2, p.core).wait_send()


class Scatter:
    def __init__(self, peers, part, from_core, over_out, from_over, sems):
        self.p, self.part, self.sems = peers, part, sems
        self.from_core, self.over_out, self.from_over = from_core, over_out, from_over

    def far_to_core(self):
        return self.p.copy(self.part.at[self.p.diag], self.from_core.at[0], self.sems, 3, self.p.core)

    def near_to_core(self):
        return self.p.copy(self.part.at[self.p.core], self.from_core.at[1], self.sems, 4, self.p.core)

    def to_over(self):
        return self.p.copy(self.over_out, self.from_over, self.sems, 5, self.p.over)

    def send_over(self):
        self.far_to_core().wait_recv()

        @pl.loop(0, self.over_out.shape[0] // ROW_CHUNK)
        def _(i):
            at = pl.ds(pl.multiple_of(i * ROW_CHUNK, ROW_CHUNK), ROW_CHUNK)
            total = self.part[self.p.over, at, :].astype(f32) + self.from_core[0, at, :].astype(f32)
            self.over_out[at, :] = total.astype(bf16)

        self.to_over().start()

    def wait(self):
        self.near_to_core().wait_recv()
        self.to_over().wait_recv()

    def rows(self, at):
        return (
            self.part[self.p.t, at, :].astype(f32)
            + self.from_core[1, at, :].astype(f32)
            + self.from_over[at, :].astype(f32)
        )

    def finish(self):
        for copy in (self.far_to_core(), self.near_to_core(), self.to_over()):
            copy.wait_send()


class Group:
    def __init__(self):
        f = lax.axis_index("fsdp")
        self.t = lax.axis_index("tp")
        self.member = f % GROUP
        self.base = f - self.member
        self.z, self.y = self.member // 2, self.member % 2

        half = self.z // 2
        self.inner = (self.z + half) % 2 == 1
        self.mate = 2 * half + 1 - self.z % 2
        self.far_inner, self.far_end = 2 - half, 3 - 3 * half

    def at(self, z, y):
        return z * 2 + y

    def ahead(self, k):
        return (self.z + k) % 4

    def behind(self, k):
        return (self.z + 4 - k) % 4

    def greet_group(self):
        barrier = pltpu.get_barrier_semaphore()
        others = [self.at(self.z, 1 - self.y)] + [self.at(self.ahead(k), self.y) for k in (1, 2, 3)]
        for member in others:
            pl.semaphore_signal(
                barrier, inc=1, device_id=(self.base + member, self.t), device_id_type=MESH
            )
        pl.semaphore_wait(barrier, 4)

    def greet(self, peers, with_diag=False):
        barrier = pltpu.get_barrier_semaphore()
        others = [self.at(self.z, 1 - self.y)] + [self.at(self.ahead(k), self.y) for k in (1, 2, 3)]
        for member in others:
            pl.semaphore_signal(
                barrier, inc=1, device_id=(self.base + member, self.t), device_id_type=MESH
            )
        near = [peers.core, peers.over] + [peers.diag] * with_diag
        for t in near:
            pl.semaphore_signal(barrier, inc=1, device_id=(peers.f, t), device_id_type=MESH)
        pl.semaphore_wait(barrier, 4 + len(near))

    def copy(self, source, target, sems, index, member, send_index=None):
        return pltpu.make_async_remote_copy(
            src_ref=source,
            dst_ref=target,
            send_sem=sems[0].at[index if send_index is None else send_index],
            recv_sem=sems[1].at[index],
            device_id=(self.base + member, self.t),
            device_id_type=MESH,
        )


class Reduce:
    def __init__(self, group, source, from_y, from_z, sems, tiles, columns=None):
        self.g, self.sems, self.columns = group, sems, columns
        self.source, self.from_y, self.from_z = source, from_y, from_z
        self.own, self.got, self.gone, self.local = tiles

    def cut(self, ref, *index):
        if self.columns is None:
            return ref.at[index]
        return ref.at[index + (slice(None), self.columns)]

    def across(self, j):
        g = self.g
        z = g.ahead(j)
        return g.copy(
            self.cut(self.source, z, 1 - g.y), self.cut(self.from_y, z), self.sems, j, g.at(g.z, 1 - g.y)
        )

    def along(self, j):
        g = self.g
        source, target = self.cut(self.gone, j - 1), self.cut(self.from_z, j - 1)
        return g.copy(source, target, self.sems, 3 + j, g.at(g.ahead(j), g.y))

    def start(self, *pieces):
        for j in pieces:
            self.across(j).start()

    def pump(self, j, before=None, then=None):
        g = self.g
        own, got = (self.own, self.got) if self.columns is None else (self.cut(self.own), self.cut(self.got))
        load_own = pltpu.make_async_copy(self.cut(self.source, g.ahead(j), g.y), own, self.local.at[0])
        load_own.start()
        self.across(j).wait_recv()
        if then is not None:
            then()
        load_got = pltpu.make_async_copy(self.cut(self.from_y, g.ahead(j)), got, self.local.at[1])
        load_got.start()
        load_own.wait()
        load_got.wait()
        if before is not None:
            before.along(j).wait_send()
        columns = slice(None) if self.columns is None else self.columns
        self.gone[j - 1, :, columns] = self.own[:, columns] + self.got[:, columns]
        self.along(j).start()

    def finish(self, reused=False, arrived=False):
        if not arrived:
            self.across(0).wait_recv()
        for j in range(4):
            self.across(j).wait_send()
        for j in (1, 2, 3):
            self.along(j).wait_recv()
            if not reused:
                self.along(j).wait_send()


def reduce_parts(payload):
    results, scratch = (), []
    for part in payload:
        rows = part.shape[2:]
        results += (jax.ShapeDtypeStruct((4,) + rows, bf16), jax.ShapeDtypeStruct((3,) + rows, bf16))
    scratch += [pltpu.SemaphoreType.DMA((7,))] * (2 * max(2, len(payload)) if payload else 0)
    if payload:
        scratch += [pltpu.VMEM(rows, bf16), pltpu.VMEM(rows, bf16), pltpu.VMEM((3,) + rows, bf16)]
        scratch += [pltpu.SemaphoreType.DMA((2,))]
    return tuple(payload), results, scratch


def reduces(group, sources, results, scratch):
    tiles = scratch[4:]
    if len(sources) == 1:
        middle, end = sources[0].shape[3] // 2, sources[0].shape[3]
        halves = (slice(0, middle), slice(middle, end))
        return [
            Reduce(group, sources[0], *results, scratch[2 * n : 2 * n + 2], tiles, columns)
            for n, columns in enumerate(halves)
        ]
    return [
        Reduce(group, source, results[2 * n], results[2 * n + 1], scratch[2 * n : 2 * n + 2], tiles)
        for n, source in enumerate(sources)
    ]


def in_turn(items):
    order = [(item, j) for item in items for j in (1, 2, 3, 0)]

    def step(n):
        def following():
            item, j = order[n + 1]
            item.start(j)

        item, j = order[n]
        if j:
            item.pump(j, then=following)
        else:
            item.across(0).wait_recv()
            following()

    return [lambda: items[0].start(1)] + [functools.partial(step, n) for n in range(len(order) - 1)]


class BlockGather:
    def __init__(self, peers, source, target, sems, first, local, columns=None):
        self.p, self.sems, self.first, self.local = peers, sems, first, local
        self.source = source if columns is None else source.at[:, columns]
        self.slot = lambda t: target.at[t] if columns is None else target.at[t, :, columns]

    def piece(self, slot, index, to, own=False):
        target = self.slot(slot)
        return self.p.copy(self.source if own else target, target, self.sems, self.first + index, to)

    def keep(self):
        return pltpu.make_async_copy(self.source, self.slot(self.p.t), self.local)

    def start(self):
        p = self.p
        self.piece(p.t, 1, p.over, True).start()
        self.piece(p.t, 0, p.core, True).start()
        self.keep().start()

    def relay(self):
        p = self.p
        self.piece(p.over, 1, p.over).wait_recv()
        self.piece(p.over, 2, p.core).start()

    def finish(self):
        p = self.p
        self.piece(p.core, 0, p.core).wait_recv()
        self.piece(p.diag, 2, p.core).wait_recv()
        self.piece(p.t, 1, p.over, True).wait_send()
        self.piece(p.t, 0, p.core, True).wait_send()
        self.piece(p.over, 2, p.core).wait_send()
        self.keep().wait()


def add_up(own, others, target, columns):
    rows = own.shape[0]
    for first in range(0, rows, 40):
        at = (slice(first, min(first + 40, rows)), columns)
        total = own[at].astype(f32)
        for other in others:
            total = total + other[at].astype(f32)
        target[at] = total.astype(target.dtype)


def last_sum_kernel(source, earlier, from_y, from_z, got, got_earlier, *scratch):
    p, g = Peers(), Group()
    scratch, (bsend, brecv, blocal, terms, mine) = scratch[:-5], scratch[-5:]
    before = BlockGather(p, earlier, got_earlier, (bsend, brecv), 0, blocal.at[0])
    items = reduces(g, [source], [from_y, from_z], scratch)
    after = [
        BlockGather(p, mine, got, (bsend, brecv), 3 + 3 * n, blocal.at[1 + n], item.columns)
        for n, item in enumerate(items)
    ]
    steps = in_turn(items)
    g.greet(p)
    steps[0]()
    before.start()

    def total(n):
        item = items[n]
        item.finish(arrived=n == 0)
        loads = [
            pltpu.make_async_copy(item.cut(source, g.z, g.y), item.cut(terms, 0), blocal.at[3]),
            pltpu.make_async_copy(item.cut(from_y, g.z), item.cut(terms, 1), blocal.at[4]),
        ]
        for k in range(3):
            loads.append(pltpu.make_async_copy(item.cut(from_z, k), item.cut(terms, 2 + k), blocal.at[5 + k]))
        for load in loads:
            load.start()
        for load in loads:
            load.wait()
        add_up(terms.at[0], [terms.at[k] for k in range(1, 5)], mine, item.columns)
        after[n].start()

    for n, step in enumerate(steps[1:]):
        if n == 3:
            before.relay()
        step()
    total(0)
    after[0].relay()
    total(1)
    before.finish()
    after[0].finish()
    after[1].relay()
    after[1].finish()


def last_sum(part, earlier, n_tp, collective_id):
    operands, results, scratch = reduce_parts([part])
    whole = jax.ShapeDtypeStruct((n_tp,) + earlier.shape, bf16)
    _, _, got, got_earlier = pl.pallas_call(
        last_sum_kernel,
        out_shape=results + (whole, whole),
        in_specs=[ANY, ANY],
        out_specs=(ANY,) * 4,
        scratch_shapes=scratch
        + [pltpu.SemaphoreType.DMA((9,))] * 2
        + [pltpu.SemaphoreType.DMA((8,)), pltpu.VMEM((5,) + earlier.shape, bf16), pltpu.VMEM(earlier.shape, bf16)],
        compiler_params=params(collective_id),
    )(part, earlier)
    return got, got_earlier


def assemble_kernel(*refs):
    inputs, refs = refs[: 7 * LAYERS], refs[7 * LAYERS :]
    qkv_ref, out_ref, fc_ref, proj_ref = refs[:4]
    vector_refs, (tiles, sems) = refs[4:13], refs[13:]
    t, f = lax.axis_index("tp"), lax.axis_index("fsdp")
    z, y = f // 2, f % 2
    loads = []
    for layer in range(LAYERS):
        for w in range(2):
            part, near, far = inputs[7 * layer + 1 + 3 * w : 7 * layer + 4 + 3 * w]
            n = 2 * layer + w
            loads.append(
                [
                    pltpu.make_async_copy(part.at[z, y], tiles.at[n, 0], sems.at[n, 0]),
                    pltpu.make_async_copy(near.at[z], tiles.at[n, 1], sems.at[n, 1]),
                    pltpu.make_async_copy(far, tiles.at[n, 2:5], sems.at[n, 2]),
                ]
            )
    for load in sum(loads, []):
        load.start()
    n_tp = inputs[0].shape[0]
    step = HEADS // n_tp * HEAD
    width = D - step * (n_tp - 1)
    counts = [step] * (n_tp - 1) + [width]
    for layer in range(LAYERS):
        got = inputs[7 * layer]
        for i in range(3):
            for k, count in enumerate(counts):
                value = got[k, :, i * WIDE : i * WIDE + count].astype(f32)
                qkv_ref[layer, :, i * D + k * step : i * D + k * step + count] = value
        for k, count in enumerate(counts):
            out_ref[layer, :, k * step : k * step + count] = got[k, :, 3 * WIDE : 3 * WIDE + count].astype(f32)
        extra = got[:, :, 3 * WIDE + step : 4 * WIDE].astype(f32)
        total = jnp.sum(extra, axis=0).T
        own = got[t, :, 3 * WIDE + step : 4 * WIDE].astype(f32).T
        skip = width - step
        for v in range(8):
            vector_refs[v][layer : layer + 1, :] = total[skip + v : skip + v + 1, :]
        vector_refs[8][layer : layer + 1, :] = own[skip + 8 : skip + 9, :]
        for w in range(2):
            n = 2 * layer + w
            for load in loads[n]:
                load.wait()
            total = tiles[n, 0].astype(f32)
            for k in range(1, 5):
                total = total + tiles[n, k].astype(f32)
            if w:
                fc_ref[layer] = total
            else:
                proj_ref[layer] = total.T


def assemble(layers):
    rows, width = layers[0][1].shape[2:]
    outs = [(LAYERS, rows, 3 * D), (LAYERS, rows, D), (LAYERS, rows, width), (LAYERS, width, rows)]
    outs += [(LAYERS, rows)] * 9
    return pl.pallas_call(
        assemble_kernel,
        out_shape=tuple(jax.ShapeDtypeStruct(o, f32) for o in outs),
        in_specs=([IN_VMEM] + [ANY] * 6) * LAYERS,
        out_specs=(IN_VMEM,) * len(outs),
        scratch_shapes=[
            pltpu.VMEM((2 * LAYERS, 5, rows, width), bf16),
            pltpu.SemaphoreType.DMA((2 * LAYERS, 3)),
        ],
        compiler_params=pltpu.CompilerParams(vmem_limit_bytes=60 * 2**20),
    )(*sum((list(layer) for layer in layers), []))


class Spread:
    def __init__(self, group, source, target, sems, chunks):
        self.g, self.source, self.target, self.sems = group, source, target, sems
        count = source.shape[1] // 128
        ends = [128 * (count * sum(chunks[: c + 1]) // sum(chunks)) for c in range(len(chunks))]
        self.columns = [slice(a, b) for a, b in zip([0] + ends, ends)]
        self.partner = group.at(group.z, 1 - group.y)
        self.origins = (group.mate, group.far_inner, group.far_end)

    def piece(self, member, c, index, to, own=False, send_index=None):
        target = self.target.at[member, :, self.columns[c]]
        source = self.source.at[:, self.columns[c]] if own else target
        send = None if send_index is None else 9 * c + send_index
        return self.g.copy(source, target, self.sems, 9 * c + index, to, send)

    def own(self, c):
        g = self.g
        arrives = jnp.where(g.inner, 2, 3)
        return [
            self.piece(g.member, c, arrives, g.at(g.far_inner, g.y), True, 2),
            self.piece(g.member, c, 1, g.at(g.mate, g.y), True),
        ]

    def own_across(self, c):
        return self.piece(self.g.member, c, 0, self.partner, True)

    def relayed(self, c, k):
        g = self.g
        return self.piece(g.at(self.origins[k - 1], g.y), c, 3 + k, self.partner)

    def passed(self, c, k):
        g = self.g
        return self.piece(g.at(self.origins[k - 1], g.y), c, k, g.at(g.mate, g.y), send_index=5 + k)

    def keep(self):
        return pltpu.make_async_copy(
            self.source, self.target.at[self.g.member], self.sems[0].at[9 * len(self.columns)]
        )

    def start(self, first=0, last=None):
        if first == 0:
            self.keep().start()
            for c in range(len(self.columns)):
                self.own_across(c).start()
        for c in range(len(self.columns))[first:last]:
            for copy in self.own(c):
                copy.start()

    def arrival(self, c, k):
        g = self.g
        self.piece(g.at(self.origins[k - 1], g.y), c, k, self.partner).wait_recv()

    def relay(self, c):
        self.arrival(c, 1)
        self.relayed(c, 1).start()

        @pl.when(self.g.inner)
        def _():
            for k in (2, 3):
                self.arrival(c, k)
                self.passed(c, k).start()
                self.relayed(c, k).start()

    def relay_late(self, c):
        @pl.when(jnp.logical_not(self.g.inner))
        def _():
            for k in (2, 3):
                self.arrival(c, k)
                self.relayed(c, k).start()

    def finish(self):
        g = self.g
        for c in range(len(self.columns)):
            self.piece(self.partner, c, 0, self.partner).wait_recv()
            for k in (1, 2, 3):
                self.piece(g.at(self.origins[k - 1], 1 - g.y), c, 3 + k, self.partner).wait_recv()
                self.relayed(c, k).wait_send()
            for copy in self.own(c) + [self.own_across(c)]:
                copy.wait_send()

            @pl.when(g.inner)
            def _(c=c):
                self.passed(c, 2).wait_send()
                self.passed(c, 3).wait_send()

        self.keep().wait()


def spread_parts(shard, chunks):
    if shard is None:
        return (), (), []
    whole = jax.ShapeDtypeStruct((GROUP,) + shard.shape, shard.dtype)
    return (shard,), (whole,), [pltpu.SemaphoreType.DMA((9 * len(chunks) + 1,))] * 2


def spread_kernel(chunks, source, target, send, recv):
    g = Group()
    g.greet_group()
    spread = Spread(g, source, target, (send, recv), chunks)
    spread.start(0, 2)
    for c in range(len(chunks)):
        spread.relay(c)
        spread.start(c + 2, c + 3)
        if c:
            spread.relay_late(c - 1)
    spread.relay_late(len(chunks) - 1)
    spread.finish()


def spread_only(shard, chunks, collective_id):
    operands, results, scratch = spread_parts(shard, chunks)
    return pl.pallas_call(
        functools.partial(spread_kernel, chunks),
        out_shape=results[0],
        in_specs=[ANY],
        out_specs=ANY,
        scratch_shapes=scratch,
        compiler_params=params(collective_id),
    )(shard)


def row_chunks(rows, body):
    @pl.loop(0, rows // ROW_CHUNK)
    def _(i):
        body(pl.ds(pl.multiple_of(i * ROW_CHUNK, ROW_CHUNK), ROW_CHUNK))


def tiles(extent, body):
    whole = extent // TILE

    @pl.loop(0, whole)
    def _(i):
        body(pl.ds(pl.multiple_of(i * TILE, TILE), TILE))

    if extent % TILE:
        body(pl.ds(whole * TILE, extent % TILE))


def pair_rows(ref, x):
    both = ref[pl.ds(2 * x, 2)]
    return both.reshape(2 * both.shape[1], both.shape[2])


def put_pair(ref, x, at, value):
    ref[pl.ds(2 * x, 2), :, at] = value.reshape(2, value.shape[0] // 2, value.shape[1]).astype(ref.dtype)


def norm_stats(x):
    centred = x - jnp.mean(x, -1, keepdims=True)
    scale = lax.rsqrt(jnp.mean(centred * centred, -1, keepdims=True) + norm_eps)
    return centred * scale, scale


FIRST_CHUNKS = (3, 3, 3, 3, 2, 2)
FF_CHUNKS = (5, 5, 4, 2)
ATTN_CHUNKS = (5, 6, 6, 5, 3)


def lanes_up(width):
    return -(-width // 128) * 128


def lanes_down(width):
    return width // 128 * 128


class FeedForward:
    def __init__(self, w_b, wfc, wproj, width, sems):
        main, end = lanes_down(width), 2 * (width - lanes_down(width))
        self.main, self.width, self.wfc, self.wproj = main, width, wfc, wproj
        self.fc = [
            pltpu.make_async_copy(w_b.at[:, :main], wfc.at[:, :main], sems[0]),
            pltpu.make_async_copy(w_b.at[:, 2 * main :], wfc.at[:, main : main + end], sems[1]),
        ]
        self.proj = pltpu.make_async_copy(w_b.at[:, main : 2 * main], wproj.at[:, :main], sems[2])

    def start(self):
        for copy in self.fc + [self.proj]:
            copy.start()

    def wait(self):
        for copy in self.fc + [self.proj]:
            copy.wait()
        self.wproj[:, self.main : self.width] = self.wfc[:, self.width : 2 * self.width - self.main]


def ff_fwd_kernel(n, *refs):
    x_ref, vec_ref, fcb_ref, wb_hbm = refs[:4]
    shard, refs = refs[4 : 4 + n], refs[4 + n :]
    out_ref, all_hbm, pre_hbm, hid_hbm = refs[:4]
    whole, refs = refs[4 : 4 + n], refs[4 + n :]
    wfc, wproj, buf, pre, hid, part, from_core, over_out, from_over, send, recv, local = refs[:12]
    p, g = Peers(), Group()
    spread = Spread(g, shard[0], whole[0], refs[12:], FF_CHUNKS) if n else None
    rows = x_ref.shape[0]
    sems = (send, recv)
    gather = Gather(p, buf, sems)
    scatter = Scatter(p, part, from_core, over_out, from_over, sems)
    width = fcb_ref.shape[1]
    weights = FeedForward(wb_hbm, wfc, wproj, width, [local.at[0], local.at[1], local.at[5]])
    weights.start()

    def norm(at):
        hat, _ = norm_stats(x_ref[at, :])
        buf[p.t, at, :] = (hat * vec_ref[5:6, :] + vec_ref[6:7, :]).astype(bf16)

    row_chunks(rows, norm)
    if n:
        g.greet(p)
    else:
        p.greet()
    gather.start()
    if n:
        spread.start(0, 1)
    gather.wait_chip()
    weights.wait()

    def up(x):
        def tile(at):
            value = mm(pair_rows(buf, x), wfc[:, at]) + fcb_ref[:, at]
            put_pair(pre, x, at, value)
            put_pair(hid, x, at, gelu_tanh(value))

        tiles(width, tile)

    def down(x):
        def tile(at):
            put_pair(part, x, at, mm(pair_rows(hid, x), wproj[at, :width], NT))

        tiles(D, tile)

    up(p.x)
    if n:
        spread.start(1, 2)
    gather.relay()
    gather.wait_diag()
    if n:
        spread.relay(0)
    keep_all = pltpu.make_async_copy(buf, all_hbm, local.at[2])
    keep_all.start()
    up(1 - p.x)
    keep_pre = pltpu.make_async_copy(pre, pre_hbm, local.at[3])
    keep_hid = pltpu.make_async_copy(hid, hid_hbm, local.at[4])
    keep_pre.start()
    keep_hid.start()
    down(1 - p.x)
    scatter.far_to_core().start()
    scatter.send_over()
    if n:
        spread.start(2, 3)
        spread.relay_late(0)
    down(p.x)
    scatter.near_to_core().start()
    if n:
        spread.relay(1)
        spread.start(3)
    scatter.wait()

    def final(at):
        out_ref[at, :] = x_ref[at, :] + scatter.rows(at) + vec_ref[7:8, :]

    row_chunks(rows, final)
    if n:
        spread.relay(2)
        spread.relay_late(1)
        spread.relay(3)
        spread.relay_late(2)
        spread.relay_late(3)
    gather.finish()
    scatter.finish()
    for copy in (keep_all, keep_pre, keep_hid):
        copy.wait()
    if n:
        spread.finish()


def scatter_scratch(n_tp, rows):
    return [
        pltpu.VMEM((n_tp, rows, D), bf16),
        pltpu.VMEM((2, rows, D), bf16),
        pltpu.VMEM((rows, D), bf16),
        pltpu.VMEM((rows, D), bf16),
        pltpu.SemaphoreType.DMA((6,)),
        pltpu.SemaphoreType.DMA((6,)),
    ]


def params(collective_id):
    return pltpu.CompilerParams(collective_id=collective_id, has_side_effects=True, vmem_limit_bytes=60 * 2**20)


def ff_fwd(x, vecs, fc_bias, w_b, n_tp, shard, collective_id):
    rows, width = x.shape[0], fc_bias.shape[1]
    block = (n_tp, rows)
    operands, results, sems = spread_parts(shard, FF_CHUNKS)
    return pl.pallas_call(
        functools.partial(ff_fwd_kernel, len(operands)),
        out_shape=(
            jax.ShapeDtypeStruct((rows, D), f32),
            jax.ShapeDtypeStruct(block + (D,), bf16),
            jax.ShapeDtypeStruct(block + (width,), f32),
            jax.ShapeDtypeStruct(block + (width,), bf16),
        )
        + results,
        in_specs=[IN_VMEM, IN_VMEM, IN_VMEM, ANY] + [ANY] * len(operands),
        out_specs=(IN_VMEM, ANY, ANY, ANY) + (ANY,) * len(operands),
        scratch_shapes=[
            pltpu.VMEM((D, lanes_up(width)), bf16),
            pltpu.VMEM((D, lanes_up(width)), bf16),
            pltpu.VMEM(block + (D,), bf16),
            pltpu.VMEM(block + (width,), f32),
            pltpu.VMEM(block + (width,), bf16),
        ]
        + scatter_scratch(n_tp, rows)
        + [pltpu.SemaphoreType.DMA((6,))]
        + sems,
        compiler_params=params(collective_id),
        cost_estimate=pl.CostEstimate(
            flops=4 * n_tp * rows * D * width, bytes_accessed=40 * 2**20, transcendentals=n_tp * rows * width
        ),
    )(x, vecs, fc_bias, w_b, *operands)


def gelu_slope(u):
    a = 0.7978845608028654
    square = u * u
    t = jnp.tanh(a * (u + 0.044715 * u * square))
    return 0.5 * (1.0 + t) + 0.5 * u * (1.0 - t * t) * (a * (1.0 + 3 * 0.044715 * square))


def norm_back(x, dy, gain):
    hat, scale = norm_stats(x)
    d_hat = dy * gain
    inner = d_hat - jnp.mean(d_hat, -1, keepdims=True) - hat * jnp.mean(d_hat * hat, -1, keepdims=True)
    return scale * inner, dy * hat


def add_rows(ref, row, value):
    ref[row : row + 1, :] += jnp.sum(value, axis=0, keepdims=True)


def ff_bwd_kernel(n, *refs):
    g_ref, x_ref, vec_ref, all_hbm, pre_hbm, hid_hbm, wb_hbm = refs[:7]
    sources, refs = refs[7 : 7 + n], refs[7 + n :]
    out_ref, sums_ref, fcb_ref, dfc_hbm, dproj_hbm = refs[:5]
    results, refs = refs[5 : 5 + 2 * n], refs[5 + 2 * n :]
    wfc, wproj, buf, other, pre, dpre, stage, part, from_core, over_out, from_over, send, recv, local = refs[:14]
    p, g = Peers(), Group()
    sums = reduces(g, sources, results, refs[14:])
    rows = x_ref.shape[0]
    n_tp, width = buf.shape[0], fcb_ref.shape[1]
    sems = (send, recv)
    gather = Gather(p, buf, sems)
    scatter = Scatter(p, part, from_core, over_out, from_over, sems)
    weights = FeedForward(wb_hbm, wfc, wproj, width, [local.at[0], local.at[2], local.at[7]])
    load_pre = pltpu.make_async_copy(pre_hbm, pre, local.at[1])
    load_other = pltpu.make_async_copy(hid_hbm, other, local.at[3])
    weights.start()
    for copy in (load_pre, load_other):
        copy.start()
    sums_ref[...] = jnp.zeros_like(sums_ref)
    fcb_ref[...] = jnp.zeros_like(fcb_ref)

    def lower(at):
        low = g_ref[at, :].astype(bf16)
        buf[p.t, at, :] = low
        add_rows(sums_ref, 7, low.astype(f32))

    row_chunks(rows, lower)
    if n:
        g.greet(p)
    else:
        p.greet()
    gather.start()
    steps = in_turn(sums) if n else []

    def advance():
        if steps:
            steps.pop(0)()

    advance()
    gather.wait_chip()
    weights.wait()
    load_pre.wait()

    def through(x):
        def tile(at):
            d_hidden = mm(pair_rows(buf, x), wproj[:, at])
            u = pre[pl.ds(2 * x, 2), :, at].reshape(2 * rows, -1)
            low = (gelu_slope(u) * d_hidden).astype(bf16)
            put_pair(dpre, x, at, low)
            fcb_ref[:, at] += jnp.sum(low.astype(f32), axis=0, keepdims=True)

        tiles(width, tile)

    def down(x):
        def tile(at):
            put_pair(part, x, at, mm(pair_rows(dpre, x), wfc[at, :width], NT))

        tiles(D, tile)

    through(p.x)
    gather.relay()
    advance()
    gather.wait_diag()
    through(1 - p.x)
    advance()
    down(1 - p.x)
    scatter.far_to_core().start()
    scatter.send_over()
    advance()
    down(p.x)
    scatter.near_to_core().start()
    advance()

    def outer(left, right, target, sem):
        whole = D // TILE
        rest = D - whole * TILE
        flat = right[...].reshape(n_tp * rows, width)

        def tile(i, size):
            at = pl.ds(pl.multiple_of(i * TILE, TILE), size)
            value = mm(left[:, :, at].reshape(n_tp * rows, size), flat, TN)
            stage[at, :] = value.astype(bf16)

        @pl.loop(0, whole)
        def _(i):
            tile(i, TILE)

        if rest:
            tile(whole, rest)
        return pltpu.make_async_copy(stage, target, sem)

    load_other.wait()
    store = outer(buf, other, dproj_hbm, local.at[4])
    store.start()
    gather.finish()
    load_all = pltpu.make_async_copy(all_hbm, buf, local.at[5])
    load_all.start()
    advance()
    scatter.wait()

    def final(at):
        dy = scatter.rows(at)
        dx, d_gain = norm_back(x_ref[at, :], dy, vec_ref[5:6, :])
        add_rows(sums_ref, 5, d_gain)
        add_rows(sums_ref, 6, dy)
        out_ref[at, :] = g_ref[at, :] + dx

    row_chunks(rows, final)
    load_all.wait()
    store.wait()
    store = outer(buf, dpre, dfc_hbm, local.at[6])
    store.start()
    while steps:
        advance()
    scatter.finish()
    store.wait()
    for i, item in enumerate(sums):
        item.finish(arrived=i == 0)


def ff_bwd(grad, x, vecs, all_rows, pre, hidden, w_b, n_tp, payload, collective_id):
    rows, width = x.shape[0], pre.shape[2]
    block = (n_tp, rows)
    operands, results, more = reduce_parts(payload)
    return pl.pallas_call(
        functools.partial(ff_bwd_kernel, len(payload)),
        out_shape=(
            jax.ShapeDtypeStruct((rows, D), f32),
            jax.ShapeDtypeStruct((8, D), f32),
            jax.ShapeDtypeStruct((1, width), f32),
            jax.ShapeDtypeStruct((D, width), bf16),
            jax.ShapeDtypeStruct((D, width), bf16),
        )
        + results,
        in_specs=[IN_VMEM] * 3 + [ANY] * (4 + len(payload)),
        out_specs=(IN_VMEM, IN_VMEM, IN_VMEM) + (ANY,) * (2 + 2 * len(payload)),
        scratch_shapes=[
            pltpu.VMEM((D, lanes_up(width)), bf16),
            pltpu.VMEM((D, lanes_up(width)), bf16),
            pltpu.VMEM(block + (D,), bf16),
            pltpu.VMEM(block + (width,), bf16),
            pltpu.VMEM(block + (width,), f32),
            pltpu.VMEM(block + (width,), bf16),
            pltpu.VMEM((D, width), bf16),
        ]
        + scatter_scratch(n_tp, rows)
        + [pltpu.SemaphoreType.DMA((8,))]
        + more,
        compiler_params=params(collective_id),
        cost_estimate=pl.CostEstimate(
            flops=8 * n_tp * rows * D * width, bytes_accessed=50 * 2**20, transcendentals=n_tp * rows * width
        ),
    )(grad, x, vecs, all_rows, pre, hidden, w_b, *operands)


HALVES = [(micro, half) for micro in range(MICRO) for half in range(2)]


def half_lanes(half):
    return slice(half * WIDE // 2, (half + 1) * WIDE // 2)


class Share:
    def __init__(self, group, kv, sems):
        self.g, self.kv, self.sems = group, kv, sems
        self.partner = group.at(group.z, 1 - group.y)

    def piece(self, member, part, index, to):
        micro, half = part
        ref = self.kv.at[member, micro, :, :, half_lanes(half)]
        return self.g.copy(ref, ref, self.sems, (2 * micro + half) * 7 + index, to)

    def own(self, part):
        g = self.g
        return [self.piece(g.member, part, 0, self.partner)] + [
            self.piece(g.member, part, k, g.at(g.ahead(k), g.y)) for k in (1, 2, 3)
        ]

    def relayed(self, part):
        g = self.g
        return [self.piece(g.at(g.behind(k), g.y), part, 3 + k, self.partner) for k in (1, 2, 3)]

    def start(self, *part):
        for copy in self.own(part):
            copy.start()

    def relay(self, *part):
        g = self.g
        for k, copy in zip((1, 2, 3), self.relayed(part)):
            self.piece(g.at(g.behind(k), g.y), part, k, self.partner).wait_recv()
            copy.start()

    def wait(self, *part):
        g = self.g
        self.piece(self.partner, part, 0, self.partner).wait_recv()
        for k in (1, 2, 3):
            self.piece(g.at(g.behind(k), 1 - g.y), part, 3 + k, self.partner).wait_recv()

    def finish(self):
        for part in HALVES:
            for copy in self.own(part) + self.relayed(part):
                copy.wait_send()


class GroupSum:
    def __init__(self, group, parts, from_y, to_z, from_z, sems):
        self.g, self.parts, self.sems = group, parts, sems
        self.from_y, self.to_z, self.from_z = from_y, to_z, from_z

    def across(self, micro, half):
        g, lanes = self.g, half_lanes(half)
        return g.copy(
            self.parts.at[micro, :, 1 - g.y, :, :, lanes],
            self.from_y.at[micro, :, :, :, lanes],
            self.sems,
            (2 * micro + half) * 4,
            g.at(g.z, 1 - g.y),
        )

    def along(self, micro, half, k):
        g, lanes = self.g, half_lanes(half)
        to = g.ahead(k)
        return g.copy(
            self.to_z.at[micro, to, :, :, lanes],
            self.from_z.at[micro, k - 1, :, :, lanes],
            self.sems,
            (2 * micro + half) * 4 + k,
            g.at(to, g.y),
        )

    def start(self, micro, half):
        self.across(micro, half).start()

    def turn(self, micro, half):
        lanes = half_lanes(half)
        self.across(micro, half).wait_recv()

        @pl.loop(0, 4)
        def _(z):
            for kv in range(2):
                total = self.parts[micro, z, self.g.y, kv, :, lanes] + self.from_y[micro, z, kv, :, lanes]
                self.to_z[micro, z, kv, :, lanes] = total

        for k in (1, 2, 3):
            self.along(micro, half, k).start()

    def wait(self, micro):
        for half in range(2):
            for k in (1, 2, 3):
                self.along(micro, half, k).wait_recv()

    def total(self, micro, kv):
        g = self.g
        value = self.parts[micro, g.z, g.y, kv].astype(f32) + self.from_y[micro, g.z, kv].astype(f32)
        for k in range(3):
            value = value + self.from_z[micro, k, kv].astype(f32)
        return value.astype(bf16)

    def finish(self, micro):
        for half in range(2):
            self.across(micro, half).wait_send()
            for k in (1, 2, 3):
                self.along(micro, half, k).wait_send()


WIDE = 512
HEAD_PAIRS = WIDE // (2 * HEAD)
PROMPT_CHUNKS = PROMPT // CHUNK
CONT_CHUNKS = CONT_LEN // CHUNK


def chunk_at(c, base=0):
    return pl.ds(pl.multiple_of(base + c * CHUNK, CHUNK), CHUNK)


def key_limit(member):
    row = lax.broadcasted_iota(jnp.int32, (1, TOK_DEV), 1)
    return jnp.where(row < PROMPT_DEV, member * PROMPT_DEV + row, PROMPT - PROMPT_DEV + row)


def half_of(value, half):
    lane = lax.broadcasted_iota(jnp.int32, value.shape, 1)
    return jnp.where((lane >= HEAD * half) & (lane < HEAD * (half + 1)), value, jnp.zeros_like(value))


def fold(value, op):
    return op(value.reshape(value.shape[0] // 8, 8, value.shape[1]), axis=0)


def over_keys(body, prompt, own, carry):
    carry = lax.fori_loop(0, PROMPT_CHUNKS, lambda c, carry: body(c, lambda i: prompt(c, i), carry), carry)
    return lax.fori_loop(
        0, CONT_CHUNKS, lambda c, carry: body(PROMPT_CHUNKS + c, lambda i: own(c, i), carry), carry
    )


def head_pairs(head, finish):
    @pl.loop(0, HEAD_PAIRS)
    def _(pair):
        lanes = pl.ds(pl.multiple_of(pair * 2 * HEAD, 2 * HEAD), 2 * HEAD)
        head(pair, lanes, 0)

        @pl.when(pair < HEAD_PAIRS - 1)
        def _():
            head(pair, lanes, 1)

        finish(pair, lanes)


def run_hooks(hooks, micro, pair, half):
    for at in range(HEAD_PAIRS):
        if half == 0 and (micro, at) in hooks:

            @pl.when(pair == at)
            def _(at=at):
                for hook in hooks[micro, at]:
                    hook()


def to_slots(target, micro, first, value, lanes):
    per = target.shape[1] // MICRO
    row = first
    while row < first + value.shape[0]:
        slot, within = row // per, row % per
        count = min(per - within, first + value.shape[0] - row)
        target[slot, micro * per + within : micro * per + within + count, lanes] = value[
            row - first : row - first + count
        ]
        row += count


def pair_to_blocks(target, x, value):
    per = value.shape[0] // (2 * MICRO)
    for core in range(2):
        for micro in range(MICRO):
            at = pl.ds(pl.multiple_of((2 * x + core) * per, per), per)
            first = (core * MICRO + micro) * per
            target[micro, at, :] = value[first : first + per]


def attn_fwd_kernel(n, *refs):
    x_ref, vec_ref, bias_ref, wqkv_hbm = refs[:4]
    shard, refs = refs[4 : 4 + n], refs[4 + n :]
    out_ref, lse_ref, all_hbm, own_hbm, kv_hbm, mix_hbm, wout_hbm = refs[:7]
    whole, refs = refs[7 : 7 + n], refs[7 + n :]
    wqkv, wout, wparts, buf, own, kv, mix, s_ref, p_ref, o_ref = refs[:10]
    part, from_core, over_out, from_over, send, recv, gsend, grecv, wsend, wrecv, local = refs[10:21]
    msend, mrecv = refs[21:23]
    p, g = Peers(), Group()
    spread = Spread(g, shard[0], whole[0], refs[23:], ATTN_CHUNKS) if n else None
    mixes = BlockGather(p, mix, mix_hbm, (msend, mrecv), 0, local.at[5])
    rows = x_ref.shape[0]
    n_tp = buf.shape[0]
    step = HEADS // n_tp * HEAD
    width = wparts.shape[1]
    sems = (send, recv)
    gather = Gather(p, buf, sems)
    scatter = Scatter(p, part, from_core, over_out, from_over, sems)
    share = Share(g, kv, (gsend, grecv))
    load_qkv = pltpu.make_async_copy(wqkv_hbm.at[:, : 3 * WIDE], wqkv, local.at[0])
    load_qkv.start()

    def rows_for(t):
        return wqkv_hbm.at[pl.ds(pl.multiple_of(t * step, 128), width), 3 * WIDE : 4 * WIDE]

    keep_part = pltpu.make_async_copy(rows_for(p.t), wparts.at[p.t], local.at[1])
    keep_part.start()
    give_parts = [
        p.copy(rows_for(t), wparts.at[p.t], (wsend, wrecv), i, t) for i, t in enumerate((p.core, p.over, p.diag))
    ]

    def norm(at):
        hat, _ = norm_stats(x_ref[at, :])
        buf[p.t, at, :] = (hat * vec_ref[0:1, :] + vec_ref[1:2, :]).astype(bf16)

    row_chunks(rows, norm)
    g.greet(p, True)
    gather.start()
    for copy in give_parts:
        copy.start()
    if n:
        spread.start(0, 1)
    gather.wait_chip()
    load_qkv.wait()

    def project(x):
        for i in range(3):
            value = mm(pair_rows(buf, x), wqkv[:, i * WIDE : (i + 1) * WIDE]) + bias_ref[i : i + 1, :]
            low = value.astype(bf16)
            if i == 0:
                low = low * HEAD ** (-0.5)
            pair_to_blocks(own.at[i], x, low)

    project(p.x)
    gather.relay()
    gather.wait_diag()
    project(1 - p.x)
    for micro in range(MICRO):
        for i in range(2):
            kv[g.member, micro, i] = own[1 + i, micro, :PROMPT_DEV, :]
    share.start(0, 0)
    if n:
        spread.start(1, 2)
    hooks = {
        (0, 1): [lambda: share.relay(0, 1), lambda: share.start(1, 0)],
        (0, 2): [lambda: share.wait(0, 1)],
        (0, 3): [lambda: share.relay(1, 0), lambda: share.start(1, 1)],
        (1, 0): [lambda: share.wait(1, 0)],
        (1, 1): [lambda: share.relay(1, 1)],
        (1, 2): [lambda: share.wait(1, 1)],
    }
    if n:
        hooks[0, 0] = [lambda: spread.start(2, 3)]
        hooks[0, 2] += [lambda: spread.relay(1), lambda: spread.relay_late(1)]
        hooks[0, 3] += [lambda: spread.start(3, 4)]
        hooks[1, 1] += [lambda: spread.relay(2), lambda: spread.relay_late(2), lambda: spread.start(4)]
    keep_all = pltpu.make_async_copy(buf, all_hbm, local.at[2])
    keep_own = pltpu.make_async_copy(own, own_hbm, local.at[3])
    keep_all.start()
    keep_own.start()
    limit = key_limit(g.member)
    sub = lax.broadcasted_iota(jnp.int32, (CHUNK, TOK_DEV), 0)

    share.relay(0, 0)
    share.start(0, 1)
    if n:
        spread.relay(0)
        spread.relay_late(0)
    share.wait(0, 0)

    for micro in range(MICRO):

        def head(pair, lanes, half, micro=micro):
            run_hooks(hooks, micro, pair, half)
            qh = half_of(own[0, micro, :, lanes], half)

            def first(c, load, top):
                s = jnp.where(sub + c * CHUNK <= limit, mm(load(0), qh, NT), -1e30)
                s_ref[chunk_at(c), :] = s
                return jnp.maximum(top, fold(s, jnp.max))

            top = over_keys(
                first,
                lambda c, i: kv[c, micro, i, :, lanes],
                lambda c, i: own[1 + i, micro, chunk_at(c, PROMPT_DEV), lanes],
                jnp.full((8, TOK_DEV), -1e30, f32),
            )
            top = jnp.max(top, axis=0, keepdims=True)

            def second(c, total):
                e = jnp.exp(s_ref[chunk_at(c), :] - top)
                p_ref[chunk_at(c), :] = e.astype(bf16)
                return total + fold(e, jnp.sum)

            total = lax.fori_loop(0, KEYS // CHUNK, second, jnp.zeros((8, TOK_DEV), f32))
            total = jnp.sum(total, axis=0, keepdims=True)
            values = kv[:, micro, 1, :, lanes].reshape(PROMPT, 2 * HEAD)
            out = mm(values, p_ref[:PROMPT, :], TN) + mm(own[2, micro, PROMPT_DEV:, lanes], p_ref[PROMPT:, :], TN)
            at = slice(HEAD * half, HEAD * (half + 1))
            o_ref[at, :] = out[at, :] / total
            lse_ref[micro, pair, half : half + 1, :] = top + jnp.log(total)

        def finish(pair, lanes, micro=micro):
            @pl.when(pair == HEAD_PAIRS - 1)
            def _():
                o_ref[HEAD:, :] = jnp.zeros((HEAD, TOK_DEV), f32)

            to_slots(mix, micro, 0, o_ref[...].T.astype(bf16), lanes)

        head_pairs(head, finish)

    keep_kv = pltpu.make_async_copy(kv, kv_hbm, local.at[4])
    keep_kv.start()
    keep_part.wait()
    for i, t in enumerate((p.core, p.over, p.diag)):
        p.copy(rows_for(t), wparts.at[t], (wsend, wrecv), i, t).wait_recv()
    for t in range(n_tp):
        count = min(WIDE, D - t * step)
        wout[:width, t * step : t * step + count] = wparts[t, :, :count]
    wout[width:, :] = jnp.zeros((WIDE - width, D), bf16)

    @pl.when(p.t < n_tp - 1)
    def _():
        wout[step:width, :] = jnp.zeros((width - step, D), bf16)

    keep_out = pltpu.make_async_copy(wout, wout_hbm, local.at[6])
    keep_out.start()

    def down(x):
        def tile(at):
            put_pair(part, x, at, mm(pair_rows(mix, x), wout[:, at]))

        tiles(D, tile)

    down(1 - p.x)
    scatter.far_to_core().start()
    scatter.send_over()
    down(p.x)
    scatter.near_to_core().start()
    if n:
        spread.relay(3)
        spread.relay_late(3)
    scatter.wait()
    mixes.start()

    def final(at):
        out_ref[at, :] = x_ref[at, :] + (scatter.rows(at) + vec_ref[4:5, :])

    row_chunks(rows, final)
    mixes.relay()
    if n:
        spread.relay(4)
        spread.relay_late(4)
    gather.finish()
    scatter.finish()
    share.finish()
    for copy in give_parts:
        copy.wait_send()
    for copy in (keep_all, keep_own, keep_kv, keep_out):
        copy.wait()
    mixes.finish()
    if n:
        spread.finish()


def attn_shapes(n_tp, rows):
    return (
        ((n_tp, rows, D), bf16),
        ((3, MICRO, TOK_DEV, WIDE), bf16),
        ((GROUP, MICRO, 2, PROMPT_DEV, WIDE), bf16),
        ((n_tp, rows, WIDE), bf16),
    )


def attn_fwd(x, vecs, biases, w_a, n_tp, shard, collective_id):
    rows = x.shape[0]
    width = D - HEADS // n_tp * HEAD * (n_tp - 1)
    saved = attn_shapes(n_tp, rows)
    operands, results, sems = spread_parts(shard, ATTN_CHUNKS)
    return pl.pallas_call(
        functools.partial(attn_fwd_kernel, len(operands)),
        out_shape=(
            jax.ShapeDtypeStruct((rows, D), f32),
            jax.ShapeDtypeStruct((MICRO, HEAD_PAIRS, 8, TOK_DEV), f32),
        )
        + tuple(jax.ShapeDtypeStruct(*s) for s in saved[:3])
        + (jax.ShapeDtypeStruct((n_tp,) + saved[3][0], bf16), jax.ShapeDtypeStruct((WIDE, D), bf16))
        + results,
        in_specs=[IN_VMEM, IN_VMEM, IN_VMEM, ANY] + [ANY] * len(operands),
        out_specs=(IN_VMEM, IN_VMEM) + (ANY,) * (5 + len(operands)),
        scratch_shapes=[pltpu.VMEM((D, 3 * WIDE), bf16), pltpu.VMEM((WIDE, D), bf16), pltpu.VMEM((n_tp, width, WIDE), bf16)]
        + [pltpu.VMEM(*s) for s in saved]
        + [
            pltpu.VMEM((KEYS, TOK_DEV), f32),
            pltpu.VMEM((KEYS, TOK_DEV), bf16),
            pltpu.VMEM((2 * HEAD, TOK_DEV), f32),
        ]
        + scatter_scratch(n_tp, rows)
        + [
            pltpu.SemaphoreType.DMA((14 * MICRO,)),
            pltpu.SemaphoreType.DMA((14 * MICRO,)),
            pltpu.SemaphoreType.DMA((3,)),
            pltpu.SemaphoreType.DMA((3,)),
            pltpu.SemaphoreType.DMA((7,)),
            pltpu.SemaphoreType.DMA((3,)),
            pltpu.SemaphoreType.DMA((3,)),
        ]
        + sems,
        compiler_params=params(collective_id),
        cost_estimate=pl.CostEstimate(flops=10**11, bytes_accessed=30 * 2**20, transcendentals=0),
    )(x, vecs, biases, w_a, *operands)


def attn_bwd_kernel(n, *refs):
    g_ref, x_ref, vec_ref, lse_ref, ff_ref, fcb_ref, all_hbm, own_hbm, kv_hbm, mix_hbm, wqkv_hbm, wout_hbm = refs[:12]
    sources, refs = refs[12 : 12 + n], refs[12 + n :]
    out_ref, dqo_hbm = refs[:2]
    results, refs = refs[2 : 2 + 2 * n], refs[2 + 2 * n :]
    (sums_ref, cols_ref, vectors), refs = refs[:3], refs[3:]
    wqkv, wout, buf, other, mixed, own, kv, gm, dkv, from_y, to_z, from_z, dkc, dqkv, stage, stage_out = refs[:16]
    p_ref, dp_ref, ds_ref, o_ref = refs[16:20]
    part, from_core, over_out, from_over, send, recv, gsend, grecv, local = refs[20:29]
    p, g = Peers(), Group()
    sums = reduces(g, sources, results, refs[29:])
    rows = x_ref.shape[0]
    n_tp = buf.shape[0]
    out_step = HEADS // n_tp * HEAD
    out_width = D - out_step * (n_tp - 1)
    sems = (send, recv)
    gather = Gather(p, buf, sems)
    scatter = Scatter(p, part, from_core, over_out, from_over, sems)
    reduce = GroupSum(g, dkv, from_y, to_z, from_z, (gsend, grecv))
    load_out = pltpu.make_async_copy(wout_hbm, wout, local.at[0])
    load_own = pltpu.make_async_copy(own_hbm, own, local.at[1])
    load_kv = pltpu.make_async_copy(kv_hbm, kv, local.at[2])
    load_qkv = pltpu.make_async_copy(wqkv_hbm.at[:, : 3 * WIDE], wqkv, local.at[3])
    load_mix = pltpu.make_async_copy(mix_hbm, mixed, local.at[4])
    load_all = pltpu.make_async_copy(all_hbm, other, local.at[6])
    for copy in (load_out, load_own, load_kv, load_qkv, load_mix, load_all):
        copy.start()
    sums_ref[...] = jnp.zeros_like(sums_ref)

    def lower(at):
        low = g_ref[at, :].astype(bf16)
        buf[p.t, at, :] = low
        add_rows(sums_ref, 4, low.astype(f32))

    row_chunks(rows, lower)
    g.greet(p)
    gather.start()
    hooks = {(1, 1): [lambda: reduce.turn(0, 0)], (1, 2): [lambda: reduce.turn(0, 1)]}
    if n:
        first_sum, second_sum = sums
        first_sum.start(1)
        hooks[0, 1] = [lambda: first_sum.pump(2)]
        hooks[0, 2] = [lambda: first_sum.pump(3)]
        hooks[1, 1] += [lambda: second_sum.start(1)]
        hooks[1, 3] = [lambda: second_sum.pump(1, first_sum)]
    gather.wait_chip()
    load_out.wait()

    def mixed_back(x):
        pair_to_blocks(gm, x, mm(pair_rows(buf, x), wout[...], NT).astype(bf16))

    mixed_back(p.x)
    if n:
        first_sum.start(2)
    gather.relay()
    gather.wait_diag()
    if n:
        first_sum.pump(1, then=lambda: first_sum.start(3))
    mixed_back(1 - p.x)
    load_own.wait()
    load_kv.wait()
    limit = key_limit(g.member)
    sub = lax.broadcasted_iota(jnp.int32, (CHUNK, TOK_DEV), 0)


    for micro in range(MICRO):

        def head(pair, lanes, half, micro=micro):
            run_hooks(hooks, micro, pair, half)
            qh = half_of(own[0, micro, :, lanes], half)
            gh = half_of(gm[micro, :, lanes], half)
            lse = lse_ref[micro, pair, half : half + 1, :]

            def first(c, load, inner):
                s = jnp.where(sub + c * CHUNK <= limit, mm(load(0), qh, NT), -1e30)
                e = jnp.exp(s - lse)
                dp = mm(load(1), gh, NT)
                p_ref[chunk_at(c), :] = e
                dp_ref[chunk_at(c), :] = dp
                return inner + fold(e * dp, jnp.sum)

            inner = over_keys(
                first,
                lambda c, i: kv[c, micro, i, :, lanes],
                lambda c, i: own[1 + i, micro, chunk_at(c, PROMPT_DEV), lanes],
                jnp.zeros((8, TOK_DEV), f32),
            )
            inner = jnp.sum(inner, axis=0, keepdims=True)

            def second(c, put):
                e = p_ref[chunk_at(c), :]
                ds = (e * (dp_ref[chunk_at(c), :] - inner)).astype(bf16)
                ds_ref[chunk_at(c), :] = ds
                put(0, mm(ds, qh))
                put(1, mm(e.astype(bf16), gh))

            @pl.loop(0, PROMPT_CHUNKS)
            def _(c):
                def put(i, value):
                    at = (micro, c // 2, c % 2, i, slice(None), lanes)
                    if half:
                        value = value + dkv[at].astype(f32)
                    dkv[at] = value.astype(bf16)

                second(c, put)

            @pl.loop(0, CONT_CHUNKS)
            def _(c):
                def put(i, value):
                    at = (i, chunk_at(c), lanes)
                    if half:
                        value = value + dkc[at].astype(f32)
                    dkc[at] = value.astype(bf16)

                second(PROMPT_CHUNKS + c, put)

            keys = kv[:, micro, 0, :, lanes].reshape(PROMPT, 2 * HEAD)
            dq = mm(keys, ds_ref[:PROMPT, :], TN) + mm(own[1, micro, PROMPT_DEV:, lanes], ds_ref[PROMPT:, :], TN)
            at = slice(HEAD * half, HEAD * (half + 1))
            o_ref[at, :] = dq[at, :] * HEAD ** (-0.5)

        def finish(pair, lanes, micro=micro):
            @pl.when(pair == HEAD_PAIRS - 1)
            def _():
                o_ref[HEAD:, :] = jnp.zeros((HEAD, TOK_DEV), f32)

            to_slots(dqkv, micro, 0, o_ref[...].T.astype(bf16), lanes)

            @pl.when(pair == HEAD_PAIRS // 2 - 1)
            def _():
                reduce.start(micro, 0)

        head_pairs(head, finish)
        reduce.start(micro, 1)
        for i in range(2):
            to_slots(dqkv, micro, PROMPT_DEV, dkc[i], slice((1 + i) * WIDE, (2 + i) * WIDE))

    load_mix.wait()
    columns = pl.ds(pl.multiple_of(p.t * out_step, 128), out_width)

    def outer(source, target, right, body):
        flat = right.reshape(n_tp * rows, right.shape[-1])

        def tile(at):
            left = source[:, :, at].reshape(n_tp * rows, -1)
            target[at, : flat.shape[1]] = mm(left, flat, TN).astype(bf16)

        body(D, tile)

    reduce.turn(1, 0)
    stage_out[:, out_width:] = jnp.zeros((D, WIDE - out_width), bf16)
    low = buf[:, :, columns].reshape(n_tp * rows, out_width)
    for t in range(n_tp):
        count = out_step if t < n_tp - 1 else out_width
        value = mm(mixed[t].reshape(n_tp * rows, WIDE), low, TN).astype(bf16)
        stage_out[t * out_step : t * out_step + count, :out_width] = value[:count, :]
    keep_out = pltpu.make_async_copy(
        stage_out.at[:, :out_step], dqo_hbm.at[:, 3 * WIDE : 3 * WIDE + out_step], local.at[5]
    )
    keep_out.start()
    reduce.turn(1, 1)
    if n:
        second_sum.start(2)
    for micro in range(MICRO):
        reduce.wait(micro)
        for i in range(2):
            to_slots(dqkv, micro, 0, reduce.total(micro, i), slice((1 + i) * WIDE, (2 + i) * WIDE))
    if n:
        second_sum.pump(2, first_sum, lambda: second_sum.start(3))
    load_qkv.wait()

    def down(x):
        def tile(at):
            put_pair(part, x, at, mm(pair_rows(dqkv, x), wqkv[at, :], NT))

        tiles(D, tile)

    down(1 - p.x)
    scatter.far_to_core().start()
    scatter.send_over()
    down(p.x)
    scatter.near_to_core().start()
    if n:
        second_sum.pump(3, first_sum, lambda: second_sum.start(0))
        first_sum.start(0)
    load_all.wait()
    outer(other, stage, dqkv[...], tiles)
    keep_qkv = pltpu.make_async_copy(stage, dqo_hbm.at[:, : 3 * WIDE], local.at[7])
    keep_qkv.start()
    cols_ref[...] = jnp.zeros_like(cols_ref)

    @pl.loop(0, n_tp * rows // ROW_CHUNK)
    def _(i):
        per = rows // ROW_CHUNK
        at = pl.ds(pl.multiple_of((i % per) * ROW_CHUNK, ROW_CHUNK), ROW_CHUNK)
        add_rows(cols_ref, 0, dqkv[i // per, at, :].astype(f32))

    scatter.wait()

    def final(at):
        dy = scatter.rows(at)
        dx, d_gain = norm_back(x_ref[at, :], dy, vec_ref[0:1, :])
        add_rows(sums_ref, 0, d_gain)
        add_rows(sums_ref, 1, dy)
        out_ref[at, :] = g_ref[at, :] + dx

    row_chunks(rows, final)
    vectors[...] = jnp.zeros_like(vectors)
    vectors[0:2, :] = sums_ref[0:2, :]
    vectors[2:3, columns] = cols_ref[:, :out_width]
    vectors[3:4, columns] = cols_ref[:, 2 * WIDE : 2 * WIDE + out_width]
    vectors[4:5, :] = sums_ref[4:5, :]
    vectors[5:8, :] = ff_ref[5:8, :]
    vectors[8:9, :] = fcb_ref[...]
    stage_out[:, out_width : out_width + 16] = vectors[...].T.astype(bf16)
    keep_rest = pltpu.make_async_copy(
        stage_out.at[:, out_step:], dqo_hbm.at[:, 3 * WIDE + out_step :], local.at[8]
    )
    keep_rest.start()
    gather.finish()
    scatter.finish()
    for micro in range(MICRO):
        reduce.finish(micro)
    keep_out.wait()
    keep_rest.wait()
    keep_qkv.wait()
    for i, item in enumerate(sums):
        item.finish(i < n - 1)


def attn_bwd(grad, x, vecs, lse, ff_sums, fc_bias_sums, all_rows, own, kv, mixed_all, w_a, w_out, n_tp, payload, collective_id):
    rows = x.shape[0]
    operands, results, more = reduce_parts(payload)
    pieces = (MICRO, 4, 2, 2, PROMPT_DEV, WIDE)
    return pl.pallas_call(
        functools.partial(attn_bwd_kernel, len(payload)),
        out_shape=(
            jax.ShapeDtypeStruct((rows, D), f32),
            jax.ShapeDtypeStruct((D, 4 * WIDE), bf16),
        )
        + results,
        in_specs=[IN_VMEM] * 6 + [ANY] * (6 + len(payload)),
        out_specs=(IN_VMEM,) + (ANY,) * (1 + 2 * len(payload)),
        scratch_shapes=[
            pltpu.VMEM((8, D), f32),
            pltpu.VMEM((1, 3 * WIDE), f32),
            pltpu.VMEM((16, D), f32),
            pltpu.VMEM((D, 3 * WIDE), bf16),
            pltpu.VMEM((WIDE, D), bf16),
            pltpu.VMEM((n_tp, rows, D), bf16),
            pltpu.VMEM((n_tp, rows, D), bf16),
            pltpu.VMEM((n_tp, n_tp, rows, WIDE), bf16),
            pltpu.VMEM((3, MICRO, TOK_DEV, WIDE), bf16),
            pltpu.VMEM((GROUP, MICRO, 2, PROMPT_DEV, WIDE), bf16),
            pltpu.VMEM((MICRO, TOK_DEV, WIDE), bf16),
            pltpu.VMEM(pieces, bf16),
            pltpu.VMEM((MICRO, 4, 2, PROMPT_DEV, WIDE), bf16),
            pltpu.VMEM((MICRO, 4, 2, PROMPT_DEV, WIDE), bf16),
            pltpu.VMEM((MICRO, 3, 2, PROMPT_DEV, WIDE), bf16),
            pltpu.VMEM((2, CONT_LEN, WIDE), bf16),
            pltpu.VMEM((n_tp, rows, 3 * WIDE), bf16),
            pltpu.VMEM((D, 3 * WIDE), bf16),
            pltpu.VMEM((D, WIDE), bf16),
            pltpu.VMEM((KEYS, TOK_DEV), f32),
            pltpu.VMEM((KEYS, TOK_DEV), f32),
            pltpu.VMEM((KEYS, TOK_DEV), bf16),
            pltpu.VMEM((2 * HEAD, TOK_DEV), f32),
        ]
        + scatter_scratch(n_tp, rows)
        + [
            pltpu.SemaphoreType.DMA((8 * MICRO,)),
            pltpu.SemaphoreType.DMA((8 * MICRO,)),
            pltpu.SemaphoreType.DMA((9,)),
        ]
        + more,
        compiler_params=params(collective_id),
        cost_estimate=pl.CostEstimate(flops=2 * 10**11, bytes_accessed=50 * 2**20, transcendentals=0),
    )(grad, x, vecs, lse, ff_sums, fc_bias_sums, all_rows, own, kv, mixed_all, w_a, w_out, *operands)


def forward_layer(x, layer, fetch, vecs, fc_bias, cols, n_tp):
    width = D - HEADS // n_tp * HEAD * (n_tp - 1)
    query_bias, value_bias = (lax.dynamic_slice_in_dim(vecs[i], cols, width) for i in (2, 3))
    biases = widen(jnp.stack([query_bias, jnp.zeros_like(query_bias), value_bias]))
    w_a = fetch.weights[layer, "a"]
    x_mid, lse, all_rows, own, kv, mixed, w_out = fetch.during(
        (layer, "b"), lambda shard: attn_fwd(x, vecs, biases, w_a, n_tp, shard, 5 + layer)
    )
    w_b = fetch.weights[layer, "b"]
    x_next, second_all, hidden_pre, hidden = fetch.during(
        (layer + 1, "a"), lambda shard: ff_fwd(x_mid, vecs, fc_bias[None], w_b, n_tp, shard, 1 + layer)
    )
    return x_next, (x, w_out, lse, all_rows, own, kv, mixed, x_mid, second_all, hidden_pre, hidden)


class Fetch:
    def __init__(self, shards):
        self.staged = lax.axis_size("fsdp") == GROUP
        self.shards, self.weights = shards, {}
        last = None
        for key, shard in shards.items():
            if self.staged:
                if last is None:
                    last = spread_only(shard, FIRST_CHUNKS, 9)
                    self.weights[key] = last.reshape(-1, shard.shape[1])
                continue
            if last is not None:
                shard, _ = lax.optimization_barrier((shard, last))
            whole = lax.all_gather(shard, "fsdp", axis=0, tiled=True)
            self.weights[key] = whole
            last = whole[:8, :128]

    def during(self, key, kernel):
        if not self.staged or key not in self.shards:
            return kernel(None)
        *results, whole = kernel(self.shards[key])
        self.weights[key] = whole.reshape(-1, whole.shape[2])
        return results


def fsdp_sum(part):
    return lax.psum_scatter(part, "fsdp", scatter_dimension=0, tiled=True).astype(f32)


def heads_joined(parts, n_tp):
    step = HEADS // n_tp * HEAD
    return jnp.concatenate([parts[t][..., :step] for t in range(n_tp - 1)] + [parts[n_tp - 1]], axis=-1)


def widen(value, axis=-1):
    pads = [(0, 0)] * value.ndim
    pads[axis] = (0, WIDE - value.shape[axis])
    return jnp.pad(value, pads)


def by_owner(part):
    return part.reshape(4, 2, -1, part.shape[1])


def owned(part, from_y, from_z):
    z, y = lax.axis_index("fsdp") // 2, lax.axis_index("fsdp") % 2
    own = lax.dynamic_index_in_dim(lax.dynamic_index_in_dim(part, z, 0, False), y, 0, False)
    near = lax.dynamic_index_in_dim(from_y, z, 0, False)
    return own.astype(f32) + near.astype(f32) + jnp.sum(from_z.astype(f32), 0)


def backward(grad, weights, vecs, saves, n_tp):
    width = D - HEADS // n_tp * HEAD * (n_tp - 1)
    staged = lax.axis_size("fsdp") == GROUP
    done, waiting = {}, {}

    def during(keys, kernel):
        keys = [key for key in keys if key in waiting]
        payload = [waiting.pop(key) for key in keys]
        results = list(kernel(payload))
        if payload:
            arrived = results[-2 * len(payload) :]
            results = results[: -2 * len(payload)]
            for i, key in enumerate(keys):
                done[key] = (payload[i], arrived[2 * i], arrived[2 * i + 1])
        return results

    def produced(key, value):
        if staged:
            waiting[key] = by_owner(value)
        else:
            done[key] = fsdp_sum(value)

    for layer in reversed(range(LAYERS)):
        w_a, w_b = weights[layer, "a"], weights[layer, "b"]
        x, w_out, lse, all_rows, own, kv, mixed_all, x_mid, second_all, hidden_pre, hidden = saves[layer]
        grad, ff_sums, fc_bias_sums, grad_fc, grad_proj = during(
            [(layer + 1, "qo")],
            lambda payload: ff_bwd(
                grad, x_mid, vecs[layer], second_all, hidden_pre, hidden, w_b, n_tp, payload, 10 + layer
            ),
        )
        produced((layer, "proj"), grad_proj)
        produced((layer, "fc"), grad_fc)
        grad, grad_qo = during(
            [(layer, "proj"), (layer, "fc")],
            lambda payload: attn_bwd(
                grad, x, vecs[layer], lse, ff_sums, fc_bias_sums, all_rows, own, kv, mixed_all,
                w_a, w_out, n_tp, payload, 20 + layer,
            ),
        )
        produced((layer, "qo"), grad_qo)
    if staged:
        got = last_sum(waiting[0, "qo"], owned(*done[1, "qo"]).astype(bf16), n_tp, 30)
        return grad, assemble([(got[k],) + done[k, "proj"] + done[k, "fc"] for k in range(LAYERS)])
    outs = []
    for layer in range(LAYERS):
        qo = done[layer, "qo"]
        got = lax.all_gather(qo.astype(bf16), "tp")
        qkv_grad = jnp.concatenate(
            [heads_joined(got[:, :, i * WIDE : i * WIDE + width], n_tp) for i in range(3)], axis=1
        )
        out_grad = heads_joined(got[:, :, 3 * WIDE : 3 * WIDE + width], n_tp)
        vector_sum = jnp.sum(got[:, :, 3 * WIDE + width : 3 * WIDE + width + 8].astype(f32), 0).T
        rest = (vector_sum[v] for v in range(8))
        outs.append((qkv_grad, out_grad, done[layer, "fc"], done[layer, "proj"].T, *rest, qo[:, 3 * WIDE + width + 8]))
    return grad, tuple(jnp.stack(pair).astype(f32) for pair in zip(*outs))


def local(
    tokens,
    qkv_weight,
    query_bias,
    value_bias,
    out_weight,
    out_bias,
    fc_weight,
    fc_bias,
    proj_weight,
    proj_bias,
    first_gain,
    first_bias,
    second_gain,
    second_bias,
    out_grad,
):
    n_tp = lax.axis_size("tp")
    tp = lax.axis_index("tp")
    row_count = tokens.shape[1]
    step = HEADS // n_tp * HEAD
    width = D - step * (n_tp - 1)
    cols = tp * step

    vectors = jnp.stack(
        [first_gain, first_bias, query_bias, value_bias, out_bias, second_gain, second_bias, proj_bias, fc_bias[:, 0]]
    ).reshape(9 * LAYERS, -1)

    shards = {}
    for layer in range(LAYERS):
        sides = [widen(lax.dynamic_slice_in_dim(qkv_weight[layer], cols + i * D, width, 1)) for i in range(3)]
        out_cols = lax.dynamic_slice_in_dim(out_weight[layer], cols, width, 1)
        if layer == 0:
            out_cols = jnp.concatenate([out_cols, vectors.T], axis=1)
        sides.append(widen(out_cols))
        shards[layer, "a"] = jnp.concatenate(sides, axis=1)
        fc, proj = fc_weight[layer], proj_weight[layer].T
        main = lanes_down(fc.shape[1])
        shards[layer, "b"] = jnp.concatenate([fc[:, :main], proj[:, :main], fc[:, main:], proj[:, main:]], axis=1)
    fetch = Fetch(shards)
    beside = 3 * WIDE + width
    vectors = fetch.weights[0, "a"][:, beside : beside + 9 * LAYERS].T.astype(f32).reshape(9, LAYERS, D)

    state = tokens.astype(f32).reshape(MICRO * row_count, D)
    saves = []
    for layer in range(LAYERS):
        state, saved = forward_layer(state, layer, fetch, vectors[:8, layer], vectors[8, layer], cols, n_tp)
        saves.append(saved)
    out_tokens = state.astype(bf16).reshape(tokens.shape)
    grad = out_grad.astype(f32).reshape(MICRO * row_count, D)
    grad, (qkv_g, out_g, fc_g, proj_g, *vec_g) = backward(
        grad, fetch.weights, [vectors[:8, layer] for layer in range(LAYERS)], saves, n_tp
    )
    return (
        out_tokens,
        grad.reshape(tokens.shape),
        qkv_g,
        vec_g[2],
        vec_g[3],
        out_g,
        vec_g[4],
        fc_g,
        vec_g[8][:, None],
        proj_g,
        vec_g[7],
        vec_g[0],
        vec_g[1],
        vec_g[5],
        vec_g[6],
    )


def solution(mesh):
    rows = P(None, ("fsdp", "tp"), None)
    weight = P(None, "fsdp", None)
    vector = P(None, "fsdp")
    fc_in = P(None, "fsdp", "tp")
    hidden = P(None, "tp", "fsdp")
    in_specs = (
        rows, weight, vector, vector, weight, vector, fc_in, hidden, hidden,
        vector, vector, vector, vector, vector, rows,
    )
    out_specs = (
        rows, rows, weight, vector, vector, weight, vector, fc_in, hidden, hidden,
        vector, vector, vector, vector, vector,
    )
    return jax.shard_map(local, mesh=mesh, in_specs=in_specs, out_specs=out_specs, check_vma=False)
```

```python
import functools

import jax
import jax.numpy as jnp
from jax import lax
from jax.experimental import pallas as pl
from jax.experimental.pallas import tpu as pltpu
from jax.sharding import PartitionSpec as P

D = 1600
HEADS = 25
HEAD = 64
GROUP = 8
PROMPT_DEV = 128
CONT_LEN = 256
TOK_DEV = 384
MICRO = 2
LAYERS = 2
PROMPT = 1024
KEYS = PROMPT + CONT_LEN
CHUNK = 128

f32 = jnp.float32
bf16 = jnp.bfloat16
norm_eps = 1e-05
NN = (((1,), (0,)), ((), ()))
NT = (((1,), (1,)), ((), ()))
TN = (((0,), (0,)), ((), ()))


def mm(left, right, dims=NN):
    return lax.dot_general(left, right, dims, preferred_element_type=f32)


def gelu_tanh(value):
    return jax.nn.gelu(value, approximate=True)


MESH = pl.DeviceIdType.MESH
ANY = pl.BlockSpec(memory_space=pl.ANY)
IN_VMEM = pl.BlockSpec(memory_space=pltpu.VMEM)
TILE = 512
ROW_CHUNK = 32


class Peers:
    def __init__(self):
        self.f = lax.axis_index("fsdp")
        self.t = lax.axis_index("tp")
        x, c = self.t // 2, self.t % 2
        self.x = x
        self.core = 2 * x + 1 - c
        self.over = 2 * (1 - x) + c
        self.diag = 2 * (1 - x) + 1 - c

    def greet(self):
        barrier = pltpu.get_barrier_semaphore()
        for t in (self.core, self.over):
            pl.semaphore_signal(barrier, inc=1, device_id=(self.f, t), device_id_type=MESH)
        pl.semaphore_wait(barrier, 2)

    def copy(self, source, target, sems, index, t):
        return pltpu.make_async_remote_copy(
            src_ref=source,
            dst_ref=target,
            send_sem=sems[0].at[index],
            recv_sem=sems[1].at[index],
            device_id=(self.f, t),
            device_id_type=MESH,
        )


class Gather:
    def __init__(self, peers, buf, sems):
        self.p, self.buf, self.sems = peers, buf, sems

    def piece(self, slot, index, t):
        return self.p.copy(self.buf.at[slot], self.buf.at[slot], self.sems, index, t)

    def start(self):
        p = self.p
        self.piece(p.t, 1, p.over).start()
        self.piece(p.t, 0, p.core).start()

    def wait_chip(self):
        self.piece(self.p.core, 0, self.p.core).wait_recv()

    def relay(self):
        p = self.p
        self.piece(p.over, 1, p.over).wait_recv()
        self.piece(p.over, 2, p.core).start()

    def wait_diag(self):
        self.piece(self.p.diag, 2, self.p.core).wait_recv()

    def finish(self):
        p = self.p
        self.piece(p.t, 1, p.over).wait_send()
        self.piece(p.t, 0, p.core).wait_send()
        self.piece(p.over, 2, p.core).wait_send()


class Scatter:
    def __init__(self, peers, part, from_core, over_out, from_over, sems):
        self.p, self.part, self.sems = peers, part, sems
        self.from_core, self.over_out, self.from_over = from_core, over_out, from_over

    def far_to_core(self):
        return self.p.copy(self.part.at[self.p.diag], self.from_core.at[0], self.sems, 3, self.p.core)

    def near_to_core(self):
        return self.p.copy(self.part.at[self.p.core], self.from_core.at[1], self.sems, 4, self.p.core)

    def to_over(self):
        return self.p.copy(self.over_out, self.from_over, self.sems, 5, self.p.over)

    def send_over(self):
        self.far_to_core().wait_recv()

        @pl.loop(0, self.over_out.shape[0] // ROW_CHUNK)
        def _(i):
            at = pl.ds(pl.multiple_of(i * ROW_CHUNK, ROW_CHUNK), ROW_CHUNK)
            total = self.part[self.p.over, at, :].astype(f32) + self.from_core[0, at, :].astype(f32)
            self.over_out[at, :] = total.astype(bf16)

        self.to_over().start()

    def wait(self):
        self.near_to_core().wait_recv()
        self.to_over().wait_recv()

    def rows(self, at):
        return (
            self.part[self.p.t, at, :].astype(f32)
            + self.from_core[1, at, :].astype(f32)
            + self.from_over[at, :].astype(f32)
        )

    def finish(self):
        for copy in (self.far_to_core(), self.near_to_core(), self.to_over()):
            copy.wait_send()


class Group:
    def __init__(self):
        f = lax.axis_index("fsdp")
        self.t = lax.axis_index("tp")
        self.member = f % GROUP
        self.base = f - self.member
        self.z, self.y = self.member // 2, self.member % 2

        half = self.z // 2
        self.inner = (self.z + half) % 2 == 1
        self.mate = 2 * half + 1 - self.z % 2
        self.far_inner, self.far_end = 2 - half, 3 - 3 * half

    def at(self, z, y):
        return z * 2 + y

    def ahead(self, k):
        return (self.z + k) % 4

    def behind(self, k):
        return (self.z + 4 - k) % 4

    def greet_group(self):
        barrier = pltpu.get_barrier_semaphore()
        others = [self.at(self.z, 1 - self.y)] + [self.at(self.ahead(k), self.y) for k in (1, 2, 3)]
        for member in others:
            pl.semaphore_signal(
                barrier, inc=1, device_id=(self.base + member, self.t), device_id_type=MESH
            )
        pl.semaphore_wait(barrier, 4)

    def greet(self, peers, with_diag=False):
        barrier = pltpu.get_barrier_semaphore()
        others = [self.at(self.z, 1 - self.y)] + [self.at(self.ahead(k), self.y) for k in (1, 2, 3)]
        for member in others:
            pl.semaphore_signal(
                barrier, inc=1, device_id=(self.base + member, self.t), device_id_type=MESH
            )
        near = [peers.core, peers.over] + [peers.diag] * with_diag
        for t in near:
            pl.semaphore_signal(barrier, inc=1, device_id=(peers.f, t), device_id_type=MESH)
        pl.semaphore_wait(barrier, 4 + len(near))

    def copy(self, source, target, sems, index, member, send_index=None):
        return pltpu.make_async_remote_copy(
            src_ref=source,
            dst_ref=target,
            send_sem=sems[0].at[index if send_index is None else send_index],
            recv_sem=sems[1].at[index],
            device_id=(self.base + member, self.t),
            device_id_type=MESH,
        )


class Reduce:
    def __init__(self, group, source, from_y, from_z, sems, tiles, columns=None):
        self.g, self.sems, self.columns = group, sems, columns
        self.source, self.from_y, self.from_z = source, from_y, from_z
        self.own, self.got, self.gone, self.local = tiles

    def cut(self, ref, *index):
        if self.columns is None:
            return ref.at[index]
        return ref.at[index + (slice(None), self.columns)]

    def across(self, j):
        g = self.g
        z = g.ahead(j)
        return g.copy(
            self.cut(self.source, z, 1 - g.y), self.cut(self.from_y, z), self.sems, j, g.at(g.z, 1 - g.y)
        )

    def along(self, j):
        g = self.g
        source, target = self.cut(self.gone, j - 1), self.cut(self.from_z, j - 1)
        return g.copy(source, target, self.sems, 3 + j, g.at(g.ahead(j), g.y))

    def start(self, *pieces):
        for j in pieces:
            self.across(j).start()

    def pump(self, j, before=None, then=None):
        g = self.g
        own, got = (self.own, self.got) if self.columns is None else (self.cut(self.own), self.cut(self.got))
        load_own = pltpu.make_async_copy(self.cut(self.source, g.ahead(j), g.y), own, self.local.at[0])
        load_own.start()
        self.across(j).wait_recv()
        if then is not None:
            then()
        load_got = pltpu.make_async_copy(self.cut(self.from_y, g.ahead(j)), got, self.local.at[1])
        load_got.start()
        load_own.wait()
        load_got.wait()
        if before is not None:
            before.along(j).wait_send()
        columns = slice(None) if self.columns is None else self.columns
        self.gone[j - 1, :, columns] = self.own[:, columns] + self.got[:, columns]
        self.along(j).start()

    def finish(self, reused=False, arrived=False):
        if not arrived:
            self.across(0).wait_recv()
        for j in range(4):
            self.across(j).wait_send()
        for j in (1, 2, 3):
            self.along(j).wait_recv()
            if not reused:
                self.along(j).wait_send()


def reduce_parts(payload):
    results, scratch = (), []
    for part in payload:
        rows = part.shape[2:]
        results += (jax.ShapeDtypeStruct((4,) + rows, bf16), jax.ShapeDtypeStruct((3,) + rows, bf16))
    scratch += [pltpu.SemaphoreType.DMA((7,))] * (2 * max(2, len(payload)) if payload else 0)
    if payload:
        scratch += [pltpu.VMEM(rows, bf16), pltpu.VMEM(rows, bf16), pltpu.VMEM((3,) + rows, bf16)]
        scratch += [pltpu.SemaphoreType.DMA((2,))]
    return tuple(payload), results, scratch


def reduces(group, sources, results, scratch):
    tiles = scratch[4:]
    if len(sources) == 1:
        middle, end = sources[0].shape[3] // 2, sources[0].shape[3]
        halves = (slice(0, middle), slice(middle, end))
        return [
            Reduce(group, sources[0], *results, scratch[2 * n : 2 * n + 2], tiles, columns)
            for n, columns in enumerate(halves)
        ]
    return [
        Reduce(group, source, results[2 * n], results[2 * n + 1], scratch[2 * n : 2 * n + 2], tiles)
        for n, source in enumerate(sources)
    ]


def in_turn(items):
    order = [(item, j) for item in items for j in (1, 2, 3, 0)]

    def step(n):
        def following():
            item, j = order[n + 1]
            item.start(j)

        item, j = order[n]
        if j:
            item.pump(j, then=following)
        else:
            item.across(0).wait_recv()
            following()

    return [lambda: items[0].start(1)] + [functools.partial(step, n) for n in range(len(order) - 1)]


class BlockGather:
    def __init__(self, peers, source, target, sems, first, local, columns=None):
        self.p, self.sems, self.first, self.local = peers, sems, first, local
        self.source = source if columns is None else source.at[:, columns]
        self.slot = lambda t: target.at[t] if columns is None else target.at[t, :, columns]

    def piece(self, slot, index, to, own=False):
        target = self.slot(slot)
        return self.p.copy(self.source if own else target, target, self.sems, self.first + index, to)

    def keep(self):
        return pltpu.make_async_copy(self.source, self.slot(self.p.t), self.local)

    def start(self):
        p = self.p
        self.piece(p.t, 1, p.over, True).start()
        self.piece(p.t, 0, p.core, True).start()
        self.keep().start()

    def relay(self):
        p = self.p
        self.piece(p.over, 1, p.over).wait_recv()
        self.piece(p.over, 2, p.core).start()

    def finish(self):
        p = self.p
        self.piece(p.core, 0, p.core).wait_recv()
        self.piece(p.diag, 2, p.core).wait_recv()
        self.piece(p.t, 1, p.over, True).wait_send()
        self.piece(p.t, 0, p.core, True).wait_send()
        self.piece(p.over, 2, p.core).wait_send()
        self.keep().wait()


def add_up(own, others, target, columns):
    rows = own.shape[0]
    for first in range(0, rows, 40):
        at = (slice(first, min(first + 40, rows)), columns)
        total = own[at].astype(f32)
        for other in others:
            total = total + other[at].astype(f32)
        target[at] = total.astype(target.dtype)


def last_sum_kernel(source, earlier, from_y, from_z, got, got_earlier, *scratch):
    p, g = Peers(), Group()
    scratch, (bsend, brecv, blocal, terms, mine) = scratch[:-5], scratch[-5:]
    before = BlockGather(p, earlier, got_earlier, (bsend, brecv), 0, blocal.at[0])
    items = reduces(g, [source], [from_y, from_z], scratch)
    after = [
        BlockGather(p, mine, got, (bsend, brecv), 3 + 3 * n, blocal.at[1 + n], item.columns)
        for n, item in enumerate(items)
    ]
    steps = in_turn(items)
    g.greet(p)
    steps[0]()
    before.start()

    def total(n):
        item = items[n]
        item.finish(arrived=n == 0)
        loads = [
            pltpu.make_async_copy(item.cut(source, g.z, g.y), item.cut(terms, 0), blocal.at[3]),
            pltpu.make_async_copy(item.cut(from_y, g.z), item.cut(terms, 1), blocal.at[4]),
        ]
        for k in range(3):
            loads.append(pltpu.make_async_copy(item.cut(from_z, k), item.cut(terms, 2 + k), blocal.at[5 + k]))
        for load in loads:
            load.start()
        for load in loads:
            load.wait()
        add_up(terms.at[0], [terms.at[k] for k in range(1, 5)], mine, item.columns)
        after[n].start()

    for n, step in enumerate(steps[1:]):
        if n == 3:
            before.relay()
        step()
    total(0)
    after[0].relay()
    total(1)
    before.finish()
    after[0].finish()
    after[1].relay()
    after[1].finish()


def last_sum(part, earlier, n_tp, collective_id):
    operands, results, scratch = reduce_parts([part])
    whole = jax.ShapeDtypeStruct((n_tp,) + earlier.shape, bf16)
    _, _, got, got_earlier = pl.pallas_call(
        last_sum_kernel,
        out_shape=results + (whole, whole),
        in_specs=[ANY, ANY],
        out_specs=(ANY,) * 4,
        scratch_shapes=scratch
        + [pltpu.SemaphoreType.DMA((9,))] * 2
        + [pltpu.SemaphoreType.DMA((8,)), pltpu.VMEM((5,) + earlier.shape, bf16), pltpu.VMEM(earlier.shape, bf16)],
        compiler_params=params(collective_id),
    )(part, earlier)
    return got, got_earlier


def assemble_kernel(*refs):
    inputs, refs = refs[: 7 * LAYERS], refs[7 * LAYERS :]
    qkv_ref, out_ref, fc_ref, proj_ref = refs[:4]
    vector_refs, (tiles, sems) = refs[4:13], refs[13:]
    t, f = lax.axis_index("tp"), lax.axis_index("fsdp")
    z, y = f // 2, f % 2
    loads = []
    for layer in range(LAYERS):
        for w in range(2):
            part, near, far = inputs[7 * layer + 1 + 3 * w : 7 * layer + 4 + 3 * w]
            n = 2 * layer + w
            loads.append(
                [
                    pltpu.make_async_copy(part.at[z, y], tiles.at[n, 0], sems.at[n, 0]),
                    pltpu.make_async_copy(near.at[z], tiles.at[n, 1], sems.at[n, 1]),
                    pltpu.make_async_copy(far, tiles.at[n, 2:5], sems.at[n, 2]),
                ]
            )
    for load in sum(loads, []):
        load.start()
    n_tp = inputs[0].shape[0]
    step = HEADS // n_tp * HEAD
    width = D - step * (n_tp - 1)
    counts = [step] * (n_tp - 1) + [width]
    for layer in range(LAYERS):
        got = inputs[7 * layer]
        for i in range(3):
            for k, count in enumerate(counts):
                value = got[k, :, i * WIDE : i * WIDE + count].astype(f32)
                qkv_ref[layer, :, i * D + k * step : i * D + k * step + count] = value
        for k, count in enumerate(counts):
            out_ref[layer, :, k * step : k * step + count] = got[k, :, 3 * WIDE : 3 * WIDE + count].astype(f32)
        extra = got[:, :, 3 * WIDE + step : 4 * WIDE].astype(f32)
        total = jnp.sum(extra, axis=0).T
        own = got[t, :, 3 * WIDE + step : 4 * WIDE].astype(f32).T
        skip = width - step
        for v in range(8):
            vector_refs[v][layer : layer + 1, :] = total[skip + v : skip + v + 1, :]
        vector_refs[8][layer : layer + 1, :] = own[skip + 8 : skip + 9, :]
        for w in range(2):
            n = 2 * layer + w
            for load in loads[n]:
                load.wait()
            total = tiles[n, 0].astype(f32)
            for k in range(1, 5):
                total = total + tiles[n, k].astype(f32)
            if w:
                fc_ref[layer] = total
            else:
                proj_ref[layer] = total.T


def assemble(layers):
    rows, width = layers[0][1].shape[2:]
    outs = [(LAYERS, rows, 3 * D), (LAYERS, rows, D), (LAYERS, rows, width), (LAYERS, width, rows)]
    outs += [(LAYERS, rows)] * 9
    return pl.pallas_call(
        assemble_kernel,
        out_shape=tuple(jax.ShapeDtypeStruct(o, f32) for o in outs),
        in_specs=([IN_VMEM] + [ANY] * 6) * LAYERS,
        out_specs=(IN_VMEM,) * len(outs),
        scratch_shapes=[
            pltpu.VMEM((2 * LAYERS, 5, rows, width), bf16),
            pltpu.SemaphoreType.DMA((2 * LAYERS, 3)),
        ],
        compiler_params=pltpu.CompilerParams(vmem_limit_bytes=60 * 2**20),
    )(*sum((list(layer) for layer in layers), []))


class Spread:
    def __init__(self, group, source, target, sems, chunks):
        self.g, self.source, self.target, self.sems = group, source, target, sems
        count = source.shape[1] // 128
        ends = [128 * (count * sum(chunks[: c + 1]) // sum(chunks)) for c in range(len(chunks))]
        self.columns = [slice(a, b) for a, b in zip([0] + ends, ends)]
        self.partner = group.at(group.z, 1 - group.y)
        self.origins = (group.mate, group.far_inner, group.far_end)

    def piece(self, member, c, index, to, own=False, send_index=None):
        target = self.target.at[member, :, self.columns[c]]
        source = self.source.at[:, self.columns[c]] if own else target
        send = None if send_index is None else 9 * c + send_index
        return self.g.copy(source, target, self.sems, 9 * c + index, to, send)

    def own(self, c):
        g = self.g
        arrives = jnp.where(g.inner, 2, 3)
        return [
            self.piece(g.member, c, arrives, g.at(g.far_inner, g.y), True, 2),
            self.piece(g.member, c, 1, g.at(g.mate, g.y), True),
        ]

    def own_across(self, c):
        return self.piece(self.g.member, c, 0, self.partner, True)

    def relayed(self, c, k):
        g = self.g
        return self.piece(g.at(self.origins[k - 1], g.y), c, 3 + k, self.partner)

    def passed(self, c, k):
        g = self.g
        return self.piece(g.at(self.origins[k - 1], g.y), c, k, g.at(g.mate, g.y), send_index=5 + k)

    def keep(self):
        return pltpu.make_async_copy(
            self.source, self.target.at[self.g.member], self.sems[0].at[9 * len(self.columns)]
        )

    def start(self, first=0, last=None):
        if first == 0:
            self.keep().start()
            for c in range(len(self.columns)):
                self.own_across(c).start()
        for c in range(len(self.columns))[first:last]:
            for copy in self.own(c):
                copy.start()

    def arrival(self, c, k):
        g = self.g
        self.piece(g.at(self.origins[k - 1], g.y), c, k, self.partner).wait_recv()

    def relay(self, c):
        self.arrival(c, 1)
        self.relayed(c, 1).start()

        @pl.when(self.g.inner)
        def _():
            for k in (2, 3):
                self.arrival(c, k)
                self.passed(c, k).start()
                self.relayed(c, k).start()

    def relay_late(self, c):
        @pl.when(jnp.logical_not(self.g.inner))
        def _():
            for k in (2, 3):
                self.arrival(c, k)
                self.relayed(c, k).start()

    def finish(self):
        g = self.g
        for c in range(len(self.columns)):
            self.piece(self.partner, c, 0, self.partner).wait_recv()
            for k in (1, 2, 3):
                self.piece(g.at(self.origins[k - 1], 1 - g.y), c, 3 + k, self.partner).wait_recv()
                self.relayed(c, k).wait_send()
            for copy in self.own(c) + [self.own_across(c)]:
                copy.wait_send()

            @pl.when(g.inner)
            def _(c=c):
                self.passed(c, 2).wait_send()
                self.passed(c, 3).wait_send()

        self.keep().wait()


def spread_parts(shard, chunks):
    if shard is None:
        return (), (), []
    whole = jax.ShapeDtypeStruct((GROUP,) + shard.shape, shard.dtype)
    return (shard,), (whole,), [pltpu.SemaphoreType.DMA((9 * len(chunks) + 1,))] * 2


def spread_kernel(chunks, source, target, send, recv):
    g = Group()
    g.greet_group()
    spread = Spread(g, source, target, (send, recv), chunks)
    spread.start(0, 2)
    for c in range(len(chunks)):
        spread.relay(c)
        spread.start(c + 2, c + 3)
        if c:
            spread.relay_late(c - 1)
    spread.relay_late(len(chunks) - 1)
    spread.finish()


def spread_only(shard, chunks, collective_id):
    operands, results, scratch = spread_parts(shard, chunks)
    return pl.pallas_call(
        functools.partial(spread_kernel, chunks),
        out_shape=results[0],
        in_specs=[ANY],
        out_specs=ANY,
        scratch_shapes=scratch,
        compiler_params=params(collective_id),
    )(shard)


def row_chunks(rows, body):
    @pl.loop(0, rows // ROW_CHUNK)
    def _(i):
        body(pl.ds(pl.multiple_of(i * ROW_CHUNK, ROW_CHUNK), ROW_CHUNK))


def tiles(extent, body):
    whole = extent // TILE

    @pl.loop(0, whole)
    def _(i):
        body(pl.ds(pl.multiple_of(i * TILE, TILE), TILE))

    if extent % TILE:
        body(pl.ds(whole * TILE, extent % TILE))


def pair_rows(ref, x):
    both = ref[pl.ds(2 * x, 2)]
    return both.reshape(2 * both.shape[1], both.shape[2])


def put_pair(ref, x, at, value):
    ref[pl.ds(2 * x, 2), :, at] = value.reshape(2, value.shape[0] // 2, value.shape[1]).astype(ref.dtype)


def norm_stats(x):
    centred = x - jnp.mean(x, -1, keepdims=True)
    scale = lax.rsqrt(jnp.mean(centred * centred, -1, keepdims=True) + norm_eps)
    return centred * scale, scale


FIRST_CHUNKS = (3, 3, 3, 3, 2, 2)
FF_CHUNKS = (5, 5, 4, 2)
ATTN_CHUNKS = (5, 6, 6, 5, 3)


def lanes_up(width):
    return -(-width // 128) * 128


def lanes_down(width):
    return width // 128 * 128


class Projections:
    def __init__(self, w_a, wqkv, step, width, sems):
        self.step, self.width, self.wqkv = step, width, wqkv
        tail = 4 * step
        self.loads = [
            pltpu.make_async_copy(w_a.at[:, i * step : (i + 1) * step], wqkv.at[:, i * WIDE : i * WIDE + step], sems[i])
            for i in range(3)
        ]
        for i, at in ((0, 0), (1, 2)):
            source = w_a.at[:, tail + 128 * i : tail + 128 * (i + 1)]
            self.loads.append(pltpu.make_async_copy(source, wqkv.at[:, at * WIDE + step : (at + 1) * WIDE], sems[3 + i]))

    def start(self):
        for load in self.loads:
            load.start()

    def wait(self):
        for load in self.loads:
            load.wait()
        step, width, wqkv = self.step, self.width, self.wqkv
        wqkv[:, WIDE + step : WIDE + width] = wqkv[:, width:WIDE]
        for i in range(3):
            wqkv[:, i * WIDE + width : (i + 1) * WIDE] = jnp.zeros((D, WIDE - width), bf16)


class FeedForward:
    def __init__(self, w_b, wfc, wproj, width, sems):
        main, end = lanes_down(width), 2 * (width - lanes_down(width))
        self.main, self.width, self.wfc, self.wproj = main, width, wfc, wproj
        self.fc = [
            pltpu.make_async_copy(w_b.at[:, :main], wfc.at[:, :main], sems[0]),
            pltpu.make_async_copy(w_b.at[:, 2 * main :], wfc.at[:, main : main + end], sems[1]),
        ]
        self.proj = pltpu.make_async_copy(w_b.at[:, main : 2 * main], wproj.at[:, :main], sems[2])

    def start(self):
        for copy in self.fc + [self.proj]:
            copy.start()

    def wait(self):
        for copy in self.fc + [self.proj]:
            copy.wait()
        self.wproj[:, self.main : self.width] = self.wfc[:, self.width : 2 * self.width - self.main]


def ff_fwd_kernel(n, *refs):
    x_ref, vec_ref, fcb_ref, wb_hbm = refs[:4]
    shard, refs = refs[4 : 4 + n], refs[4 + n :]
    out_ref, all_hbm, pre_hbm, hid_hbm = refs[:4]
    whole, refs = refs[4 : 4 + n], refs[4 + n :]
    wfc, wproj, buf, pre, hid, part, from_core, over_out, from_over, send, recv, local = refs[:12]
    p, g = Peers(), Group()
    spread = Spread(g, shard[0], whole[0], refs[12:], FF_CHUNKS) if n else None
    rows = x_ref.shape[0]
    sems = (send, recv)
    gather = Gather(p, buf, sems)
    scatter = Scatter(p, part, from_core, over_out, from_over, sems)
    width = fcb_ref.shape[1]
    weights = FeedForward(wb_hbm, wfc, wproj, width, [local.at[0], local.at[1], local.at[5]])
    weights.start()

    def norm(at):
        hat, _ = norm_stats(x_ref[at, :])
        buf[p.t, at, :] = (hat * vec_ref[5:6, :] + vec_ref[6:7, :]).astype(bf16)

    row_chunks(rows, norm)
    if n:
        g.greet(p)
    else:
        p.greet()
    gather.start()
    if n:
        spread.start(0, 1)
    gather.wait_chip()
    weights.wait()

    def up(x):
        def tile(at):
            value = mm(pair_rows(buf, x), wfc[:, at]) + fcb_ref[:, at]
            put_pair(pre, x, at, value)
            put_pair(hid, x, at, gelu_tanh(value))

        tiles(width, tile)

    def down(x):
        def tile(at):
            put_pair(part, x, at, mm(pair_rows(hid, x), wproj[at, :width], NT))

        tiles(D, tile)

    up(p.x)
    if n:
        spread.start(1, 2)
    gather.relay()
    gather.wait_diag()
    if n:
        spread.relay(0)
    keep_all = pltpu.make_async_copy(buf, all_hbm, local.at[2])
    keep_all.start()
    up(1 - p.x)
    keep_pre = pltpu.make_async_copy(pre, pre_hbm, local.at[3])
    keep_hid = pltpu.make_async_copy(hid, hid_hbm, local.at[4])
    keep_pre.start()
    keep_hid.start()
    down(1 - p.x)
    scatter.far_to_core().start()
    scatter.send_over()
    if n:
        spread.start(2, 3)
        spread.relay_late(0)
    down(p.x)
    scatter.near_to_core().start()
    if n:
        spread.relay(1)
        spread.start(3)
    scatter.wait()

    def final(at):
        out_ref[at, :] = x_ref[at, :] + scatter.rows(at) + vec_ref[7:8, :]

    row_chunks(rows, final)
    if n:
        spread.relay(2)
        spread.relay_late(1)
        spread.relay(3)
        spread.relay_late(2)
        spread.relay_late(3)
    gather.finish()
    scatter.finish()
    for copy in (keep_all, keep_pre, keep_hid):
        copy.wait()
    if n:
        spread.finish()


def scatter_scratch(n_tp, rows):
    return [
        pltpu.VMEM((n_tp, rows, D), bf16),
        pltpu.VMEM((2, rows, D), bf16),
        pltpu.VMEM((rows, D), bf16),
        pltpu.VMEM((rows, D), bf16),
        pltpu.SemaphoreType.DMA((6,)),
        pltpu.SemaphoreType.DMA((6,)),
    ]


def params(collective_id):
    return pltpu.CompilerParams(collective_id=collective_id, has_side_effects=True, vmem_limit_bytes=60 * 2**20)


def ff_fwd(x, vecs, fc_bias, w_b, n_tp, shard, collective_id):
    rows, width = x.shape[0], fc_bias.shape[1]
    block = (n_tp, rows)
    operands, results, sems = spread_parts(shard, FF_CHUNKS)
    return pl.pallas_call(
        functools.partial(ff_fwd_kernel, len(operands)),
        out_shape=(
            jax.ShapeDtypeStruct((rows, D), f32),
            jax.ShapeDtypeStruct(block + (D,), bf16),
            jax.ShapeDtypeStruct(block + (width,), f32),
            jax.ShapeDtypeStruct(block + (width,), bf16),
        )
        + results,
        in_specs=[IN_VMEM, IN_VMEM, IN_VMEM, ANY] + [ANY] * len(operands),
        out_specs=(IN_VMEM, ANY, ANY, ANY) + (ANY,) * len(operands),
        scratch_shapes=[
            pltpu.VMEM((D, lanes_up(width)), bf16),
            pltpu.VMEM((D, lanes_up(width)), bf16),
            pltpu.VMEM(block + (D,), bf16),
            pltpu.VMEM(block + (width,), f32),
            pltpu.VMEM(block + (width,), bf16),
        ]
        + scatter_scratch(n_tp, rows)
        + [pltpu.SemaphoreType.DMA((6,))]
        + sems,
        compiler_params=params(collective_id),
        cost_estimate=pl.CostEstimate(
            flops=4 * n_tp * rows * D * width, bytes_accessed=40 * 2**20, transcendentals=n_tp * rows * width
        ),
    )(x, vecs, fc_bias, w_b, *operands)


def gelu_slope(u):
    a = 0.7978845608028654
    square = u * u
    t = jnp.tanh(a * (u + 0.044715 * u * square))
    return 0.5 * (1.0 + t) + 0.5 * u * (1.0 - t * t) * (a * (1.0 + 3 * 0.044715 * square))


def norm_back(x, dy, gain):
    hat, scale = norm_stats(x)
    d_hat = dy * gain
    inner = d_hat - jnp.mean(d_hat, -1, keepdims=True) - hat * jnp.mean(d_hat * hat, -1, keepdims=True)
    return scale * inner, dy * hat


def add_rows(ref, row, value):
    ref[row : row + 1, :] += jnp.sum(value, axis=0, keepdims=True)


def ff_bwd_kernel(n, *refs):
    g_ref, x_ref, vec_ref, all_hbm, pre_hbm, hid_hbm, wb_hbm = refs[:7]
    sources, refs = refs[7 : 7 + n], refs[7 + n :]
    out_ref, sums_ref, fcb_ref, dfc_hbm, dproj_hbm = refs[:5]
    results, refs = refs[5 : 5 + 2 * n], refs[5 + 2 * n :]
    wfc, wproj, buf, other, pre, dpre, stage, part, from_core, over_out, from_over, send, recv, local = refs[:14]
    p, g = Peers(), Group()
    sums = reduces(g, sources, results, refs[14:])
    rows = x_ref.shape[0]
    n_tp, width = buf.shape[0], fcb_ref.shape[1]
    sems = (send, recv)
    gather = Gather(p, buf, sems)
    scatter = Scatter(p, part, from_core, over_out, from_over, sems)
    weights = FeedForward(wb_hbm, wfc, wproj, width, [local.at[0], local.at[2], local.at[7]])
    load_pre = pltpu.make_async_copy(pre_hbm, pre, local.at[1])
    load_other = pltpu.make_async_copy(hid_hbm, other, local.at[3])
    weights.start()
    for copy in (load_pre, load_other):
        copy.start()
    sums_ref[...] = jnp.zeros_like(sums_ref)
    fcb_ref[...] = jnp.zeros_like(fcb_ref)

    def lower(at):
        low = g_ref[at, :].astype(bf16)
        buf[p.t, at, :] = low
        add_rows(sums_ref, 7, low.astype(f32))

    row_chunks(rows, lower)
    if n:
        g.greet(p)
    else:
        p.greet()
    gather.start()
    steps = in_turn(sums) if n else []

    def advance():
        if steps:
            steps.pop(0)()

    advance()
    gather.wait_chip()
    weights.wait()
    load_pre.wait()

    def through(x):
        def tile(at):
            d_hidden = mm(pair_rows(buf, x), wproj[:, at])
            u = pre[pl.ds(2 * x, 2), :, at].reshape(2 * rows, -1)
            low = (gelu_slope(u) * d_hidden).astype(bf16)
            put_pair(dpre, x, at, low)
            fcb_ref[:, at] += jnp.sum(low.astype(f32), axis=0, keepdims=True)

        tiles(width, tile)

    def down(x):
        def tile(at):
            put_pair(part, x, at, mm(pair_rows(dpre, x), wfc[at, :width], NT))

        tiles(D, tile)

    through(p.x)
    gather.relay()
    advance()
    gather.wait_diag()
    through(1 - p.x)
    advance()
    down(1 - p.x)
    scatter.far_to_core().start()
    scatter.send_over()
    advance()
    down(p.x)
    scatter.near_to_core().start()
    advance()

    def outer(left, right, target, sem):
        whole = D // TILE
        rest = D - whole * TILE
        flat = right[...].reshape(n_tp * rows, width)

        def tile(i, size):
            at = pl.ds(pl.multiple_of(i * TILE, TILE), size)
            value = mm(left[:, :, at].reshape(n_tp * rows, size), flat, TN)
            stage[at, :] = value.astype(bf16)

        @pl.loop(0, whole)
        def _(i):
            tile(i, TILE)

        if rest:
            tile(whole, rest)
        return pltpu.make_async_copy(stage, target, sem)

    load_other.wait()
    store = outer(buf, other, dproj_hbm, local.at[4])
    store.start()
    gather.finish()
    load_all = pltpu.make_async_copy(all_hbm, buf, local.at[5])
    load_all.start()
    advance()
    scatter.wait()

    def final(at):
        dy = scatter.rows(at)
        dx, d_gain = norm_back(x_ref[at, :], dy, vec_ref[5:6, :])
        add_rows(sums_ref, 5, d_gain)
        add_rows(sums_ref, 6, dy)
        out_ref[at, :] = g_ref[at, :] + dx

    row_chunks(rows, final)
    load_all.wait()
    store.wait()
    store = outer(buf, dpre, dfc_hbm, local.at[6])
    store.start()
    while steps:
        advance()
    scatter.finish()
    store.wait()
    for i, item in enumerate(sums):
        item.finish(arrived=i == 0)


def ff_bwd(grad, x, vecs, all_rows, pre, hidden, w_b, n_tp, payload, collective_id):
    rows, width = x.shape[0], pre.shape[2]
    block = (n_tp, rows)
    operands, results, more = reduce_parts(payload)
    return pl.pallas_call(
        functools.partial(ff_bwd_kernel, len(payload)),
        out_shape=(
            jax.ShapeDtypeStruct((rows, D), f32),
            jax.ShapeDtypeStruct((8, D), f32),
            jax.ShapeDtypeStruct((1, width), f32),
            jax.ShapeDtypeStruct((D, width), bf16),
            jax.ShapeDtypeStruct((D, width), bf16),
        )
        + results,
        in_specs=[IN_VMEM] * 3 + [ANY] * (4 + len(payload)),
        out_specs=(IN_VMEM, IN_VMEM, IN_VMEM) + (ANY,) * (2 + 2 * len(payload)),
        scratch_shapes=[
            pltpu.VMEM((D, lanes_up(width)), bf16),
            pltpu.VMEM((D, lanes_up(width)), bf16),
            pltpu.VMEM(block + (D,), bf16),
            pltpu.VMEM(block + (width,), bf16),
            pltpu.VMEM(block + (width,), f32),
            pltpu.VMEM(block + (width,), bf16),
            pltpu.VMEM((D, width), bf16),
        ]
        + scatter_scratch(n_tp, rows)
        + [pltpu.SemaphoreType.DMA((8,))]
        + more,
        compiler_params=params(collective_id),
        cost_estimate=pl.CostEstimate(
            flops=8 * n_tp * rows * D * width, bytes_accessed=50 * 2**20, transcendentals=n_tp * rows * width
        ),
    )(grad, x, vecs, all_rows, pre, hidden, w_b, *operands)


HALVES = [(micro, half) for micro in range(MICRO) for half in range(2)]


def half_lanes(half):
    return slice(half * WIDE // 2, (half + 1) * WIDE // 2)


class Share:
    def __init__(self, group, kv, sems):
        self.g, self.kv, self.sems = group, kv, sems
        self.partner = group.at(group.z, 1 - group.y)

    def piece(self, member, part, index, to):
        micro, half = part
        ref = self.kv.at[member, micro, :, :, half_lanes(half)]
        return self.g.copy(ref, ref, self.sems, (2 * micro + half) * 7 + index, to)

    def own(self, part):
        g = self.g
        return [self.piece(g.member, part, 0, self.partner)] + [
            self.piece(g.member, part, k, g.at(g.ahead(k), g.y)) for k in (1, 2, 3)
        ]

    def relayed(self, part):
        g = self.g
        return [self.piece(g.at(g.behind(k), g.y), part, 3 + k, self.partner) for k in (1, 2, 3)]

    def start(self, *part):
        for copy in self.own(part):
            copy.start()

    def relay(self, *part):
        g = self.g
        for k, copy in zip((1, 2, 3), self.relayed(part)):
            self.piece(g.at(g.behind(k), g.y), part, k, self.partner).wait_recv()
            copy.start()

    def wait(self, *part):
        g = self.g
        self.piece(self.partner, part, 0, self.partner).wait_recv()
        for k in (1, 2, 3):
            self.piece(g.at(g.behind(k), 1 - g.y), part, 3 + k, self.partner).wait_recv()

    def finish(self):
        for part in HALVES:
            for copy in self.own(part) + self.relayed(part):
                copy.wait_send()


class GroupSum:
    def __init__(self, group, parts, from_y, to_z, from_z, sems):
        self.g, self.parts, self.sems = group, parts, sems
        self.from_y, self.to_z, self.from_z = from_y, to_z, from_z

    def across(self, micro, half):
        g, lanes = self.g, half_lanes(half)
        return g.copy(
            self.parts.at[micro, :, 1 - g.y, :, :, lanes],
            self.from_y.at[micro, :, :, :, lanes],
            self.sems,
            (2 * micro + half) * 4,
            g.at(g.z, 1 - g.y),
        )

    def along(self, micro, half, k):
        g, lanes = self.g, half_lanes(half)
        to = g.ahead(k)
        return g.copy(
            self.to_z.at[micro, to, :, :, lanes],
            self.from_z.at[micro, k - 1, :, :, lanes],
            self.sems,
            (2 * micro + half) * 4 + k,
            g.at(to, g.y),
        )

    def start(self, micro, half):
        self.across(micro, half).start()

    def turn(self, micro, half):
        lanes = half_lanes(half)
        self.across(micro, half).wait_recv()

        @pl.loop(0, 4)
        def _(z):
            for kv in range(2):
                total = self.parts[micro, z, self.g.y, kv, :, lanes] + self.from_y[micro, z, kv, :, lanes]
                self.to_z[micro, z, kv, :, lanes] = total

        for k in (1, 2, 3):
            self.along(micro, half, k).start()

    def wait(self, micro):
        for half in range(2):
            for k in (1, 2, 3):
                self.along(micro, half, k).wait_recv()

    def total(self, micro, kv):
        g = self.g
        value = self.parts[micro, g.z, g.y, kv].astype(f32) + self.from_y[micro, g.z, kv].astype(f32)
        for k in range(3):
            value = value + self.from_z[micro, k, kv].astype(f32)
        return value.astype(bf16)

    def finish(self, micro):
        for half in range(2):
            self.across(micro, half).wait_send()
            for k in (1, 2, 3):
                self.along(micro, half, k).wait_send()


WIDE = 512
HEAD_PAIRS = WIDE // (2 * HEAD)
PROMPT_CHUNKS = PROMPT // CHUNK
CONT_CHUNKS = CONT_LEN // CHUNK


def chunk_at(c, base=0):
    return pl.ds(pl.multiple_of(base + c * CHUNK, CHUNK), CHUNK)


def key_limit(member):
    row = lax.broadcasted_iota(jnp.int32, (1, TOK_DEV), 1)
    return jnp.where(row < PROMPT_DEV, member * PROMPT_DEV + row, PROMPT - PROMPT_DEV + row)


def half_of(value, half):
    lane = lax.broadcasted_iota(jnp.int32, value.shape, 1)
    return jnp.where((lane >= HEAD * half) & (lane < HEAD * (half + 1)), value, jnp.zeros_like(value))


def fold(value, op):
    return op(value.reshape(value.shape[0] // 8, 8, value.shape[1]), axis=0)


def over_keys(body, prompt, own, carry):
    carry = lax.fori_loop(0, PROMPT_CHUNKS, lambda c, carry: body(c, lambda i: prompt(c, i), carry), carry)
    return lax.fori_loop(
        0, CONT_CHUNKS, lambda c, carry: body(PROMPT_CHUNKS + c, lambda i: own(c, i), carry), carry
    )


def head_pairs(head, finish):
    @pl.loop(0, HEAD_PAIRS)
    def _(pair):
        lanes = pl.ds(pl.multiple_of(pair * 2 * HEAD, 2 * HEAD), 2 * HEAD)
        head(pair, lanes, 0)

        @pl.when(pair < HEAD_PAIRS - 1)
        def _():
            head(pair, lanes, 1)

        finish(pair, lanes)


def run_hooks(hooks, micro, pair, half):
    for at in range(HEAD_PAIRS):
        if half == 0 and (micro, at) in hooks:

            @pl.when(pair == at)
            def _(at=at):
                for hook in hooks[micro, at]:
                    hook()


def to_slots(target, micro, first, value, lanes):
    per = target.shape[1] // MICRO
    row = first
    while row < first + value.shape[0]:
        slot, within = row // per, row % per
        count = min(per - within, first + value.shape[0] - row)
        target[slot, micro * per + within : micro * per + within + count, lanes] = value[
            row - first : row - first + count
        ]
        row += count


def pair_to_blocks(target, x, value):
    per = value.shape[0] // (2 * MICRO)
    for core in range(2):
        for micro in range(MICRO):
            at = pl.ds(pl.multiple_of((2 * x + core) * per, per), per)
            first = (core * MICRO + micro) * per
            target[micro, at, :] = value[first : first + per]


def attn_fwd_kernel(n, *refs):
    x_ref, vec_ref, bias_ref, wqkv_hbm = refs[:4]
    shard, refs = refs[4 : 4 + n], refs[4 + n :]
    out_ref, lse_ref, all_hbm, own_hbm, kv_hbm, mix_hbm, wout_hbm = refs[:7]
    whole, refs = refs[7 : 7 + n], refs[7 + n :]
    wqkv, wout, wparts, buf, own, kv, mix, s_ref, p_ref, o_ref = refs[:10]
    part, from_core, over_out, from_over, send, recv, gsend, grecv, wsend, wrecv, local = refs[10:21]
    msend, mrecv = refs[21:23]
    p, g = Peers(), Group()
    spread = Spread(g, shard[0], whole[0], refs[23:], ATTN_CHUNKS) if n else None
    mixes = BlockGather(p, mix, mix_hbm, (msend, mrecv), 0, local.at[5])
    rows = x_ref.shape[0]
    n_tp = buf.shape[0]
    step = HEADS // n_tp * HEAD
    width = wparts.shape[1]
    sems = (send, recv)
    gather = Gather(p, buf, sems)
    scatter = Scatter(p, part, from_core, over_out, from_over, sems)
    share = Share(g, kv, (gsend, grecv))
    projections = Projections(wqkv_hbm, wqkv, step, width, [local.at[k] for k in (0, 7, 8, 9, 10)])
    projections.start()

    spans = ((3 * step, 4 * step, 0, step), (4 * step + 128, 4 * step + 256, step, WIDE))

    def rows_for(t, k):
        return wqkv_hbm.at[pl.ds(pl.multiple_of(t * step, 128), width), spans[k][0] : spans[k][1]]

    def part_of(t, k):
        return wparts.at[t, :, spans[k][2] : spans[k][3]]

    keep_parts = [
        pltpu.make_async_copy(rows_for(p.t, k), part_of(p.t, k), local.at[1 + 10 * k]) for k in range(2)
    ]
    for copy in keep_parts:
        copy.start()
    near = [(2 * i + k, t, k) for i, t in enumerate((p.core, p.over, p.diag)) for k in range(2)]
    give_parts = [p.copy(rows_for(t, k), part_of(p.t, k), (wsend, wrecv), i, t) for i, t, k in near]

    def norm(at):
        hat, _ = norm_stats(x_ref[at, :])
        buf[p.t, at, :] = (hat * vec_ref[0:1, :] + vec_ref[1:2, :]).astype(bf16)

    row_chunks(rows, norm)
    g.greet(p, True)
    gather.start()
    for copy in give_parts:
        copy.start()
    if n:
        spread.start(0, 1)
    gather.wait_chip()
    projections.wait()

    def project(x):
        for i in range(3):
            value = mm(pair_rows(buf, x), wqkv[:, i * WIDE : (i + 1) * WIDE]) + bias_ref[i : i + 1, :]
            low = value.astype(bf16)
            if i == 0:
                low = low * HEAD ** (-0.5)
            pair_to_blocks(own.at[i], x, low)

    project(p.x)
    gather.relay()
    gather.wait_diag()
    project(1 - p.x)
    for micro in range(MICRO):
        for i in range(2):
            kv[g.member, micro, i] = own[1 + i, micro, :PROMPT_DEV, :]
    share.start(0, 0)
    if n:
        spread.start(1, 2)
    hooks = {
        (0, 1): [lambda: share.relay(0, 1), lambda: share.start(1, 0)],
        (0, 2): [lambda: share.wait(0, 1)],
        (0, 3): [lambda: share.relay(1, 0), lambda: share.start(1, 1)],
        (1, 0): [lambda: share.wait(1, 0)],
        (1, 1): [lambda: share.relay(1, 1)],
        (1, 2): [lambda: share.wait(1, 1)],
    }
    if n:
        hooks[0, 0] = [lambda: spread.start(2, 3)]
        hooks[0, 2] += [lambda: spread.relay(1), lambda: spread.relay_late(1)]
        hooks[0, 3] += [lambda: spread.start(3, 4)]
        hooks[1, 1] += [lambda: spread.relay(2), lambda: spread.relay_late(2), lambda: spread.start(4)]
    keep_all = pltpu.make_async_copy(buf, all_hbm, local.at[2])
    keep_own = pltpu.make_async_copy(own, own_hbm, local.at[3])
    keep_all.start()
    keep_own.start()
    limit = key_limit(g.member)
    sub = lax.broadcasted_iota(jnp.int32, (CHUNK, TOK_DEV), 0)

    share.relay(0, 0)
    share.start(0, 1)
    if n:
        spread.relay(0)
        spread.relay_late(0)
    share.wait(0, 0)

    for micro in range(MICRO):

        def head(pair, lanes, half, micro=micro):
            run_hooks(hooks, micro, pair, half)
            qh = half_of(own[0, micro, :, lanes], half)

            def first(c, load, top):
                s = jnp.where(sub + c * CHUNK <= limit, mm(load(0), qh, NT), -1e30)
                s_ref[chunk_at(c), :] = s
                return jnp.maximum(top, fold(s, jnp.max))

            top = over_keys(
                first,
                lambda c, i: kv[c, micro, i, :, lanes],
                lambda c, i: own[1 + i, micro, chunk_at(c, PROMPT_DEV), lanes],
                jnp.full((8, TOK_DEV), -1e30, f32),
            )
            top = jnp.max(top, axis=0, keepdims=True)

            def second(c, total):
                e = jnp.exp(s_ref[chunk_at(c), :] - top)
                p_ref[chunk_at(c), :] = e.astype(bf16)
                return total + fold(e, jnp.sum)

            total = lax.fori_loop(0, KEYS // CHUNK, second, jnp.zeros((8, TOK_DEV), f32))
            total = jnp.sum(total, axis=0, keepdims=True)
            values = kv[:, micro, 1, :, lanes].reshape(PROMPT, 2 * HEAD)
            out = mm(values, p_ref[:PROMPT, :], TN) + mm(own[2, micro, PROMPT_DEV:, lanes], p_ref[PROMPT:, :], TN)
            at = slice(HEAD * half, HEAD * (half + 1))
            o_ref[at, :] = out[at, :] / total
            lse_ref[micro, pair, half : half + 1, :] = top + jnp.log(total)

        def finish(pair, lanes, micro=micro):
            @pl.when(pair == HEAD_PAIRS - 1)
            def _():
                o_ref[HEAD:, :] = jnp.zeros((HEAD, TOK_DEV), f32)

            to_slots(mix, micro, 0, o_ref[...].T.astype(bf16), lanes)

        head_pairs(head, finish)

    keep_kv = pltpu.make_async_copy(kv, kv_hbm, local.at[4])
    keep_kv.start()
    for copy in keep_parts:
        copy.wait()
    for i, t, k in near:
        p.copy(rows_for(t, k), part_of(t, k), (wsend, wrecv), i, t).wait_recv()
    for t in range(n_tp):
        wout[:width, t * step : (t + 1) * step] = wparts[t, :, :step]
    wout[:width, n_tp * step :] = wparts[n_tp - 1, :, width : 2 * width - step]
    wout[width:, :] = jnp.zeros((WIDE - width, D), bf16)

    @pl.when(p.t < n_tp - 1)
    def _():
        wout[step:width, :] = jnp.zeros((width - step, D), bf16)

    keep_out = pltpu.make_async_copy(wout, wout_hbm, local.at[6])
    keep_out.start()

    def down(x):
        def tile(at):
            put_pair(part, x, at, mm(pair_rows(mix, x), wout[:, at]))

        tiles(D, tile)

    down(1 - p.x)
    scatter.far_to_core().start()
    scatter.send_over()
    down(p.x)
    scatter.near_to_core().start()
    if n:
        spread.relay(3)
        spread.relay_late(3)
    scatter.wait()
    mixes.start()

    def final(at):
        out_ref[at, :] = x_ref[at, :] + (scatter.rows(at) + vec_ref[4:5, :])

    row_chunks(rows, final)
    mixes.relay()
    if n:
        spread.relay(4)
        spread.relay_late(4)
    gather.finish()
    scatter.finish()
    share.finish()
    for copy in give_parts:
        copy.wait_send()
    for copy in (keep_all, keep_own, keep_kv, keep_out):
        copy.wait()
    mixes.finish()
    if n:
        spread.finish()


def attn_shapes(n_tp, rows):
    return (
        ((n_tp, rows, D), bf16),
        ((3, MICRO, TOK_DEV, WIDE), bf16),
        ((GROUP, MICRO, 2, PROMPT_DEV, WIDE), bf16),
        ((n_tp, rows, WIDE), bf16),
    )


def attn_fwd(x, vecs, biases, w_a, n_tp, shard, collective_id):
    rows = x.shape[0]
    width = D - HEADS // n_tp * HEAD * (n_tp - 1)
    saved = attn_shapes(n_tp, rows)
    operands, results, sems = spread_parts(shard, ATTN_CHUNKS)
    return pl.pallas_call(
        functools.partial(attn_fwd_kernel, len(operands)),
        out_shape=(
            jax.ShapeDtypeStruct((rows, D), f32),
            jax.ShapeDtypeStruct((MICRO, HEAD_PAIRS, 8, TOK_DEV), f32),
        )
        + tuple(jax.ShapeDtypeStruct(*s) for s in saved[:3])
        + (jax.ShapeDtypeStruct((n_tp,) + saved[3][0], bf16), jax.ShapeDtypeStruct((WIDE, D), bf16))
        + results,
        in_specs=[IN_VMEM, IN_VMEM, IN_VMEM, ANY] + [ANY] * len(operands),
        out_specs=(IN_VMEM, IN_VMEM) + (ANY,) * (5 + len(operands)),
        scratch_shapes=[pltpu.VMEM((D, 3 * WIDE), bf16), pltpu.VMEM((WIDE, D), bf16), pltpu.VMEM((n_tp, width, WIDE), bf16)]
        + [pltpu.VMEM(*s) for s in saved]
        + [
            pltpu.VMEM((KEYS, TOK_DEV), f32),
            pltpu.VMEM((KEYS, TOK_DEV), bf16),
            pltpu.VMEM((2 * HEAD, TOK_DEV), f32),
        ]
        + scatter_scratch(n_tp, rows)
        + [
            pltpu.SemaphoreType.DMA((14 * MICRO,)),
            pltpu.SemaphoreType.DMA((14 * MICRO,)),
            pltpu.SemaphoreType.DMA((6,)),
            pltpu.SemaphoreType.DMA((6,)),
            pltpu.SemaphoreType.DMA((12,)),
            pltpu.SemaphoreType.DMA((3,)),
            pltpu.SemaphoreType.DMA((3,)),
        ]
        + sems,
        compiler_params=params(collective_id),
        cost_estimate=pl.CostEstimate(flops=10**11, bytes_accessed=30 * 2**20, transcendentals=0),
    )(x, vecs, biases, w_a, *operands)


def attn_bwd_kernel(n, *refs):
    g_ref, x_ref, vec_ref, lse_ref, ff_ref, fcb_ref, all_hbm, own_hbm, kv_hbm, mix_hbm, wqkv_hbm, wout_hbm = refs[:12]
    sources, refs = refs[12 : 12 + n], refs[12 + n :]
    out_ref, dqo_hbm = refs[:2]
    results, refs = refs[2 : 2 + 2 * n], refs[2 + 2 * n :]
    (sums_ref, cols_ref, vectors), refs = refs[:3], refs[3:]
    wqkv, wout, buf, other, mixed, own, kv, gm, dkv, from_y, to_z, from_z, dkc, dqkv, stage, stage_out = refs[:16]
    p_ref, dp_ref, ds_ref, o_ref = refs[16:20]
    part, from_core, over_out, from_over, send, recv, gsend, grecv, local = refs[20:29]
    p, g = Peers(), Group()
    sums = reduces(g, sources, results, refs[29:])
    rows = x_ref.shape[0]
    n_tp = buf.shape[0]
    out_step = HEADS // n_tp * HEAD
    out_width = D - out_step * (n_tp - 1)
    sems = (send, recv)
    gather = Gather(p, buf, sems)
    scatter = Scatter(p, part, from_core, over_out, from_over, sems)
    reduce = GroupSum(g, dkv, from_y, to_z, from_z, (gsend, grecv))
    load_out = pltpu.make_async_copy(wout_hbm, wout, local.at[0])
    load_own = pltpu.make_async_copy(own_hbm, own, local.at[1])
    load_kv = pltpu.make_async_copy(kv_hbm, kv, local.at[2])
    projections = Projections(wqkv_hbm, wqkv, out_step, out_width, [local.at[k] for k in (3, 9, 10, 11, 12)])
    projections.start()
    load_mix = pltpu.make_async_copy(mix_hbm, mixed, local.at[4])
    load_all = pltpu.make_async_copy(all_hbm, other, local.at[6])
    for copy in (load_out, load_own, load_kv, load_mix, load_all):
        copy.start()
    sums_ref[...] = jnp.zeros_like(sums_ref)

    def lower(at):
        low = g_ref[at, :].astype(bf16)
        buf[p.t, at, :] = low
        add_rows(sums_ref, 4, low.astype(f32))

    row_chunks(rows, lower)
    g.greet(p)
    gather.start()
    hooks = {(1, 1): [lambda: reduce.turn(0, 0)], (1, 2): [lambda: reduce.turn(0, 1)]}
    if n:
        first_sum, second_sum = sums
        first_sum.start(1)
        hooks[0, 1] = [lambda: first_sum.pump(2)]
        hooks[0, 2] = [lambda: first_sum.pump(3)]
        hooks[1, 1] += [lambda: second_sum.start(1)]
        hooks[1, 3] = [lambda: second_sum.pump(1, first_sum)]
    gather.wait_chip()
    load_out.wait()

    def mixed_back(x):
        pair_to_blocks(gm, x, mm(pair_rows(buf, x), wout[...], NT).astype(bf16))

    mixed_back(p.x)
    if n:
        first_sum.start(2)
    gather.relay()
    gather.wait_diag()
    if n:
        first_sum.pump(1, then=lambda: first_sum.start(3))
    mixed_back(1 - p.x)
    load_own.wait()
    load_kv.wait()
    limit = key_limit(g.member)
    sub = lax.broadcasted_iota(jnp.int32, (CHUNK, TOK_DEV), 0)


    for micro in range(MICRO):

        def head(pair, lanes, half, micro=micro):
            run_hooks(hooks, micro, pair, half)
            qh = half_of(own[0, micro, :, lanes], half)
            gh = half_of(gm[micro, :, lanes], half)
            lse = lse_ref[micro, pair, half : half + 1, :]

            def first(c, load, inner):
                s = jnp.where(sub + c * CHUNK <= limit, mm(load(0), qh, NT), -1e30)
                e = jnp.exp(s - lse)
                dp = mm(load(1), gh, NT)
                p_ref[chunk_at(c), :] = e
                dp_ref[chunk_at(c), :] = dp
                return inner + fold(e * dp, jnp.sum)

            inner = over_keys(
                first,
                lambda c, i: kv[c, micro, i, :, lanes],
                lambda c, i: own[1 + i, micro, chunk_at(c, PROMPT_DEV), lanes],
                jnp.zeros((8, TOK_DEV), f32),
            )
            inner = jnp.sum(inner, axis=0, keepdims=True)

            def second(c, put):
                e = p_ref[chunk_at(c), :]
                ds = (e * (dp_ref[chunk_at(c), :] - inner)).astype(bf16)
                ds_ref[chunk_at(c), :] = ds
                put(0, mm(ds, qh))
                put(1, mm(e.astype(bf16), gh))

            @pl.loop(0, PROMPT_CHUNKS)
            def _(c):
                def put(i, value):
                    at = (micro, c // 2, c % 2, i, slice(None), lanes)
                    if half:
                        value = value + dkv[at].astype(f32)
                    dkv[at] = value.astype(bf16)

                second(c, put)

            @pl.loop(0, CONT_CHUNKS)
            def _(c):
                def put(i, value):
                    at = (i, chunk_at(c), lanes)
                    if half:
                        value = value + dkc[at].astype(f32)
                    dkc[at] = value.astype(bf16)

                second(PROMPT_CHUNKS + c, put)

            keys = kv[:, micro, 0, :, lanes].reshape(PROMPT, 2 * HEAD)
            dq = mm(keys, ds_ref[:PROMPT, :], TN) + mm(own[1, micro, PROMPT_DEV:, lanes], ds_ref[PROMPT:, :], TN)
            at = slice(HEAD * half, HEAD * (half + 1))
            o_ref[at, :] = dq[at, :] * HEAD ** (-0.5)

        def finish(pair, lanes, micro=micro):
            @pl.when(pair == HEAD_PAIRS - 1)
            def _():
                o_ref[HEAD:, :] = jnp.zeros((HEAD, TOK_DEV), f32)

            to_slots(dqkv, micro, 0, o_ref[...].T.astype(bf16), lanes)

            @pl.when(pair == HEAD_PAIRS // 2 - 1)
            def _():
                reduce.start(micro, 0)

        head_pairs(head, finish)
        reduce.start(micro, 1)
        for i in range(2):
            to_slots(dqkv, micro, PROMPT_DEV, dkc[i], slice((1 + i) * WIDE, (2 + i) * WIDE))

    load_mix.wait()
    columns = pl.ds(pl.multiple_of(p.t * out_step, 128), out_width)

    def outer(source, target, right, body):
        flat = right.reshape(n_tp * rows, right.shape[-1])

        def tile(at):
            left = source[:, :, at].reshape(n_tp * rows, -1)
            target[at, : flat.shape[1]] = mm(left, flat, TN).astype(bf16)

        body(D, tile)

    reduce.turn(1, 0)
    stage_out[:, out_width:] = jnp.zeros((D, WIDE - out_width), bf16)
    low = buf[:, :, columns].reshape(n_tp * rows, out_width)
    for t in range(n_tp):
        count = out_step if t < n_tp - 1 else out_width
        value = mm(mixed[t].reshape(n_tp * rows, WIDE), low, TN).astype(bf16)
        stage_out[t * out_step : t * out_step + count, :out_width] = value[:count, :]
    keep_out = pltpu.make_async_copy(
        stage_out.at[:, :out_step], dqo_hbm.at[:, 3 * WIDE : 3 * WIDE + out_step], local.at[5]
    )
    keep_out.start()
    reduce.turn(1, 1)
    if n:
        second_sum.start(2)
    for micro in range(MICRO):
        reduce.wait(micro)
        for i in range(2):
            to_slots(dqkv, micro, 0, reduce.total(micro, i), slice((1 + i) * WIDE, (2 + i) * WIDE))
    if n:
        second_sum.pump(2, first_sum, lambda: second_sum.start(3))
    projections.wait()

    def down(x):
        def tile(at):
            put_pair(part, x, at, mm(pair_rows(dqkv, x), wqkv[at, :], NT))

        tiles(D, tile)

    down(1 - p.x)
    scatter.far_to_core().start()
    scatter.send_over()
    down(p.x)
    scatter.near_to_core().start()
    if n:
        second_sum.pump(3, first_sum, lambda: second_sum.start(0))
        first_sum.start(0)
    load_all.wait()
    outer(other, stage, dqkv[...], tiles)
    keep_qkv = pltpu.make_async_copy(stage, dqo_hbm.at[:, : 3 * WIDE], local.at[7])
    keep_qkv.start()
    cols_ref[...] = jnp.zeros_like(cols_ref)

    @pl.loop(0, n_tp * rows // ROW_CHUNK)
    def _(i):
        per = rows // ROW_CHUNK
        at = pl.ds(pl.multiple_of((i % per) * ROW_CHUNK, ROW_CHUNK), ROW_CHUNK)
        add_rows(cols_ref, 0, dqkv[i // per, at, :].astype(f32))

    scatter.wait()

    def final(at):
        dy = scatter.rows(at)
        dx, d_gain = norm_back(x_ref[at, :], dy, vec_ref[0:1, :])
        add_rows(sums_ref, 0, d_gain)
        add_rows(sums_ref, 1, dy)
        out_ref[at, :] = g_ref[at, :] + dx

    row_chunks(rows, final)
    vectors[...] = jnp.zeros_like(vectors)
    vectors[0:2, :] = sums_ref[0:2, :]
    vectors[2:3, columns] = cols_ref[:, :out_width]
    vectors[3:4, columns] = cols_ref[:, 2 * WIDE : 2 * WIDE + out_width]
    vectors[4:5, :] = sums_ref[4:5, :]
    vectors[5:8, :] = ff_ref[5:8, :]
    vectors[8:9, :] = fcb_ref[...]
    stage_out[:, out_width : out_width + 16] = vectors[...].T.astype(bf16)
    keep_rest = pltpu.make_async_copy(
        stage_out.at[:, out_step:], dqo_hbm.at[:, 3 * WIDE + out_step :], local.at[8]
    )
    keep_rest.start()
    gather.finish()
    scatter.finish()
    for micro in range(MICRO):
        reduce.finish(micro)
    keep_out.wait()
    keep_rest.wait()
    keep_qkv.wait()
    for i, item in enumerate(sums):
        item.finish(i < n - 1)


def attn_bwd(grad, x, vecs, lse, ff_sums, fc_bias_sums, all_rows, own, kv, mixed_all, w_a, w_out, n_tp, payload, collective_id):
    rows = x.shape[0]
    operands, results, more = reduce_parts(payload)
    pieces = (MICRO, 4, 2, 2, PROMPT_DEV, WIDE)
    return pl.pallas_call(
        functools.partial(attn_bwd_kernel, len(payload)),
        out_shape=(
            jax.ShapeDtypeStruct((rows, D), f32),
            jax.ShapeDtypeStruct((D, 4 * WIDE), bf16),
        )
        + results,
        in_specs=[IN_VMEM] * 6 + [ANY] * (6 + len(payload)),
        out_specs=(IN_VMEM,) + (ANY,) * (1 + 2 * len(payload)),
        scratch_shapes=[
            pltpu.VMEM((8, D), f32),
            pltpu.VMEM((1, 3 * WIDE), f32),
            pltpu.VMEM((16, D), f32),
            pltpu.VMEM((D, 3 * WIDE), bf16),
            pltpu.VMEM((WIDE, D), bf16),
            pltpu.VMEM((n_tp, rows, D), bf16),
            pltpu.VMEM((n_tp, rows, D), bf16),
            pltpu.VMEM((n_tp, n_tp, rows, WIDE), bf16),
            pltpu.VMEM((3, MICRO, TOK_DEV, WIDE), bf16),
            pltpu.VMEM((GROUP, MICRO, 2, PROMPT_DEV, WIDE), bf16),
            pltpu.VMEM((MICRO, TOK_DEV, WIDE), bf16),
            pltpu.VMEM(pieces, bf16),
            pltpu.VMEM((MICRO, 4, 2, PROMPT_DEV, WIDE), bf16),
            pltpu.VMEM((MICRO, 4, 2, PROMPT_DEV, WIDE), bf16),
            pltpu.VMEM((MICRO, 3, 2, PROMPT_DEV, WIDE), bf16),
            pltpu.VMEM((2, CONT_LEN, WIDE), bf16),
            pltpu.VMEM((n_tp, rows, 3 * WIDE), bf16),
            pltpu.VMEM((D, 3 * WIDE), bf16),
            pltpu.VMEM((D, WIDE), bf16),
            pltpu.VMEM((KEYS, TOK_DEV), f32),
            pltpu.VMEM((KEYS, TOK_DEV), f32),
            pltpu.VMEM((KEYS, TOK_DEV), bf16),
            pltpu.VMEM((2 * HEAD, TOK_DEV), f32),
        ]
        + scatter_scratch(n_tp, rows)
        + [
            pltpu.SemaphoreType.DMA((8 * MICRO,)),
            pltpu.SemaphoreType.DMA((8 * MICRO,)),
            pltpu.SemaphoreType.DMA((13,)),
        ]
        + more,
        compiler_params=params(collective_id),
        cost_estimate=pl.CostEstimate(flops=2 * 10**11, bytes_accessed=50 * 2**20, transcendentals=0),
    )(grad, x, vecs, lse, ff_sums, fc_bias_sums, all_rows, own, kv, mixed_all, w_a, w_out, *operands)


def forward_layer(x, layer, fetch, vecs, fc_bias, cols, n_tp):
    width = D - HEADS // n_tp * HEAD * (n_tp - 1)
    query_bias, value_bias = (lax.dynamic_slice_in_dim(vecs[i], cols, width) for i in (2, 3))
    biases = widen(jnp.stack([query_bias, jnp.zeros_like(query_bias), value_bias]))
    w_a = fetch.weights[layer, "a"]
    x_mid, lse, all_rows, own, kv, mixed, w_out = fetch.during(
        (layer, "b"), lambda shard: attn_fwd(x, vecs, biases, w_a, n_tp, shard, 5 + layer)
    )
    w_b = fetch.weights[layer, "b"]
    x_next, second_all, hidden_pre, hidden = fetch.during(
        (layer + 1, "a"), lambda shard: ff_fwd(x_mid, vecs, fc_bias[None], w_b, n_tp, shard, 1 + layer)
    )
    return x_next, (x, w_out, lse, all_rows, own, kv, mixed, x_mid, second_all, hidden_pre, hidden)


class Fetch:
    def __init__(self, shards):
        self.staged = lax.axis_size("fsdp") == GROUP
        self.shards, self.weights = shards, {}
        last = None
        for key, shard in shards.items():
            if self.staged:
                if last is None:
                    last = spread_only(shard, FIRST_CHUNKS, 9)
                    self.weights[key] = last.reshape(-1, shard.shape[1])
                continue
            if last is not None:
                shard, _ = lax.optimization_barrier((shard, last))
            whole = lax.all_gather(shard, "fsdp", axis=0, tiled=True)
            self.weights[key] = whole
            last = whole[:8, :128]

    def during(self, key, kernel):
        if not self.staged or key not in self.shards:
            return kernel(None)
        *results, whole = kernel(self.shards[key])
        self.weights[key] = whole.reshape(-1, whole.shape[2])
        return results


def fsdp_sum(part):
    return lax.psum_scatter(part, "fsdp", scatter_dimension=0, tiled=True).astype(f32)


def heads_joined(parts, n_tp):
    step = HEADS // n_tp * HEAD
    return jnp.concatenate([parts[t][..., :step] for t in range(n_tp - 1)] + [parts[n_tp - 1]], axis=-1)


def widen(value, axis=-1):
    pads = [(0, 0)] * value.ndim
    pads[axis] = (0, WIDE - value.shape[axis])
    return jnp.pad(value, pads)


def by_owner(part):
    return part.reshape(4, 2, -1, part.shape[1])


def owned(part, from_y, from_z):
    z, y = lax.axis_index("fsdp") // 2, lax.axis_index("fsdp") % 2
    own = lax.dynamic_index_in_dim(lax.dynamic_index_in_dim(part, z, 0, False), y, 0, False)
    near = lax.dynamic_index_in_dim(from_y, z, 0, False)
    return own.astype(f32) + near.astype(f32) + jnp.sum(from_z.astype(f32), 0)


def backward(grad, weights, vecs, saves, n_tp):
    width = D - HEADS // n_tp * HEAD * (n_tp - 1)
    staged = lax.axis_size("fsdp") == GROUP
    done, waiting = {}, {}

    def during(keys, kernel):
        keys = [key for key in keys if key in waiting]
        payload = [waiting.pop(key) for key in keys]
        results = list(kernel(payload))
        if payload:
            arrived = results[-2 * len(payload) :]
            results = results[: -2 * len(payload)]
            for i, key in enumerate(keys):
                done[key] = (payload[i], arrived[2 * i], arrived[2 * i + 1])
        return results

    def produced(key, value):
        if staged:
            waiting[key] = by_owner(value)
        else:
            done[key] = fsdp_sum(value)

    for layer in reversed(range(LAYERS)):
        w_a, w_b = weights[layer, "a"], weights[layer, "b"]
        x, w_out, lse, all_rows, own, kv, mixed_all, x_mid, second_all, hidden_pre, hidden = saves[layer]
        grad, ff_sums, fc_bias_sums, grad_fc, grad_proj = during(
            [(layer + 1, "qo")],
            lambda payload: ff_bwd(
                grad, x_mid, vecs[layer], second_all, hidden_pre, hidden, w_b, n_tp, payload, 10 + layer
            ),
        )
        produced((layer, "proj"), grad_proj)
        produced((layer, "fc"), grad_fc)
        grad, grad_qo = during(
            [(layer, "proj"), (layer, "fc")],
            lambda payload: attn_bwd(
                grad, x, vecs[layer], lse, ff_sums, fc_bias_sums, all_rows, own, kv, mixed_all,
                w_a, w_out, n_tp, payload, 20 + layer,
            ),
        )
        produced((layer, "qo"), grad_qo)
    if staged:
        got = last_sum(waiting[0, "qo"], owned(*done[1, "qo"]).astype(bf16), n_tp, 30)
        return grad, assemble([(got[k],) + done[k, "proj"] + done[k, "fc"] for k in range(LAYERS)])
    outs = []
    for layer in range(LAYERS):
        qo = done[layer, "qo"]
        got = lax.all_gather(qo.astype(bf16), "tp")
        qkv_grad = jnp.concatenate(
            [heads_joined(got[:, :, i * WIDE : i * WIDE + width], n_tp) for i in range(3)], axis=1
        )
        out_grad = heads_joined(got[:, :, 3 * WIDE : 3 * WIDE + width], n_tp)
        vector_sum = jnp.sum(got[:, :, 3 * WIDE + width : 3 * WIDE + width + 8].astype(f32), 0).T
        rest = (vector_sum[v] for v in range(8))
        outs.append((qkv_grad, out_grad, done[layer, "fc"], done[layer, "proj"].T, *rest, qo[:, 3 * WIDE + width + 8]))
    return grad, tuple(jnp.stack(pair).astype(f32) for pair in zip(*outs))


def local(
    tokens,
    qkv_weight,
    query_bias,
    value_bias,
    out_weight,
    out_bias,
    fc_weight,
    fc_bias,
    proj_weight,
    proj_bias,
    first_gain,
    first_bias,
    second_gain,
    second_bias,
    out_grad,
):
    n_tp = lax.axis_size("tp")
    tp = lax.axis_index("tp")
    row_count = tokens.shape[1]
    step = HEADS // n_tp * HEAD
    width = D - step * (n_tp - 1)
    cols = tp * step

    vectors = jnp.stack(
        [first_gain, first_bias, query_bias, value_bias, out_bias, second_gain, second_bias, proj_bias, fc_bias[:, 0]]
    ).reshape(9 * LAYERS, -1)

    shards = {}
    for layer in range(LAYERS):
        sides = [lax.dynamic_slice_in_dim(qkv_weight[layer], cols + i * D, width, 1) for i in range(3)]
        sides.append(lax.dynamic_slice_in_dim(out_weight[layer], cols, width, 1))
        sides = [side[:, :step] for side in sides] + [side[:, step:] for side in sides]
        if layer == 0:
            sides.append(jnp.pad(vectors.T, ((0, 0), (0, 128 - 9 * LAYERS))))
        shards[layer, "a"] = jnp.concatenate(sides, axis=1)
        fc, proj = fc_weight[layer], proj_weight[layer].T
        main = lanes_down(fc.shape[1])
        shards[layer, "b"] = jnp.concatenate([fc[:, :main], proj[:, :main], fc[:, main:], proj[:, main:]], axis=1)
    fetch = Fetch(shards)
    beside = 4 * width
    vectors = fetch.weights[0, "a"][:, beside : beside + 9 * LAYERS].T.astype(f32).reshape(9, LAYERS, D)

    state = tokens.astype(f32).reshape(MICRO * row_count, D)
    saves = []
    for layer in range(LAYERS):
        state, saved = forward_layer(state, layer, fetch, vectors[:8, layer], vectors[8, layer], cols, n_tp)
        saves.append(saved)
    out_tokens = state.astype(bf16).reshape(tokens.shape)
    grad = out_grad.astype(f32).reshape(MICRO * row_count, D)
    grad, (qkv_g, out_g, fc_g, proj_g, *vec_g) = backward(
        grad, fetch.weights, [vectors[:8, layer] for layer in range(LAYERS)], saves, n_tp
    )
    return (
        out_tokens,
        grad.reshape(tokens.shape),
        qkv_g,
        vec_g[2],
        vec_g[3],
        out_g,
        vec_g[4],
        fc_g,
        vec_g[8][:, None],
        proj_g,
        vec_g[7],
        vec_g[0],
        vec_g[1],
        vec_g[5],
        vec_g[6],
    )


def solution(mesh):
    rows = P(None, ("fsdp", "tp"), None)
    weight = P(None, "fsdp", None)
    vector = P(None, "fsdp")
    fc_in = P(None, "fsdp", "tp")
    hidden = P(None, "tp", "fsdp")
    in_specs = (
        rows, weight, vector, vector, weight, vector, fc_in, hidden, hidden,
        vector, vector, vector, vector, vector, rows,
    )
    out_specs = (
        rows, rows, weight, vector, vector, weight, vector, fc_in, hidden, hidden,
        vector, vector, vector, vector, vector,
    )
    return jax.shard_map(local, mesh=mesh, in_specs=in_specs, out_specs=out_specs, check_vma=False)
```

```python
import functools

import jax
import jax.numpy as jnp
from jax import lax
from jax.experimental import pallas as pl
from jax.experimental.pallas import tpu as pltpu
from jax.sharding import PartitionSpec as P

D = 1600
HEADS = 25
HEAD = 64
GROUP = 8
PROMPT_DEV = 128
CONT_LEN = 256
TOK_DEV = 384
MICRO = 2
LAYERS = 2
PROMPT = 1024
KEYS = PROMPT + CONT_LEN
CHUNK = 128

f32 = jnp.float32
bf16 = jnp.bfloat16
norm_eps = 1e-05
NN = (((1,), (0,)), ((), ()))
NT = (((1,), (1,)), ((), ()))
TN = (((0,), (0,)), ((), ()))


def mm(left, right, dims=NN):
    return lax.dot_general(left, right, dims, preferred_element_type=f32)


def gelu_tanh(value):
    return jax.nn.gelu(value, approximate=True)


MESH = pl.DeviceIdType.MESH
ANY = pl.BlockSpec(memory_space=pl.ANY)
IN_VMEM = pl.BlockSpec(memory_space=pltpu.VMEM)
TILE = 512
ROW_CHUNK = 32


class Peers:
    def __init__(self):
        self.f = lax.axis_index("fsdp")
        self.t = lax.axis_index("tp")
        x, c = self.t // 2, self.t % 2
        self.x = x
        self.core = 2 * x + 1 - c
        self.over = 2 * (1 - x) + c
        self.diag = 2 * (1 - x) + 1 - c

    def greet(self):
        barrier = pltpu.get_barrier_semaphore()
        for t in (self.core, self.over):
            pl.semaphore_signal(barrier, inc=1, device_id=(self.f, t), device_id_type=MESH)
        pl.semaphore_wait(barrier, 2)

    def copy(self, source, target, sems, index, t):
        return pltpu.make_async_remote_copy(
            src_ref=source,
            dst_ref=target,
            send_sem=sems[0].at[index],
            recv_sem=sems[1].at[index],
            device_id=(self.f, t),
            device_id_type=MESH,
        )


class Gather:
    def __init__(self, peers, buf, sems):
        self.p, self.buf, self.sems = peers, buf, sems

    def piece(self, slot, index, t):
        return self.p.copy(self.buf.at[slot], self.buf.at[slot], self.sems, index, t)

    def start(self):
        p = self.p
        self.piece(p.t, 1, p.over).start()
        self.piece(p.t, 0, p.core).start()

    def wait_chip(self):
        self.piece(self.p.core, 0, self.p.core).wait_recv()

    def relay(self):
        p = self.p
        self.piece(p.over, 1, p.over).wait_recv()
        self.piece(p.over, 2, p.core).start()

    def wait_diag(self):
        self.piece(self.p.diag, 2, self.p.core).wait_recv()

    def finish(self):
        p = self.p
        self.piece(p.t, 1, p.over).wait_send()
        self.piece(p.t, 0, p.core).wait_send()
        self.piece(p.over, 2, p.core).wait_send()


class Scatter:
    def __init__(self, peers, part, from_core, over_out, from_over, sems):
        self.p, self.part, self.sems = peers, part, sems
        self.from_core, self.over_out, self.from_over = from_core, over_out, from_over

    def far_to_core(self):
        return self.p.copy(self.part.at[self.p.diag], self.from_core.at[0], self.sems, 3, self.p.core)

    def near_to_core(self):
        return self.p.copy(self.part.at[self.p.core], self.from_core.at[1], self.sems, 4, self.p.core)

    def to_over(self):
        return self.p.copy(self.over_out, self.from_over, self.sems, 5, self.p.over)

    def send_over(self):
        self.far_to_core().wait_recv()

        @pl.loop(0, self.over_out.shape[0] // ROW_CHUNK)
        def _(i):
            at = pl.ds(pl.multiple_of(i * ROW_CHUNK, ROW_CHUNK), ROW_CHUNK)
            total = self.part[self.p.over, at, :].astype(f32) + self.from_core[0, at, :].astype(f32)
            self.over_out[at, :] = total.astype(bf16)

        self.to_over().start()

    def wait(self):
        self.near_to_core().wait_recv()
        self.to_over().wait_recv()

    def rows(self, at):
        return (
            self.part[self.p.t, at, :].astype(f32)
            + self.from_core[1, at, :].astype(f32)
            + self.from_over[at, :].astype(f32)
        )

    def finish(self):
        for copy in (self.far_to_core(), self.near_to_core(), self.to_over()):
            copy.wait_send()


class Group:
    def __init__(self):
        f = lax.axis_index("fsdp")
        self.t = lax.axis_index("tp")
        self.member = f % GROUP
        self.base = f - self.member
        self.z, self.y = self.member // 2, self.member % 2

        half = self.z // 2
        self.inner = (self.z + half) % 2 == 1
        self.mate = 2 * half + 1 - self.z % 2
        self.far_inner, self.far_end = 2 - half, 3 - 3 * half

    def at(self, z, y):
        return z * 2 + y

    def ahead(self, k):
        return (self.z + k) % 4

    def behind(self, k):
        return (self.z + 4 - k) % 4

    def greet_group(self):
        barrier = pltpu.get_barrier_semaphore()
        others = [self.at(self.z, 1 - self.y)] + [self.at(self.ahead(k), self.y) for k in (1, 2, 3)]
        for member in others:
            pl.semaphore_signal(
                barrier, inc=1, device_id=(self.base + member, self.t), device_id_type=MESH
            )
        pl.semaphore_wait(barrier, 4)

    def greet(self, peers, with_diag=False):
        barrier = pltpu.get_barrier_semaphore()
        others = [self.at(self.z, 1 - self.y)] + [self.at(self.ahead(k), self.y) for k in (1, 2, 3)]
        for member in others:
            pl.semaphore_signal(
                barrier, inc=1, device_id=(self.base + member, self.t), device_id_type=MESH
            )
        near = [peers.core, peers.over] + [peers.diag] * with_diag
        for t in near:
            pl.semaphore_signal(barrier, inc=1, device_id=(peers.f, t), device_id_type=MESH)
        pl.semaphore_wait(barrier, 4 + len(near))

    def copy(self, source, target, sems, index, member, send_index=None):
        return pltpu.make_async_remote_copy(
            src_ref=source,
            dst_ref=target,
            send_sem=sems[0].at[index if send_index is None else send_index],
            recv_sem=sems[1].at[index],
            device_id=(self.base + member, self.t),
            device_id_type=MESH,
        )


class Reduce:
    def __init__(self, group, source, from_y, from_z, sems, tiles, columns=None):
        self.g, self.sems, self.columns = group, sems, columns
        self.source, self.from_y, self.from_z = source, from_y, from_z
        self.own, self.got, self.gone, self.local = tiles

    def cut(self, ref, *index):
        if self.columns is None:
            return ref.at[index]
        return ref.at[index + (slice(None), self.columns)]

    def across(self, j):
        g = self.g
        z = g.ahead(j)
        return g.copy(
            self.cut(self.source, z, 1 - g.y), self.cut(self.from_y, z), self.sems, j, g.at(g.z, 1 - g.y)
        )

    def along(self, j):
        g = self.g
        source, target = self.cut(self.gone, j - 1), self.cut(self.from_z, j - 1)
        return g.copy(source, target, self.sems, 3 + j, g.at(g.ahead(j), g.y))

    def start(self, *pieces):
        for j in pieces:
            self.across(j).start()

    def pump(self, j, before=None, then=None):
        g = self.g
        own, got = (self.own, self.got) if self.columns is None else (self.cut(self.own), self.cut(self.got))
        load_own = pltpu.make_async_copy(self.cut(self.source, g.ahead(j), g.y), own, self.local.at[0])
        load_own.start()
        self.across(j).wait_recv()
        if then is not None:
            then()
        load_got = pltpu.make_async_copy(self.cut(self.from_y, g.ahead(j)), got, self.local.at[1])
        load_got.start()
        load_own.wait()
        load_got.wait()
        if before is not None:
            before.along(j).wait_send()
        columns = slice(None) if self.columns is None else self.columns
        self.gone[j - 1, :, columns] = self.own[:, columns] + self.got[:, columns]
        self.along(j).start()

    def finish(self, reused=False, arrived=False):
        if not arrived:
            self.across(0).wait_recv()
        for j in range(4):
            self.across(j).wait_send()
        for j in (1, 2, 3):
            self.along(j).wait_recv()
            if not reused:
                self.along(j).wait_send()


def reduce_parts(payload):
    results, scratch = (), []
    for part in payload:
        rows = part.shape[2:]
        results += (jax.ShapeDtypeStruct((4,) + rows, bf16), jax.ShapeDtypeStruct((3,) + rows, bf16))
    scratch += [pltpu.SemaphoreType.DMA((7,))] * (2 * max(2, len(payload)) if payload else 0)
    if payload:
        scratch += [pltpu.VMEM(rows, bf16), pltpu.VMEM(rows, bf16), pltpu.VMEM((3,) + rows, bf16)]
        scratch += [pltpu.SemaphoreType.DMA((2,))]
    return tuple(payload), results, scratch


def reduces(group, sources, results, scratch):
    tiles = scratch[4:]
    if len(sources) == 1:
        middle, end = sources[0].shape[3] // 2, sources[0].shape[3]
        halves = (slice(0, middle), slice(middle, end))
        return [
            Reduce(group, sources[0], *results, scratch[2 * n : 2 * n + 2], tiles, columns)
            for n, columns in enumerate(halves)
        ]
    return [
        Reduce(group, source, results[2 * n], results[2 * n + 1], scratch[2 * n : 2 * n + 2], tiles)
        for n, source in enumerate(sources)
    ]


def in_turn(items):
    order = [(item, j) for item in items for j in (1, 2, 3, 0)]

    def step(n):
        def following():
            item, j = order[n + 1]
            item.start(j)

        item, j = order[n]
        if j:
            item.pump(j, then=following)
        else:
            item.across(0).wait_recv()
            following()

    return [lambda: items[0].start(1)] + [functools.partial(step, n) for n in range(len(order) - 1)]


class BlockGather:
    def __init__(self, peers, source, target, sems, first, local, columns=None):
        self.p, self.sems, self.first, self.local = peers, sems, first, local
        self.source = source if columns is None else source.at[:, columns]
        self.slot = lambda t: target.at[t] if columns is None else target.at[t, :, columns]

    def piece(self, slot, index, to, own=False):
        target = self.slot(slot)
        return self.p.copy(self.source if own else target, target, self.sems, self.first + index, to)

    def keep(self):
        return pltpu.make_async_copy(self.source, self.slot(self.p.t), self.local)

    def start(self):
        p = self.p
        self.piece(p.t, 1, p.over, True).start()
        self.piece(p.t, 0, p.core, True).start()
        self.keep().start()

    def relay(self):
        p = self.p
        self.piece(p.over, 1, p.over).wait_recv()
        self.piece(p.over, 2, p.core).start()

    def finish(self):
        p = self.p
        self.piece(p.core, 0, p.core).wait_recv()
        self.piece(p.diag, 2, p.core).wait_recv()
        self.piece(p.t, 1, p.over, True).wait_send()
        self.piece(p.t, 0, p.core, True).wait_send()
        self.piece(p.over, 2, p.core).wait_send()
        self.keep().wait()


def add_up(own, others, target, columns):
    rows = own.shape[0]
    for first in range(0, rows, 40):
        at = (slice(first, min(first + 40, rows)), columns)
        total = own[at].astype(f32)
        for other in others:
            total = total + other[at].astype(f32)
        target[at] = total.astype(target.dtype)


def last_sum_kernel(source, part, near, far, from_y, from_z, got, got_earlier, *scratch):
    p, g = Peers(), Group()
    scratch, (bsend, brecv, blocal, terms, mine, earlier) = scratch[:-6], scratch[-6:]
    before = BlockGather(p, earlier, got_earlier, (bsend, brecv), 0, blocal.at[0])
    items = reduces(g, [source], [from_y, from_z], scratch)
    after = [
        BlockGather(p, mine, got, (bsend, brecv), 3 + 3 * n, blocal.at[1 + n], item.columns)
        for n, item in enumerate(items)
    ]
    steps = in_turn(items)
    g.greet(p)
    steps[0]()
    loads = [
        pltpu.make_async_copy(part.at[g.z, g.y], terms.at[0], blocal.at[3]),
        pltpu.make_async_copy(near.at[g.z], terms.at[1], blocal.at[4]),
        pltpu.make_async_copy(far, terms.at[2:5], blocal.at[5]),
    ]
    for load in loads:
        load.start()
    for load in loads:
        load.wait()
    add_up(terms.at[0], [terms.at[k] for k in range(1, 5)], earlier, slice(None))
    before.start()

    def total(n):
        item = items[n]
        item.finish(arrived=n == 0)
        loads = [
            pltpu.make_async_copy(item.cut(source, g.z, g.y), item.cut(terms, 0), blocal.at[3]),
            pltpu.make_async_copy(item.cut(from_y, g.z), item.cut(terms, 1), blocal.at[4]),
        ]
        for k in range(3):
            loads.append(pltpu.make_async_copy(item.cut(from_z, k), item.cut(terms, 2 + k), blocal.at[5 + k]))
        for load in loads:
            load.start()
        for load in loads:
            load.wait()
        add_up(terms.at[0], [terms.at[k] for k in range(1, 5)], mine, item.columns)
        after[n].start()

    for n, step in enumerate(steps[1:]):
        if n == 3:
            before.relay()
        step()
    total(0)
    after[0].relay()
    total(1)
    before.finish()
    after[0].finish()
    after[1].relay()
    after[1].finish()


def last_sum(part, earlier, n_tp, collective_id):
    operands, results, scratch = reduce_parts([part])
    rows = part.shape[2:]
    whole = jax.ShapeDtypeStruct((n_tp,) + rows, bf16)
    _, _, got, got_earlier = pl.pallas_call(
        last_sum_kernel,
        out_shape=results + (whole, whole),
        in_specs=[ANY] * 4,
        out_specs=(ANY,) * 4,
        scratch_shapes=scratch
        + [pltpu.SemaphoreType.DMA((9,))] * 2
        + [pltpu.SemaphoreType.DMA((8,)), pltpu.VMEM((5,) + rows, bf16), pltpu.VMEM(rows, bf16), pltpu.VMEM(rows, bf16)],
        compiler_params=params(collective_id),
    )(part, *earlier)
    return got, got_earlier


def assemble_kernel(*refs):
    inputs, refs = refs[: 7 * LAYERS], refs[7 * LAYERS :]
    qkv_ref, out_ref, fc_ref, proj_ref = refs[:4]
    vector_refs, (tiles, sems) = refs[4:13], refs[13:]
    t, f = lax.axis_index("tp"), lax.axis_index("fsdp")
    z, y = f // 2, f % 2
    loads = []
    for layer in range(LAYERS):
        for w in range(2):
            part, near, far = inputs[7 * layer + 1 + 3 * w : 7 * layer + 4 + 3 * w]
            n = 2 * layer + w
            loads.append(
                [
                    pltpu.make_async_copy(part.at[z, y], tiles.at[n, 0], sems.at[n, 0]),
                    pltpu.make_async_copy(near.at[z], tiles.at[n, 1], sems.at[n, 1]),
                    pltpu.make_async_copy(far, tiles.at[n, 2:5], sems.at[n, 2]),
                ]
            )
    for load in sum(loads, []):
        load.start()
    n_tp = inputs[0].shape[0]
    step = HEADS // n_tp * HEAD
    width = D - step * (n_tp - 1)
    counts = [step] * (n_tp - 1) + [width]
    for layer in range(LAYERS):
        got = inputs[7 * layer]
        for i in range(3):
            for k, count in enumerate(counts):
                value = got[k, :, i * WIDE : i * WIDE + count].astype(f32)
                qkv_ref[layer, :, i * D + k * step : i * D + k * step + count] = value
        for k, count in enumerate(counts):
            out_ref[layer, :, k * step : k * step + count] = got[k, :, 3 * WIDE : 3 * WIDE + count].astype(f32)
        extra = got[:, :, 3 * WIDE + step : 4 * WIDE].astype(f32)
        total = jnp.sum(extra, axis=0).T
        own = got[t, :, 3 * WIDE + step : 4 * WIDE].astype(f32).T
        skip = width - step
        for v in range(8):
            vector_refs[v][layer : layer + 1, :] = total[skip + v : skip + v + 1, :]
        vector_refs[8][layer : layer + 1, :] = own[skip + 8 : skip + 9, :]
        for w in range(2):
            n = 2 * layer + w
            for load in loads[n]:
                load.wait()
            total = tiles[n, 0].astype(f32)
            for k in range(1, 5):
                total = total + tiles[n, k].astype(f32)
            if w:
                fc_ref[layer] = total
            else:
                proj_ref[layer] = total.T


def assemble(layers):
    rows, width = layers[0][1].shape[2:]
    outs = [(LAYERS, rows, 3 * D), (LAYERS, rows, D), (LAYERS, rows, width), (LAYERS, width, rows)]
    outs += [(LAYERS, rows)] * 9
    return pl.pallas_call(
        assemble_kernel,
        out_shape=tuple(jax.ShapeDtypeStruct(o, f32) for o in outs),
        in_specs=([IN_VMEM] + [ANY] * 6) * LAYERS,
        out_specs=(IN_VMEM,) * len(outs),
        scratch_shapes=[
            pltpu.VMEM((2 * LAYERS, 5, rows, width), bf16),
            pltpu.SemaphoreType.DMA((2 * LAYERS, 3)),
        ],
        compiler_params=pltpu.CompilerParams(vmem_limit_bytes=60 * 2**20),
    )(*sum((list(layer) for layer in layers), []))


class Spread:
    def __init__(self, group, source, target, sems, chunks):
        self.g, self.source, self.target, self.sems = group, source, target, sems
        count = source.shape[1] // 128
        ends = [128 * (count * sum(chunks[: c + 1]) // sum(chunks)) for c in range(len(chunks))]
        self.columns = [slice(a, b) for a, b in zip([0] + ends, ends)]
        self.partner = group.at(group.z, 1 - group.y)
        self.origins = (group.mate, group.far_inner, group.far_end)

    def piece(self, member, c, index, to, own=False, send_index=None):
        target = self.target.at[member, :, self.columns[c]]
        source = self.source.at[:, self.columns[c]] if own else target
        send = None if send_index is None else 9 * c + send_index
        return self.g.copy(source, target, self.sems, 9 * c + index, to, send)

    def own(self, c):
        g = self.g
        arrives = jnp.where(g.inner, 2, 3)
        return [
            self.piece(g.member, c, arrives, g.at(g.far_inner, g.y), True, 2),
            self.piece(g.member, c, 1, g.at(g.mate, g.y), True),
        ]

    def own_across(self, c):
        return self.piece(self.g.member, c, 0, self.partner, True)

    def relayed(self, c, k):
        g = self.g
        return self.piece(g.at(self.origins[k - 1], g.y), c, 3 + k, self.partner)

    def passed(self, c, k):
        g = self.g
        return self.piece(g.at(self.origins[k - 1], g.y), c, k, g.at(g.mate, g.y), send_index=5 + k)

    def keep(self):
        return pltpu.make_async_copy(
            self.source, self.target.at[self.g.member], self.sems[0].at[9 * len(self.columns)]
        )

    def start(self, first=0, last=None):
        if first == 0:
            self.keep().start()
            for c in range(len(self.columns)):
                self.own_across(c).start()
        for c in range(len(self.columns))[first:last]:
            for copy in self.own(c):
                copy.start()

    def arrival(self, c, k):
        g = self.g
        self.piece(g.at(self.origins[k - 1], g.y), c, k, self.partner).wait_recv()

    def relay(self, c):
        self.arrival(c, 1)
        self.relayed(c, 1).start()

        @pl.when(self.g.inner)
        def _():
            for k in (2, 3):
                self.arrival(c, k)
                self.passed(c, k).start()
                self.relayed(c, k).start()

    def relay_late(self, c):
        @pl.when(jnp.logical_not(self.g.inner))
        def _():
            for k in (2, 3):
                self.arrival(c, k)
                self.relayed(c, k).start()

    def finish(self):
        g = self.g
        for c in range(len(self.columns)):
            self.piece(self.partner, c, 0, self.partner).wait_recv()
            for k in (1, 2, 3):
                self.piece(g.at(self.origins[k - 1], 1 - g.y), c, 3 + k, self.partner).wait_recv()
                self.relayed(c, k).wait_send()
            for copy in self.own(c) + [self.own_across(c)]:
                copy.wait_send()

            @pl.when(g.inner)
            def _(c=c):
                self.passed(c, 2).wait_send()
                self.passed(c, 3).wait_send()

        self.keep().wait()


def spread_parts(shard, chunks):
    if shard is None:
        return (), (), []
    whole = jax.ShapeDtypeStruct((GROUP,) + shard.shape, shard.dtype)
    return (shard,), (whole,), [pltpu.SemaphoreType.DMA((9 * len(chunks) + 1,))] * 2


def spread_kernel(chunks, source, target, send, recv):
    g = Group()
    g.greet_group()
    spread = Spread(g, source, target, (send, recv), chunks)
    spread.start(0, 2)
    for c in range(len(chunks)):
        spread.relay(c)
        spread.start(c + 2, c + 3)
        if c:
            spread.relay_late(c - 1)
    spread.relay_late(len(chunks) - 1)
    spread.finish()


def spread_only(shard, chunks, collective_id):
    operands, results, scratch = spread_parts(shard, chunks)
    return pl.pallas_call(
        functools.partial(spread_kernel, chunks),
        out_shape=results[0],
        in_specs=[ANY],
        out_specs=ANY,
        scratch_shapes=scratch,
        compiler_params=params(collective_id),
    )(shard)


def row_chunks(rows, body):
    @pl.loop(0, rows // ROW_CHUNK)
    def _(i):
        body(pl.ds(pl.multiple_of(i * ROW_CHUNK, ROW_CHUNK), ROW_CHUNK))


def tiles(extent, body):
    whole = extent // TILE

    @pl.loop(0, whole)
    def _(i):
        body(pl.ds(pl.multiple_of(i * TILE, TILE), TILE))

    if extent % TILE:
        body(pl.ds(whole * TILE, extent % TILE))


def pair_rows(ref, x):
    both = ref[pl.ds(2 * x, 2)]
    return both.reshape(2 * both.shape[1], both.shape[2])


def put_pair(ref, x, at, value):
    ref[pl.ds(2 * x, 2), :, at] = value.reshape(2, value.shape[0] // 2, value.shape[1]).astype(ref.dtype)


def norm_stats(x):
    centred = x - jnp.mean(x, -1, keepdims=True)
    scale = lax.rsqrt(jnp.mean(centred * centred, -1, keepdims=True) + norm_eps)
    return centred * scale, scale


FIRST_CHUNKS = (3, 3, 3, 3, 2, 2)
FF_CHUNKS = (5, 5, 4, 2)
ATTN_CHUNKS = (5, 6, 6, 5, 3)


def lanes_up(width):
    return -(-width // 128) * 128


def lanes_down(width):
    return width // 128 * 128


class Projections:
    def __init__(self, w_a, wqkv, step, width, sems):
        self.step, self.width, self.wqkv = step, width, wqkv
        tail = 4 * step
        self.loads = [
            pltpu.make_async_copy(w_a.at[:, i * step : (i + 1) * step], wqkv.at[:, i * WIDE : i * WIDE + step], sems[i])
            for i in range(3)
        ]
        for i, at in ((0, 0), (1, 2)):
            source = w_a.at[:, tail + 128 * i : tail + 128 * (i + 1)]
            self.loads.append(pltpu.make_async_copy(source, wqkv.at[:, at * WIDE + step : (at + 1) * WIDE], sems[3 + i]))

    def start(self):
        for load in self.loads:
            load.start()

    def wait(self):
        for load in self.loads:
            load.wait()
        step, width, wqkv = self.step, self.width, self.wqkv
        wqkv[:, WIDE + step : WIDE + width] = wqkv[:, width:WIDE]
        for i in range(3):
            wqkv[:, i * WIDE + width : (i + 1) * WIDE] = jnp.zeros((D, WIDE - width), bf16)


class FeedForward:
    def __init__(self, w_b, wfc, wproj, width, sems):
        main, end = lanes_down(width), 2 * (width - lanes_down(width))
        self.main, self.width, self.wfc, self.wproj = main, width, wfc, wproj
        self.fc = [
            pltpu.make_async_copy(w_b.at[:, :main], wfc.at[:, :main], sems[0]),
            pltpu.make_async_copy(w_b.at[:, 2 * main :], wfc.at[:, main : main + end], sems[1]),
        ]
        self.proj = pltpu.make_async_copy(w_b.at[:, main : 2 * main], wproj.at[:, :main], sems[2])

    def start(self):
        for copy in self.fc + [self.proj]:
            copy.start()

    def wait(self):
        for copy in self.fc + [self.proj]:
            copy.wait()
        self.wproj[:, self.main : self.width] = self.wfc[:, self.width : 2 * self.width - self.main]


def ff_fwd_kernel(n, *refs):
    x_ref, vec_ref, fcb_ref, wb_hbm = refs[:4]
    shard, refs = refs[4 : 4 + n], refs[4 + n :]
    out_ref, all_hbm, pre_hbm, hid_hbm = refs[:4]
    whole, refs = refs[4 : 4 + n], refs[4 + n :]
    wfc, wproj, buf, pre, hid, part, from_core, over_out, from_over, send, recv, local = refs[:12]
    p, g = Peers(), Group()
    spread = Spread(g, shard[0], whole[0], refs[12:], FF_CHUNKS) if n else None
    rows = x_ref.shape[0]
    sems = (send, recv)
    gather = Gather(p, buf, sems)
    scatter = Scatter(p, part, from_core, over_out, from_over, sems)
    width = fcb_ref.shape[1]
    weights = FeedForward(wb_hbm, wfc, wproj, width, [local.at[0], local.at[1], local.at[5]])
    weights.start()

    def norm(at):
        hat, _ = norm_stats(x_ref[at, :])
        buf[p.t, at, :] = (hat * vec_ref[5:6, :] + vec_ref[6:7, :]).astype(bf16)

    row_chunks(rows, norm)
    if n:
        g.greet(p)
    else:
        p.greet()
    gather.start()
    if n:
        spread.start(0, 1)
    gather.wait_chip()
    weights.wait()

    def up(x):
        def tile(at):
            value = mm(pair_rows(buf, x), wfc[:, at]) + fcb_ref[:, at]
            put_pair(pre, x, at, value)
            put_pair(hid, x, at, gelu_tanh(value))

        tiles(width, tile)

    def down(x):
        def tile(at):
            put_pair(part, x, at, mm(pair_rows(hid, x), wproj[at, :width], NT))

        tiles(D, tile)

    up(p.x)
    if n:
        spread.start(1, 2)
    gather.relay()
    gather.wait_diag()
    if n:
        spread.relay(0)
    keep_all = pltpu.make_async_copy(buf, all_hbm, local.at[2])
    keep_all.start()
    up(1 - p.x)
    keep_pre = pltpu.make_async_copy(pre, pre_hbm, local.at[3])
    keep_hid = pltpu.make_async_copy(hid, hid_hbm, local.at[4])
    keep_pre.start()
    keep_hid.start()
    down(1 - p.x)
    scatter.far_to_core().start()
    scatter.send_over()
    if n:
        spread.start(2, 3)
        spread.relay_late(0)
    down(p.x)
    scatter.near_to_core().start()
    if n:
        spread.relay(1)
        spread.start(3)
    scatter.wait()

    def final(at):
        out_ref[at, :] = x_ref[at, :] + scatter.rows(at) + vec_ref[7:8, :]

    row_chunks(rows, final)
    if n:
        spread.relay(2)
        spread.relay_late(1)
        spread.relay(3)
        spread.relay_late(2)
        spread.relay_late(3)
    gather.finish()
    scatter.finish()
    for copy in (keep_all, keep_pre, keep_hid):
        copy.wait()
    if n:
        spread.finish()


def scatter_scratch(n_tp, rows):
    return [
        pltpu.VMEM((n_tp, rows, D), bf16),
        pltpu.VMEM((2, rows, D), bf16),
        pltpu.VMEM((rows, D), bf16),
        pltpu.VMEM((rows, D), bf16),
        pltpu.SemaphoreType.DMA((6,)),
        pltpu.SemaphoreType.DMA((6,)),
    ]


def params(collective_id):
    return pltpu.CompilerParams(collective_id=collective_id, has_side_effects=True, vmem_limit_bytes=60 * 2**20)


def ff_fwd(x, vecs, fc_bias, w_b, n_tp, shard, collective_id):
    rows, width = x.shape[0], fc_bias.shape[1]
    block = (n_tp, rows)
    operands, results, sems = spread_parts(shard, FF_CHUNKS)
    return pl.pallas_call(
        functools.partial(ff_fwd_kernel, len(operands)),
        out_shape=(
            jax.ShapeDtypeStruct((rows, D), f32),
            jax.ShapeDtypeStruct(block + (D,), bf16),
            jax.ShapeDtypeStruct(block + (width,), f32),
            jax.ShapeDtypeStruct(block + (width,), bf16),
        )
        + results,
        in_specs=[IN_VMEM, IN_VMEM, IN_VMEM, ANY] + [ANY] * len(operands),
        out_specs=(IN_VMEM, ANY, ANY, ANY) + (ANY,) * len(operands),
        scratch_shapes=[
            pltpu.VMEM((D, lanes_up(width)), bf16),
            pltpu.VMEM((D, lanes_up(width)), bf16),
            pltpu.VMEM(block + (D,), bf16),
            pltpu.VMEM(block + (width,), f32),
            pltpu.VMEM(block + (width,), bf16),
        ]
        + scatter_scratch(n_tp, rows)
        + [pltpu.SemaphoreType.DMA((6,))]
        + sems,
        compiler_params=params(collective_id),
        cost_estimate=pl.CostEstimate(
            flops=4 * n_tp * rows * D * width, bytes_accessed=40 * 2**20, transcendentals=n_tp * rows * width
        ),
    )(x, vecs, fc_bias, w_b, *operands)


def gelu_slope(u):
    a = 0.7978845608028654
    square = u * u
    t = jnp.tanh(a * (u + 0.044715 * u * square))
    return 0.5 * (1.0 + t) + 0.5 * u * (1.0 - t * t) * (a * (1.0 + 3 * 0.044715 * square))


def norm_back(x, dy, gain):
    hat, scale = norm_stats(x)
    d_hat = dy * gain
    inner = d_hat - jnp.mean(d_hat, -1, keepdims=True) - hat * jnp.mean(d_hat * hat, -1, keepdims=True)
    return scale * inner, dy * hat


def add_rows(ref, row, value):
    ref[row : row + 1, :] += jnp.sum(value, axis=0, keepdims=True)


def ff_bwd_kernel(n, *refs):
    g_ref, x_ref, vec_ref, all_hbm, pre_hbm, hid_hbm, wb_hbm = refs[:7]
    sources, refs = refs[7 : 7 + n], refs[7 + n :]
    out_ref, sums_ref, fcb_ref, dfc_hbm, dproj_hbm = refs[:5]
    results, refs = refs[5 : 5 + 2 * n], refs[5 + 2 * n :]
    wfc, wproj, buf, other, pre, dpre, stage, part, from_core, over_out, from_over, send, recv, local = refs[:14]
    p, g = Peers(), Group()
    sums = reduces(g, sources, results, refs[14:])
    rows = x_ref.shape[0]
    n_tp, width = buf.shape[0], fcb_ref.shape[1]
    sems = (send, recv)
    gather = Gather(p, buf, sems)
    scatter = Scatter(p, part, from_core, over_out, from_over, sems)
    weights = FeedForward(wb_hbm, wfc, wproj, width, [local.at[0], local.at[2], local.at[7]])
    load_pre = pltpu.make_async_copy(pre_hbm, pre, local.at[1])
    load_other = pltpu.make_async_copy(hid_hbm, other, local.at[3])
    weights.start()
    for copy in (load_pre, load_other):
        copy.start()
    sums_ref[...] = jnp.zeros_like(sums_ref)
    fcb_ref[...] = jnp.zeros_like(fcb_ref)

    def lower(at):
        low = g_ref[at, :].astype(bf16)
        buf[p.t, at, :] = low
        add_rows(sums_ref, 7, low.astype(f32))

    row_chunks(rows, lower)
    if n:
        g.greet(p)
    else:
        p.greet()
    gather.start()
    steps = in_turn(sums) if n else []

    def advance():
        if steps:
            steps.pop(0)()

    advance()
    gather.wait_chip()
    weights.wait()
    load_pre.wait()

    def through(x):
        def tile(at):
            d_hidden = mm(pair_rows(buf, x), wproj[:, at])
            u = pre[pl.ds(2 * x, 2), :, at].reshape(2 * rows, -1)
            low = (gelu_slope(u) * d_hidden).astype(bf16)
            put_pair(dpre, x, at, low)
            fcb_ref[:, at] += jnp.sum(low.astype(f32), axis=0, keepdims=True)

        tiles(width, tile)

    def down(x):
        def tile(at):
            put_pair(part, x, at, mm(pair_rows(dpre, x), wfc[at, :width], NT))

        tiles(D, tile)

    through(p.x)
    gather.relay()
    advance()
    gather.wait_diag()
    through(1 - p.x)
    advance()
    down(1 - p.x)
    scatter.far_to_core().start()
    scatter.send_over()
    advance()
    down(p.x)
    scatter.near_to_core().start()
    advance()

    def outer(left, right, target, sem):
        whole = D // TILE
        rest = D - whole * TILE
        flat = right[...].reshape(n_tp * rows, width)

        def tile(i, size):
            at = pl.ds(pl.multiple_of(i * TILE, TILE), size)
            value = mm(left[:, :, at].reshape(n_tp * rows, size), flat, TN)
            stage[at, :] = value.astype(bf16)

        @pl.loop(0, whole)
        def _(i):
            tile(i, TILE)

        if rest:
            tile(whole, rest)
        return pltpu.make_async_copy(stage, target, sem)

    load_other.wait()
    store = outer(buf, other, dproj_hbm, local.at[4])
    store.start()
    gather.finish()
    load_all = pltpu.make_async_copy(all_hbm, buf, local.at[5])
    load_all.start()
    advance()
    scatter.wait()

    def final(at):
        dy = scatter.rows(at)
        dx, d_gain = norm_back(x_ref[at, :], dy, vec_ref[5:6, :])
        add_rows(sums_ref, 5, d_gain)
        add_rows(sums_ref, 6, dy)
        out_ref[at, :] = g_ref[at, :] + dx

    row_chunks(rows, final)
    load_all.wait()
    store.wait()
    store = outer(buf, dpre, dfc_hbm, local.at[6])
    store.start()
    while steps:
        advance()
    scatter.finish()
    store.wait()
    for i, item in enumerate(sums):
        item.finish(arrived=i == 0)


def ff_bwd(grad, x, vecs, all_rows, pre, hidden, w_b, n_tp, payload, collective_id):
    rows, width = x.shape[0], pre.shape[2]
    block = (n_tp, rows)
    operands, results, more = reduce_parts(payload)
    return pl.pallas_call(
        functools.partial(ff_bwd_kernel, len(payload)),
        out_shape=(
            jax.ShapeDtypeStruct((rows, D), f32),
            jax.ShapeDtypeStruct((8, D), f32),
            jax.ShapeDtypeStruct((1, width), f32),
            jax.ShapeDtypeStruct((D, width), bf16),
            jax.ShapeDtypeStruct((D, width), bf16),
        )
        + results,
        in_specs=[IN_VMEM] * 3 + [ANY] * (4 + len(payload)),
        out_specs=(IN_VMEM, IN_VMEM, IN_VMEM) + (ANY,) * (2 + 2 * len(payload)),
        scratch_shapes=[
            pltpu.VMEM((D, lanes_up(width)), bf16),
            pltpu.VMEM((D, lanes_up(width)), bf16),
            pltpu.VMEM(block + (D,), bf16),
            pltpu.VMEM(block + (width,), bf16),
            pltpu.VMEM(block + (width,), f32),
            pltpu.VMEM(block + (width,), bf16),
            pltpu.VMEM((D, width), bf16),
        ]
        + scatter_scratch(n_tp, rows)
        + [pltpu.SemaphoreType.DMA((8,))]
        + more,
        compiler_params=params(collective_id),
        cost_estimate=pl.CostEstimate(
            flops=8 * n_tp * rows * D * width, bytes_accessed=50 * 2**20, transcendentals=n_tp * rows * width
        ),
    )(grad, x, vecs, all_rows, pre, hidden, w_b, *operands)


HALVES = [(micro, half) for micro in range(MICRO) for half in range(2)]


def half_lanes(half):
    return slice(half * WIDE // 2, (half + 1) * WIDE // 2)


class Share:
    def __init__(self, group, kv, sems):
        self.g, self.kv, self.sems = group, kv, sems
        self.partner = group.at(group.z, 1 - group.y)

    def piece(self, member, part, index, to):
        micro, half = part
        ref = self.kv.at[member, micro, :, :, half_lanes(half)]
        return self.g.copy(ref, ref, self.sems, (2 * micro + half) * 7 + index, to)

    def own(self, part):
        g = self.g
        return [self.piece(g.member, part, 0, self.partner)] + [
            self.piece(g.member, part, k, g.at(g.ahead(k), g.y)) for k in (1, 2, 3)
        ]

    def relayed(self, part):
        g = self.g
        return [self.piece(g.at(g.behind(k), g.y), part, 3 + k, self.partner) for k in (1, 2, 3)]

    def start(self, *part):
        for copy in self.own(part):
            copy.start()

    def relay(self, *part):
        g = self.g
        for k, copy in zip((1, 2, 3), self.relayed(part)):
            self.piece(g.at(g.behind(k), g.y), part, k, self.partner).wait_recv()
            copy.start()

    def wait(self, *part):
        g = self.g
        self.piece(self.partner, part, 0, self.partner).wait_recv()
        for k in (1, 2, 3):
            self.piece(g.at(g.behind(k), 1 - g.y), part, 3 + k, self.partner).wait_recv()

    def finish(self):
        for part in HALVES:
            for copy in self.own(part) + self.relayed(part):
                copy.wait_send()


class GroupSum:
    def __init__(self, group, parts, from_y, to_z, from_z, sems):
        self.g, self.parts, self.sems = group, parts, sems
        self.from_y, self.to_z, self.from_z = from_y, to_z, from_z

    def across(self, micro, half):
        g, lanes = self.g, half_lanes(half)
        return g.copy(
            self.parts.at[micro, :, 1 - g.y, :, :, lanes],
            self.from_y.at[micro, :, :, :, lanes],
            self.sems,
            (2 * micro + half) * 4,
            g.at(g.z, 1 - g.y),
        )

    def along(self, micro, half, k):
        g, lanes = self.g, half_lanes(half)
        to = g.ahead(k)
        return g.copy(
            self.to_z.at[micro, to, :, :, lanes],
            self.from_z.at[micro, k - 1, :, :, lanes],
            self.sems,
            (2 * micro + half) * 4 + k,
            g.at(to, g.y),
        )

    def start(self, micro, half):
        self.across(micro, half).start()

    def turn(self, micro, half):
        lanes = half_lanes(half)
        self.across(micro, half).wait_recv()

        @pl.loop(0, 4)
        def _(z):
            for kv in range(2):
                total = self.parts[micro, z, self.g.y, kv, :, lanes] + self.from_y[micro, z, kv, :, lanes]
                self.to_z[micro, z, kv, :, lanes] = total

        for k in (1, 2, 3):
            self.along(micro, half, k).start()

    def wait(self, micro):
        for half in range(2):
            for k in (1, 2, 3):
                self.along(micro, half, k).wait_recv()

    def total(self, micro, kv):
        g = self.g
        value = self.parts[micro, g.z, g.y, kv].astype(f32) + self.from_y[micro, g.z, kv].astype(f32)
        for k in range(3):
            value = value + self.from_z[micro, k, kv].astype(f32)
        return value.astype(bf16)

    def finish(self, micro):
        for half in range(2):
            self.across(micro, half).wait_send()
            for k in (1, 2, 3):
                self.along(micro, half, k).wait_send()


WIDE = 512
HEAD_PAIRS = WIDE // (2 * HEAD)
PROMPT_CHUNKS = PROMPT // CHUNK
CONT_CHUNKS = CONT_LEN // CHUNK


def chunk_at(c, base=0):
    return pl.ds(pl.multiple_of(base + c * CHUNK, CHUNK), CHUNK)


def key_limit(member):
    row = lax.broadcasted_iota(jnp.int32, (1, TOK_DEV), 1)
    return jnp.where(row < PROMPT_DEV, member * PROMPT_DEV + row, PROMPT - PROMPT_DEV + row)


def half_of(value, half):
    lane = lax.broadcasted_iota(jnp.int32, value.shape, 1)
    return jnp.where((lane >= HEAD * half) & (lane < HEAD * (half + 1)), value, jnp.zeros_like(value))


def fold(value, op):
    return op(value.reshape(value.shape[0] // 8, 8, value.shape[1]), axis=0)


def over_keys(body, prompt, own, carry):
    carry = lax.fori_loop(0, PROMPT_CHUNKS, lambda c, carry: body(c, lambda i: prompt(c, i), carry), carry)
    return lax.fori_loop(
        0, CONT_CHUNKS, lambda c, carry: body(PROMPT_CHUNKS + c, lambda i: own(c, i), carry), carry
    )


def head_pairs(head, finish):
    @pl.loop(0, HEAD_PAIRS)
    def _(pair):
        lanes = pl.ds(pl.multiple_of(pair * 2 * HEAD, 2 * HEAD), 2 * HEAD)
        head(pair, lanes, 0)

        @pl.when(pair < HEAD_PAIRS - 1)
        def _():
            head(pair, lanes, 1)

        finish(pair, lanes)


def run_hooks(hooks, micro, pair, half):
    for at in range(HEAD_PAIRS):
        if half == 0 and (micro, at) in hooks:

            @pl.when(pair == at)
            def _(at=at):
                for hook in hooks[micro, at]:
                    hook()


def to_slots(target, micro, first, value, lanes):
    per = target.shape[1] // MICRO
    row = first
    while row < first + value.shape[0]:
        slot, within = row // per, row % per
        count = min(per - within, first + value.shape[0] - row)
        target[slot, micro * per + within : micro * per + within + count, lanes] = value[
            row - first : row - first + count
        ]
        row += count


def pair_to_blocks(target, x, value):
    per = value.shape[0] // (2 * MICRO)
    for core in range(2):
        for micro in range(MICRO):
            at = pl.ds(pl.multiple_of((2 * x + core) * per, per), per)
            first = (core * MICRO + micro) * per
            target[micro, at, :] = value[first : first + per]


def attn_fwd_kernel(n, *refs):
    x_ref, vec_ref, bias_ref, wqkv_hbm = refs[:4]
    shard, refs = refs[4 : 4 + n], refs[4 + n :]
    out_ref, lse_ref, all_hbm, own_hbm, kv_hbm, mix_hbm, wout_hbm = refs[:7]
    whole, refs = refs[7 : 7 + n], refs[7 + n :]
    wqkv, wout, wparts, buf, own, kv, mix, s_ref, p_ref, o_ref = refs[:10]
    part, from_core, over_out, from_over, send, recv, gsend, grecv, wsend, wrecv, local = refs[10:21]
    msend, mrecv = refs[21:23]
    p, g = Peers(), Group()
    spread = Spread(g, shard[0], whole[0], refs[23:], ATTN_CHUNKS) if n else None
    mixes = BlockGather(p, mix, mix_hbm, (msend, mrecv), 0, local.at[5])
    rows = x_ref.shape[0]
    n_tp = buf.shape[0]
    step = HEADS // n_tp * HEAD
    width = wparts.shape[1]
    sems = (send, recv)
    gather = Gather(p, buf, sems)
    scatter = Scatter(p, part, from_core, over_out, from_over, sems)
    share = Share(g, kv, (gsend, grecv))
    projections = Projections(wqkv_hbm, wqkv, step, width, [local.at[k] for k in (0, 7, 8, 9, 10)])
    projections.start()

    spans = ((3 * step, 4 * step, 0, step), (4 * step + 128, 4 * step + 256, step, WIDE))

    def rows_for(t, k):
        return wqkv_hbm.at[pl.ds(pl.multiple_of(t * step, 128), width), spans[k][0] : spans[k][1]]

    def part_of(t, k):
        return wparts.at[t, :, spans[k][2] : spans[k][3]]

    keep_parts = [
        pltpu.make_async_copy(rows_for(p.t, k), part_of(p.t, k), local.at[1 + 10 * k]) for k in range(2)
    ]
    for copy in keep_parts:
        copy.start()
    near = [(2 * i + k, t, k) for i, t in enumerate((p.core, p.over, p.diag)) for k in range(2)]
    give_parts = [p.copy(rows_for(t, k), part_of(p.t, k), (wsend, wrecv), i, t) for i, t, k in near]

    def norm(at):
        hat, _ = norm_stats(x_ref[at, :])
        buf[p.t, at, :] = (hat * vec_ref[0:1, :] + vec_ref[1:2, :]).astype(bf16)

    row_chunks(rows, norm)
    g.greet(p, True)
    gather.start()
    for copy in give_parts:
        copy.start()
    if n:
        spread.start(0, 1)
    gather.wait_chip()
    projections.wait()

    def project(x):
        for i in range(3):
            value = mm(pair_rows(buf, x), wqkv[:, i * WIDE : (i + 1) * WIDE]) + bias_ref[i : i + 1, :]
            low = value.astype(bf16)
            if i == 0:
                low = low * HEAD ** (-0.5)
            pair_to_blocks(own.at[i], x, low)

    project(p.x)
    gather.relay()
    gather.wait_diag()
    project(1 - p.x)
    for micro in range(MICRO):
        for i in range(2):
            kv[g.member, micro, i] = own[1 + i, micro, :PROMPT_DEV, :]
    share.start(0, 0)
    if n:
        spread.start(1, 2)
    hooks = {
        (0, 1): [lambda: share.relay(0, 1), lambda: share.start(1, 0)],
        (0, 2): [lambda: share.wait(0, 1)],
        (0, 3): [lambda: share.relay(1, 0), lambda: share.start(1, 1)],
        (1, 0): [lambda: share.wait(1, 0)],
        (1, 1): [lambda: share.relay(1, 1)],
        (1, 2): [lambda: share.wait(1, 1)],
    }
    if n:
        hooks[0, 0] = [lambda: spread.start(2, 3)]
        hooks[0, 2] += [lambda: spread.relay(1), lambda: spread.relay_late(1)]
        hooks[0, 3] += [lambda: spread.start(3, 4)]
        hooks[1, 1] += [lambda: spread.relay(2), lambda: spread.relay_late(2), lambda: spread.start(4)]
    keep_all = pltpu.make_async_copy(buf, all_hbm, local.at[2])
    keep_own = pltpu.make_async_copy(own, own_hbm, local.at[3])
    keep_all.start()
    keep_own.start()
    limit = key_limit(g.member)
    sub = lax.broadcasted_iota(jnp.int32, (CHUNK, TOK_DEV), 0)

    share.relay(0, 0)
    share.start(0, 1)
    if n:
        spread.relay(0)
        spread.relay_late(0)
    share.wait(0, 0)

    for micro in range(MICRO):

        def head(pair, lanes, half, micro=micro):
            run_hooks(hooks, micro, pair, half)
            qh = half_of(own[0, micro, :, lanes], half)

            def first(c, load, top):
                s = jnp.where(sub + c * CHUNK <= limit, mm(load(0), qh, NT), -1e30)
                s_ref[chunk_at(c), :] = s
                return jnp.maximum(top, fold(s, jnp.max))

            top = over_keys(
                first,
                lambda c, i: kv[c, micro, i, :, lanes],
                lambda c, i: own[1 + i, micro, chunk_at(c, PROMPT_DEV), lanes],
                jnp.full((8, TOK_DEV), -1e30, f32),
            )
            top = jnp.max(top, axis=0, keepdims=True)

            def second(c, total):
                e = jnp.exp(s_ref[chunk_at(c), :] - top)
                p_ref[chunk_at(c), :] = e.astype(bf16)
                return total + fold(e, jnp.sum)

            total = lax.fori_loop(0, KEYS // CHUNK, second, jnp.zeros((8, TOK_DEV), f32))
            total = jnp.sum(total, axis=0, keepdims=True)
            values = kv[:, micro, 1, :, lanes].reshape(PROMPT, 2 * HEAD)
            out = mm(values, p_ref[:PROMPT, :], TN) + mm(own[2, micro, PROMPT_DEV:, lanes], p_ref[PROMPT:, :], TN)
            at = slice(HEAD * half, HEAD * (half + 1))
            o_ref[at, :] = out[at, :] / total
            lse_ref[micro, pair, half : half + 1, :] = top + jnp.log(total)

        def finish(pair, lanes, micro=micro):
            @pl.when(pair == HEAD_PAIRS - 1)
            def _():
                o_ref[HEAD:, :] = jnp.zeros((HEAD, TOK_DEV), f32)

            to_slots(mix, micro, 0, o_ref[...].T.astype(bf16), lanes)

        head_pairs(head, finish)

    keep_kv = pltpu.make_async_copy(kv, kv_hbm, local.at[4])
    keep_kv.start()
    for copy in keep_parts:
        copy.wait()
    for i, t, k in near:
        p.copy(rows_for(t, k), part_of(t, k), (wsend, wrecv), i, t).wait_recv()
    for t in range(n_tp):
        wout[:width, t * step : (t + 1) * step] = wparts[t, :, :step]
    wout[:width, n_tp * step :] = wparts[n_tp - 1, :, width : 2 * width - step]
    wout[width:, :] = jnp.zeros((WIDE - width, D), bf16)

    @pl.when(p.t < n_tp - 1)
    def _():
        wout[step:width, :] = jnp.zeros((width - step, D), bf16)

    keep_out = pltpu.make_async_copy(wout, wout_hbm, local.at[6])
    keep_out.start()

    def down(x):
        def tile(at):
            put_pair(part, x, at, mm(pair_rows(mix, x), wout[:, at]))

        tiles(D, tile)

    down(1 - p.x)
    scatter.far_to_core().start()
    scatter.send_over()
    down(p.x)
    scatter.near_to_core().start()
    if n:
        spread.relay(3)
        spread.relay_late(3)
    scatter.wait()
    mixes.start()

    def final(at):
        out_ref[at, :] = x_ref[at, :] + (scatter.rows(at) + vec_ref[4:5, :])

    row_chunks(rows, final)
    mixes.relay()
    if n:
        spread.relay(4)
        spread.relay_late(4)
    gather.finish()
    scatter.finish()
    share.finish()
    for copy in give_parts:
        copy.wait_send()
    for copy in (keep_all, keep_own, keep_kv, keep_out):
        copy.wait()
    mixes.finish()
    if n:
        spread.finish()


def attn_shapes(n_tp, rows):
    return (
        ((n_tp, rows, D), bf16),
        ((3, MICRO, TOK_DEV, WIDE), bf16),
        ((GROUP, MICRO, 2, PROMPT_DEV, WIDE), bf16),
        ((n_tp, rows, WIDE), bf16),
    )


def attn_fwd(x, vecs, biases, w_a, n_tp, shard, collective_id):
    rows = x.shape[0]
    width = D - HEADS // n_tp * HEAD * (n_tp - 1)
    saved = attn_shapes(n_tp, rows)
    operands, results, sems = spread_parts(shard, ATTN_CHUNKS)
    return pl.pallas_call(
        functools.partial(attn_fwd_kernel, len(operands)),
        out_shape=(
            jax.ShapeDtypeStruct((rows, D), f32),
            jax.ShapeDtypeStruct((MICRO, HEAD_PAIRS, 8, TOK_DEV), f32),
        )
        + tuple(jax.ShapeDtypeStruct(*s) for s in saved[:3])
        + (jax.ShapeDtypeStruct((n_tp,) + saved[3][0], bf16), jax.ShapeDtypeStruct((WIDE, D), bf16))
        + results,
        in_specs=[IN_VMEM, IN_VMEM, IN_VMEM, ANY] + [ANY] * len(operands),
        out_specs=(IN_VMEM, IN_VMEM) + (ANY,) * (5 + len(operands)),
        scratch_shapes=[pltpu.VMEM((D, 3 * WIDE), bf16), pltpu.VMEM((WIDE, D), bf16), pltpu.VMEM((n_tp, width, WIDE), bf16)]
        + [pltpu.VMEM(*s) for s in saved]
        + [
            pltpu.VMEM((KEYS, TOK_DEV), f32),
            pltpu.VMEM((KEYS, TOK_DEV), bf16),
            pltpu.VMEM((2 * HEAD, TOK_DEV), f32),
        ]
        + scatter_scratch(n_tp, rows)
        + [
            pltpu.SemaphoreType.DMA((14 * MICRO,)),
            pltpu.SemaphoreType.DMA((14 * MICRO,)),
            pltpu.SemaphoreType.DMA((6,)),
            pltpu.SemaphoreType.DMA((6,)),
            pltpu.SemaphoreType.DMA((12,)),
            pltpu.SemaphoreType.DMA((3,)),
            pltpu.SemaphoreType.DMA((3,)),
        ]
        + sems,
        compiler_params=params(collective_id),
        cost_estimate=pl.CostEstimate(flops=10**11, bytes_accessed=30 * 2**20, transcendentals=0),
    )(x, vecs, biases, w_a, *operands)


def attn_bwd_kernel(n, *refs):
    g_ref, x_ref, vec_ref, lse_ref, ff_ref, fcb_ref, all_hbm, own_hbm, kv_hbm, mix_hbm, wqkv_hbm, wout_hbm = refs[:12]
    sources, refs = refs[12 : 12 + n], refs[12 + n :]
    out_ref, dqo_hbm = refs[:2]
    results, refs = refs[2 : 2 + 2 * n], refs[2 + 2 * n :]
    (sums_ref, cols_ref, vectors), refs = refs[:3], refs[3:]
    wqkv, wout, buf, other, mixed, own, kv, gm, dkv, from_y, to_z, from_z, dkc, dqkv, stage, stage_out = refs[:16]
    p_ref, dp_ref, ds_ref, o_ref = refs[16:20]
    part, from_core, over_out, from_over, send, recv, gsend, grecv, local = refs[20:29]
    p, g = Peers(), Group()
    sums = reduces(g, sources, results, refs[29:])
    rows = x_ref.shape[0]
    n_tp = buf.shape[0]
    out_step = HEADS // n_tp * HEAD
    out_width = D - out_step * (n_tp - 1)
    sems = (send, recv)
    gather = Gather(p, buf, sems)
    scatter = Scatter(p, part, from_core, over_out, from_over, sems)
    reduce = GroupSum(g, dkv, from_y, to_z, from_z, (gsend, grecv))
    load_out = pltpu.make_async_copy(wout_hbm, wout, local.at[0])
    load_own = pltpu.make_async_copy(own_hbm, own, local.at[1])
    load_kv = pltpu.make_async_copy(kv_hbm, kv, local.at[2])
    projections = Projections(wqkv_hbm, wqkv, out_step, out_width, [local.at[k] for k in (3, 9, 10, 11, 12)])
    projections.start()
    load_mix = pltpu.make_async_copy(mix_hbm, mixed, local.at[4])
    load_all = pltpu.make_async_copy(all_hbm, other, local.at[6])
    for copy in (load_out, load_own, load_kv, load_mix, load_all):
        copy.start()
    sums_ref[...] = jnp.zeros_like(sums_ref)

    def lower(at):
        low = g_ref[at, :].astype(bf16)
        buf[p.t, at, :] = low
        add_rows(sums_ref, 4, low.astype(f32))

    row_chunks(rows, lower)
    g.greet(p)
    gather.start()
    hooks = {(1, 1): [lambda: reduce.turn(0, 0)], (1, 2): [lambda: reduce.turn(0, 1)]}
    if n:
        first_sum, second_sum = sums
        first_sum.start(1)
        hooks[0, 1] = [lambda: first_sum.pump(2)]
        hooks[0, 2] = [lambda: first_sum.pump(3)]
        hooks[1, 1] += [lambda: second_sum.start(1)]
        hooks[1, 3] = [lambda: second_sum.pump(1, first_sum)]
    gather.wait_chip()
    load_out.wait()

    def mixed_back(x):
        pair_to_blocks(gm, x, mm(pair_rows(buf, x), wout[...], NT).astype(bf16))

    mixed_back(p.x)
    if n:
        first_sum.start(2)
    gather.relay()
    gather.wait_diag()
    if n:
        first_sum.pump(1, then=lambda: first_sum.start(3))
    mixed_back(1 - p.x)
    load_own.wait()
    load_kv.wait()
    limit = key_limit(g.member)
    sub = lax.broadcasted_iota(jnp.int32, (CHUNK, TOK_DEV), 0)


    for micro in range(MICRO):

        def head(pair, lanes, half, micro=micro):
            run_hooks(hooks, micro, pair, half)
            qh = half_of(own[0, micro, :, lanes], half)
            gh = half_of(gm[micro, :, lanes], half)
            lse = lse_ref[micro, pair, half : half + 1, :]

            def first(c, load, inner):
                s = jnp.where(sub + c * CHUNK <= limit, mm(load(0), qh, NT), -1e30)
                e = jnp.exp(s - lse)
                dp = mm(load(1), gh, NT)
                p_ref[chunk_at(c), :] = e
                dp_ref[chunk_at(c), :] = dp
                return inner + fold(e * dp, jnp.sum)

            inner = over_keys(
                first,
                lambda c, i: kv[c, micro, i, :, lanes],
                lambda c, i: own[1 + i, micro, chunk_at(c, PROMPT_DEV), lanes],
                jnp.zeros((8, TOK_DEV), f32),
            )
            inner = jnp.sum(inner, axis=0, keepdims=True)

            def second(c, put):
                e = p_ref[chunk_at(c), :]
                ds = (e * (dp_ref[chunk_at(c), :] - inner)).astype(bf16)
                ds_ref[chunk_at(c), :] = ds
                put(0, mm(ds, qh))
                put(1, mm(e.astype(bf16), gh))

            @pl.loop(0, PROMPT_CHUNKS)
            def _(c):
                def put(i, value):
                    at = (micro, c // 2, c % 2, i, slice(None), lanes)
                    if half:
                        value = value + dkv[at].astype(f32)
                    dkv[at] = value.astype(bf16)

                second(c, put)

            @pl.loop(0, CONT_CHUNKS)
            def _(c):
                def put(i, value):
                    at = (i, chunk_at(c), lanes)
                    if half:
                        value = value + dkc[at].astype(f32)
                    dkc[at] = value.astype(bf16)

                second(PROMPT_CHUNKS + c, put)

            keys = kv[:, micro, 0, :, lanes].reshape(PROMPT, 2 * HEAD)
            dq = mm(keys, ds_ref[:PROMPT, :], TN) + mm(own[1, micro, PROMPT_DEV:, lanes], ds_ref[PROMPT:, :], TN)
            at = slice(HEAD * half, HEAD * (half + 1))
            o_ref[at, :] = dq[at, :] * HEAD ** (-0.5)

        def finish(pair, lanes, micro=micro):
            @pl.when(pair == HEAD_PAIRS - 1)
            def _():
                o_ref[HEAD:, :] = jnp.zeros((HEAD, TOK_DEV), f32)

            to_slots(dqkv, micro, 0, o_ref[...].T.astype(bf16), lanes)

            @pl.when(pair == HEAD_PAIRS // 2 - 1)
            def _():
                reduce.start(micro, 0)

        head_pairs(head, finish)
        reduce.start(micro, 1)
        for i in range(2):
            to_slots(dqkv, micro, PROMPT_DEV, dkc[i], slice((1 + i) * WIDE, (2 + i) * WIDE))

    load_mix.wait()
    columns = pl.ds(pl.multiple_of(p.t * out_step, 128), out_width)

    def outer(source, target, right, body):
        flat = right.reshape(n_tp * rows, right.shape[-1])

        def tile(at):
            left = source[:, :, at].reshape(n_tp * rows, -1)
            target[at, : flat.shape[1]] = mm(left, flat, TN).astype(bf16)

        body(D, tile)

    reduce.turn(1, 0)
    stage_out[:, out_width:] = jnp.zeros((D, WIDE - out_width), bf16)
    low = buf[:, :, columns].reshape(n_tp * rows, out_width)
    for t in range(n_tp):
        count = out_step if t < n_tp - 1 else out_width
        value = mm(mixed[t].reshape(n_tp * rows, WIDE), low, TN).astype(bf16)
        stage_out[t * out_step : t * out_step + count, :out_width] = value[:count, :]
    keep_out = pltpu.make_async_copy(
        stage_out.at[:, :out_step], dqo_hbm.at[:, 3 * WIDE : 3 * WIDE + out_step], local.at[5]
    )
    keep_out.start()
    reduce.turn(1, 1)
    if n:
        second_sum.start(2)
    for micro in range(MICRO):
        reduce.wait(micro)
        for i in range(2):
            to_slots(dqkv, micro, 0, reduce.total(micro, i), slice((1 + i) * WIDE, (2 + i) * WIDE))
    if n:
        second_sum.pump(2, first_sum, lambda: second_sum.start(3))
    projections.wait()

    def down(x):
        def tile(at):
            put_pair(part, x, at, mm(pair_rows(dqkv, x), wqkv[at, :], NT))

        tiles(D, tile)

    down(1 - p.x)
    scatter.far_to_core().start()
    scatter.send_over()
    down(p.x)
    scatter.near_to_core().start()
    if n:
        second_sum.pump(3, first_sum, lambda: second_sum.start(0))
        first_sum.start(0)
    load_all.wait()
    outer(other, stage, dqkv[...], tiles)
    keep_qkv = pltpu.make_async_copy(stage, dqo_hbm.at[:, : 3 * WIDE], local.at[7])
    keep_qkv.start()
    cols_ref[...] = jnp.zeros_like(cols_ref)

    @pl.loop(0, n_tp * rows // ROW_CHUNK)
    def _(i):
        per = rows // ROW_CHUNK
        at = pl.ds(pl.multiple_of((i % per) * ROW_CHUNK, ROW_CHUNK), ROW_CHUNK)
        add_rows(cols_ref, 0, dqkv[i // per, at, :].astype(f32))

    scatter.wait()

    def final(at):
        dy = scatter.rows(at)
        dx, d_gain = norm_back(x_ref[at, :], dy, vec_ref[0:1, :])
        add_rows(sums_ref, 0, d_gain)
        add_rows(sums_ref, 1, dy)
        out_ref[at, :] = g_ref[at, :] + dx

    row_chunks(rows, final)
    vectors[...] = jnp.zeros_like(vectors)
    vectors[0:2, :] = sums_ref[0:2, :]
    vectors[2:3, columns] = cols_ref[:, :out_width]
    vectors[3:4, columns] = cols_ref[:, 2 * WIDE : 2 * WIDE + out_width]
    vectors[4:5, :] = sums_ref[4:5, :]
    vectors[5:8, :] = ff_ref[5:8, :]
    vectors[8:9, :] = fcb_ref[...]
    stage_out[:, out_width : out_width + 16] = vectors[...].T.astype(bf16)
    keep_rest = pltpu.make_async_copy(
        stage_out.at[:, out_step:], dqo_hbm.at[:, 3 * WIDE + out_step :], local.at[8]
    )
    keep_rest.start()
    gather.finish()
    scatter.finish()
    for micro in range(MICRO):
        reduce.finish(micro)
    keep_out.wait()
    keep_rest.wait()
    keep_qkv.wait()
    for i, item in enumerate(sums):
        item.finish(i < n - 1)


def attn_bwd(grad, x, vecs, lse, ff_sums, fc_bias_sums, all_rows, own, kv, mixed_all, w_a, w_out, n_tp, payload, collective_id):
    rows = x.shape[0]
    operands, results, more = reduce_parts(payload)
    pieces = (MICRO, 4, 2, 2, PROMPT_DEV, WIDE)
    return pl.pallas_call(
        functools.partial(attn_bwd_kernel, len(payload)),
        out_shape=(
            jax.ShapeDtypeStruct((rows, D), f32),
            jax.ShapeDtypeStruct((D, 4 * WIDE), bf16),
        )
        + results,
        in_specs=[IN_VMEM] * 6 + [ANY] * (6 + len(payload)),
        out_specs=(IN_VMEM,) + (ANY,) * (1 + 2 * len(payload)),
        scratch_shapes=[
            pltpu.VMEM((8, D), f32),
            pltpu.VMEM((1, 3 * WIDE), f32),
            pltpu.VMEM((16, D), f32),
            pltpu.VMEM((D, 3 * WIDE), bf16),
            pltpu.VMEM((WIDE, D), bf16),
            pltpu.VMEM((n_tp, rows, D), bf16),
            pltpu.VMEM((n_tp, rows, D), bf16),
            pltpu.VMEM((n_tp, n_tp, rows, WIDE), bf16),
            pltpu.VMEM((3, MICRO, TOK_DEV, WIDE), bf16),
            pltpu.VMEM((GROUP, MICRO, 2, PROMPT_DEV, WIDE), bf16),
            pltpu.VMEM((MICRO, TOK_DEV, WIDE), bf16),
            pltpu.VMEM(pieces, bf16),
            pltpu.VMEM((MICRO, 4, 2, PROMPT_DEV, WIDE), bf16),
            pltpu.VMEM((MICRO, 4, 2, PROMPT_DEV, WIDE), bf16),
            pltpu.VMEM((MICRO, 3, 2, PROMPT_DEV, WIDE), bf16),
            pltpu.VMEM((2, CONT_LEN, WIDE), bf16),
            pltpu.VMEM((n_tp, rows, 3 * WIDE), bf16),
            pltpu.VMEM((D, 3 * WIDE), bf16),
            pltpu.VMEM((D, WIDE), bf16),
            pltpu.VMEM((KEYS, TOK_DEV), f32),
            pltpu.VMEM((KEYS, TOK_DEV), f32),
            pltpu.VMEM((KEYS, TOK_DEV), bf16),
            pltpu.VMEM((2 * HEAD, TOK_DEV), f32),
        ]
        + scatter_scratch(n_tp, rows)
        + [
            pltpu.SemaphoreType.DMA((8 * MICRO,)),
            pltpu.SemaphoreType.DMA((8 * MICRO,)),
            pltpu.SemaphoreType.DMA((13,)),
        ]
        + more,
        compiler_params=params(collective_id),
        cost_estimate=pl.CostEstimate(flops=2 * 10**11, bytes_accessed=50 * 2**20, transcendentals=0),
    )(grad, x, vecs, lse, ff_sums, fc_bias_sums, all_rows, own, kv, mixed_all, w_a, w_out, *operands)


def forward_layer(x, layer, fetch, vecs, fc_bias, cols, n_tp):
    width = D - HEADS // n_tp * HEAD * (n_tp - 1)
    query_bias, value_bias = (lax.dynamic_slice_in_dim(vecs[i], cols, width) for i in (2, 3))
    biases = widen(jnp.stack([query_bias, jnp.zeros_like(query_bias), value_bias]))
    w_a = fetch.weights[layer, "a"]
    x_mid, lse, all_rows, own, kv, mixed, w_out = fetch.during(
        (layer, "b"), lambda shard: attn_fwd(x, vecs, biases, w_a, n_tp, shard, 5 + layer)
    )
    w_b = fetch.weights[layer, "b"]
    x_next, second_all, hidden_pre, hidden = fetch.during(
        (layer + 1, "a"), lambda shard: ff_fwd(x_mid, vecs, fc_bias[None], w_b, n_tp, shard, 1 + layer)
    )
    return x_next, (x, w_out, lse, all_rows, own, kv, mixed, x_mid, second_all, hidden_pre, hidden)


class Fetch:
    def __init__(self, shards):
        self.staged = lax.axis_size("fsdp") == GROUP
        self.shards, self.weights = shards, {}
        last = None
        for key, shard in shards.items():
            if self.staged:
                if last is None:
                    last = spread_only(shard, FIRST_CHUNKS, 9)
                    self.weights[key] = last.reshape(-1, shard.shape[1])
                continue
            if last is not None:
                shard, _ = lax.optimization_barrier((shard, last))
            whole = lax.all_gather(shard, "fsdp", axis=0, tiled=True)
            self.weights[key] = whole
            last = whole[:8, :128]

    def during(self, key, kernel):
        if not self.staged or key not in self.shards:
            return kernel(None)
        *results, whole = kernel(self.shards[key])
        self.weights[key] = whole.reshape(-1, whole.shape[2])
        return results


def fsdp_sum(part):
    return lax.psum_scatter(part, "fsdp", scatter_dimension=0, tiled=True).astype(f32)


def heads_joined(parts, n_tp):
    step = HEADS // n_tp * HEAD
    return jnp.concatenate([parts[t][..., :step] for t in range(n_tp - 1)] + [parts[n_tp - 1]], axis=-1)


def widen(value, axis=-1):
    pads = [(0, 0)] * value.ndim
    pads[axis] = (0, WIDE - value.shape[axis])
    return jnp.pad(value, pads)


def by_owner(part):
    return part.reshape(4, 2, -1, part.shape[1])


def backward(grad, weights, vecs, saves, n_tp):
    width = D - HEADS // n_tp * HEAD * (n_tp - 1)
    staged = lax.axis_size("fsdp") == GROUP
    done, waiting = {}, {}

    def during(keys, kernel):
        keys = [key for key in keys if key in waiting]
        payload = [waiting.pop(key) for key in keys]
        results = list(kernel(payload))
        if payload:
            arrived = results[-2 * len(payload) :]
            results = results[: -2 * len(payload)]
            for i, key in enumerate(keys):
                done[key] = (payload[i], arrived[2 * i], arrived[2 * i + 1])
        return results

    def produced(key, value):
        if staged:
            waiting[key] = by_owner(value)
        else:
            done[key] = fsdp_sum(value)

    for layer in reversed(range(LAYERS)):
        w_a, w_b = weights[layer, "a"], weights[layer, "b"]
        x, w_out, lse, all_rows, own, kv, mixed_all, x_mid, second_all, hidden_pre, hidden = saves[layer]
        grad, ff_sums, fc_bias_sums, grad_fc, grad_proj = during(
            [(layer + 1, "qo")],
            lambda payload: ff_bwd(
                grad, x_mid, vecs[layer], second_all, hidden_pre, hidden, w_b, n_tp, payload, 10 + layer
            ),
        )
        produced((layer, "proj"), grad_proj)
        produced((layer, "fc"), grad_fc)
        grad, grad_qo = during(
            [(layer, "proj"), (layer, "fc")],
            lambda payload: attn_bwd(
                grad, x, vecs[layer], lse, ff_sums, fc_bias_sums, all_rows, own, kv, mixed_all,
                w_a, w_out, n_tp, payload, 20 + layer,
            ),
        )
        produced((layer, "qo"), grad_qo)
    if staged:
        got = last_sum(waiting[0, "qo"], done[1, "qo"], n_tp, 30)
        return grad, assemble([(got[k],) + done[k, "proj"] + done[k, "fc"] for k in range(LAYERS)])
    outs = []
    for layer in range(LAYERS):
        qo = done[layer, "qo"]
        got = lax.all_gather(qo.astype(bf16), "tp")
        qkv_grad = jnp.concatenate(
            [heads_joined(got[:, :, i * WIDE : i * WIDE + width], n_tp) for i in range(3)], axis=1
        )
        out_grad = heads_joined(got[:, :, 3 * WIDE : 3 * WIDE + width], n_tp)
        vector_sum = jnp.sum(got[:, :, 3 * WIDE + width : 3 * WIDE + width + 8].astype(f32), 0).T
        rest = (vector_sum[v] for v in range(8))
        outs.append((qkv_grad, out_grad, done[layer, "fc"], done[layer, "proj"].T, *rest, qo[:, 3 * WIDE + width + 8]))
    return grad, tuple(jnp.stack(pair).astype(f32) for pair in zip(*outs))


def local(
    tokens,
    qkv_weight,
    query_bias,
    value_bias,
    out_weight,
    out_bias,
    fc_weight,
    fc_bias,
    proj_weight,
    proj_bias,
    first_gain,
    first_bias,
    second_gain,
    second_bias,
    out_grad,
):
    n_tp = lax.axis_size("tp")
    tp = lax.axis_index("tp")
    row_count = tokens.shape[1]
    step = HEADS // n_tp * HEAD
    width = D - step * (n_tp - 1)
    cols = tp * step

    vectors = jnp.stack(
        [first_gain, first_bias, query_bias, value_bias, out_bias, second_gain, second_bias, proj_bias, fc_bias[:, 0]]
    ).reshape(9 * LAYERS, -1)

    shards = {}
    for layer in range(LAYERS):
        sides = [lax.dynamic_slice_in_dim(qkv_weight[layer], cols + i * D, width, 1) for i in range(3)]
        sides.append(lax.dynamic_slice_in_dim(out_weight[layer], cols, width, 1))
        sides = [side[:, :step] for side in sides] + [side[:, step:] for side in sides]
        if layer == 0:
            sides.append(jnp.pad(vectors.T, ((0, 0), (0, 128 - 9 * LAYERS))))
        shards[layer, "a"] = jnp.concatenate(sides, axis=1)
        fc, proj = fc_weight[layer], proj_weight[layer].T
        main = lanes_down(fc.shape[1])
        shards[layer, "b"] = jnp.concatenate([fc[:, :main], proj[:, :main], fc[:, main:], proj[:, main:]], axis=1)
    fetch = Fetch(shards)
    beside = 4 * width
    vectors = fetch.weights[0, "a"][:, beside : beside + 9 * LAYERS].T.astype(f32).reshape(9, LAYERS, D)

    state = tokens.astype(f32).reshape(MICRO * row_count, D)
    saves = []
    for layer in range(LAYERS):
        state, saved = forward_layer(state, layer, fetch, vectors[:8, layer], vectors[8, layer], cols, n_tp)
        saves.append(saved)
    out_tokens = state.astype(bf16).reshape(tokens.shape)
    grad = out_grad.astype(f32).reshape(MICRO * row_count, D)
    grad, (qkv_g, out_g, fc_g, proj_g, *vec_g) = backward(
        grad, fetch.weights, [vectors[:8, layer] for layer in range(LAYERS)], saves, n_tp
    )
    return (
        out_tokens,
        grad.reshape(tokens.shape),
        qkv_g,
        vec_g[2],
        vec_g[3],
        out_g,
        vec_g[4],
        fc_g,
        vec_g[8][:, None],
        proj_g,
        vec_g[7],
        vec_g[0],
        vec_g[1],
        vec_g[5],
        vec_g[6],
    )


def solution(mesh):
    rows = P(None, ("fsdp", "tp"), None)
    weight = P(None, "fsdp", None)
    vector = P(None, "fsdp")
    fc_in = P(None, "fsdp", "tp")
    hidden = P(None, "tp", "fsdp")
    in_specs = (
        rows, weight, vector, vector, weight, vector, fc_in, hidden, hidden,
        vector, vector, vector, vector, vector, rows,
    )
    out_specs = (
        rows, rows, weight, vector, vector, weight, vector, fc_in, hidden, hidden,
        vector, vector, vector, vector, vector,
    )
    return jax.shard_map(local, mesh=mesh, in_specs=in_specs, out_specs=out_specs, check_vma=False)
```
